32 devices in a mesh: gx: 4 (over z), gy: 4 (over y, core), gz: 2 (over x).
Axes of the slice: x: 2, y: 2, z: 4, core: 2. Of those that a mesh axis runs over, the one named last changes fastest.
Arguments:
- hidden_atoms: float32 [256, 256], P(('gx', 'gy', 'gz')), may hold values from -6 to 6
- edge_states: float32 [7680, 512], P(('gx', 'gy', 'gz')), may hold values from -6 to 6
- edge_vectors: float32 [3, 7680], P(None, ('gx', 'gy', 'gz')), may hold values from -11 to 11, as said below
- atom_tags: int32 [256], P(('gx', 'gy', 'gz')), may hold values from 0 to 2
- send_list: int32 [128], P(('gx', 'gy', 'gz')), may hold values from 0 to 7, as said below
- sources: int32 [7680], P(('gx', 'gy', 'gz')), may hold values from 0 to 115, as said below
- trip_slots: int32 [7680, 8], P(('gx', 'gy', 'gz')), may hold values from 0 to 29
- triplet_mask: int32 [7680, 8], P(('gx', 'gy', 'gz')), may hold values 0 or 1
- quad_slots: int32 [7680, 8], P(('gx', 'gy', 'gz')), may hold values from 0 to 29
- quad_mask: int32 [7680, 8], P(('gx', 'gy', 'gz')), may hold values 0 or 1
- edge_mask: int32 [7680], P(('gx', 'gy', 'gz')), may hold values 0 or 1
- w_inputs: bfloat16 [2, 512, 512], replicated, may hold values from -0.25 to 0.25
- w_radial: bfloat16 [5, 128, 512], replicated, may hold values from -0.5 to 0.5
- w_trip_down: bfloat16 [512, 64], replicated, may hold values from -0.25 to 0.25
- triplet_bilinear_weight: bfloat16 [1024, 64], replicated, may hold values from -0.75 to 0.75
- w_trip_up: bfloat16 [64, 512], replicated, may hold values from -0.75 to 0.75
- w_quad_down: bfloat16 [512, 32], replicated, may hold values from -0.25 to 0.25
- w_quad_bil: bfloat16 [1024, 32], replicated, may hold values from -1 to 1
- w_quad_up: bfloat16 [32, 512], replicated, may hold values from -1 to 1
- w_atom_edge: bfloat16 [2, 256, 512], replicated, may hold values from -0.375 to 0.375
- w_residual: bfloat16 [2, 512, 512], replicated, may hold values from -0.25 to 0.25
- w_edge_atom: bfloat16 [2, 512, 256], replicated, may hold values from -0.25 to 0.25
- w_atom_dense: bfloat16 [4, 256, 256], replicated, may hold values from -0.375 to 0.375
- tag_table: bfloat16 [3, 256], replicated, may hold values from -4 to 4
- cot_atoms: float32 [256, 256], P(('gx', 'gy', 'gz')), may hold values from -6 to 6
- cot_edges: float32 [7680, 512], P(('gx', 'gy', 'gz')), may hold values from -6 to 6
- cot_energy: float32 [256, 256], P(('gx', 'gy', 'gz')), may hold values from -6 to 6
Outputs:
- atoms_out: float32 [256, 256], P(('gx', 'gy', 'gz'))
- edges_out: float32 [7680, 512], P(('gx', 'gy', 'gz'))
- energy_out: float32 [256, 256], P(('gx', 'gy', 'gz'))
- grad_atoms: float32 [256, 256], P(('gx', 'gy', 'gz'))
- grad_edges: float32 [7680, 512], P(('gx', 'gy', 'gz'))
- grad_inputs: float32 [2, 512, 512], replicated
- grad_radial: float32 [5, 128, 512], replicated
- grad_trip_down: float32 [512, 64], replicated
- grad_trip_bil: float32 [1024, 64], replicated
- grad_trip_up: float32 [64, 512], replicated
- grad_quad_down: float32 [512, 32], replicated
- grad_quad_bil: float32 [1024, 32], replicated
- grad_quad_up: float32 [32, 512], replicated
- grad_atom_edge: float32 [2, 256, 512], replicated
- grad_residual: float32 [2, 512, 512], replicated
- grad_edge_atom: float32 [2, 512, 256], replicated
- grad_atom_dense: float32 [4, 256, 256], replicated
- grad_tag_table: float32 [3, 256], replicated
The draws below stay inside these ranges and needn't reach their ends.
Inputs may be any that keep to these rules, and one draw needn't show every extreme that they name: `edge_vectors`: each column's length lies between 2 and 11. `send_list`: the 4 entries of one device are distinct local atom numbers. `sources`: A value under 8 is a local atom other than the edge's target; a value 8 + b * 4 + r names border atom r of the neighbour at offset (b // 9 - 1, (b // 3) % 3 - 1, b % 3 - 1), never offset (0, 0, 0) and never beyond either end of gz.
All inputs are finite; a program needn't handle non-finite values. No bound on the sum of `triplet_mask` or of `quad_mask` or of `edge_mask` on one device may be relied on, other than what follows from the above.
Results may differ from the reference program's by a relative error of at most 0.0009.
Values sent between devices are 32-bit elements; how exact they have to be, the bound alone decides.
No kernel may reach another device: no remote copies, remote signals or barrier semaphores. Data moves between devices by JAX's collectives and lax.ppermute only.
A program may use at most 128 MiB of HBM per device.

```python
import functools
import math
import jax
import jax.numpy as jnp
from jax import lax

ATOM_EMB = 256
EDGE_EMB = 512
TRIPLET_WIDTH = 64
QUAD_EMB = 32
RBF_N = 128
ANGULAR_COUNT = 16
SBF_N = 32
NBR = 30
TRIP_SLOTS = 8
QUAD_SLOTS = 8
A_DEV = 8
SEND = 4
E_DEV = 240
ATOMS = 256
EDGES = 7680
N_GX = 4
N_GY = 4
N_GZ = 2
DEVICES = 32


def draw_edge_vectors(key, part):
    key = jax.random.fold_in(key, 11)
    key_radius, key_height, key_angle = jax.random.split(key, 3)
    radius = jax.random.uniform(key_radius, (EDGES,), jnp.float32, 2.0, 11.0)
    height = jax.random.uniform(key_height, (EDGES,), jnp.float32, -1.0, 1.0)
    angle = jax.random.uniform(key_angle, (EDGES,), jnp.float32, -math.pi, math.pi)
    planar = jnp.sqrt(jnp.maximum(1.0 - height * height, 0.0))
    return jnp.stack([radius * planar * jnp.cos(angle), radius * planar * jnp.sin(angle), radius * height]).astype(jnp.float32)


def draw_send_list(key, part):
    key = jax.random.fold_in(key, 12)
    keys = jax.random.split(key, DEVICES)
    orders = jax.vmap(lambda single: jax.random.permutation(single, A_DEV))(keys)
    return orders[:, :SEND].reshape(-1).astype(jnp.int32)


def draw_sources(key, part):
    key = jax.random.fold_in(key, 13)
    key_pick, key_local, key_x, key_y, key_z, key_row = jax.random.split(key, 6)
    edge = jnp.arange(EDGES)
    device = edge // E_DEV
    within = edge % E_DEV
    atom = within // NBR
    coord_z = device % N_GZ
    pick = jax.random.randint(key_pick, (EDGES,), 0, 2)
    local = (atom + jax.random.randint(key_local, (EDGES,), 1, A_DEV)) % A_DEV
    block_x = jax.random.randint(key_x, (EDGES,), 0, 3)
    block_y = jax.random.randint(key_y, (EDGES,), 0, 3)
    lowest = jnp.where(coord_z == 0, 1, 0)
    highest = jnp.where(coord_z == N_GZ - 1, 1, 2)
    block_z = lowest + jax.random.randint(key_z, (EDGES,), 0, 6) % (highest - lowest + 1)
    block = block_x * 9 + block_y * 3 + block_z
    row = jax.random.randint(key_row, (EDGES,), 0, SEND)
    border = A_DEV + block * SEND + row
    chosen = jnp.where((pick == 1) | (block == 13), local, border)
    chosen = jnp.where((within == 0) & (coord_z < N_GZ - 1), A_DEV + 27 * SEND - 1, chosen)
    chosen = jnp.where(within == NBR, 0, chosen)
    return chosen.astype(jnp.int32)


def set_ends(values, stream_key, least, high):
    spot = [jax.random.randint(jax.random.fold_in(stream_key, axis), (), 0, length) for axis, length in enumerate(values.shape)]
    widest = values.shape.index(max(values.shape))
    neighbour = spot[:widest] + [(spot[widest] + 1) % values.shape[widest]] + spot[widest + 1:]
    return values.at[tuple(spot)].set(least).at[tuple(neighbour)].set(high)


def level_of(key, shape, cuts, low, top_value):
    def one(axis_at, shards_of):
        steps = jax.random.uniform(jax.random.fold_in(jax.random.fold_in(key, 6), axis_at), (shards_of,), jnp.float32, low / len(cuts), top_value / len(cuts))
        return jnp.repeat(jnp.exp(steps), shape[axis_at] // shards_of).reshape((-1,) + (1,) * (len(shape) - axis_at - 1))

    gain = one(*cuts[0])
    for cut in cuts[1:]:
        gain = gain * one(*cut)
    return gain


def bell_draw(key, extent, width, limit, cuts=(), kind=jnp.bfloat16):
    values = width * jax.random.normal(key, extent, jnp.float32)
    if cuts:
        values = values * level_of(key, extent, cuts, -0.22, 0.18)
    return jnp.clip(values, -limit, limit).astype(kind)


def setup_inputs(seed: int = 0) -> dict:
    seeds = jax.random.split(jax.random.key(seed), 28)
    return {
        "hidden_atoms": bell_draw(seeds[0], (ATOMS, ATOM_EMB), 1.0, 6.0, ((0, 32),), jnp.float32),
        "edge_states": bell_draw(seeds[1], (EDGES, EDGE_EMB), 1.0, 6.0, ((0, 32),), jnp.float32),
        "edge_vectors": draw_edge_vectors(jax.random.fold_in(seeds[27], 71), 0),
        "atom_tags": set_ends(jax.random.randint(seeds[3], (ATOMS,), 0, 3), jax.random.fold_in(seeds[3], 1), 0, 2).astype(jnp.int32),
        "send_list": draw_send_list(jax.random.fold_in(seeds[27], 71), 0),
        "sources": draw_sources(jax.random.fold_in(seeds[27], 71), 0),
        "trip_slots": set_ends(jax.random.randint(seeds[6], (EDGES, TRIP_SLOTS), 0, NBR), jax.random.fold_in(seeds[6], 1), 0, NBR - 1).astype(jnp.int32),
        "triplet_mask": set_ends((jax.random.randint(seeds[7], (EDGES, TRIP_SLOTS), 0, 4) < 3).astype(jnp.int32), jax.random.fold_in(seeds[7], 1), 0, 1),
        "quad_slots": set_ends(jax.random.randint(seeds[8], (EDGES, QUAD_SLOTS), 0, NBR), jax.random.fold_in(seeds[8], 1), 0, NBR - 1).astype(jnp.int32),
        "quad_mask": set_ends((jax.random.randint(seeds[9], (EDGES, QUAD_SLOTS), 0, 4) < 3).astype(jnp.int32), jax.random.fold_in(seeds[9], 1), 0, 1),
        "edge_mask": set_ends((jax.random.randint(seeds[10], (EDGES,), 0, 5) < 4).astype(jnp.int32), jax.random.fold_in(seeds[10], 1), 0, 1),
        "w_inputs": bell_draw(seeds[11], (2, EDGE_EMB, EDGE_EMB), EDGE_EMB ** -0.5, 0.25),
        "w_radial": bell_draw(seeds[12], (5, RBF_N, EDGE_EMB), RBF_N ** -0.5, 0.5),
        "w_trip_down": bell_draw(seeds[13], (EDGE_EMB, TRIPLET_WIDTH), EDGE_EMB ** -0.5, 0.25),
        "triplet_bilinear_weight": bell_draw(seeds[14], (ANGULAR_COUNT * TRIPLET_WIDTH, TRIPLET_WIDTH), TRIPLET_WIDTH ** -0.5, 0.75),
        "w_trip_up": bell_draw(seeds[15], (TRIPLET_WIDTH, EDGE_EMB), TRIPLET_WIDTH ** -0.5, 0.75),
        "w_quad_down": bell_draw(seeds[16], (EDGE_EMB, QUAD_EMB), EDGE_EMB ** -0.5, 0.25),
        "w_quad_bil": bell_draw(seeds[17], (SBF_N * QUAD_EMB, QUAD_EMB), QUAD_EMB ** -0.5, 1.0),
        "w_quad_up": bell_draw(seeds[18], (QUAD_EMB, EDGE_EMB), QUAD_EMB ** -0.5, 1.0),
        "w_atom_edge": bell_draw(seeds[19], (2, ATOM_EMB, EDGE_EMB), ATOM_EMB ** -0.5, 0.375),
        "w_residual": bell_draw(seeds[20], (2, EDGE_EMB, EDGE_EMB), EDGE_EMB ** -0.5, 0.25),
        "w_edge_atom": bell_draw(seeds[21], (2, EDGE_EMB, ATOM_EMB), EDGE_EMB ** -0.5, 0.25),
        "w_atom_dense": bell_draw(seeds[22], (4, ATOM_EMB, ATOM_EMB), ATOM_EMB ** -0.5, 0.375),
        "tag_table": bell_draw(seeds[23], (3, ATOM_EMB), 1.0, 4.0),
        "cot_atoms": bell_draw(seeds[24], (ATOMS, ATOM_EMB), 1.0, 6.0, ((0, 32),), jnp.float32),
        "cot_edges": bell_draw(seeds[25], (EDGES, EDGE_EMB), 1.0, 6.0, ((0, 32),), jnp.float32),
        "cot_energy": bell_draw(seeds[26], (ATOMS, ATOM_EMB), 1.0, 6.0, ((0, 32),), jnp.float32),
    }


HIGHEST = lax.Precision.HIGHEST
cutoff_radius = 12.0
root_half = 0.7071067811865476

@jax.custom_vjp
def low(v):
    return lax.optimization_barrier(v.astype(jnp.bfloat16)).astype(jnp.float32)

@jax.custom_vjp
def low_back(v):
    return v

def low_keep(v):
    return (low(v), None)

def low_pass(kept, grad):
    return (grad,)

def back_keep(v):
    return (v, None)

def back_low(kept, grad):
    return (low(grad),)
low.defvjp(low_keep, low_pass)
low_back.defvjp(back_keep, back_low)

def scaled_silu(values):
    return jax.nn.silu(values) / 0.6

def matmul(left, right):
    return jnp.dot(left, right, precision=HIGHEST, preferred_element_type=jnp.float32)

def envelope(scaled):
    return 1.0 - 28.0 * scaled ** 6 + 48.0 * scaled ** 7 - 21.0 * scaled ** 8

def radial_basis(lengths, count):
    scaled = lengths / cutoff_radius
    orders = jnp.arange(1, count + 1).astype(jnp.float32)
    return envelope(scaled)[:, None] * jnp.sin(math.pi * scaled[:, None] * orders[None, :]) / scaled[:, None]

def legendre_terms(cosine, count):
    terms = [jnp.ones_like(cosine), cosine]
    for degree in range(1, count - 1):
        terms.append(((2 * degree + 1) * cosine * terms[degree] - degree * terms[degree - 1]) / (degree + 1))
    return jnp.stack(terms[:count], axis=-1)

def spherical_basis(cosine, lengths, count):
    poly = legendre_terms(cosine, count // 2)
    scaled = lengths / cutoff_radius
    shaped = envelope(scaled)
    first = shaped * jnp.sin(math.pi * scaled) / scaled
    second = shaped * jnp.sin(2.0 * math.pi * scaled) / scaled
    return jnp.concatenate([poly * first[..., None], poly * second[..., None]], axis=-1)

def forward(context, hidden_atoms, edge_states, weights):
    w_inputs, w_radial, w_trip_down, triplet_bilinear_weight, w_trip_up, w_quad_down, w_quad_bil, w_quad_up, w_atom_edge, w_residual, w_edge_atom, w_atom_dense, tag_table = weights
    onehot, radial, source_atom, trip_index, triplet_basis, quad_index, quad_basis, live_edges = context
    edge_count = edge_states.shape[0]
    tagged = hidden_atoms + matmul(onehot, tag_table)
    trip_start = scaled_silu(matmul(edge_states, w_inputs[0])) * matmul(radial, w_radial[0])
    trip_down = scaled_silu(matmul(trip_start, w_trip_down)) * live_edges[:, None]
    quad_start = scaled_silu(matmul(edge_states, w_inputs[1])) * matmul(radial, w_radial[1])
    quad_down = scaled_silu(matmul(quad_start, w_quad_down)) * live_edges[:, None]
    trip_sum = jnp.einsum('ejc,ejf->ecf', triplet_basis, trip_down[trip_index], precision=HIGHEST)
    trip_sum = trip_sum.reshape(edge_count, -1) / math.sqrt(TRIP_SLOTS)
    trip_out = scaled_silu(matmul(scaled_silu(matmul(trip_sum, triplet_bilinear_weight)), w_trip_up))
    quad_sum = jnp.einsum('ejc,ejf->ecf', quad_basis, quad_down[quad_index], precision=HIGHEST)
    quad_sum = quad_sum.reshape(edge_count, -1) / math.sqrt(QUAD_SLOTS)
    quad_out = scaled_silu(matmul(scaled_silu(matmul(quad_sum, w_quad_bil)), w_quad_up))
    targets = jnp.arange(edge_count) // NBR
    atom_msg = scaled_silu(matmul(tagged, w_atom_edge[0])[source_atom] + matmul(tagged, w_atom_edge[1])[targets])
    atom_msg = atom_msg * matmul(radial, w_radial[2])
    merged = (edge_states + trip_out + quad_out + atom_msg) * 0.5
    edges_out = (merged + scaled_silu(matmul(scaled_silu(matmul(merged, w_residual[0])), w_residual[1]))) * root_half
    weighted = edges_out * live_edges[:, None]
    gathered = lax.optimization_barrier(jnp.sum((weighted * matmul(radial, w_radial[3])).reshape(-1, NBR, EDGE_EMB), axis=1)) / math.sqrt(NBR)
    updated = (tagged + scaled_silu(matmul(gathered, w_edge_atom[0]))) * root_half
    atoms_out = (updated + scaled_silu(matmul(scaled_silu(matmul(updated, w_atom_dense[0])), w_atom_dense[1]))) * root_half
    summary = lax.optimization_barrier(jnp.sum((weighted * matmul(radial, w_radial[4])).reshape(-1, NBR, EDGE_EMB), axis=1)) / math.sqrt(NBR)
    energy_out = scaled_silu(matmul(scaled_silu(matmul(summary, w_edge_atom[1]) + matmul(atoms_out, w_atom_dense[2])), w_atom_dense[3]))
    return (atoms_out, edges_out, energy_out)

def reference(hidden_atoms, edge_states, edge_vectors, atom_tags, send_list, sources, trip_slots, triplet_mask, quad_slots, quad_mask, edge_mask, w_inputs, w_radial, w_trip_down, triplet_bilinear_weight, w_trip_up, w_quad_down, w_quad_bil, w_quad_up, w_atom_edge, w_residual, w_edge_atom, w_atom_dense, tag_table, cot_atoms, cot_edges, cot_energy):
    edge_total = edge_states.shape[0]
    device = (jnp.arange(edge_total) // E_DEV).astype(jnp.int32)
    coord_x = device // (N_GY * N_GZ)
    coord_y = device // N_GZ % N_GY
    coord_z = device % N_GZ
    offset = jnp.maximum(sources - A_DEV, 0)
    block = offset // SEND
    row_in = offset % SEND
    owner = ((coord_x + block // 9 - 1) % N_GX * (N_GY * N_GZ) + (coord_y + block // 3 % 3 - 1) % N_GY * N_GZ + (coord_z + block % 3 - 1) % N_GZ).astype(jnp.int32)
    remote = owner * A_DEV + send_list[(owner * SEND + row_in).astype(jnp.int32)]
    source_atom = jnp.where(sources < A_DEV, device * A_DEV + sources, remote).astype(jnp.int32)
    vectors = edge_vectors.T
    lengths = jnp.sqrt(lax.optimization_barrier(jnp.sum(vectors * vectors, axis=1)))
    unit = vectors / lengths[:, None]
    radial = radial_basis(lengths, RBF_N)
    trip_index = (source_atom[:, None] * NBR + trip_slots).astype(jnp.int32)
    triplet_cosine = -lax.optimization_barrier(jnp.sum(unit[:, None, :] * unit[trip_index], axis=-1))
    triplet_basis = legendre_terms(triplet_cosine, ANGULAR_COUNT) * triplet_mask[..., None].astype(jnp.float32)
    quad_index = (source_atom[:, None] * NBR + quad_slots).astype(jnp.int32)
    cos_quad = -lax.optimization_barrier(jnp.sum(unit[:, None, :] * unit[quad_index], axis=-1))
    quad_basis = spherical_basis(cos_quad, lengths[quad_index], SBF_N) * quad_mask[..., None].astype(jnp.float32)
    onehot = (atom_tags[:, None] == jnp.arange(3)[None, :]).astype(jnp.float32)
    live_edges = edge_mask.astype(jnp.float32)
    context = (onehot, radial, source_atom, trip_index, triplet_basis, quad_index, quad_basis, live_edges)
    weights = tuple((weight.astype(jnp.float32) for weight in (w_inputs, w_radial, w_trip_down, triplet_bilinear_weight, w_trip_up, w_quad_down, w_quad_bil, w_quad_up, w_atom_edge, w_residual, w_edge_atom, w_atom_dense, tag_table)))
    outputs, pullback = jax.vjp(functools.partial(forward, context), hidden_atoms, edge_states, weights)
    grad_atoms, grad_edges, grad_weights = pullback((cot_atoms, cot_edges, cot_energy))
    return (outputs[0], outputs[1], outputs[2], grad_atoms, grad_edges, grad_weights[0], grad_weights[1], grad_weights[2], grad_weights[3], grad_weights[4], grad_weights[5], grad_weights[6], grad_weights[7], grad_weights[8], grad_weights[9], grad_weights[10], grad_weights[11], grad_weights[12])
```

```python
import functools
import math

import jax
import jax.numpy as jnp
from jax import lax
from jax.experimental import pallas as pl
from jax.experimental.pallas import tpu as pltpu
from jax.sharding import Mesh
from jax.sharding import PartitionSpec as P

BF = jnp.bfloat16
F32 = jnp.float32
ROWS = ("gx", "gyh", "gyl", "gz")
GY = ("gyh", "gyl")
ATOMS, SEND, SLOTS, EDGES = 8, 4, 30, 240
ATOM_W, EDGE_W, TRIP_W, QUAD_W, RADIAL = 256, 512, 64, 32, 128
ANGLES, PICKS = 16, 8
PAIRS = 17
BLOCK = 16
BLOCKS = EDGES // BLOCK
root_half = 0.7071067811865476
NN = (((1,), (0,)), ((), ()))
NT = (((1,), (1,)), ((), ()))
TN = (((0,), (0,)), ((), ()))


def shifted(value, axis, steps, wrap):
    count = lax.axis_size(axis)
    pairs = [(i, (i + steps) % count) for i in range(count) if wrap or 0 <= i + steps < count]
    return lax.ppermute(value, axis, pairs)


def planes_of(value):
    if lax.axis_size("gz") == 2:
        other = lax.ppermute(value, "gz", [(0, 1), (1, 0)])
        top = lax.axis_index("gz") == 1
        return jnp.stack([jnp.where(top, other, value), jnp.where(top, value, other)])
    return jnp.stack([shifted(value, "gz", 1, False), value, shifted(value, "gz", -1, False)])


def with_halo(value):
    value = planes_of(value)
    value = jnp.concatenate([shifted(value, "gx", 1, True), value, shifted(value, "gx", -1, True)])
    return shifted(value, GY, 1, True), value, shifted(value, GY, -1, True)


def bits_of(axis):
    count = lax.axis_size(axis)
    return [(axis, b) for b in range(count.bit_length() - 1)]


def swap(value, axis, bit):
    count = lax.axis_size(axis)
    return lax.ppermute(value, axis, [(i, i ^ (1 << bit)) for i in range(count)])


def bit_value(axis, bit):
    return (lax.axis_index(axis) >> bit) & 1


def part(arrays, at, size):
    total = lax.dynamic_slice_in_dim(arrays[0], at, size)
    for x in arrays[1:]:
        total = total + lax.dynamic_slice_in_dim(x, at, size)
    return total


class Chain:
    def __init__(self):
        self.last = None

    def after(self, values):
        if self.last is not None:
            self.last, values = lax.optimization_barrier((self.last, values))
        return values

    def step(self, value):
        self.last = value
        return value


def halved(chain, arrays, axis, bit):
    arrays = chain.after(arrays)
    half = arrays[0].shape[0] // 2
    one = bit_value(axis, bit)
    send = chain.step(part(arrays, (1 - one) * half, half))
    got = swap(send, axis, bit)
    send, arrays = lax.optimization_barrier((send, arrays))
    return [part(arrays, one * half, half), got]


def joined_halves(value, other, axis, bit):
    one = bit_value(axis, bit) == 1
    return jnp.concatenate([jnp.where(one, other, value), jnp.where(one, value, other)])


def reduction(chain, first, second):
    across, along = bits_of("gz"), bits_of("gyh")
    lanes = [first, second]
    for plan in ((across, along), (along, across)):
        for i in range(2):
            for axis, bit in plan[i]:
                lanes[i] = halved(chain, lanes[i], axis, bit)
        yield
    sizes = [x[0].shape[0] for x in lanes]
    joint = [jnp.concatenate(pair) for pair in zip(*chain.after(lanes))]
    for axis, bit in bits_of("gx"):
        joint = halved(chain, joint, axis, bit)
        yield
    joint = chain.after(joint)
    value = chain.step(sum(joint[1:], joint[0]))
    for axis, bit in bits_of("gx")[::-1]:
        other = swap(value, axis, bit)
        yield
        value, other = chain.after((value, other))
        value = chain.step(joined_halves(value, other, axis, bit))
    values = [value[: sizes[0]], value[sizes[0] :]]
    for plan in ((along, across), (across, along)):
        for turn in range(max(len(across), len(along))):
            others = [None, None]
            for i in range(2):
                if turn < len(plan[i]):
                    others[i] = swap(values[i], *plan[i][::-1][turn])
            yield
            for i in range(2):
                if turn < len(plan[i]):
                    values[i], others[i] = chain.after((values[i], others[i]))
                    values[i] = chain.step(joined_halves(values[i], others[i], *plan[i][::-1][turn]))
    others = [swap(x, "gyl", 0) for x in values]
    yield
    values, others = chain.after((values, others))
    return [(value, chain.step(other)) for value, other in zip(values, others)]


def iota(shape, dim):
    return lax.broadcasted_iota(jnp.int32, shape, dim)


def dot(left, right, dims=NN):
    return lax.dot_general(left, right, dims, preferred_element_type=F32)


def halves(x):
    high = x.astype(BF)
    return high, (x - high.astype(F32)).astype(BF)


def stacked(x):
    high, low = halves(x)
    if x.shape[0] % 16 == 0:
        return jnp.concatenate([high, low], axis=0)
    return jnp.concatenate([high.astype(F32), low.astype(F32)], axis=0).astype(BF)


def folded(x):
    half = x.shape[0] // 2
    return x[:half] + x[half:]


def times(x, weight, dims=NN):
    return folded(dot(stacked(x), weight, dims))


def side_by_side(x):
    return jnp.concatenate(halves(x), axis=1)


def side_sum(x):
    half = x.shape[1] // 2
    return x[:, :half] + x[:, half:]


def weight_grad(x, y):
    x_high, x_low = halves(x)
    y_high, y_low = halves(y)
    left, right = [x_high, x_high, x_low], [y_high, y_low, y_high]
    if x.shape[0] % 16 == 0:
        return dot(jnp.concatenate(left, axis=0), jnp.concatenate(right, axis=0), TN)
    left = jnp.concatenate([p.astype(F32) for p in left], axis=0).astype(BF)
    right = jnp.concatenate([p.astype(F32) for p in right], axis=0).astype(BF)
    return dot(left, right, TN)


def onehot(hit):
    return jnp.where(hit, 1.0, 0.0).astype(BF)


def sigmoid(v):
    return 1.0 / (1.0 + jnp.exp(-v))


def act(v):
    return v * sigmoid(v) * (1.0 / 0.6)


def act_and_slope(v):
    s = sigmoid(v)
    return v * s * (1.0 / 0.6), s * (1.0 + v * (1.0 - s)) * (1.0 / 0.6)


def sin_pi(t):
    n = jnp.floor(t + 0.5)
    r = t - n
    odd = n - 2.0 * jnp.floor(n * 0.5)
    q = r * r
    total = jnp.zeros_like(r)
    for k in range(6, -1, -1):
        total = total * q + (-1.0) ** k * math.pi ** (2 * k + 1) / math.factorial(2 * k + 1)
    return total * r * (1.0 - 2.0 * odd)


def to_column(row):
    n = row.shape[1]
    same = iota((n, n), 0) == iota((n, n), 1)
    return jnp.sum(jnp.where(same, row, jnp.zeros_like(row)), axis=1, keepdims=True)


def send_column(send, rows):
    shape = (rows, SEND)
    hit = (iota(shape, 0) & (SEND - 1)) == iota(shape, 1)
    return jnp.sum(jnp.where(hit, send, 0), axis=1, keepdims=True)


def send_lanes(send):
    shape = (8, 128)
    hit = iota(shape, 0) == (iota(shape, 1) & (SEND - 1))
    return jnp.sum(jnp.where(hit, send_column(send, 8), 0), axis=0, keepdims=True)


def paid(row, send):
    edge = send * SLOTS + 2 * (row >> 3) + ((row >> 2) & 1)
    return jnp.where(row < 120, edge, -1)


def atom_of(edge):
    total = jnp.zeros_like(edge)
    for a in range(1, ATOMS):
        total = total + jnp.where(edge >= a * SLOTS, 1, 0)
    return total


def radial_of(length):
    x = length / 12.0
    x2 = x * x
    x4 = x2 * x2
    envelope = 1.0 - 28.0 * (x4 * x2) + 48.0 * (x4 * x2 * x) - 21.0 * (x4 * x4)
    orders = (iota((1, RADIAL), 1) + 1).astype(F32)
    return envelope * sin_pi(x * orders) / x


def geometry(unit):
    own = atom_of(iota((8, EDGES), 1)) == iota((8, EDGES), 0)
    edge = iota((EDGES, 128), 0)
    slot = edge - atom_of(edge) * SLOTS
    total = jnp.zeros((24, 128), F32)
    for k in range(3):
        x = jnp.where(own, unit[k : k + 1, :], 0.0)
        high = x.astype(BF).astype(F32)
        mid = (x - high).astype(BF).astype(F32)
        parts = jnp.concatenate([high, mid, x - high - mid], axis=0).astype(BF)
        total = total + dot(parts, onehot(iota((EDGES, 128), 1) == slot + 32 * k))
    return total[0:8] + total[8:16] + total[16:24]


def local_rows(index):
    return (index & 7) * SLOTS + 2 * (index >> 4) + ((index >> 3) & 1)


def start_kernel(
    edge, vec, mask, hidden, tag_row, send_row, table, w_in, w_rad, w_trip, w_quad,
    payload, local, tagged, pre, downs, rads, radial_out, columns,
):
    vectors = vec[...]
    length = jnp.sqrt(jnp.sum(vectors * vectors, axis=0, keepdims=True))
    unit = vectors / length
    geo = geometry(unit)
    live = to_column(jnp.where(mask[...] > 0, 1.0, 0.0))
    parts = [live] + [to_column(unit[k : k + 1, :]) for k in range(3)]
    columns[...] = jnp.concatenate(parts + [jnp.zeros((EDGES, 124), F32)], axis=1)
    send = send_column(send_row[...], 8)
    pay = paid(iota((128, 1), 0), send_column(send_row[...], 128))
    tags = to_column(tag_row[...])
    radial = radial_of(to_column(length))
    radial_out[...] = radial
    split = stacked(radial)
    for k in range(5):
        rads[k] = folded(dot(split, w_rad[k]))
    split = stacked(edge[...])
    pre[0] = folded(dot(split, w_in[0]))
    pre[1] = folded(dot(split, w_in[1]))
    trip_pre = times(act(pre[0]) * rads[0], w_trip[...], NT)
    quad_pre = times(act(pre[1]) * rads[1], w_quad[...], NT)
    downs[...] = jnp.concatenate([trip_pre, quad_pre, jnp.zeros((EDGES, 32), F32)], axis=1)
    trip = act(trip_pre) * live
    quad = act(quad_pre) * live
    rows = jnp.concatenate([trip, quad * radial[:, 0:1], quad * radial[:, 1:2]], axis=1)
    rows = side_by_side(rows)
    shape = (EDGES, EDGES)
    place = onehot(local_rows(iota(shape, 0)) == iota(shape, 1))
    local[0:15] = side_sum(dot(place, rows)).reshape(15, 16, 128)
    place = onehot(pay == iota((128, EDGES), 1))
    payload[0:16] = side_sum(dot(place, rows)).reshape(16, 8, 128)
    tag = hidden[...]
    for t in range(3):
        tag = tag + jnp.where(tags == t, table[t : t + 1, :].astype(F32), 0.0)
    tagged[...] = tag
    local[15] = jnp.concatenate([tag[:, :128], tag[:, 128:]], axis=0)
    local[16] = jnp.concatenate([geo, jnp.zeros((8, 128), F32)], axis=0)
    both = jnp.concatenate([tag, geo], axis=1)
    sent = jnp.zeros((8, 384), F32)
    for a in range(ATOMS):
        sent = sent + jnp.where(send == a, both[a : a + 1, :], 0.0)
    payload[15] = jnp.where(iota((8, 128), 0) < 4, sent[:, :128], sent[:, 128:256])
    payload[16] = sent[:, 256:]


def split_cores(core, whole, keep, send):
    half = whole.shape[0] // 2
    upper = core[0] == 1
    low, high = whole[:half], whole[half:]
    keep[...] = jnp.where(upper, high, low)
    send[...] = jnp.where(upper, low, high)


def segments(shape, edge_dim, atom_dim):
    edge, atom = iota(shape, edge_dim), iota(shape, atom_dim) & 7
    return onehot((edge >= atom * SLOTS) & (edge < atom * SLOTS + SLOTS))


def legendre(cosine):
    before, now = jnp.ones_like(cosine), cosine
    yield before
    yield now
    for k in range(1, ANGLES - 1):
        before, now = now, ((2 * k + 1) / (k + 1)) * cosine * now - (k / (k + 1)) * before
        yield now


def main_kernel(
    halo_before, halo_here, halo_after, local, tagged, edge, columns, rads, radial,
    src_cols, slots, marks,
    trip_bil, trip_up, quad_bil, quad_up, w_ae, w_res, w_ea, w_ad,
    cot_atoms, cot_edges, cot_energy, core,
    atoms_out, edges_out, energy_out, grad_edges, grad_tag,
    cosines, grad_sums, grad_src, keep, send, grad_rads, atom_rows, quad_up_grad,
    table, sums, weight, kept, cos_table, first,
):
    live = columns[:, 0:1]
    halos = (halo_before, halo_here, halo_after)
    group = halo_here.shape[0] * 8
    depth = 3 * group + 16
    lanes = iota((EDGES, depth), 1)
    place = jnp.concatenate(
        [onehot(src_cols[:, 0:1] == lanes), onehot(src_cols[:, 1:2] == lanes)], axis=0
    )

    def rows_at(p):
        parts = [h[:, p].reshape(group, 128) for h in halos]
        return jnp.concatenate(parts + [local[p]], axis=0)

    def gather_pair(p, carry):
        got = dot(place, side_by_side(rows_at(p))).astype(BF)
        table[2 * p] = got[:EDGES]
        table[2 * p + 1] = got[EDGES:]
        return carry

    lax.fori_loop(0, 16, gather_pair, 0)

    rows = rows_at(16)
    high, low = halves(rows)
    rest = (rows - high.astype(F32) - low.astype(F32)).astype(BF)
    got = dot(place[:EDGES], jnp.concatenate([high, low, rest], axis=1))
    got = got[:, :128] + got[:, 128:256] + got[:, 256:]
    cos_table[...] = -(
        columns[:, 1:2] * got
        + columns[:, 2:3] * pltpu.roll(got, 96, 1)
        + columns[:, 3:4] * pltpu.roll(got, 64, 1)
    )

    for k in range(ANGLES):
        top = trip_bil[:, k * 64 : k * 64 + 64].astype(F32)
        top = jnp.concatenate([top, jnp.zeros((64, 64), F32)], axis=1)
        low_left = quad_bil[:, k * 32 : k * 32 + 32].astype(F32)
        low_right = quad_bil[:, 512 + k * 32 : 544 + k * 32].astype(F32)
        bottom = jnp.concatenate([jnp.zeros((32, 64), F32), low_left, low_right], axis=1)
        piece = jnp.concatenate([top, bottom, jnp.zeros((32, 128), F32)], axis=0)
        weight[:, k * 128 : (k + 1) * 128] = piece.astype(BF)

    trip_lanes = iota((128, 128), 1) < TRIP_W
    scale = 1.0 / math.sqrt(PICKS)

    def basis_block(b, carry):
        at = pl.multiple_of(b * BLOCK, BLOCK)
        own = pl.ds(at, BLOCK)
        wide = iota((BLOCK, 512), 1)
        mark = marks[own, :]
        hits = [jnp.where(mark[:, t : t + 1] == wide, 1.0, 0.0) for t in range(2 * PICKS)]
        hits = jnp.concatenate(hits, axis=0).astype(BF)
        got = side_sum(dot(hits, table[:, own, :].reshape(512, 256)))
        picked = jnp.where(trip_lanes, got[:128], got[128:]) * scale
        picked = picked.reshape(PICKS, BLOCK, 128)
        cos_here = cos_table[own, :]
        slot = slots[own, :]
        low_lanes = iota((BLOCK, 128), 1) < TRIP_W
        for h in range(2):
            rows = slice(8 * h, 8 * h + 8)
            cos = []
            for j in range(PICKS):
                index = jnp.where(
                    low_lanes[rows], slot[rows, j : j + 1], slot[rows, PICKS + j : PICKS + j + 1]
                )
                cos.append(jnp.take_along_axis(cos_here[rows], index, axis=1))
            cos = jnp.stack(cos)
            cosines[2 * b + h] = cos
            values = picked[:, rows]
            for k, poly in enumerate(legendre(cos)):
                sums[pl.ds(pl.multiple_of(at + 8 * h, 8), 8), k * 128 : (k + 1) * 128] = jnp.sum(
                    poly * values, axis=0
                )
        return carry

    lax.fori_loop(0, BLOCKS, basis_block, 0)

    down = times(sums[...], weight[...], NT)
    down_act, down_slope = act_and_slope(down)
    trip_h, quad_h = down_act[:, :64], down_act[:, 64:96]
    trip_pre = times(trip_h, trip_up[...])
    quad_pre = times(quad_h, quad_up[...])
    src = jnp.concatenate(
        [side_sum(table[30].astype(F32)), side_sum(table[31].astype(F32))], axis=1
    )
    target = times(tagged[...], w_ae[1])
    spread = segments((EDGES, 16), 0, 1)
    gathers = segments((8, EDGES), 1, 0)

    def to_edges(x):
        return dot(spread, stacked(x))

    def to_atoms(x):
        return side_sum(dot(gathers, side_by_side(x)))

    atom_pre = times(src, w_ae[0]) + to_edges(target)
    atom_act, atom_slope = act_and_slope(atom_pre)
    trip_act, trip_slope = act_and_slope(trip_pre)
    quad_act, quad_slope = act_and_slope(quad_pre)
    merged = (edge[...] + trip_act + quad_act + atom_act * rads[2]) * 0.5
    kept[0] = merged
    first_act, first_slope = act_and_slope(times(merged, w_res[0]))
    kept[1] = first_act
    second_act, second_slope = act_and_slope(times(first_act, w_res[1]))
    new_edges = (merged + second_act) * root_half
    edges_out[...] = new_edges
    weighted = new_edges * live
    root_slots = 1.0 / math.sqrt(SLOTS)
    gathered = to_atoms(weighted * rads[3]) * root_slots
    summary = to_atoms(weighted * rads[4]) * root_slots
    gate_act, gate_slope = act_and_slope(times(gathered, w_ea[0]))
    updated = (tagged[...] + gate_act) * root_half
    a0_act, a0_slope = act_and_slope(times(updated, w_ad[0]))
    a1_act, a1_slope = act_and_slope(times(a0_act, w_ad[1]))
    new_atoms = (updated + a1_act) * root_half
    atoms_out[...] = new_atoms
    e_act, e_slope = act_and_slope(times(summary, w_ea[1]) + times(new_atoms, w_ad[2]))
    out_act, out_slope = act_and_slope(times(e_act, w_ad[3]))
    energy_out[...] = out_act

    d_out = cot_energy[...] * out_slope
    d_e = times(d_out, w_ad[3], NT) * e_slope
    d_summary = times(d_e, w_ea[1], NT)
    d_atoms = (cot_atoms[...] + times(d_e, w_ad[2], NT)) * root_half
    d_a1 = d_atoms * a1_slope
    d_a0 = times(d_a1, w_ad[1], NT) * a0_slope
    d_updated = (d_atoms + times(d_a0, w_ad[0], NT)) * root_half
    d_gate = d_updated * gate_slope
    d_gathered = times(d_gate, w_ea[0], NT)

    d_gathered = to_edges(d_gathered * root_slots)
    d_summary = to_edges(d_summary * root_slots)
    grad_rads[1] = weighted * d_gathered
    grad_rads[2] = weighted * d_summary
    d_new = cot_edges[...] + live * (d_gathered * rads[3] + d_summary * rads[4])
    d_new = d_new * root_half
    d_second = d_new * second_slope
    kept[3] = d_second
    d_first = times(d_second, w_res[1], NT) * first_slope
    kept[2] = d_first
    d_merged = (d_new + times(d_first, w_res[0], NT)) * 0.5
    grad_edges[...] = d_merged
    grad_rads[0] = d_merged * atom_act
    d_atom = d_merged * rads[2] * atom_slope
    kept[4] = d_atom
    d_trip = d_merged * trip_slope
    d_quad = d_merged * quad_slope
    d_target = to_atoms(d_atom)
    grad_tag[...] = d_updated + times(d_target, w_ae[1], NT)
    d_down = jnp.concatenate(
        [times(d_trip, trip_up[...], NT), times(d_quad, quad_up[...], NT), jnp.zeros((EDGES, 32), F32)],
        axis=1,
    )
    d_down = d_down * down_slope
    grad_src[...] = times(d_atom, w_ae[0], NT)

    first[0:512] = weight_grad(kept[0], kept[2])
    first[512:768] = weight_grad(src, kept[4])
    first[896:1408] = weight_grad(kept[1], kept[3])
    first[1408:1664] = weight_grad(tagged[...], d_target)
    bil = weight_grad(d_down, sums[...])
    for m in range(8):
        tile = [bil[0:64, k * 128 : k * 128 + 64] for k in (2 * m, 2 * m + 1)]
        row = 768 + 64 * (m // 4)
        first[row : row + 64, (m % 4) * 128 : (m % 4 + 1) * 128] = jnp.concatenate(tile, axis=1)
    for half in range(2):
        for m in range(4):
            at = 64 + 32 * half
            tile = [bil[64:96, k * 128 + at : k * 128 + at + 32] for k in range(4 * m, 4 * m + 4)]
            row = 1728 + 32 * half
            first[row : row + 32, m * 128 : (m + 1) * 128] = jnp.concatenate(tile, axis=1)
    first[1664:1728] = weight_grad(down_act, d_trip)[:64]
    quad_up_grad[...] = weight_grad(down_act, d_quad)[64:96]
    atom_rows[...] = jnp.concatenate(
        [gathered, summary, updated, a0_act, new_atoms, e_act, d_a0, d_a1, d_e, d_out, d_gate], axis=1
    )
    split_cores(core, first, keep, send)
    grad_sums[...] = times(d_down, weight[...])


def late_kernel(grad_rads, radial, atom_rows, quad_up_grad, core, keep, send, second):
    atoms = atom_rows[...]
    gathered, summary = atoms[:, :512], atoms[:, 512:1024]
    updated, a0_act, new_atoms, e_act, d_a0, d_a1, d_e, d_out, d_gate = [
        atoms[:, at : at + 256] for at in range(1024, 3328, 256)
    ]
    second[0:512, 0:256] = weight_grad(gathered, d_gate)
    second[0:512, 256:512] = weight_grad(summary, d_e)
    second[512:768, 0:256] = weight_grad(updated, d_a0)
    second[512:768, 256:512] = weight_grad(a0_act, d_a1)
    second[768:1024, 0:256] = weight_grad(new_atoms, d_e)
    second[768:1024, 256:512] = weight_grad(e_act, d_out)
    for k in range(3):
        second[1024 + 128 * k : 1152 + 128 * k] = weight_grad(radial[...], grad_rads[k])
    second[1408:1440] = quad_up_grad[...]
    second[1440:1536] = jnp.zeros((96, 512), F32)
    split_cores(core, second, keep, send)


def scatter_kernel(
    cosines, sums, grad_src, src_rows, mark_rows,
    back_before, back_here, back_after, back_local,
    table,
):
    group = back_here.shape[0] * 8
    depth = 3 * group + 16
    trip_lanes = iota((128, 128), 1) < TRIP_W
    scale = 1.0 / math.sqrt(PICKS)

    def basis_back(b, carry):
        at = pl.multiple_of(b * BLOCK, BLOCK)
        own = pl.ds(at, BLOCK)
        parts = []
        for h in range(2):
            total = jnp.zeros((PICKS, 8, 128), F32)
            for k, poly in enumerate(legendre(cosines[2 * b + h])):
                total = total + poly * sums[pl.ds(pl.multiple_of(at + 8 * h, 8), 8), k * 128 : (k + 1) * 128]
            parts.append(total * scale)
        grad = jnp.concatenate(parts, axis=1).reshape(128, 128)
        grad = jnp.concatenate(
            [jnp.where(trip_lanes, grad, 0.0), jnp.where(trip_lanes, 0.0, grad)], axis=0
        )
        hits = onehot(mark_rows[b] == iota((512, 256), 0))
        got = side_by_side(side_sum(dot(hits, side_by_side(grad))))
        table[:, own, :] = got.reshape(32, BLOCK, 256)
        return carry

    lax.fori_loop(0, BLOCKS, basis_back, 0)
    table[30] = side_by_side(grad_src[:, :128])
    table[31] = side_by_side(grad_src[:, 128:])
    rows = iota((depth, EDGES), 0)
    place_even = onehot(src_rows[0:1, :] == rows)
    place_odd = onehot(src_rows[1:2, :] == rows)

    def scatter_pair(p, carry):
        got = side_sum(dot(place_even, table[2 * p]) + dot(place_odd, table[2 * p + 1]))
        for i, back in enumerate((back_before, back_here, back_after)):
            back[:, p] = got[i * group : (i + 1) * group].reshape(group // 8, 8, 128)
        back_local[p] = got[3 * group :]
        return carry

    lax.fori_loop(0, 16, scatter_pair, 0)


def finish_kernel(
    back_local, returned, grad_late, tag_late, edge, radial, columns, pre, downs, rads, tag_row, send_row,
    w_in, w_trip, w_quad, core,
    grad_atoms, grad_edges, keep_first, send_first, keep_second, send_second,
    first, second,
):
    shape = (EDGES, 256)
    lane = iota(shape, 1)
    place = onehot((local_rows(lane) == iota(shape, 0)) & (lane < EDGES))
    rows = dot(place, side_by_side(back_local[...].reshape(256, 128)))
    pay = paid(iota((1, 128), 1), send_lanes(send_row[...]))
    place = onehot(pay == iota((EDGES, 128), 0))
    send = send_column(send_row[...], 8)
    tags = to_column(tag_row[...])
    rows = side_sum(rows + dot(place, side_by_side(returned[...].reshape(128, 128))))
    back = returned[15]
    tag = tag_late[...] + jnp.concatenate([back_local[15, 0:8], back_local[15, 8:16]], axis=1)
    atom = iota((8, 1), 0)
    for r in range(SEND):
        piece = jnp.concatenate([back[r : r + 1], back[4 + r : 5 + r]], axis=1)
        tag = tag + jnp.where(send[r : r + 1, :] == atom, piece, 0.0)
    grad_atoms[...] = tag
    table = [
        jnp.sum(jnp.where(tags == t, tag, 0.0), axis=0, keepdims=True) for t in range(3)
    ]
    table = jnp.concatenate(table + [jnp.zeros((29, ATOM_W), F32)], axis=0)
    d_trip = rows[:, :64]
    d_quad = rows[:, 64:96] * radial[:, 0:1] + rows[:, 96:128] * radial[:, 1:2]
    total = grad_late[...]
    for k, (d_row, down, weight, out) in enumerate(
        ((d_trip, slice(0, 64), w_trip, first), (d_quad, slice(64, 96), w_quad, second))
    ):
        d_down = d_row * columns[:, 0:1] * act_and_slope(downs[:, down])[1]
        value, slope = act_and_slope(pre[k])
        d_start = times(d_down, weight[...])
        d_pre = d_start * rads[k] * slope
        total = total + times(d_pre, w_in[k], NT)
        out[0:512] = weight_grad(edge[...], d_pre)
        out[512:640] = weight_grad(radial[...], d_start * value)
        down_grad = weight_grad(d_down, value * rads[k])
        if k == 0:
            out[640:704] = down_grad
            out[704:768] = jnp.zeros((64, 512), F32)
        else:
            out[640:672] = down_grad
            out[672:704, 0:256] = table
            out[672:704, 256:512] = jnp.zeros((32, 256), F32)
            out[704:768] = jnp.zeros((64, 512), F32)
    grad_edges[...] = total
    split_cores(core, first, keep_first, send_first)
    split_cores(core, second, keep_second, send_second)


def call(kernel, outs, args, scratch=(), micros=1):
    flops = int(micros * 1.15e9)
    return pl.pallas_call(
        kernel,
        out_shape=[jax.ShapeDtypeStruct(shape, F32) for shape in outs],
        in_specs=[pl.BlockSpec(memory_space=pltpu.SMEM if x.ndim == 1 else pltpu.VMEM) for x in args],
        out_specs=[pl.BlockSpec(memory_space=pltpu.VMEM)] * len(outs),
        scratch_shapes=list(scratch),
        compiler_params=pltpu.CompilerParams(vmem_limit_bytes=56 * 1024 * 1024),
        cost_estimate=pl.CostEstimate(flops=flops, bytes_accessed=4 << 20, transcendentals=0),
    )(*args)


def per_device(
    hidden_atoms,
    edge_states,
    edge_vectors,
    atom_tags,
    send_list,
    sources,
    trip_slots,
    triplet_mask,
    quad_slots,
    quad_mask,
    edge_mask,
    w_inputs,
    w_radial,
    w_trip_down,
    triplet_bilinear_weight,
    w_trip_up,
    w_quad_down,
    w_quad_bil,
    w_quad_up,
    w_atom_edge,
    w_residual,
    w_edge_atom,
    w_atom_dense,
    tag_table,
    cot_atoms,
    cot_edges,
    cot_energy,
):
    planes = 2 if lax.axis_size("gz") == 2 else 3
    group = 3 * planes

    offset = jnp.maximum(sources - ATOMS, 0)
    block, border = offset // SEND, offset % SEND
    step_x, step_y, step_z = block // 9, block // 3 % 3, block % 3
    if planes == 2:
        step_z = jnp.clip(step_z - 1 + lax.axis_index("gz"), 0, 1)
    block = (step_y * 3 + step_x) * planes + step_z
    inside = sources < ATOMS
    even = jnp.where(inside, 3 * group * 8 + sources, block * 8 + border)
    src = jnp.stack([even, even + jnp.where(inside, ATOMS, SEND)])
    slots = jnp.concatenate([trip_slots, quad_slots], axis=1)
    masks = jnp.concatenate([triplet_mask, quad_mask], axis=1)
    marks = jnp.where(masks > 0, slots * BLOCK + (jnp.arange(EDGES) % BLOCK)[:, None], -1)
    mark_rows = marks.reshape(BLOCKS, BLOCK, 2 * PICKS).transpose(0, 2, 1)
    mark_rows = mark_rows.reshape(BLOCKS, 1, 2 * PICKS * BLOCK)
    trip_down_t, quad_down_t = w_trip_down.T, w_quad_down.T

    tag_row, send_row = atom_tags[None, :], send_list[None, :]
    payload, local, tagged, pre, downs, rads, radial, columns = call(
        start_kernel,
        [(PAIRS, 8, 128), (PAIRS, 16, 128), (8, 256), (2, EDGES, 512), (EDGES, 128), (5, EDGES, 512)]
        + [(EDGES, 128)] * 2,
        [edge_states, edge_vectors, edge_mask[None, :], hidden_atoms, tag_row, send_row, tag_table,
         w_inputs, w_radial, trip_down_t, quad_down_t],
        micros=5,
    )
    core = bit_value("gyl", 0)[None]
    before, here, after = with_halo(payload)
    (
        atoms_out, edges_out, energy_out, grad_edges, grad_tag,
        cosines, grad_sums, grad_src, keep_a, send_a, grad_rads, atom_rows, quad_up_grad,
    ) = call(
        main_kernel,
        [(8, 256), (EDGES, 512), (8, 256), (EDGES, 512), (8, 256)]
        + [(2 * BLOCKS, PICKS, 8, 128), (EDGES, 2048), (EDGES, 256), (896, 512), (896, 512)]
        + [(3, EDGES, 512), (8, 3328), (32, 512)],
        [before, here, after, local, tagged, edge_states, columns, rads, radial,
         src.T, slots, marks,
         triplet_bilinear_weight.T, w_trip_up, w_quad_bil.T, w_quad_up, w_atom_edge, w_residual,
         w_edge_atom, w_atom_dense, cot_atoms, cot_edges, cot_energy, core],
        scratch=[
            pltpu.VMEM((32, EDGES, 256), BF),
            pltpu.VMEM((EDGES, 2048), F32),
            pltpu.VMEM((128, 2048), BF),
            pltpu.VMEM((5, EDGES, 512), F32),
            pltpu.VMEM((EDGES, 128), F32),
            pltpu.VMEM((1792, 512), F32),
        ],
        micros=26,
    )
    chain = Chain()
    got_a = swap(send_a, "gyl", 0)
    keep_b, send_b = call(
        late_kernel,
        [(768, 512)] * 2,
        [grad_rads, radial, atom_rows, quad_up_grad, core],
        scratch=[pltpu.VMEM((1536, 512), F32)],
        micros=4,
    )
    late = reduction(chain, [keep_a, got_a], [keep_b, swap(send_b, "gyl", 0)])
    next(late)
    grad_sums = chain.after(grad_sums)
    back_before, back_here, back_after, back_local = call(
        scatter_kernel,
        [(group, 16, 8, 128)] * 3 + [(16, 16, 128)],
        [cosines, grad_sums, grad_src, src, mark_rows],
        scratch=[pltpu.VMEM((32, EDGES, 256), BF)],
        micros=13,
    )
    got = shifted(back_before, GY, -1, True), shifted(back_after, GY, 1, True)
    chain.step(back_local)
    next(late)
    got, value = chain.after((got, back_here))
    value = chain.step(value + got[0] + got[1])
    first_plane, middle, last_plane = value[:planes], value[planes : 2 * planes], value[2 * planes :]
    got = shifted(first_plane, "gx", -1, True), shifted(last_plane, "gx", 1, True)
    got, middle = chain.after((got, middle))
    value = chain.step(middle + got[0] + got[1])
    next(late)
    if planes == 2:
        top = lax.axis_index("gz") == 1
        mine = jnp.where(top, value[1], value[0])
        theirs = jnp.where(top, value[0], value[1])
        returned = mine + lax.ppermute(theirs, "gz", [(0, 1), (1, 0)])
    else:
        returned = value[1] + shifted(value[0], "gz", -1, False) + shifted(value[2], "gz", 1, False)
    grad_atoms, grad_edges, keep_c, send_c, keep_d, send_d = call(
        finish_kernel,
        [(8, 256), (EDGES, 512)] + [(384, 512)] * 4,
        [back_local, returned, grad_edges, grad_tag, edge_states, radial, columns, pre, downs, rads,
         tag_row, send_row, w_inputs, trip_down_t, quad_down_t, core],
        scratch=[pltpu.VMEM((768, 512), F32)] * 2,
        micros=7,
    )
    got_c, got_d = swap(send_c, "gyl", 0), swap(send_d, "gyl", 0)
    early = reduction(chain, [keep_c, got_c], [keep_d, got_d])
    chain.step(keep_c)
    running = {"L": late, "E": early}
    done = {}

    def resume(name):
        if name in done:
            return
        try:
            next(running[name])
        except StopIteration as end:
            done[name] = end.value

    for name in "LELEELELEELEELEEL":
        resume(name)
    while len(done) < 2:
        resume("E")
        resume("L")
    upper = bit_value("gyl", 0) == 1

    def both(name, i):
        mine, other = done[name][i]
        return jnp.where(upper, other, mine), jnp.where(upper, mine, other)

    (a_low, a_high), (b_low, b_high) = both("L", 0), both("L", 1)
    (c_low, c_high), (d_low, d_high) = both("E", 0), both("E", 1)

    def pair(x, width):
        return jnp.stack([x[:, :width], x[:, width:]])

    def joined(x):
        half = x.shape[0] // 2
        return jnp.concatenate([x[:half], x[half:]], axis=1)

    grad_radial = [c_high[128:256], d_high[128:256]] + [
        b_high[256 + 128 * k : 384 + 128 * k] for k in range(3)
    ]
    grad_inputs = jnp.concatenate([c_low, c_high[:128], d_low, d_high[:128]])
    return (
        atoms_out,
        edges_out,
        energy_out,
        grad_atoms,
        grad_edges,
        grad_inputs.reshape(2, 512, 512),
        jnp.stack(grad_radial),
        c_high[256:320].T,
        joined(a_low[768:896]).T,
        a_high[768:832],
        d_high[256:288].T,
        joined(a_high[832:896]).T,
        b_high[640:672],
        jnp.stack([a_low[512:768], a_high[512:768]]),
        jnp.stack([a_low[:512], a_high[:512]]),
        pair(b_low[:512], 256),
        jnp.concatenate([pair(b_low[512:768], 256), pair(b_high[:256], 256)]),
        d_high[288:291, :256],
    )


def solution(mesh):
    size = dict(mesh.shape)
    inner = Mesh(mesh.devices.reshape(size["gx"], size["gy"] // 2, 2, size["gz"]), ROWS)
    flat, columns, vector, whole = P(ROWS, None), P(None, ROWS), P(ROWS), P()
    placed = [flat, flat, columns] + [vector] * 3 + [flat] * 4 + [vector] + [whole] * 13 + [flat] * 3
    return jax.shard_map(
        per_device,
        mesh=inner,
        in_specs=tuple(placed),
        out_specs=tuple([flat] * 5 + [whole] * 13),
        check_vma=False,
    )
```

```python
import functools
import math

import jax
import jax.numpy as jnp
from jax import lax
from jax.experimental import pallas as pl
from jax.experimental.pallas import tpu as pltpu
from jax.sharding import Mesh
from jax.sharding import PartitionSpec as P

BF = jnp.bfloat16
F32 = jnp.float32
ROWS = ("gx", "gyh", "gyl", "gz")
GY = ("gyh", "gyl")
ATOMS, SEND, SLOTS, EDGES = 8, 4, 30, 240
ATOM_W, EDGE_W, TRIP_W, QUAD_W, RADIAL = 256, 512, 64, 32, 128
ANGLES, PICKS = 16, 8
PAIRS = 17
BLOCK = 16
BLOCKS = EDGES // BLOCK
root_half = 0.7071067811865476
NN = (((1,), (0,)), ((), ()))
NT = (((1,), (1,)), ((), ()))
TN = (((0,), (0,)), ((), ()))


def shifted(value, axis, steps, wrap):
    count = lax.axis_size(axis)
    pairs = [(i, (i + steps) % count) for i in range(count) if wrap or 0 <= i + steps < count]
    return lax.ppermute(value, axis, pairs)


def planes_of(value):
    if lax.axis_size("gz") == 2:
        other = lax.ppermute(value, "gz", [(0, 1), (1, 0)])
        top = lax.axis_index("gz") == 1
        return jnp.stack([jnp.where(top, other, value), jnp.where(top, value, other)])
    return jnp.stack([shifted(value, "gz", 1, False), value, shifted(value, "gz", -1, False)])


def with_halo(value):
    value = planes_of(value)
    value = jnp.concatenate([shifted(value, "gx", 1, True), value, shifted(value, "gx", -1, True)])
    return shifted(value, GY, 1, True), value, shifted(value, GY, -1, True)


def bits_of(axis):
    count = lax.axis_size(axis)
    return [(axis, b) for b in range(count.bit_length() - 1)]


def swap(value, axis, bit):
    count = lax.axis_size(axis)
    return lax.ppermute(value, axis, [(i, i ^ (1 << bit)) for i in range(count)])


def bit_value(axis, bit):
    return (lax.axis_index(axis) >> bit) & 1


def part(arrays, at, size):
    total = lax.dynamic_slice_in_dim(arrays[0], at, size)
    for x in arrays[1:]:
        total = total + lax.dynamic_slice_in_dim(x, at, size)
    return total


class Chain:
    def __init__(self):
        self.last = None

    def after(self, values):
        if self.last is not None:
            self.last, values = lax.optimization_barrier((self.last, values))
        return values

    def step(self, value):
        self.last = value
        return value


def halved(chain, arrays, axis, bit, tight=False):
    arrays = chain.after(arrays)
    half = arrays[0].shape[0] // 2
    one = bit_value(axis, bit)
    send = chain.step(part(arrays, (1 - one) * half, half))
    got = swap(send, axis, bit)
    send, arrays = lax.optimization_barrier((send, arrays))
    keep = part(arrays, one * half, half)
    if tight:
        chain.step((send, keep))
    return [keep, got]


def joined_halves(value, other, axis, bit):
    one = bit_value(axis, bit) == 1
    return jnp.concatenate([jnp.where(one, other, value), jnp.where(one, value, other)])


def reduction(chain, first, second, tight=False):
    across, along = bits_of("gz"), bits_of("gyh")
    lanes = [first, second]
    for turn, plan in enumerate(((across, along), (along, across))):
        for i in range(2):
            for axis, bit in plan[i]:
                lanes[i] = halved(chain, lanes[i], axis, bit, tight and turn == 1)
        yield
    sizes = [x[0].shape[0] for x in lanes]
    joint = [jnp.concatenate(pair) for pair in zip(*chain.after(lanes))]
    for axis, bit in bits_of("gx"):
        joint = halved(chain, joint, axis, bit, tight)
        yield
    joint = chain.after(joint)
    value = chain.step(sum(joint[1:], joint[0]))
    for axis, bit in bits_of("gx")[::-1]:
        other = swap(value, axis, bit)
        yield
        value, other = chain.after((value, other))
        value = chain.step(joined_halves(value, other, axis, bit))
    values = [value[: sizes[0]], value[sizes[0] :]]
    for plan in ((along, across), (across, along)):
        for turn in range(max(len(across), len(along))):
            others = [None, None]
            for i in range(2):
                if turn < len(plan[i]):
                    others[i] = swap(values[i], *plan[i][::-1][turn])
            yield
            for i in range(2):
                if turn < len(plan[i]):
                    values[i], others[i] = chain.after((values[i], others[i]))
                    values[i] = chain.step(joined_halves(values[i], others[i], *plan[i][::-1][turn]))
    others = [swap(x, "gyl", 0) for x in values]
    yield
    values, others = chain.after((values, others))
    return [(value, chain.step(other)) for value, other in zip(values, others)]


def iota(shape, dim):
    return lax.broadcasted_iota(jnp.int32, shape, dim)


def dot(left, right, dims=NN):
    return lax.dot_general(left, right, dims, preferred_element_type=F32)


def halves(x):
    high = x.astype(BF)
    return high, (x - high.astype(F32)).astype(BF)


def stacked(x):
    high, low = halves(x)
    if x.shape[0] % 16 == 0:
        return jnp.concatenate([high, low], axis=0)
    return jnp.concatenate([high.astype(F32), low.astype(F32)], axis=0).astype(BF)


def folded(x):
    half = x.shape[0] // 2
    return x[:half] + x[half:]


def times(x, weight, dims=NN):
    return folded(dot(stacked(x), weight, dims))


def side_by_side(x):
    return jnp.concatenate(halves(x), axis=1)


def side_sum(x):
    half = x.shape[1] // 2
    return x[:, :half] + x[:, half:]


def weight_grad(x, y):
    x_high, x_low = halves(x)
    y_high, y_low = halves(y)
    left, right = [x_high, x_high, x_low], [y_high, y_low, y_high]
    if x.shape[0] % 16 == 0:
        return dot(jnp.concatenate(left, axis=0), jnp.concatenate(right, axis=0), TN)
    left = jnp.concatenate([p.astype(F32) for p in left], axis=0).astype(BF)
    right = jnp.concatenate([p.astype(F32) for p in right], axis=0).astype(BF)
    return dot(left, right, TN)


def onehot(hit):
    return jnp.where(hit, 1.0, 0.0).astype(BF)


def sigmoid(v):
    return 1.0 / (1.0 + jnp.exp(-v))


def act(v):
    return v * sigmoid(v) * (1.0 / 0.6)


def act_and_slope(v):
    s = sigmoid(v)
    return v * s * (1.0 / 0.6), s * (1.0 + v * (1.0 - s)) * (1.0 / 0.6)


def sin_pi(t):
    n = jnp.floor(t + 0.5)
    r = t - n
    odd = n - 2.0 * jnp.floor(n * 0.5)
    q = r * r
    total = jnp.zeros_like(r)
    for k in range(6, -1, -1):
        total = total * q + (-1.0) ** k * math.pi ** (2 * k + 1) / math.factorial(2 * k + 1)
    return total * r * (1.0 - 2.0 * odd)


def to_column(row):
    n = row.shape[1]
    same = iota((n, n), 0) == iota((n, n), 1)
    return jnp.sum(jnp.where(same, row, jnp.zeros_like(row)), axis=1, keepdims=True)


def send_column(send, rows):
    shape = (rows, SEND)
    hit = (iota(shape, 0) & (SEND - 1)) == iota(shape, 1)
    return jnp.sum(jnp.where(hit, send, 0), axis=1, keepdims=True)


def send_lanes(send):
    shape = (8, 128)
    hit = iota(shape, 0) == (iota(shape, 1) & (SEND - 1))
    return jnp.sum(jnp.where(hit, send_column(send, 8), 0), axis=0, keepdims=True)


def paid(row, send):
    edge = send * SLOTS + 2 * (row >> 3) + ((row >> 2) & 1)
    return jnp.where(row < 120, edge, -1)


def atom_of(edge):
    total = jnp.zeros_like(edge)
    for a in range(1, ATOMS):
        total = total + jnp.where(edge >= a * SLOTS, 1, 0)
    return total


def radial_of(length):
    x = length / 12.0
    x2 = x * x
    x4 = x2 * x2
    envelope = 1.0 - 28.0 * (x4 * x2) + 48.0 * (x4 * x2 * x) - 21.0 * (x4 * x4)
    orders = (iota((1, RADIAL), 1) + 1).astype(F32)
    return envelope * sin_pi(x * orders) / x


def geometry(unit):
    own = atom_of(iota((8, EDGES), 1)) == iota((8, EDGES), 0)
    edge = iota((EDGES, 128), 0)
    slot = edge - atom_of(edge) * SLOTS
    total = jnp.zeros((24, 128), F32)
    for k in range(3):
        x = jnp.where(own, unit[k : k + 1, :], 0.0)
        high = x.astype(BF).astype(F32)
        mid = (x - high).astype(BF).astype(F32)
        parts = jnp.concatenate([high, mid, x - high - mid], axis=0).astype(BF)
        total = total + dot(parts, onehot(iota((EDGES, 128), 1) == slot + 32 * k))
    return total[0:8] + total[8:16] + total[16:24]


def local_rows(index):
    return (index & 7) * SLOTS + 2 * (index >> 4) + ((index >> 3) & 1)


def start_kernel(
    edge, vec, mask, hidden, tag_row, send_row, table, w_in, w_rad, w_trip, w_quad,
    payload, local, tagged, pre, downs, rads, radial_out, columns,
):
    vectors = vec[...]
    length = jnp.sqrt(jnp.sum(vectors * vectors, axis=0, keepdims=True))
    unit = vectors / length
    geo = geometry(unit)
    live = to_column(jnp.where(mask[...] > 0, 1.0, 0.0))
    parts = [live] + [to_column(unit[k : k + 1, :]) for k in range(3)]
    columns[...] = jnp.concatenate(parts + [jnp.zeros((EDGES, 124), F32)], axis=1)
    send = send_column(send_row[...], 8)
    pay = paid(iota((128, 1), 0), send_column(send_row[...], 128))
    tags = to_column(tag_row[...])
    radial = radial_of(to_column(length))
    radial_out[...] = radial
    split = stacked(radial)
    for k in range(5):
        rads[k] = folded(dot(split, w_rad[k]))
    split = stacked(edge[...])
    pre[0] = folded(dot(split, w_in[0]))
    pre[1] = folded(dot(split, w_in[1]))
    trip_pre = times(act(pre[0]) * rads[0], w_trip[...], NT)
    quad_pre = times(act(pre[1]) * rads[1], w_quad[...], NT)
    downs[...] = jnp.concatenate([trip_pre, quad_pre, jnp.zeros((EDGES, 32), F32)], axis=1)
    trip = act(trip_pre) * live
    quad = act(quad_pre) * live
    rows = jnp.concatenate([trip, quad * radial[:, 0:1], quad * radial[:, 1:2]], axis=1)
    rows = side_by_side(rows)
    shape = (EDGES, EDGES)
    place = onehot(local_rows(iota(shape, 0)) == iota(shape, 1))
    local[0:15] = side_sum(dot(place, rows)).reshape(15, 16, 128)
    place = onehot(pay == iota((128, EDGES), 1))
    payload[0:16] = side_sum(dot(place, rows)).reshape(16, 8, 128)
    tag = hidden[...]
    for t in range(3):
        tag = tag + jnp.where(tags == t, table[t : t + 1, :].astype(F32), 0.0)
    tagged[...] = tag
    local[15] = jnp.concatenate([tag[:, :128], tag[:, 128:]], axis=0)
    local[16] = jnp.concatenate([geo, jnp.zeros((8, 128), F32)], axis=0)
    both = jnp.concatenate([tag, geo], axis=1)
    sent = jnp.zeros((8, 384), F32)
    for a in range(ATOMS):
        sent = sent + jnp.where(send == a, both[a : a + 1, :], 0.0)
    payload[15] = jnp.where(iota((8, 128), 0) < 4, sent[:, :128], sent[:, 128:256])
    payload[16] = sent[:, 256:]


def split_cores(core, whole, keep, send):
    half = whole.shape[0] // 2
    upper = core[0] == 1
    low, high = whole[:half], whole[half:]
    keep[...] = jnp.where(upper, high, low)
    send[...] = jnp.where(upper, low, high)


def segments(shape, edge_dim, atom_dim):
    edge, atom = iota(shape, edge_dim), iota(shape, atom_dim) & 7
    return onehot((edge >= atom * SLOTS) & (edge < atom * SLOTS + SLOTS))


def legendre(cosine):
    before, now = jnp.ones_like(cosine), cosine
    yield before
    yield now
    for k in range(1, ANGLES - 1):
        before, now = now, ((2 * k + 1) / (k + 1)) * cosine * now - (k / (k + 1)) * before
        yield now


def main_kernel(
    halo_before, halo_here, halo_after, local, tagged, edge, columns, rads, radial,
    src_cols, slots, marks,
    trip_bil, trip_up, quad_bil, quad_up, w_ae, w_res, w_ea, w_ad,
    cot_atoms, cot_edges, cot_energy, core,
    atoms_out, edges_out, energy_out, grad_edges, grad_tag,
    cosines, grad_sums, grad_src, keep, send, grad_rads, atom_rows, quad_up_grad,
    table, sums, weight, kept, cos_table, first,
):
    live = columns[:, 0:1]
    halos = (halo_before, halo_here, halo_after)
    group = halo_here.shape[0] * 8
    depth = 3 * group + 16
    lanes = iota((EDGES, depth), 1)
    place = jnp.concatenate(
        [onehot(src_cols[:, 0:1] == lanes), onehot(src_cols[:, 1:2] == lanes)], axis=0
    )

    def rows_at(p):
        parts = [h[:, p].reshape(group, 128) for h in halos]
        return jnp.concatenate(parts + [local[p]], axis=0)

    def gather_pair(p, carry):
        got = dot(place, side_by_side(rows_at(p))).astype(BF)
        table[2 * p] = got[:EDGES]
        table[2 * p + 1] = got[EDGES:]
        return carry

    lax.fori_loop(0, 16, gather_pair, 0)

    rows = rows_at(16)
    high, low = halves(rows)
    rest = (rows - high.astype(F32) - low.astype(F32)).astype(BF)
    got = dot(place[:EDGES], jnp.concatenate([high, low, rest], axis=1))
    got = got[:, :128] + got[:, 128:256] + got[:, 256:]
    cos_table[...] = -(
        columns[:, 1:2] * got
        + columns[:, 2:3] * pltpu.roll(got, 96, 1)
        + columns[:, 3:4] * pltpu.roll(got, 64, 1)
    )

    for k in range(ANGLES):
        top = trip_bil[:, k * 64 : k * 64 + 64].astype(F32)
        top = jnp.concatenate([top, jnp.zeros((64, 64), F32)], axis=1)
        low_left = quad_bil[:, k * 32 : k * 32 + 32].astype(F32)
        low_right = quad_bil[:, 512 + k * 32 : 544 + k * 32].astype(F32)
        bottom = jnp.concatenate([jnp.zeros((32, 64), F32), low_left, low_right], axis=1)
        piece = jnp.concatenate([top, bottom, jnp.zeros((32, 128), F32)], axis=0)
        weight[:, k * 128 : (k + 1) * 128] = piece.astype(BF)

    trip_lanes = iota((128, 128), 1) < TRIP_W
    scale = 1.0 / math.sqrt(PICKS)

    def basis_block(b, carry):
        at = pl.multiple_of(b * BLOCK, BLOCK)
        own = pl.ds(at, BLOCK)
        wide = iota((BLOCK, 512), 1)
        mark = marks[own, :]
        hits = [jnp.where(mark[:, t : t + 1] == wide, 1.0, 0.0) for t in range(2 * PICKS)]
        hits = jnp.concatenate(hits, axis=0).astype(BF)
        got = side_sum(dot(hits, table[:, own, :].reshape(512, 256)))
        picked = jnp.where(trip_lanes, got[:128], got[128:]) * scale
        picked = picked.reshape(PICKS, BLOCK, 128)
        cos_here = cos_table[own, :]
        slot = slots[own, :]
        low_lanes = iota((BLOCK, 128), 1) < TRIP_W
        for h in range(2):
            rows = slice(8 * h, 8 * h + 8)
            cos = []
            for j in range(PICKS):
                index = jnp.where(
                    low_lanes[rows], slot[rows, j : j + 1], slot[rows, PICKS + j : PICKS + j + 1]
                )
                cos.append(jnp.take_along_axis(cos_here[rows], index, axis=1))
            cos = jnp.stack(cos)
            cosines[2 * b + h] = cos
            values = picked[:, rows]
            for k, poly in enumerate(legendre(cos)):
                sums[pl.ds(pl.multiple_of(at + 8 * h, 8), 8), k * 128 : (k + 1) * 128] = jnp.sum(
                    poly * values, axis=0
                )
        return carry

    lax.fori_loop(0, BLOCKS, basis_block, 0)

    down = times(sums[...], weight[...], NT)
    down_act, down_slope = act_and_slope(down)
    trip_h, quad_h = down_act[:, :64], down_act[:, 64:96]
    trip_pre = times(trip_h, trip_up[...])
    quad_pre = times(quad_h, quad_up[...])
    src = jnp.concatenate(
        [side_sum(table[30].astype(F32)), side_sum(table[31].astype(F32))], axis=1
    )
    target = times(tagged[...], w_ae[1])
    spread = segments((EDGES, 16), 0, 1)
    gathers = segments((8, EDGES), 1, 0)

    def to_edges(x):
        return dot(spread, stacked(x))

    def to_atoms(x):
        return side_sum(dot(gathers, side_by_side(x)))

    atom_pre = times(src, w_ae[0]) + to_edges(target)
    atom_act, atom_slope = act_and_slope(atom_pre)
    trip_act, trip_slope = act_and_slope(trip_pre)
    quad_act, quad_slope = act_and_slope(quad_pre)
    merged = (edge[...] + trip_act + quad_act + atom_act * rads[2]) * 0.5
    kept[0] = merged
    first_act, first_slope = act_and_slope(times(merged, w_res[0]))
    kept[1] = first_act
    second_act, second_slope = act_and_slope(times(first_act, w_res[1]))
    new_edges = (merged + second_act) * root_half
    edges_out[...] = new_edges
    weighted = new_edges * live
    root_slots = 1.0 / math.sqrt(SLOTS)
    gathered = to_atoms(weighted * rads[3]) * root_slots
    summary = to_atoms(weighted * rads[4]) * root_slots
    gate_act, gate_slope = act_and_slope(times(gathered, w_ea[0]))
    updated = (tagged[...] + gate_act) * root_half
    a0_act, a0_slope = act_and_slope(times(updated, w_ad[0]))
    a1_act, a1_slope = act_and_slope(times(a0_act, w_ad[1]))
    new_atoms = (updated + a1_act) * root_half
    atoms_out[...] = new_atoms
    e_act, e_slope = act_and_slope(times(summary, w_ea[1]) + times(new_atoms, w_ad[2]))
    out_act, out_slope = act_and_slope(times(e_act, w_ad[3]))
    energy_out[...] = out_act

    d_out = cot_energy[...] * out_slope
    d_e = times(d_out, w_ad[3], NT) * e_slope
    d_summary = times(d_e, w_ea[1], NT)
    d_atoms = (cot_atoms[...] + times(d_e, w_ad[2], NT)) * root_half
    d_a1 = d_atoms * a1_slope
    d_a0 = times(d_a1, w_ad[1], NT) * a0_slope
    d_updated = (d_atoms + times(d_a0, w_ad[0], NT)) * root_half
    d_gate = d_updated * gate_slope
    d_gathered = times(d_gate, w_ea[0], NT)

    d_gathered = to_edges(d_gathered * root_slots)
    d_summary = to_edges(d_summary * root_slots)
    grad_rads[1] = weighted * d_gathered
    grad_rads[2] = weighted * d_summary
    d_new = cot_edges[...] + live * (d_gathered * rads[3] + d_summary * rads[4])
    d_new = d_new * root_half
    d_second = d_new * second_slope
    kept[3] = d_second
    d_first = times(d_second, w_res[1], NT) * first_slope
    kept[2] = d_first
    d_merged = (d_new + times(d_first, w_res[0], NT)) * 0.5
    grad_edges[...] = d_merged
    grad_rads[0] = d_merged * atom_act
    d_atom = d_merged * rads[2] * atom_slope
    kept[4] = d_atom
    d_trip = d_merged * trip_slope
    d_quad = d_merged * quad_slope
    d_target = to_atoms(d_atom)
    grad_tag[...] = d_updated + times(d_target, w_ae[1], NT)
    d_down = jnp.concatenate(
        [times(d_trip, trip_up[...], NT), times(d_quad, quad_up[...], NT), jnp.zeros((EDGES, 32), F32)],
        axis=1,
    )
    d_down = d_down * down_slope
    grad_src[...] = times(d_atom, w_ae[0], NT)

    first[0:512] = weight_grad(kept[0], kept[2])
    first[512:768] = weight_grad(src, kept[4])
    first[896:1408] = weight_grad(kept[1], kept[3])
    first[1408:1664] = weight_grad(tagged[...], d_target)
    bil = weight_grad(d_down, sums[...])
    for m in range(8):
        tile = [bil[0:64, k * 128 : k * 128 + 64] for k in (2 * m, 2 * m + 1)]
        row = 768 + 64 * (m // 4)
        first[row : row + 64, (m % 4) * 128 : (m % 4 + 1) * 128] = jnp.concatenate(tile, axis=1)
    for half in range(2):
        for m in range(4):
            at = 64 + 32 * half
            tile = [bil[64:96, k * 128 + at : k * 128 + at + 32] for k in range(4 * m, 4 * m + 4)]
            row = 1728 + 32 * half
            first[row : row + 32, m * 128 : (m + 1) * 128] = jnp.concatenate(tile, axis=1)
    first[1664:1728] = weight_grad(down_act, d_trip)[:64]
    quad_up_grad[...] = weight_grad(down_act, d_quad)[64:96]
    atom_rows[...] = jnp.concatenate(
        [gathered, summary, updated, a0_act, new_atoms, e_act, d_a0, d_a1, d_e, d_out, d_gate], axis=1
    )
    split_cores(core, first, keep, send)
    grad_sums[...] = times(d_down, weight[...])


def late_kernel(grad_rads, radial, atom_rows, quad_up_grad, core, keep, send, second):
    atoms = atom_rows[...]
    gathered, summary = atoms[:, :512], atoms[:, 512:1024]
    updated, a0_act, new_atoms, e_act, d_a0, d_a1, d_e, d_out, d_gate = [
        atoms[:, at : at + 256] for at in range(1024, 3328, 256)
    ]
    second[0:512, 0:256] = weight_grad(gathered, d_gate)
    second[0:512, 256:512] = weight_grad(summary, d_e)
    second[512:768, 0:256] = weight_grad(updated, d_a0)
    second[512:768, 256:512] = weight_grad(a0_act, d_a1)
    second[768:1024, 0:256] = weight_grad(new_atoms, d_e)
    second[768:1024, 256:512] = weight_grad(e_act, d_out)
    for k in range(3):
        second[1024 + 128 * k : 1152 + 128 * k] = weight_grad(radial[...], grad_rads[k])
    second[1408:1440] = quad_up_grad[...]
    second[1440:1536] = jnp.zeros((96, 512), F32)
    split_cores(core, second, keep, send)


def scatter_kernel(
    cosines, sums, grad_src, src_rows, mark_rows,
    back_before, back_here, back_after, back_local,
    table,
):
    group = back_here.shape[0] * 8
    depth = 3 * group + 16
    trip_lanes = iota((128, 128), 1) < TRIP_W
    scale = 1.0 / math.sqrt(PICKS)

    def basis_back(b, carry):
        at = pl.multiple_of(b * BLOCK, BLOCK)
        own = pl.ds(at, BLOCK)
        parts = []
        for h in range(2):
            total = jnp.zeros((PICKS, 8, 128), F32)
            for k, poly in enumerate(legendre(cosines[2 * b + h])):
                total = total + poly * sums[pl.ds(pl.multiple_of(at + 8 * h, 8), 8), k * 128 : (k + 1) * 128]
            parts.append(total * scale)
        grad = jnp.concatenate(parts, axis=1).reshape(128, 128)
        grad = jnp.concatenate(
            [jnp.where(trip_lanes, grad, 0.0), jnp.where(trip_lanes, 0.0, grad)], axis=0
        )
        hits = onehot(mark_rows[b] == iota((512, 256), 0))
        got = side_by_side(side_sum(dot(hits, side_by_side(grad))))
        table[:, own, :] = got.reshape(32, BLOCK, 256)
        return carry

    lax.fori_loop(0, BLOCKS, basis_back, 0)
    table[30] = side_by_side(grad_src[:, :128])
    table[31] = side_by_side(grad_src[:, 128:])
    rows = iota((depth, EDGES), 0)
    place_even = onehot(src_rows[0:1, :] == rows)
    place_odd = onehot(src_rows[1:2, :] == rows)

    def scatter_pair(p, carry):
        got = side_sum(dot(place_even, table[2 * p]) + dot(place_odd, table[2 * p + 1]))
        for i, back in enumerate((back_before, back_here, back_after)):
            back[:, p] = got[i * group : (i + 1) * group].reshape(group // 8, 8, 128)
        back_local[p] = got[3 * group :]
        return carry

    lax.fori_loop(0, 16, scatter_pair, 0)


def finish_kernel(
    back_local, returned, grad_late, tag_late, edge, radial, columns, pre, downs, rads, tag_row, send_row,
    w_in, w_trip, w_quad, core,
    grad_atoms, grad_edges, keep_first, send_first, keep_second, send_second,
    first, second,
):
    shape = (EDGES, 256)
    lane = iota(shape, 1)
    place = onehot((local_rows(lane) == iota(shape, 0)) & (lane < EDGES))
    rows = dot(place, side_by_side(back_local[...].reshape(256, 128)))
    pay = paid(iota((1, 128), 1), send_lanes(send_row[...]))
    place = onehot(pay == iota((EDGES, 128), 0))
    send = send_column(send_row[...], 8)
    tags = to_column(tag_row[...])
    rows = side_sum(rows + dot(place, side_by_side(returned[...].reshape(128, 128))))
    back = returned[15]
    tag = tag_late[...] + jnp.concatenate([back_local[15, 0:8], back_local[15, 8:16]], axis=1)
    atom = iota((8, 1), 0)
    for r in range(SEND):
        piece = jnp.concatenate([back[r : r + 1], back[4 + r : 5 + r]], axis=1)
        tag = tag + jnp.where(send[r : r + 1, :] == atom, piece, 0.0)
    grad_atoms[...] = tag
    table = [
        jnp.sum(jnp.where(tags == t, tag, 0.0), axis=0, keepdims=True) for t in range(3)
    ]
    table = jnp.concatenate(table + [jnp.zeros((29, ATOM_W), F32)], axis=0)
    d_trip = rows[:, :64]
    d_quad = rows[:, 64:96] * radial[:, 0:1] + rows[:, 96:128] * radial[:, 1:2]
    total = grad_late[...]
    for k, (d_row, down, weight, out) in enumerate(
        ((d_trip, slice(0, 64), w_trip, first), (d_quad, slice(64, 96), w_quad, second))
    ):
        d_down = d_row * columns[:, 0:1] * act_and_slope(downs[:, down])[1]
        value, slope = act_and_slope(pre[k])
        d_start = times(d_down, weight[...])
        d_pre = d_start * rads[k] * slope
        total = total + times(d_pre, w_in[k], NT)
        out[0:512] = weight_grad(edge[...], d_pre)
        out[512:640] = weight_grad(radial[...], d_start * value)
        down_grad = weight_grad(d_down, value * rads[k])
        if k == 0:
            out[640:704] = down_grad
            out[704:768] = jnp.zeros((64, 512), F32)
        else:
            out[640:672] = down_grad
            out[672:704, 0:256] = table
            out[672:704, 256:512] = jnp.zeros((32, 256), F32)
            out[704:768] = jnp.zeros((64, 512), F32)
    grad_edges[...] = total
    split_cores(core, first, keep_first, send_first)
    split_cores(core, second, keep_second, send_second)


def late_outputs(
    a_mine, a_other, b_mine, b_other, core,
    res, ae, trip_bil, trip_up, quad_bil, quad_up, rad, ea, ad,
):
    upper = core[0] == 1

    def rows(mine, other, at, size):
        half = mine.shape[0]
        where = slice(at % half, at % half + size)
        if at < half:
            return jnp.where(upper, other[where], mine[where])
        return jnp.where(upper, mine[where], other[where])

    a = lambda at, size: rows(a_mine, a_other, at, size)
    b = lambda at, size: rows(b_mine, b_other, at, size)
    for k in range(2):
        res[k] = a(896 * k, 512)
        ae[k] = a(896 * k + 512, 256)
        trip_bil[:, 512 * k : 512 * k + 512] = a(768 + 64 * k, 64)
        quad_bil[:, 512 * k : 512 * k + 512] = a(1728 + 32 * k, 32)
    trip_up[...] = a(1664, 64)
    quad_up[...] = b(1408, 32)
    for k in range(3):
        rad[k] = b(1024 + 128 * k, 128)
    both = b(0, 512)
    ea[0], ea[1] = both[:, :256], both[:, 256:]
    both = b(512, 256)
    ad[0], ad[1] = both[:, :256], both[:, 256:]
    both = b(768, 256)
    ad[2], ad[3] = both[:, :256], both[:, 256:]


def early_outputs(c_mine, c_other, d_mine, d_other, late_rad, core, inputs, rad, trip_down, quad_down, tags):
    upper = core[0] == 1
    for k, (mine, other) in enumerate(((c_mine, c_other), (d_mine, d_other))):
        inputs[k, 0:384] = jnp.where(upper, other[...], mine[...])
        high = jnp.where(upper, mine[...], other[...])
        inputs[k, 384:512] = high[:128]
        rad[k] = high[128:256]
        if k == 0:
            trip_down[...] = high[256:320]
        else:
            quad_down[...] = high[256:288]
            tags[...] = high[288:291, :256]
    rad[2:5] = late_rad[...]


def call(kernel, outs, args, scratch=(), micros=1):
    flops = int(micros * 1.15e9)
    return pl.pallas_call(
        kernel,
        out_shape=[jax.ShapeDtypeStruct(shape, F32) for shape in outs],
        in_specs=[pl.BlockSpec(memory_space=pltpu.SMEM if x.ndim == 1 else pltpu.VMEM) for x in args],
        out_specs=[pl.BlockSpec(memory_space=pltpu.VMEM)] * len(outs),
        scratch_shapes=list(scratch),
        compiler_params=pltpu.CompilerParams(vmem_limit_bytes=56 * 1024 * 1024),
        cost_estimate=pl.CostEstimate(flops=flops, bytes_accessed=1 << 10, transcendentals=0),
    )(*args)


def per_device(
    hidden_atoms,
    edge_states,
    edge_vectors,
    atom_tags,
    send_list,
    sources,
    trip_slots,
    triplet_mask,
    quad_slots,
    quad_mask,
    edge_mask,
    w_inputs,
    w_radial,
    w_trip_down,
    triplet_bilinear_weight,
    w_trip_up,
    w_quad_down,
    w_quad_bil,
    w_quad_up,
    w_atom_edge,
    w_residual,
    w_edge_atom,
    w_atom_dense,
    tag_table,
    cot_atoms,
    cot_edges,
    cot_energy,
):
    planes = 2 if lax.axis_size("gz") == 2 else 3
    group = 3 * planes

    offset = jnp.maximum(sources - ATOMS, 0)
    block, border = offset // SEND, offset % SEND
    step_x, step_y, step_z = block // 9, block // 3 % 3, block % 3
    if planes == 2:
        step_z = jnp.clip(step_z - 1 + lax.axis_index("gz"), 0, 1)
    block = (step_y * 3 + step_x) * planes + step_z
    inside = sources < ATOMS
    even = jnp.where(inside, 3 * group * 8 + sources, block * 8 + border)
    src = jnp.stack([even, even + jnp.where(inside, ATOMS, SEND)])
    slots = jnp.concatenate([trip_slots, quad_slots], axis=1)
    masks = jnp.concatenate([triplet_mask, quad_mask], axis=1)
    marks = jnp.where(masks > 0, slots * BLOCK + (jnp.arange(EDGES) % BLOCK)[:, None], -1)
    mark_rows = marks.reshape(BLOCKS, BLOCK, 2 * PICKS).transpose(0, 2, 1)
    mark_rows = mark_rows.reshape(BLOCKS, 1, 2 * PICKS * BLOCK)
    trip_down_t, quad_down_t = w_trip_down.T, w_quad_down.T

    tag_row, send_row = atom_tags[None, :], send_list[None, :]
    payload, local, tagged, pre, downs, rads, radial, columns = call(
        start_kernel,
        [(PAIRS, 8, 128), (PAIRS, 16, 128), (8, 256), (2, EDGES, 512), (EDGES, 128), (5, EDGES, 512)]
        + [(EDGES, 128)] * 2,
        [edge_states, edge_vectors, edge_mask[None, :], hidden_atoms, tag_row, send_row, tag_table,
         w_inputs, w_radial, trip_down_t, quad_down_t],
        micros=5,
    )
    core = bit_value("gyl", 0)[None]
    before, here, after = with_halo(payload)
    (
        atoms_out, edges_out, energy_out, grad_edges, grad_tag,
        cosines, grad_sums, grad_src, keep_a, send_a, grad_rads, atom_rows, quad_up_grad,
    ) = call(
        main_kernel,
        [(8, 256), (EDGES, 512), (8, 256), (EDGES, 512), (8, 256)]
        + [(2 * BLOCKS, PICKS, 8, 128), (EDGES, 2048), (EDGES, 256), (896, 512), (896, 512)]
        + [(3, EDGES, 512), (8, 3328), (32, 512)],
        [before, here, after, local, tagged, edge_states, columns, rads, radial,
         src.T, slots, marks,
         triplet_bilinear_weight.T, w_trip_up, w_quad_bil.T, w_quad_up, w_atom_edge, w_residual,
         w_edge_atom, w_atom_dense, cot_atoms, cot_edges, cot_energy, core],
        scratch=[
            pltpu.VMEM((32, EDGES, 256), BF),
            pltpu.VMEM((EDGES, 2048), F32),
            pltpu.VMEM((128, 2048), BF),
            pltpu.VMEM((5, EDGES, 512), F32),
            pltpu.VMEM((EDGES, 128), F32),
            pltpu.VMEM((1792, 512), F32),
        ],
        micros=26,
    )
    chain = Chain()
    got_a = swap(send_a, "gyl", 0)
    keep_b, send_b = call(
        late_kernel,
        [(768, 512)] * 2,
        [grad_rads, radial, atom_rows, quad_up_grad, core],
        scratch=[pltpu.VMEM((1536, 512), F32)],
        micros=4,
    )
    late = reduction(chain, [keep_a, got_a], [keep_b, swap(send_b, "gyl", 0)], True)
    next(late)
    grad_sums = chain.after(grad_sums)
    back_before, back_here, back_after, back_local = call(
        scatter_kernel,
        [(group, 16, 8, 128)] * 3 + [(16, 16, 128)],
        [cosines, grad_sums, grad_src, src, mark_rows],
        scratch=[pltpu.VMEM((32, EDGES, 256), BF)],
        micros=13,
    )
    got = shifted(back_before, GY, -1, True), shifted(back_after, GY, 1, True)
    chain.step(back_local)
    next(late)
    got, value = chain.after((got, back_here))
    value = chain.step(value + got[0] + got[1])
    first_plane, middle, last_plane = value[:planes], value[planes : 2 * planes], value[2 * planes :]
    got = shifted(first_plane, "gx", -1, True), shifted(last_plane, "gx", 1, True)
    got, middle = chain.after((got, middle))
    value = chain.step(middle + got[0] + got[1])
    next(late)
    if planes == 2:
        top = lax.axis_index("gz") == 1
        mine = jnp.where(top, value[1], value[0])
        theirs = jnp.where(top, value[0], value[1])
        returned = mine + lax.ppermute(theirs, "gz", [(0, 1), (1, 0)])
    else:
        returned = value[1] + shifted(value[0], "gz", -1, False) + shifted(value[2], "gz", 1, False)
    returned = chain.after(returned)
    grad_atoms, grad_edges, keep_c, send_c, keep_d, send_d = call(
        finish_kernel,
        [(8, 256), (EDGES, 512)] + [(384, 512)] * 4,
        [back_local, returned, grad_edges, grad_tag, edge_states, radial, columns, pre, downs, rads,
         tag_row, send_row, w_inputs, trip_down_t, quad_down_t, core],
        scratch=[pltpu.VMEM((768, 512), F32)] * 2,
        micros=7,
    )
    next(late)
    send_c, send_d = chain.after((send_c, send_d))
    got_c, got_d = swap(send_c, "gyl", 0), swap(send_d, "gyl", 0)
    early = reduction(chain, [keep_c, got_c], [keep_d, got_d])
    running = {"L": late, "E": early}
    done = {}

    def resume(name):
        if name in done:
            return
        try:
            next(running[name])
        except StopIteration as end:
            done[name] = end.value

    for name in "ELEELELEELEELEL":
        resume(name)
    while "L" not in done:
        resume("L")
    (a_mine, a_other), (b_mine, b_other) = done["L"]
    g_res, g_ae, g_trip_bil, g_trip_up, g_quad_bil, g_quad_up, g_rad, g_ea, g_ad = call(
        late_outputs,
        [(2, 512, 512), (2, 256, 512), (64, 1024), (64, 512), (32, 1024), (32, 512), (3, 128, 512)]
        + [(2, 512, 256), (4, 256, 256)],
        [a_mine, a_other, b_mine, b_other, core],
        micros=5,
    )
    chain.step(g_rad)
    while "E" not in done:
        resume("E")
    (c_mine, c_other), (d_mine, d_other) = done["E"]
    g_inputs, g_rad, g_trip_down, g_quad_down, g_tags = call(
        early_outputs,
        [(2, 512, 512), (5, 128, 512), (64, 512), (32, 512), (3, 256)],
        [c_mine, c_other, d_mine, d_other, g_rad, core],
        micros=3,
    )
    return (
        atoms_out,
        edges_out,
        energy_out,
        grad_atoms,
        grad_edges,
        g_inputs,
        g_rad,
        g_trip_down.T,
        g_trip_bil.T,
        g_trip_up,
        g_quad_down.T,
        g_quad_bil.T,
        g_quad_up,
        g_ae,
        g_res,
        g_ea,
        g_ad,
        g_tags,
    )


def solution(mesh):
    size = dict(mesh.shape)
    inner = Mesh(mesh.devices.reshape(size["gx"], size["gy"] // 2, 2, size["gz"]), ROWS)
    flat, columns, vector, whole = P(ROWS, None), P(None, ROWS), P(ROWS), P()
    placed = [flat, flat, columns] + [vector] * 3 + [flat] * 4 + [vector] + [whole] * 13 + [flat] * 3
    return jax.shard_map(
        per_device,
        mesh=inner,
        in_specs=tuple(placed),
        out_specs=tuple([flat] * 5 + [whole] * 13),
        check_vma=False,
    )
```

```python
import functools
import math

import jax
import jax.numpy as jnp
from jax import lax
from jax.experimental import pallas as pl
from jax.experimental.pallas import tpu as pltpu
from jax.sharding import Mesh
from jax.sharding import PartitionSpec as P

BF = jnp.bfloat16
F32 = jnp.float32
ROWS = ("gx", "gyh", "gyl", "gz")
GY = ("gyh", "gyl")
ATOMS, SEND, SLOTS, EDGES = 8, 4, 30, 240
ATOM_W, EDGE_W, TRIP_W, QUAD_W, RADIAL = 256, 512, 64, 32, 128
ANGLES, PICKS = 16, 8
PAIRS = 17
BLOCK = 16
BLOCKS = EDGES // BLOCK
root_half = 0.7071067811865476
NN = (((1,), (0,)), ((), ()))
NT = (((1,), (1,)), ((), ()))
TN = (((0,), (0,)), ((), ()))


def shifted(value, axis, steps, wrap):
    count = lax.axis_size(axis)
    pairs = [(i, (i + steps) % count) for i in range(count) if wrap or 0 <= i + steps < count]
    return lax.ppermute(value, axis, pairs)


def planes_of(value):
    if lax.axis_size("gz") == 2:
        other = lax.ppermute(value, "gz", [(0, 1), (1, 0)])
        top = lax.axis_index("gz") == 1
        return jnp.stack([jnp.where(top, other, value), jnp.where(top, value, other)])
    return jnp.stack([shifted(value, "gz", 1, False), value, shifted(value, "gz", -1, False)])


def with_halo(value):
    value = planes_of(value)
    value = jnp.concatenate([shifted(value, "gx", 1, True), value, shifted(value, "gx", -1, True)])
    return shifted(value, GY, 1, True), value, shifted(value, GY, -1, True)


def bits_of(axis):
    count = lax.axis_size(axis)
    return [(axis, b) for b in range(count.bit_length() - 1)]


def swap(value, axis, bit):
    count = lax.axis_size(axis)
    return lax.ppermute(value, axis, [(i, i ^ (1 << bit)) for i in range(count)])


def bit_value(axis, bit):
    return (lax.axis_index(axis) >> bit) & 1


def part(arrays, at, size):
    total = lax.dynamic_slice_in_dim(arrays[0], at, size)
    for x in arrays[1:]:
        total = total + lax.dynamic_slice_in_dim(x, at, size)
    return total


class Chain:
    def __init__(self):
        self.last = None

    def after(self, values):
        if self.last is not None:
            self.last, values = lax.optimization_barrier((self.last, values))
        return values

    def step(self, value):
        self.last = value
        return value


def halved(chain, arrays, axis, bit, tight=False):
    arrays = chain.after(arrays)
    half = arrays[0].shape[0] // 2
    one = bit_value(axis, bit)
    send = chain.step(part(arrays, (1 - one) * half, half))
    got = swap(send, axis, bit)
    send, arrays = lax.optimization_barrier((send, arrays))
    keep = part(arrays, one * half, half)
    if tight:
        chain.step((send, keep))
    return [keep, got]


def joined_halves(value, other, axis, bit):
    one = bit_value(axis, bit) == 1
    return jnp.concatenate([jnp.where(one, other, value), jnp.where(one, value, other)])


def reduction(chain, first, second, tight=False):
    across, along = bits_of("gz"), bits_of("gyh")
    lanes = [first, second]
    for turn, plan in enumerate(((across, along), (along, across))):
        for i in range(2):
            for axis, bit in plan[i]:
                lanes[i] = halved(chain, lanes[i], axis, bit, tight and turn == 1)
        yield
    sizes = [x[0].shape[0] for x in lanes]
    joint = [jnp.concatenate(pair) for pair in zip(*chain.after(lanes))]
    for axis, bit in bits_of("gx"):
        joint = halved(chain, joint, axis, bit, tight)
        yield
    joint = chain.after(joint)
    value = chain.step(sum(joint[1:], joint[0]))
    for axis, bit in bits_of("gx")[::-1]:
        other = swap(value, axis, bit)
        yield
        value, other = chain.after((value, other))
        value = chain.step(joined_halves(value, other, axis, bit))
    values = [value[: sizes[0]], value[sizes[0] :]]
    for plan in ((along, across), (across, along)):
        for turn in range(max(len(across), len(along))):
            others = [None, None]
            for i in range(2):
                if turn < len(plan[i]):
                    others[i] = swap(values[i], *plan[i][::-1][turn])
            yield
            for i in range(2):
                if turn < len(plan[i]):
                    values[i], others[i] = chain.after((values[i], others[i]))
                    values[i] = chain.step(joined_halves(values[i], others[i], *plan[i][::-1][turn]))
    others = [swap(x, "gyl", 0) for x in values]
    yield
    values, others = chain.after((values, others))
    return [(value, chain.step(other)) for value, other in zip(values, others)]


def iota(shape, dim):
    return lax.broadcasted_iota(jnp.int32, shape, dim)


def dot(left, right, dims=NN):
    return lax.dot_general(left, right, dims, preferred_element_type=F32)


def halves(x):
    high = x.astype(BF)
    return high, (x - high.astype(F32)).astype(BF)


def stacked(x):
    high, low = halves(x)
    if x.shape[0] % 16 == 0:
        return jnp.concatenate([high, low], axis=0)
    return jnp.concatenate([high.astype(F32), low.astype(F32)], axis=0).astype(BF)


def folded(x):
    half = x.shape[0] // 2
    return x[:half] + x[half:]


def times(x, weight, dims=NN):
    return folded(dot(stacked(x), weight, dims))


def side_by_side(x):
    return jnp.concatenate(halves(x), axis=1)


def side_sum(x):
    half = x.shape[1] // 2
    return x[:, :half] + x[:, half:]


def weight_grad(x, y):
    x_high, x_low = halves(x)
    y_high, y_low = halves(y)
    left, right = [x_high, x_high, x_low], [y_high, y_low, y_high]
    if x.shape[0] % 16 == 0:
        return dot(jnp.concatenate(left, axis=0), jnp.concatenate(right, axis=0), TN)
    left = jnp.concatenate([p.astype(F32) for p in left], axis=0).astype(BF)
    right = jnp.concatenate([p.astype(F32) for p in right], axis=0).astype(BF)
    return dot(left, right, TN)


def onehot(hit):
    return jnp.where(hit, 1.0, 0.0).astype(BF)


def sigmoid(v):
    return 1.0 / (1.0 + jnp.exp(-v))


def act(v):
    return v * sigmoid(v) * (1.0 / 0.6)


def act_and_slope(v):
    s = sigmoid(v)
    return v * s * (1.0 / 0.6), s * (1.0 + v * (1.0 - s)) * (1.0 / 0.6)


def sin_pi(t):
    n = jnp.floor(t + 0.5)
    r = t - n
    odd = n - 2.0 * jnp.floor(n * 0.5)
    q = r * r
    total = jnp.zeros_like(r)
    for k in range(6, -1, -1):
        total = total * q + (-1.0) ** k * math.pi ** (2 * k + 1) / math.factorial(2 * k + 1)
    return total * r * (1.0 - 2.0 * odd)


def to_column(row):
    n = row.shape[1]
    same = iota((n, n), 0) == iota((n, n), 1)
    return jnp.sum(jnp.where(same, row, jnp.zeros_like(row)), axis=1, keepdims=True)


def send_column(send, rows):
    shape = (rows, SEND)
    hit = (iota(shape, 0) & (SEND - 1)) == iota(shape, 1)
    return jnp.sum(jnp.where(hit, send, 0), axis=1, keepdims=True)


def send_lanes(send):
    shape = (8, 128)
    hit = iota(shape, 0) == (iota(shape, 1) & (SEND - 1))
    return jnp.sum(jnp.where(hit, send_column(send, 8), 0), axis=0, keepdims=True)


def paid(row, send):
    edge = send * SLOTS + 2 * (row >> 3) + ((row >> 2) & 1)
    return jnp.where(row < 120, edge, -1)


def atom_of(edge):
    total = jnp.zeros_like(edge)
    for a in range(1, ATOMS):
        total = total + jnp.where(edge >= a * SLOTS, 1, 0)
    return total


def radial_of(length):
    x = length / 12.0
    x2 = x * x
    x4 = x2 * x2
    envelope = 1.0 - 28.0 * (x4 * x2) + 48.0 * (x4 * x2 * x) - 21.0 * (x4 * x4)
    orders = (iota((1, RADIAL), 1) + 1).astype(F32)
    return envelope * sin_pi(x * orders) / x


def geometry(unit):
    own = atom_of(iota((8, EDGES), 1)) == iota((8, EDGES), 0)
    edge = iota((EDGES, 128), 0)
    slot = edge - atom_of(edge) * SLOTS
    total = jnp.zeros((24, 128), F32)
    for k in range(3):
        x = jnp.where(own, unit[k : k + 1, :], 0.0)
        high = x.astype(BF).astype(F32)
        mid = (x - high).astype(BF).astype(F32)
        parts = jnp.concatenate([high, mid, x - high - mid], axis=0).astype(BF)
        total = total + dot(parts, onehot(iota((EDGES, 128), 1) == slot + 32 * k))
    return total[0:8] + total[8:16] + total[16:24]


def local_rows(index):
    return (index & 7) * SLOTS + 2 * (index >> 4) + ((index >> 3) & 1)


def start_kernel(
    edge, vec, mask, hidden, tag_row, send_row, table, w_in, w_rad, w_trip, w_quad,
    payload, local, tagged, pre, downs, rads, radial_out, columns,
):
    vectors = vec[...]
    length = jnp.sqrt(jnp.sum(vectors * vectors, axis=0, keepdims=True))
    unit = vectors / length
    geo = geometry(unit)
    live = to_column(jnp.where(mask[...] > 0, 1.0, 0.0))
    parts = [live] + [to_column(unit[k : k + 1, :]) for k in range(3)]
    columns[...] = jnp.concatenate(parts + [jnp.zeros((EDGES, 124), F32)], axis=1)
    send = send_column(send_row[...], 8)
    pay = paid(iota((128, 1), 0), send_column(send_row[...], 128))
    tags = to_column(tag_row[...])
    radial = radial_of(to_column(length))
    radial_out[...] = radial
    split = stacked(radial)
    for k in range(5):
        rads[k] = folded(dot(split, w_rad[k]))
    split = stacked(edge[...])
    pre[0] = folded(dot(split, w_in[0]))
    pre[1] = folded(dot(split, w_in[1]))
    trip_pre = times(act(pre[0]) * rads[0], w_trip[...], NT)
    quad_pre = times(act(pre[1]) * rads[1], w_quad[...], NT)
    downs[...] = jnp.concatenate([trip_pre, quad_pre, jnp.zeros((EDGES, 32), F32)], axis=1)
    trip = act(trip_pre) * live
    quad = act(quad_pre) * live
    rows = jnp.concatenate([trip, quad * radial[:, 0:1], quad * radial[:, 1:2]], axis=1)
    rows = side_by_side(rows)
    shape = (EDGES, EDGES)
    place = onehot(local_rows(iota(shape, 0)) == iota(shape, 1))
    local[0:15] = side_sum(dot(place, rows)).reshape(15, 16, 128)
    place = onehot(pay == iota((128, EDGES), 1))
    payload[0:16] = side_sum(dot(place, rows)).reshape(16, 8, 128)
    tag = hidden[...]
    for t in range(3):
        tag = tag + jnp.where(tags == t, table[t : t + 1, :].astype(F32), 0.0)
    tagged[...] = tag
    local[15] = jnp.concatenate([tag[:, :128], tag[:, 128:]], axis=0)
    local[16] = jnp.concatenate([geo, jnp.zeros((8, 128), F32)], axis=0)
    both = jnp.concatenate([tag, geo], axis=1)
    sent = jnp.zeros((8, 384), F32)
    for a in range(ATOMS):
        sent = sent + jnp.where(send == a, both[a : a + 1, :], 0.0)
    payload[15] = jnp.where(iota((8, 128), 0) < 4, sent[:, :128], sent[:, 128:256])
    payload[16] = sent[:, 256:]


def split_cores(core, whole, keep, send):
    half = whole.shape[0] // 2
    upper = core[0] == 1
    low, high = whole[:half], whole[half:]
    keep[...] = jnp.where(upper, high, low)
    send[...] = jnp.where(upper, low, high)


def segments(shape, edge_dim, atom_dim):
    edge, atom = iota(shape, edge_dim), iota(shape, atom_dim) & 7
    return onehot((edge >= atom * SLOTS) & (edge < atom * SLOTS + SLOTS))


def lead(k):
    return math.comb(2 * k, k) / 2.0**k


def ratio(k):
    return k * k / (4.0 * k * k - 1.0)


def monic(cosine):
    before, now = jnp.ones_like(cosine), cosine
    yield before
    yield now
    for k in range(1, ANGLES - 1):
        before, now = now, cosine * now - ratio(k) * before
        yield now


def looped(count, step, body):
    def turn(t, carry):
        for i in range(step):
            body(t * step + i)
        return carry

    lax.fori_loop(0, count // step, turn, 0)


def main_kernel(
    halo_before, halo_here, halo_after, local, tagged, edge, columns, rads, radial,
    src_cols, slots, marks,
    trip_bil, trip_up, quad_bil, quad_up, w_ae, w_res, w_ea, w_ad,
    cot_atoms, cot_edges, cot_energy, core,
    atoms_out, edges_out, energy_out, grad_edges, grad_tag,
    cosines, grad_sums, grad_src, keep, send, grad_rads, atom_rows, quad_up_grad,
    table, sums, weight, kept, cos_table, first,
):
    live = columns[:, 0:1]
    halos = (halo_before, halo_here, halo_after)
    group = halo_here.shape[0] * 8
    depth = 3 * group + 16
    lanes = iota((EDGES, depth), 1)
    place = jnp.concatenate(
        [onehot(src_cols[:, 0:1] == lanes), onehot(src_cols[:, 1:2] == lanes)], axis=0
    )

    def rows_at(p):
        parts = [h[:, p].reshape(group, 128) for h in halos]
        return jnp.concatenate(parts + [local[p]], axis=0)

    def gather_pair(p):
        got = dot(place, side_by_side(rows_at(p))).astype(BF)
        table[2 * p] = got[:EDGES]
        table[2 * p + 1] = got[EDGES:]

    looped(16, 4, gather_pair)

    rows = rows_at(16)
    high, low = halves(rows)
    rest = (rows - high.astype(F32) - low.astype(F32)).astype(BF)
    got = dot(place[:EDGES], jnp.concatenate([high, low, rest], axis=1))
    got = got[:, :128] + got[:, 128:256] + got[:, 256:]
    cos_table[...] = -(
        columns[:, 1:2] * got
        + columns[:, 2:3] * pltpu.roll(got, 96, 1)
        + columns[:, 3:4] * pltpu.roll(got, 64, 1)
    )

    for k in range(ANGLES):
        top = trip_bil[:, k * 64 : k * 64 + 64].astype(F32)
        top = jnp.concatenate([top, jnp.zeros((64, 64), F32)], axis=1)
        low_left = quad_bil[:, k * 32 : k * 32 + 32].astype(F32)
        low_right = quad_bil[:, 512 + k * 32 : 544 + k * 32].astype(F32)
        bottom = jnp.concatenate([jnp.zeros((32, 64), F32), low_left, low_right], axis=1)
        piece = jnp.concatenate([top, bottom, jnp.zeros((32, 128), F32)], axis=0)
        weight[:, k * 128 : (k + 1) * 128] = piece.astype(BF)

    trip_lanes = iota((128, 128), 1) < TRIP_W
    scale = 1.0 / math.sqrt(PICKS)

    def basis_block(b):
        at = pl.multiple_of(b * BLOCK, BLOCK)
        own = pl.ds(at, BLOCK)
        wide = iota((BLOCK, 512), 1)
        mark = marks[own, :]
        hits = [jnp.where(mark[:, t : t + 1] == wide, 1.0, 0.0) for t in range(2 * PICKS)]
        hits = jnp.concatenate(hits, axis=0).astype(BF)
        got = side_sum(dot(hits, table[:, own, :].reshape(512, 256)))
        picked = jnp.where(trip_lanes, got[:128], got[128:])
        picked = picked.reshape(PICKS, BLOCK, 128)
        cos_here = cos_table[own, :]
        slot = slots[own, :]
        low_lanes = iota((BLOCK, 128), 1) < TRIP_W
        for h in range(2):
            rows = slice(8 * h, 8 * h + 8)
            cos = []
            for j in range(PICKS):
                index = jnp.where(
                    low_lanes[rows], slot[rows, j : j + 1], slot[rows, PICKS + j : PICKS + j + 1]
                )
                cos.append(jnp.take_along_axis(cos_here[rows], index, axis=1))
            cos = jnp.stack(cos)
            cosines[2 * b + h] = cos
            values = picked[:, rows]
            for k, poly in enumerate(monic(cos)):
                total = jnp.sum(poly * values, axis=0) * (lead(k) * scale)
                sums[pl.ds(pl.multiple_of(at + 8 * h, 8), 8), k * 128 : (k + 1) * 128] = total

    looped(BLOCKS, 3, basis_block)

    down = times(sums[...], weight[...], NT)
    down_act, down_slope = act_and_slope(down)
    trip_h, quad_h = down_act[:, :64], down_act[:, 64:96]
    trip_pre = times(trip_h, trip_up[...])
    quad_pre = times(quad_h, quad_up[...])
    src = jnp.concatenate(
        [side_sum(table[30].astype(F32)), side_sum(table[31].astype(F32))], axis=1
    )
    target = times(tagged[...], w_ae[1])
    spread = segments((EDGES, 16), 0, 1)
    gathers = segments((8, EDGES), 1, 0)

    def to_edges(x):
        return dot(spread, stacked(x))

    def to_atoms(x):
        return side_sum(dot(gathers, side_by_side(x)))

    atom_pre = times(src, w_ae[0]) + to_edges(target)
    atom_act, atom_slope = act_and_slope(atom_pre)
    trip_act, trip_slope = act_and_slope(trip_pre)
    quad_act, quad_slope = act_and_slope(quad_pre)
    merged = (edge[...] + trip_act + quad_act + atom_act * rads[2]) * 0.5
    kept[0] = merged
    first_act, first_slope = act_and_slope(times(merged, w_res[0]))
    kept[1] = first_act
    second_act, second_slope = act_and_slope(times(first_act, w_res[1]))
    new_edges = (merged + second_act) * root_half
    edges_out[...] = new_edges
    weighted = new_edges * live
    root_slots = 1.0 / math.sqrt(SLOTS)
    gathered = to_atoms(weighted * rads[3]) * root_slots
    summary = to_atoms(weighted * rads[4]) * root_slots
    gate_act, gate_slope = act_and_slope(times(gathered, w_ea[0]))
    updated = (tagged[...] + gate_act) * root_half
    a0_act, a0_slope = act_and_slope(times(updated, w_ad[0]))
    a1_act, a1_slope = act_and_slope(times(a0_act, w_ad[1]))
    new_atoms = (updated + a1_act) * root_half
    atoms_out[...] = new_atoms
    e_act, e_slope = act_and_slope(times(summary, w_ea[1]) + times(new_atoms, w_ad[2]))
    out_act, out_slope = act_and_slope(times(e_act, w_ad[3]))
    energy_out[...] = out_act

    d_out = cot_energy[...] * out_slope
    d_e = times(d_out, w_ad[3], NT) * e_slope
    d_summary = times(d_e, w_ea[1], NT)
    d_atoms = (cot_atoms[...] + times(d_e, w_ad[2], NT)) * root_half
    d_a1 = d_atoms * a1_slope
    d_a0 = times(d_a1, w_ad[1], NT) * a0_slope
    d_updated = (d_atoms + times(d_a0, w_ad[0], NT)) * root_half
    d_gate = d_updated * gate_slope
    d_gathered = times(d_gate, w_ea[0], NT)

    d_gathered = to_edges(d_gathered * root_slots)
    d_summary = to_edges(d_summary * root_slots)
    grad_rads[1] = weighted * d_gathered
    grad_rads[2] = weighted * d_summary
    d_new = cot_edges[...] + live * (d_gathered * rads[3] + d_summary * rads[4])
    d_new = d_new * root_half
    d_second = d_new * second_slope
    kept[3] = d_second
    d_first = times(d_second, w_res[1], NT) * first_slope
    kept[2] = d_first
    d_merged = (d_new + times(d_first, w_res[0], NT)) * 0.5
    grad_edges[...] = d_merged
    grad_rads[0] = d_merged * atom_act
    d_atom = d_merged * rads[2] * atom_slope
    kept[4] = d_atom
    d_trip = d_merged * trip_slope
    d_quad = d_merged * quad_slope
    d_target = to_atoms(d_atom)
    grad_tag[...] = d_updated + times(d_target, w_ae[1], NT)
    d_down = jnp.concatenate(
        [times(d_trip, trip_up[...], NT), times(d_quad, quad_up[...], NT), jnp.zeros((EDGES, 32), F32)],
        axis=1,
    )
    d_down = d_down * down_slope
    grad_src[...] = times(d_atom, w_ae[0], NT)

    first[0:512] = weight_grad(kept[0], kept[2])
    first[512:768] = weight_grad(src, kept[4])
    first[896:1408] = weight_grad(kept[1], kept[3])
    first[1408:1664] = weight_grad(tagged[...], d_target)
    bil = weight_grad(d_down, sums[...])
    for m in range(8):
        tile = [bil[0:64, k * 128 : k * 128 + 64] for k in (2 * m, 2 * m + 1)]
        row = 768 + 64 * (m // 4)
        first[row : row + 64, (m % 4) * 128 : (m % 4 + 1) * 128] = jnp.concatenate(tile, axis=1)
    for half in range(2):
        for m in range(4):
            at = 64 + 32 * half
            tile = [bil[64:96, k * 128 + at : k * 128 + at + 32] for k in range(4 * m, 4 * m + 4)]
            row = 1728 + 32 * half
            first[row : row + 32, m * 128 : (m + 1) * 128] = jnp.concatenate(tile, axis=1)
    first[1664:1728] = weight_grad(down_act, d_trip)[:64]
    quad_up_grad[...] = weight_grad(down_act, d_quad)[64:96]
    atom_rows[...] = jnp.concatenate(
        [gathered, summary, updated, a0_act, new_atoms, e_act, d_a0, d_a1, d_e, d_out, d_gate], axis=1
    )
    split_cores(core, first, keep, send)
    grad_sums[...] = times(d_down, weight[...])


def late_kernel(grad_rads, radial, atom_rows, quad_up_grad, core, keep, send, second):
    atoms = atom_rows[...]
    gathered, summary = atoms[:, :512], atoms[:, 512:1024]
    updated, a0_act, new_atoms, e_act, d_a0, d_a1, d_e, d_out, d_gate = [
        atoms[:, at : at + 256] for at in range(1024, 3328, 256)
    ]
    second[0:512, 0:256] = weight_grad(gathered, d_gate)
    second[0:512, 256:512] = weight_grad(summary, d_e)
    second[512:768, 0:256] = weight_grad(updated, d_a0)
    second[512:768, 256:512] = weight_grad(a0_act, d_a1)
    second[768:1024, 0:256] = weight_grad(new_atoms, d_e)
    second[768:1024, 256:512] = weight_grad(e_act, d_out)
    for k in range(3):
        second[1024 + 128 * k : 1152 + 128 * k] = weight_grad(radial[...], grad_rads[k])
    second[1408:1440] = quad_up_grad[...]
    second[1440:1536] = jnp.zeros((96, 512), F32)
    split_cores(core, second, keep, send)


def scatter_kernel(
    cosines, sums, grad_src, src_rows, mark_rows,
    back_before, back_here, back_after, back_local,
    table,
):
    group = back_here.shape[0] * 8
    depth = 3 * group + 16
    trip_lanes = iota((128, 128), 1) < TRIP_W
    scale = 1.0 / math.sqrt(PICKS)

    def basis_back(b):
        at = pl.multiple_of(b * BLOCK, BLOCK)
        own = pl.ds(at, BLOCK)
        parts = []
        for h in range(2):
            cos = cosines[2 * b + h]
            own_rows = pl.ds(pl.multiple_of(at + 8 * h, 8), 8)
            after = total = None
            for k in range(ANGLES - 1, -1, -1):
                term = sums[own_rows, k * 128 : (k + 1) * 128] * (lead(k) * scale)
                if total is None:
                    after, total = None, jnp.broadcast_to(term, cos.shape)
                elif after is None:
                    after, total = total, term + cos * total
                else:
                    after, total = total, term + cos * total - ratio(k + 1) * after
            parts.append(total)
        grad = jnp.concatenate(parts, axis=1).reshape(128, 128)
        grad = jnp.concatenate(
            [jnp.where(trip_lanes, grad, 0.0), jnp.where(trip_lanes, 0.0, grad)], axis=0
        )
        hits = onehot(mark_rows[b] == iota((512, 256), 0))
        got = side_by_side(side_sum(dot(hits, side_by_side(grad))))
        table[:, own, :] = got.reshape(32, BLOCK, 256)

    looped(BLOCKS, 3, basis_back)
    table[30] = side_by_side(grad_src[:, :128])
    table[31] = side_by_side(grad_src[:, 128:])
    rows = iota((depth, EDGES), 0)
    place_even = onehot(src_rows[0:1, :] == rows)
    place_odd = onehot(src_rows[1:2, :] == rows)

    def scatter_pair(p):
        got = side_sum(dot(place_even, table[2 * p]) + dot(place_odd, table[2 * p + 1]))
        for i, back in enumerate((back_before, back_here, back_after)):
            back[:, p] = got[i * group : (i + 1) * group].reshape(group // 8, 8, 128)
        back_local[p] = got[3 * group :]

    looped(16, 4, scatter_pair)


def finish_kernel(
    back_local, returned, grad_late, tag_late, edge, radial, columns, pre, downs, rads, tag_row, send_row,
    w_in, w_trip, w_quad, core,
    grad_atoms, grad_edges, keep_first, send_first, keep_second, send_second,
    first, second,
):
    shape = (EDGES, 256)
    lane = iota(shape, 1)
    place = onehot((local_rows(lane) == iota(shape, 0)) & (lane < EDGES))
    rows = dot(place, side_by_side(back_local[...].reshape(256, 128)))
    pay = paid(iota((1, 128), 1), send_lanes(send_row[...]))
    place = onehot(pay == iota((EDGES, 128), 0))
    send = send_column(send_row[...], 8)
    tags = to_column(tag_row[...])
    rows = side_sum(rows + dot(place, side_by_side(returned[...].reshape(128, 128))))
    back = returned[15]
    tag = tag_late[...] + jnp.concatenate([back_local[15, 0:8], back_local[15, 8:16]], axis=1)
    atom = iota((8, 1), 0)
    for r in range(SEND):
        piece = jnp.concatenate([back[r : r + 1], back[4 + r : 5 + r]], axis=1)
        tag = tag + jnp.where(send[r : r + 1, :] == atom, piece, 0.0)
    grad_atoms[...] = tag
    table = [
        jnp.sum(jnp.where(tags == t, tag, 0.0), axis=0, keepdims=True) for t in range(3)
    ]
    table = jnp.concatenate(table + [jnp.zeros((29, ATOM_W), F32)], axis=0)
    d_trip = rows[:, :64]
    d_quad = rows[:, 64:96] * radial[:, 0:1] + rows[:, 96:128] * radial[:, 1:2]
    total = grad_late[...]
    for k, (d_row, down, weight, out) in enumerate(
        ((d_trip, slice(0, 64), w_trip, first), (d_quad, slice(64, 96), w_quad, second))
    ):
        d_down = d_row * columns[:, 0:1] * act_and_slope(downs[:, down])[1]
        value, slope = act_and_slope(pre[k])
        d_start = times(d_down, weight[...])
        d_pre = d_start * rads[k] * slope
        total = total + times(d_pre, w_in[k], NT)
        out[0:512] = weight_grad(edge[...], d_pre)
        out[512:640] = weight_grad(radial[...], d_start * value)
        down_grad = weight_grad(d_down, value * rads[k])
        if k == 0:
            out[640:704] = down_grad
            out[704:768] = jnp.zeros((64, 512), F32)
        else:
            out[640:672] = down_grad
            out[672:704, 0:256] = table
            out[672:704, 256:512] = jnp.zeros((32, 256), F32)
            out[704:768] = jnp.zeros((64, 512), F32)
    grad_edges[...] = total
    split_cores(core, first, keep_first, send_first)
    split_cores(core, second, keep_second, send_second)


def late_outputs(
    a_mine, a_other, b_mine, b_other, core,
    res, ae, trip_bil, trip_up, quad_bil, quad_up, rad, ea, ad,
):
    upper = core[0] == 1

    def rows(mine, other, at, size):
        half = mine.shape[0]
        where = slice(at % half, at % half + size)
        if at < half:
            return jnp.where(upper, other[where], mine[where])
        return jnp.where(upper, mine[where], other[where])

    a = lambda at, size: rows(a_mine, a_other, at, size)
    b = lambda at, size: rows(b_mine, b_other, at, size)
    for k in range(2):
        res[k] = a(896 * k, 512)
        ae[k] = a(896 * k + 512, 256)
        trip_bil[:, 512 * k : 512 * k + 512] = a(768 + 64 * k, 64)
        quad_bil[:, 512 * k : 512 * k + 512] = a(1728 + 32 * k, 32)
    trip_up[...] = a(1664, 64)
    quad_up[...] = b(1408, 32)
    for k in range(3):
        rad[k] = b(1024 + 128 * k, 128)
    both = b(0, 512)
    ea[0], ea[1] = both[:, :256], both[:, 256:]
    both = b(512, 256)
    ad[0], ad[1] = both[:, :256], both[:, 256:]
    both = b(768, 256)
    ad[2], ad[3] = both[:, :256], both[:, 256:]


def early_outputs(c_mine, c_other, d_mine, d_other, late_rad, core, inputs, rad, trip_down, quad_down, tags):
    upper = core[0] == 1
    for k, (mine, other) in enumerate(((c_mine, c_other), (d_mine, d_other))):
        inputs[k, 0:384] = jnp.where(upper, other[...], mine[...])
        high = jnp.where(upper, mine[...], other[...])
        inputs[k, 384:512] = high[:128]
        rad[k] = high[128:256]
        if k == 0:
            trip_down[...] = high[256:320]
        else:
            quad_down[...] = high[256:288]
            tags[...] = high[288:291, :256]
    rad[2:5] = late_rad[...]


def call(kernel, outs, args, scratch=(), micros=1):
    flops = int(micros * 1.15e9)
    return pl.pallas_call(
        kernel,
        out_shape=[jax.ShapeDtypeStruct(shape, F32) for shape in outs],
        in_specs=[pl.BlockSpec(memory_space=pltpu.SMEM if x.ndim == 1 else pltpu.VMEM) for x in args],
        out_specs=[pl.BlockSpec(memory_space=pltpu.VMEM)] * len(outs),
        scratch_shapes=list(scratch),
        compiler_params=pltpu.CompilerParams(vmem_limit_bytes=56 * 1024 * 1024),
        cost_estimate=pl.CostEstimate(flops=flops, bytes_accessed=1 << 10, transcendentals=0),
    )(*args)


def per_device(
    hidden_atoms,
    edge_states,
    edge_vectors,
    atom_tags,
    send_list,
    sources,
    trip_slots,
    triplet_mask,
    quad_slots,
    quad_mask,
    edge_mask,
    w_inputs,
    w_radial,
    w_trip_down,
    triplet_bilinear_weight,
    w_trip_up,
    w_quad_down,
    w_quad_bil,
    w_quad_up,
    w_atom_edge,
    w_residual,
    w_edge_atom,
    w_atom_dense,
    tag_table,
    cot_atoms,
    cot_edges,
    cot_energy,
):
    planes = 2 if lax.axis_size("gz") == 2 else 3
    group = 3 * planes

    offset = jnp.maximum(sources - ATOMS, 0)
    block, border = offset // SEND, offset % SEND
    step_x, step_y, step_z = block // 9, block // 3 % 3, block % 3
    if planes == 2:
        step_z = jnp.clip(step_z - 1 + lax.axis_index("gz"), 0, 1)
    block = (step_y * 3 + step_x) * planes + step_z
    inside = sources < ATOMS
    even = jnp.where(inside, 3 * group * 8 + sources, block * 8 + border)
    src = jnp.stack([even, even + jnp.where(inside, ATOMS, SEND)])
    slots = jnp.concatenate([trip_slots, quad_slots], axis=1)
    masks = jnp.concatenate([triplet_mask, quad_mask], axis=1)
    marks = jnp.where(masks > 0, slots * BLOCK + (jnp.arange(EDGES) % BLOCK)[:, None], -1)
    mark_rows = marks.reshape(BLOCKS, BLOCK, 2 * PICKS).transpose(0, 2, 1)
    mark_rows = mark_rows.reshape(BLOCKS, 1, 2 * PICKS * BLOCK)
    trip_down_t, quad_down_t = w_trip_down.T, w_quad_down.T

    tag_row, send_row = atom_tags[None, :], send_list[None, :]
    payload, local, tagged, pre, downs, rads, radial, columns = call(
        start_kernel,
        [(PAIRS, 8, 128), (PAIRS, 16, 128), (8, 256), (2, EDGES, 512), (EDGES, 128), (5, EDGES, 512)]
        + [(EDGES, 128)] * 2,
        [edge_states, edge_vectors, edge_mask[None, :], hidden_atoms, tag_row, send_row, tag_table,
         w_inputs, w_radial, trip_down_t, quad_down_t],
        micros=5,
    )
    core = bit_value("gyl", 0)[None]
    before, here, after = with_halo(payload)
    (
        atoms_out, edges_out, energy_out, grad_edges, grad_tag,
        cosines, grad_sums, grad_src, keep_a, send_a, grad_rads, atom_rows, quad_up_grad,
    ) = call(
        main_kernel,
        [(8, 256), (EDGES, 512), (8, 256), (EDGES, 512), (8, 256)]
        + [(2 * BLOCKS, PICKS, 8, 128), (EDGES, 2048), (EDGES, 256), (896, 512), (896, 512)]
        + [(3, EDGES, 512), (8, 3328), (32, 512)],
        [before, here, after, local, tagged, edge_states, columns, rads, radial,
         src.T, slots, marks,
         triplet_bilinear_weight.T, w_trip_up, w_quad_bil.T, w_quad_up, w_atom_edge, w_residual,
         w_edge_atom, w_atom_dense, cot_atoms, cot_edges, cot_energy, core],
        scratch=[
            pltpu.VMEM((32, EDGES, 256), BF),
            pltpu.VMEM((EDGES, 2048), F32),
            pltpu.VMEM((128, 2048), BF),
            pltpu.VMEM((5, EDGES, 512), F32),
            pltpu.VMEM((EDGES, 128), F32),
            pltpu.VMEM((1792, 512), F32),
        ],
        micros=26,
    )
    chain = Chain()
    got_a = swap(send_a, "gyl", 0)
    keep_b, send_b = call(
        late_kernel,
        [(768, 512)] * 2,
        [grad_rads, radial, atom_rows, quad_up_grad, core],
        scratch=[pltpu.VMEM((1536, 512), F32)],
        micros=4,
    )
    late = reduction(chain, [keep_a, got_a], [keep_b, swap(send_b, "gyl", 0)], True)
    next(late)
    grad_sums = chain.after(grad_sums)
    back_before, back_here, back_after, back_local = call(
        scatter_kernel,
        [(group, 16, 8, 128)] * 3 + [(16, 16, 128)],
        [cosines, grad_sums, grad_src, src, mark_rows],
        scratch=[pltpu.VMEM((32, EDGES, 256), BF)],
        micros=13,
    )
    got = shifted(back_before, GY, -1, True), shifted(back_after, GY, 1, True)
    chain.step(back_local)
    next(late)
    got, value = chain.after((got, back_here))
    value = chain.step(value + got[0] + got[1])
    first_plane, middle, last_plane = value[:planes], value[planes : 2 * planes], value[2 * planes :]
    got = shifted(first_plane, "gx", -1, True), shifted(last_plane, "gx", 1, True)
    got, middle = chain.after((got, middle))
    value = chain.step(middle + got[0] + got[1])
    next(late)
    if planes == 2:
        top = lax.axis_index("gz") == 1
        mine = jnp.where(top, value[1], value[0])
        theirs = jnp.where(top, value[0], value[1])
        returned = mine + lax.ppermute(theirs, "gz", [(0, 1), (1, 0)])
    else:
        returned = value[1] + shifted(value[0], "gz", -1, False) + shifted(value[2], "gz", 1, False)
    returned = chain.after(returned)
    grad_atoms, grad_edges, keep_c, send_c, keep_d, send_d = call(
        finish_kernel,
        [(8, 256), (EDGES, 512)] + [(384, 512)] * 4,
        [back_local, returned, grad_edges, grad_tag, edge_states, radial, columns, pre, downs, rads,
         tag_row, send_row, w_inputs, trip_down_t, quad_down_t, core],
        scratch=[pltpu.VMEM((768, 512), F32)] * 2,
        micros=7,
    )
    next(late)
    send_c, send_d = chain.after((send_c, send_d))
    got_c, got_d = swap(send_c, "gyl", 0), swap(send_d, "gyl", 0)
    early = reduction(chain, [keep_c, got_c], [keep_d, got_d])
    running = {"L": late, "E": early}
    done = {}

    def resume(name):
        if name in done:
            return
        try:
            next(running[name])
        except StopIteration as end:
            done[name] = end.value

    for name in "ELELELEELEELE":
        resume(name)
    while "L" not in done:
        resume("L")
    (a_mine, a_other), (b_mine, b_other) = done["L"]
    g_res, g_ae, g_trip_bil, g_trip_up, g_quad_bil, g_quad_up, g_rad, g_ea, g_ad = call(
        late_outputs,
        [(2, 512, 512), (2, 256, 512), (64, 1024), (64, 512), (32, 1024), (32, 512), (3, 128, 512)]
        + [(2, 512, 256), (4, 256, 256)],
        [a_mine, a_other, b_mine, b_other, core],
        micros=5,
    )
    chain.step(g_rad)
    while "E" not in done:
        resume("E")
    (c_mine, c_other), (d_mine, d_other) = done["E"]
    g_inputs, g_rad, g_trip_down, g_quad_down, g_tags = call(
        early_outputs,
        [(2, 512, 512), (5, 128, 512), (64, 512), (32, 512), (3, 256)],
        [c_mine, c_other, d_mine, d_other, g_rad, core],
        micros=3,
    )
    return (
        atoms_out,
        edges_out,
        energy_out,
        grad_atoms,
        grad_edges,
        g_inputs,
        g_rad,
        g_trip_down.T,
        g_trip_bil.T,
        g_trip_up,
        g_quad_down.T,
        g_quad_bil.T,
        g_quad_up,
        g_ae,
        g_res,
        g_ea,
        g_ad,
        g_tags,
    )


def solution(mesh):
    size = dict(mesh.shape)
    inner = Mesh(mesh.devices.reshape(size["gx"], size["gy"] // 2, 2, size["gz"]), ROWS)
    flat, columns, vector, whole = P(ROWS, None), P(None, ROWS), P(ROWS), P()
    placed = [flat, flat, columns] + [vector] * 3 + [flat] * 4 + [vector] + [whole] * 13 + [flat] * 3
    return jax.shard_map(
        per_device,
        mesh=inner,
        in_specs=tuple(placed),
        out_specs=tuple([flat] * 5 + [whole] * 13),
        check_vma=False,
    )
```

```python
import itertools
import math

import jax
import jax.numpy as jnp
from jax import lax
from jax.experimental import pallas as pl
from jax.experimental.pallas import tpu as pltpu
from jax.sharding import Mesh
from jax.sharding import PartitionSpec as P

BF = jnp.bfloat16
F32 = jnp.float32
ROWS = ("gx", "gyh", "gyl", "gz")
GY = ("gyh", "gyl")
ATOMS, SEND, SLOTS, EDGES = 8, 4, 30, 240
ATOM_W, EDGE_W, TRIP_W, QUAD_W, RADIAL = 256, 512, 64, 32, 128
ANGLES, PICKS = 16, 8
PAIRS = 17
BLOCK = 16
BLOCKS = EDGES // BLOCK
root_half = 0.7071067811865476
NN = (((1,), (0,)), ((), ()))
NT = (((1,), (1,)), ((), ()))
TN = (((0,), (0,)), ((), ()))


def shifted(value, axis, steps, wrap):
    count = lax.axis_size(axis)
    pairs = [(i, (i + steps) % count) for i in range(count) if wrap or 0 <= i + steps < count]
    return lax.ppermute(value, axis, pairs)


def planes_of(value):
    if lax.axis_size("gz") == 2:
        other = lax.ppermute(value, "gz", [(0, 1), (1, 0)])
        top = lax.axis_index("gz") == 1
        return jnp.stack([jnp.where(top, other, value), jnp.where(top, value, other)])
    return jnp.stack([shifted(value, "gz", 1, False), value, shifted(value, "gz", -1, False)])


def with_halo(value):
    value = planes_of(value)
    value = jnp.concatenate([shifted(value, "gx", 1, True), value, shifted(value, "gx", -1, True)])
    return shifted(value, GY, 1, True), value, shifted(value, GY, -1, True)


def bits_of(axis):
    count = lax.axis_size(axis)
    return [(axis, b) for b in range(count.bit_length() - 1)]


def swap(value, axis, bit):
    count = lax.axis_size(axis)
    return lax.ppermute(value, axis, [(i, i ^ (1 << bit)) for i in range(count)])


def bit_value(axis, bit):
    return (lax.axis_index(axis) >> bit) & 1


class Chain:
    def __init__(self):
        self.last = None

    def after(self, values):
        if self.last is not None:
            self.last, values = lax.optimization_barrier((self.last, values))
        return values

    def step(self, value):
        self.last = value
        return value


def upper_half(me, axis, bit):
    return ((me[ROWS.index(axis)] >> bit) & 1) == 1


def halved(chain, me, lanes, bits, weight):
    def kernel(me_ref, *refs):
        for i, (axis, bit) in enumerate(bits):
            x, y, send, keep = refs[2 * i], refs[2 * i + 1], refs[count + 2 * i], refs[count + 2 * i + 1]
            half = x.shape[0] // 2
            upper = upper_half(me_ref, axis, bit)
            low, high = x[:half] + y[:half], x[half:] + y[half:]
            send[...] = jnp.where(upper, low, high)
            keep[...] = jnp.where(upper, high, low)

    count = 2 * len(lanes)
    shapes = [(x.shape[0] // 2, x.shape[1]) for lane in lanes for x in lane]
    args = [me] + chain.after([x for lane in lanes for x in lane])
    outs = chain.step(call(kernel, shapes, args, weight=weight))
    return [(outs[2 * i + 1], swap(outs[2 * i], *bits[i])) for i in range(len(lanes))]


def halved_joint(chain, me, lanes, axis, bit, weight):
    def kernel(me_ref, *refs):
        send, keep, total = refs[-3:]
        at = 0
        for x, y in zip(refs[:-3:2], refs[1:-3:2]):
            total[at : at + x.shape[0]] = x[...] + y[...]
            at += x.shape[0]
        upper = upper_half(me_ref, axis, bit)
        low, high = total[:half], total[half:]
        send[...] = jnp.where(upper, low, high)
        keep[...] = jnp.where(upper, high, low)

    rows, width = sum(x.shape[0] for x, _ in lanes), lanes[0][0].shape[1]
    half = rows // 2
    args = [me] + chain.after([x for lane in lanes for x in lane])
    outs = call(kernel, [(half, width)] * 2, args, [pltpu.VMEM((rows, width), F32)], weight)
    send, keep = chain.step(outs)
    return keep, swap(send, axis, bit)


def joined(chain, me, lanes, bits, weight, cuts=None):
    def kernel(me_ref, *refs):
        for i, (axis, bit) in enumerate(bits):
            mine, other = refs[2 * i], refs[2 * i + 1]
            upper = upper_half(me_ref, axis, bit)
            low, high = jnp.where(upper, other[...], mine[...]), jnp.where(upper, mine[...], other[...])
            whole = refs[count + i] if cuts is None else refs[-1]
            half = mine.shape[0]
            whole[:half] = low
            whole[half:] = high
        at = 0
        for out, size in zip(refs[count:], cuts or ()):
            out[...] = refs[-1][at : at + size]
            at += size

    count = 2 * len(lanes)
    width = lanes[0][0].shape[1]
    shapes = [(2 * x.shape[0], width) for x, _ in lanes]
    scratch = [] if cuts is None else [pltpu.VMEM(shapes[0], F32)]
    shapes = shapes if cuts is None else [(size, width) for size in cuts]
    args = [me] + chain.after([x for lane in lanes for x in lane])
    return list(chain.step(call(kernel, shapes, args, scratch, weight)))


def added(chain, pair, weight):
    def kernel(x, y, out):
        out[...] = x[...] + y[...]

    return chain.step(call(kernel, [pair[0].shape], chain.after(list(pair)), weight=weight))[0]


def reduction(chain, me, first, second, weights):
    across, along = bits_of("gz"), bits_of("gyh")
    lanes = [first, second]
    step = itertools.count(1).__next__
    turns = range(max(len(across), len(along)))
    for plan in ((across, along), (along, across)):
        for turn in turns:
            on = [i for i in range(2) if turn < len(plan[i])]
            for i, got in zip(on, halved(chain, me, [lanes[i] for i in on], [plan[i][turn] for i in on], weights(step()))):
                lanes[i] = got
            yield
    sizes = [x.shape[0] for x, _ in lanes]
    for axis, bit in bits_of("gx"):
        if bit == 0:
            joint = halved_joint(chain, me, lanes, axis, bit, weights(step()))
        else:
            (joint,) = halved(chain, me, [joint], [(axis, bit)], weights(step()))
        yield
    value = added(chain, joint, weights(step()))
    for axis, bit in bits_of("gx")[::-1]:
        other = swap(value, axis, bit)
        yield
        if bit == 0:
            values = joined(chain, me, [(value, other)], [(axis, bit)], weights(step()), sizes)
        else:
            (value,) = joined(chain, me, [(value, other)], [(axis, bit)], weights(step()))
    for plan in ((along[::-1], across[::-1]), (across[::-1], along[::-1])):
        for turn in turns:
            on = [i for i in range(2) if turn < len(plan[i])]
            others = [swap(values[i], *plan[i][turn]) for i in on]
            yield
            pairs = [(values[i], x) for i, x in zip(on, others)]
            for i, got in zip(on, joined(chain, me, pairs, [plan[i][turn] for i in on], weights(step()))):
                values[i] = got
    others = [swap(x, "gyl", 0) for x in values]
    yield
    return [(value, other) for value, other in zip(values, others)]


def return_along(chain, here, got, planes):
    def kernel(x, y, z, *outs):
        for i, out in enumerate(outs):
            cut = slice(i * planes, (i + 1) * planes)
            out[...] = x[cut] + y[cut] + z[cut]

    shapes = [(planes,) + here.shape[1:]] * 3
    return chain.step(call(kernel, shapes, chain.after([here, *got]), weight=0))


def return_up(chain, me, middle, got, planes):
    def kernel(me_ref, x, y, z, *outs):
        if planes == 2:
            top = upper_half(me_ref, "gz", 0)
            low, high = x[0] + y[0] + z[0], x[1] + y[1] + z[1]
            outs[0][...] = jnp.where(top, high, low)
            outs[1][...] = jnp.where(top, low, high)
        else:
            for i, out in enumerate(outs):
                out[...] = x[i] + y[i] + z[i]

    shapes = [middle.shape[1:]] * planes
    return chain.step(call(kernel, shapes, [me] + chain.after([middle, *got]), weight=0))


def iota(shape, dim):
    return lax.broadcasted_iota(jnp.int32, shape, dim)


def dot(left, right, dims=NN):
    return lax.dot_general(left, right, dims, preferred_element_type=F32)


def halves(x):
    high = x.astype(BF)
    return high, (x - high.astype(F32)).astype(BF)


def stacked(x):
    high, low = halves(x)
    if x.shape[0] % 16 == 0:
        return jnp.concatenate([high, low], axis=0)
    return jnp.concatenate([high.astype(F32), low.astype(F32)], axis=0).astype(BF)


def folded(x):
    half = x.shape[0] // 2
    return x[:half] + x[half:]


def times(x, weight, dims=NN):
    return folded(dot(stacked(x), weight, dims))


def side_by_side(x):
    return jnp.concatenate(halves(x), axis=1)


def side_sum(x):
    half = x.shape[1] // 2
    return x[:, :half] + x[:, half:]


def weight_grad(x, y):
    x_high, x_low = halves(x)
    y_high, y_low = halves(y)
    left, right = [x_high, x_high, x_low], [y_high, y_low, y_high]
    if x.shape[0] % 16 == 0:
        return dot(jnp.concatenate(left, axis=0), jnp.concatenate(right, axis=0), TN)
    left = jnp.concatenate([p.astype(F32) for p in left], axis=0).astype(BF)
    right = jnp.concatenate([p.astype(F32) for p in right], axis=0).astype(BF)
    return dot(left, right, TN)


def onehot(hit):
    return jnp.where(hit, 1.0, 0.0).astype(BF)


def sigmoid(v):
    return 1.0 / (1.0 + jnp.exp(-v))


def act(v):
    return v * sigmoid(v) * (1.0 / 0.6)


def act_and_slope(v):
    s = sigmoid(v)
    return v * s * (1.0 / 0.6), s * (1.0 + v * (1.0 - s)) * (1.0 / 0.6)


def sin_pi(t):
    n = jnp.floor(t + 0.5)
    r = t - n
    odd = n - 2.0 * jnp.floor(n * 0.5)
    q = r * r
    total = jnp.zeros_like(r)
    for k in range(6, -1, -1):
        total = total * q + (-1.0) ** k * math.pi ** (2 * k + 1) / math.factorial(2 * k + 1)
    return total * r * (1.0 - 2.0 * odd)


def to_column(row):
    n = row.shape[1]
    same = iota((n, n), 0) == iota((n, n), 1)
    return jnp.sum(jnp.where(same, row, jnp.zeros_like(row)), axis=1, keepdims=True)


def send_column(send, rows):
    shape = (rows, SEND)
    hit = (iota(shape, 0) & (SEND - 1)) == iota(shape, 1)
    return jnp.sum(jnp.where(hit, send, 0), axis=1, keepdims=True)


def send_lanes(send):
    shape = (8, 128)
    hit = iota(shape, 0) == (iota(shape, 1) & (SEND - 1))
    return jnp.sum(jnp.where(hit, send_column(send, 8), 0), axis=0, keepdims=True)


def paid(row, send):
    edge = send * SLOTS + 2 * (row >> 3) + ((row >> 2) & 1)
    return jnp.where(row < 120, edge, -1)


def atom_of(edge):
    total = jnp.zeros_like(edge)
    for a in range(1, ATOMS):
        total = total + jnp.where(edge >= a * SLOTS, 1, 0)
    return total


def radial_of(length):
    x = length / 12.0
    x2 = x * x
    x4 = x2 * x2
    envelope = 1.0 - 28.0 * (x4 * x2) + 48.0 * (x4 * x2 * x) - 21.0 * (x4 * x4)
    orders = (iota((1, RADIAL), 1) + 1).astype(F32)
    return envelope * sin_pi(x * orders) / x


def geometry(unit):
    own = atom_of(iota((8, EDGES), 1)) == iota((8, EDGES), 0)
    edge = iota((EDGES, 128), 0)
    slot = edge - atom_of(edge) * SLOTS
    total = jnp.zeros((24, 128), F32)
    for k in range(3):
        x = jnp.where(own, unit[k : k + 1, :], 0.0)
        high = x.astype(BF).astype(F32)
        mid = (x - high).astype(BF).astype(F32)
        parts = jnp.concatenate([high, mid, x - high - mid], axis=0).astype(BF)
        total = total + dot(parts, onehot(iota((EDGES, 128), 1) == slot + 32 * k))
    return total[0:8] + total[8:16] + total[16:24]


def local_rows(index):
    return (index & 7) * SLOTS + 2 * (index >> 4) + ((index >> 3) & 1)


def start_kernel(
    edge, vec, mask, hidden, tag_row, send_row, table, w_in, w_rad, w_trip, w_quad,
    payload, local, tagged, pre, downs, rads, radial_out, columns,
):
    vectors = vec[...]
    length = jnp.sqrt(jnp.sum(vectors * vectors, axis=0, keepdims=True))
    unit = vectors / length
    geo = geometry(unit)
    live = to_column(jnp.where(mask[...] > 0, 1.0, 0.0))
    parts = [live] + [to_column(unit[k : k + 1, :]) for k in range(3)]
    columns[...] = jnp.concatenate(parts + [jnp.zeros((EDGES, 124), F32)], axis=1)
    send = send_column(send_row[...], 8)
    pay = paid(iota((128, 1), 0), send_column(send_row[...], 128))
    tags = to_column(tag_row[...])
    radial = radial_of(to_column(length))
    radial_out[...] = radial
    split = stacked(radial)
    for k in range(5):
        rads[k] = folded(dot(split, w_rad[k]))
    split = stacked(edge[...])
    pre[0] = folded(dot(split, w_in[0]))
    pre[1] = folded(dot(split, w_in[1]))
    trip_pre = times(act(pre[0]) * rads[0], w_trip[...], NT)
    quad_pre = times(act(pre[1]) * rads[1], w_quad[...], NT)
    downs[...] = jnp.concatenate([trip_pre, quad_pre, jnp.zeros((EDGES, 32), F32)], axis=1)
    trip = act(trip_pre) * live
    quad = act(quad_pre) * live
    rows = jnp.concatenate([trip, quad * radial[:, 0:1], quad * radial[:, 1:2]], axis=1)
    rows = side_by_side(rows)
    shape = (EDGES, EDGES)
    place = onehot(local_rows(iota(shape, 0)) == iota(shape, 1))
    local[0:15] = side_sum(dot(place, rows)).reshape(15, 16, 128)
    place = onehot(pay == iota((128, EDGES), 1))
    payload[0:16] = side_sum(dot(place, rows)).reshape(16, 8, 128)
    tag = hidden[...]
    for t in range(3):
        tag = tag + jnp.where(tags == t, table[t : t + 1, :].astype(F32), 0.0)
    tagged[...] = tag
    local[15] = jnp.concatenate([tag[:, :128], tag[:, 128:]], axis=0)
    local[16] = jnp.concatenate([geo, jnp.zeros((8, 128), F32)], axis=0)
    both = jnp.concatenate([tag, geo], axis=1)
    sent = jnp.zeros((8, 384), F32)
    for a in range(ATOMS):
        sent = sent + jnp.where(send == a, both[a : a + 1, :], 0.0)
    payload[15] = jnp.where(iota((8, 128), 0) < 4, sent[:, :128], sent[:, 128:256])
    payload[16] = sent[:, 256:]


def split_cores(core, whole, keep, send):
    half = whole.shape[0] // 2
    upper = core[0] == 1
    low, high = whole[:half], whole[half:]
    keep[...] = jnp.where(upper, high, low)
    send[...] = jnp.where(upper, low, high)


def segments(shape, edge_dim, atom_dim):
    edge, atom = iota(shape, edge_dim), iota(shape, atom_dim) & 7
    return onehot((edge >= atom * SLOTS) & (edge < atom * SLOTS + SLOTS))


def lead(k):
    return math.comb(2 * k, k) / 2.0**k


def ratio(k):
    return k * k / (4.0 * k * k - 1.0)


def monic(cosine):
    before, now = jnp.ones_like(cosine), cosine
    yield before
    yield now
    for k in range(1, ANGLES - 1):
        before, now = now, cosine * now - ratio(k) * before
        yield now


def looped(count, step, body):
    def turn(t, carry):
        for i in range(step):
            body(t * step + i)
        return carry

    lax.fori_loop(0, count // step, turn, 0)


def main_kernel(
    halo_before, halo_here, halo_after, local, tagged, edge, columns, rads, radial,
    src_cols, slots, marks,
    trip_bil, trip_up, quad_bil, quad_up, w_ae, w_res, w_ea, w_ad,
    cot_atoms, cot_edges, cot_energy, core,
    atoms_out, edges_out, energy_out, grad_edges, grad_tag,
    cosines, grad_sums, grad_src, keep, send, grad_rads, atom_rows, quad_up_grad,
    table, sums, weight, kept, cos_table, first,
):
    live = columns[:, 0:1]
    halos = (halo_before, halo_here, halo_after)
    group = halo_here.shape[0] * 8
    depth = 3 * group + 16
    lanes = iota((EDGES, depth), 1)
    place = jnp.concatenate(
        [onehot(src_cols[:, 0:1] == lanes), onehot(src_cols[:, 1:2] == lanes)], axis=0
    )

    def rows_at(p):
        parts = [h[:, p].reshape(group, 128) for h in halos]
        return jnp.concatenate(parts + [local[p]], axis=0)

    def gather_pair(p):
        got = dot(place, side_by_side(rows_at(p))).astype(BF)
        table[2 * p] = got[:EDGES]
        table[2 * p + 1] = got[EDGES:]

    looped(16, 4, gather_pair)

    rows = rows_at(16)
    high, low = halves(rows)
    rest = (rows - high.astype(F32) - low.astype(F32)).astype(BF)
    got = dot(place[:EDGES], jnp.concatenate([high, low, rest], axis=1))
    got = got[:, :128] + got[:, 128:256] + got[:, 256:]
    cos_table[...] = -(
        columns[:, 1:2] * got
        + columns[:, 2:3] * pltpu.roll(got, 96, 1)
        + columns[:, 3:4] * pltpu.roll(got, 64, 1)
    )

    for k in range(ANGLES):
        top = trip_bil[:, k * 64 : k * 64 + 64].astype(F32)
        top = jnp.concatenate([top, jnp.zeros((64, 64), F32)], axis=1)
        low_left = quad_bil[:, k * 32 : k * 32 + 32].astype(F32)
        low_right = quad_bil[:, 512 + k * 32 : 544 + k * 32].astype(F32)
        bottom = jnp.concatenate([jnp.zeros((32, 64), F32), low_left, low_right], axis=1)
        piece = jnp.concatenate([top, bottom, jnp.zeros((32, 128), F32)], axis=0)
        weight[:, k * 128 : (k + 1) * 128] = piece.astype(BF)

    trip_lanes = iota((128, 128), 1) < TRIP_W
    scale = 1.0 / math.sqrt(PICKS)

    def basis_block(b):
        at = pl.multiple_of(b * BLOCK, BLOCK)
        own = pl.ds(at, BLOCK)
        wide = iota((BLOCK, 512), 1)
        mark = marks[own, :]
        hits = [jnp.where(mark[:, t : t + 1] == wide, 1.0, 0.0) for t in range(2 * PICKS)]
        hits = jnp.concatenate(hits, axis=0).astype(BF)
        got = side_sum(dot(hits, table[:, own, :].reshape(512, 256)))
        picked = jnp.where(trip_lanes, got[:128], got[128:])
        picked = picked.reshape(PICKS, BLOCK, 128)
        cos_here = cos_table[own, :]
        slot = slots[own, :]
        low_lanes = iota((BLOCK, 128), 1) < TRIP_W
        for h in range(2):
            rows = slice(8 * h, 8 * h + 8)
            cos = []
            for j in range(PICKS):
                index = jnp.where(
                    low_lanes[rows], slot[rows, j : j + 1], slot[rows, PICKS + j : PICKS + j + 1]
                )
                cos.append(jnp.take_along_axis(cos_here[rows], index, axis=1))
            cos = jnp.stack(cos)
            cosines[2 * b + h] = cos
            values = picked[:, rows]
            for k, poly in enumerate(monic(cos)):
                total = jnp.sum(poly * values, axis=0) * (lead(k) * scale)
                sums[pl.ds(pl.multiple_of(at + 8 * h, 8), 8), k * 128 : (k + 1) * 128] = total

    looped(BLOCKS, 3, basis_block)

    down = times(sums[...], weight[...], NT)
    down_act, down_slope = act_and_slope(down)
    trip_h, quad_h = down_act[:, :64], down_act[:, 64:96]
    trip_pre = times(trip_h, trip_up[...])
    quad_pre = times(quad_h, quad_up[...])
    src = jnp.concatenate(
        [side_sum(table[30].astype(F32)), side_sum(table[31].astype(F32))], axis=1
    )
    target = times(tagged[...], w_ae[1])
    spread = segments((EDGES, 16), 0, 1)
    gathers = segments((8, EDGES), 1, 0)

    def to_edges(x):
        return dot(spread, stacked(x))

    def to_atoms(x):
        return side_sum(dot(gathers, side_by_side(x)))

    atom_pre = times(src, w_ae[0]) + to_edges(target)
    atom_act, atom_slope = act_and_slope(atom_pre)
    trip_act, trip_slope = act_and_slope(trip_pre)
    quad_act, quad_slope = act_and_slope(quad_pre)
    merged = (edge[...] + trip_act + quad_act + atom_act * rads[2]) * 0.5
    kept[0] = merged
    first_act, first_slope = act_and_slope(times(merged, w_res[0]))
    kept[1] = first_act
    second_act, second_slope = act_and_slope(times(first_act, w_res[1]))
    new_edges = (merged + second_act) * root_half
    edges_out[...] = new_edges
    weighted = new_edges * live
    root_slots = 1.0 / math.sqrt(SLOTS)
    gathered = to_atoms(weighted * rads[3]) * root_slots
    summary = to_atoms(weighted * rads[4]) * root_slots
    gate_act, gate_slope = act_and_slope(times(gathered, w_ea[0]))
    updated = (tagged[...] + gate_act) * root_half
    a0_act, a0_slope = act_and_slope(times(updated, w_ad[0]))
    a1_act, a1_slope = act_and_slope(times(a0_act, w_ad[1]))
    new_atoms = (updated + a1_act) * root_half
    atoms_out[...] = new_atoms
    e_act, e_slope = act_and_slope(times(summary, w_ea[1]) + times(new_atoms, w_ad[2]))
    out_act, out_slope = act_and_slope(times(e_act, w_ad[3]))
    energy_out[...] = out_act

    d_out = cot_energy[...] * out_slope
    d_e = times(d_out, w_ad[3], NT) * e_slope
    d_summary = times(d_e, w_ea[1], NT)
    d_atoms = (cot_atoms[...] + times(d_e, w_ad[2], NT)) * root_half
    d_a1 = d_atoms * a1_slope
    d_a0 = times(d_a1, w_ad[1], NT) * a0_slope
    d_updated = (d_atoms + times(d_a0, w_ad[0], NT)) * root_half
    d_gate = d_updated * gate_slope
    d_gathered = times(d_gate, w_ea[0], NT)

    d_gathered = to_edges(d_gathered * root_slots)
    d_summary = to_edges(d_summary * root_slots)
    grad_rads[1] = weighted * d_gathered
    grad_rads[2] = weighted * d_summary
    d_new = cot_edges[...] + live * (d_gathered * rads[3] + d_summary * rads[4])
    d_new = d_new * root_half
    d_second = d_new * second_slope
    kept[3] = d_second
    d_first = times(d_second, w_res[1], NT) * first_slope
    kept[2] = d_first
    d_merged = (d_new + times(d_first, w_res[0], NT)) * 0.5
    grad_edges[...] = d_merged
    grad_rads[0] = d_merged * atom_act
    d_atom = d_merged * rads[2] * atom_slope
    kept[4] = d_atom
    d_trip = d_merged * trip_slope
    d_quad = d_merged * quad_slope
    d_target = to_atoms(d_atom)
    grad_tag[...] = d_updated + times(d_target, w_ae[1], NT)
    d_down = jnp.concatenate(
        [times(d_trip, trip_up[...], NT), times(d_quad, quad_up[...], NT), jnp.zeros((EDGES, 32), F32)],
        axis=1,
    )
    d_down = d_down * down_slope
    grad_src[...] = times(d_atom, w_ae[0], NT)

    first[0:512] = weight_grad(kept[0], kept[2])
    first[512:768] = weight_grad(src, kept[4])
    first[896:1408] = weight_grad(kept[1], kept[3])
    first[1408:1664] = weight_grad(tagged[...], d_target)
    bil = weight_grad(d_down, sums[...])
    for m in range(8):
        tile = [bil[0:64, k * 128 : k * 128 + 64] for k in (2 * m, 2 * m + 1)]
        row = 768 + 64 * (m // 4)
        first[row : row + 64, (m % 4) * 128 : (m % 4 + 1) * 128] = jnp.concatenate(tile, axis=1)
    for half in range(2):
        for m in range(4):
            at = 64 + 32 * half
            tile = [bil[64:96, k * 128 + at : k * 128 + at + 32] for k in range(4 * m, 4 * m + 4)]
            row = 1728 + 32 * half
            first[row : row + 32, m * 128 : (m + 1) * 128] = jnp.concatenate(tile, axis=1)
    first[1664:1728] = weight_grad(down_act, d_trip)[:64]
    quad_up_grad[...] = weight_grad(down_act, d_quad)[64:96]
    atom_rows[...] = jnp.concatenate(
        [gathered, summary, updated, a0_act, new_atoms, e_act, d_a0, d_a1, d_e, d_out, d_gate], axis=1
    )
    split_cores(core, first, keep, send)
    grad_sums[...] = times(d_down, weight[...])


def late_kernel(grad_rads, radial, atom_rows, quad_up_grad, core, keep, send, second):
    atoms = atom_rows[...]
    gathered, summary = atoms[:, :512], atoms[:, 512:1024]
    updated, a0_act, new_atoms, e_act, d_a0, d_a1, d_e, d_out, d_gate = [
        atoms[:, at : at + 256] for at in range(1024, 3328, 256)
    ]
    second[0:512, 0:256] = weight_grad(gathered, d_gate)
    second[0:512, 256:512] = weight_grad(summary, d_e)
    second[512:768, 0:256] = weight_grad(updated, d_a0)
    second[512:768, 256:512] = weight_grad(a0_act, d_a1)
    second[768:1024, 0:256] = weight_grad(new_atoms, d_e)
    second[768:1024, 256:512] = weight_grad(e_act, d_out)
    for k in range(3):
        second[1024 + 128 * k : 1152 + 128 * k] = weight_grad(radial[...], grad_rads[k])
    second[1408:1440] = quad_up_grad[...]
    second[1440:1536] = jnp.zeros((96, 512), F32)
    split_cores(core, second, keep, send)


def scatter_kernel(
    cosines, sums, grad_src, src_rows, mark_rows,
    back_before, back_here, back_after, back_local,
    table,
):
    group = back_here.shape[0] * 8
    depth = 3 * group + 16
    trip_lanes = iota((128, 128), 1) < TRIP_W
    scale = 1.0 / math.sqrt(PICKS)

    def basis_back(b):
        at = pl.multiple_of(b * BLOCK, BLOCK)
        own = pl.ds(at, BLOCK)
        parts = []
        for h in range(2):
            cos = cosines[2 * b + h]
            own_rows = pl.ds(pl.multiple_of(at + 8 * h, 8), 8)
            after = total = None
            for k in range(ANGLES - 1, -1, -1):
                term = sums[own_rows, k * 128 : (k + 1) * 128] * (lead(k) * scale)
                if total is None:
                    after, total = None, jnp.broadcast_to(term, cos.shape)
                elif after is None:
                    after, total = total, term + cos * total
                else:
                    after, total = total, term + cos * total - ratio(k + 1) * after
            parts.append(total)
        grad = jnp.concatenate(parts, axis=1).reshape(128, 128)
        grad = jnp.concatenate(
            [jnp.where(trip_lanes, grad, 0.0), jnp.where(trip_lanes, 0.0, grad)], axis=0
        )
        hits = onehot(mark_rows[b] == iota((512, 256), 0))
        got = side_by_side(side_sum(dot(hits, side_by_side(grad))))
        table[:, own, :] = got.reshape(32, BLOCK, 256)

    looped(BLOCKS, 3, basis_back)
    table[30] = side_by_side(grad_src[:, :128])
    table[31] = side_by_side(grad_src[:, 128:])
    rows = iota((depth, EDGES), 0)
    place_even = onehot(src_rows[0:1, :] == rows)
    place_odd = onehot(src_rows[1:2, :] == rows)

    def scatter_pair(p):
        got = side_sum(dot(place_even, table[2 * p]) + dot(place_odd, table[2 * p + 1]))
        for i, back in enumerate((back_before, back_here, back_after)):
            back[:, p] = got[i * group : (i + 1) * group].reshape(group // 8, 8, 128)
        back_local[p] = got[3 * group :]

    looped(16, 4, scatter_pair)


def finish_kernel(
    back_local, returned, grad_late, tag_late, edge, radial, columns, pre, downs, rads, tag_row, send_row,
    w_in, w_trip, w_quad, core,
    grad_atoms, grad_edges, keep_first, send_first, keep_second, send_second,
    first, second,
):
    shape = (EDGES, 256)
    lane = iota(shape, 1)
    place = onehot((local_rows(lane) == iota(shape, 0)) & (lane < EDGES))
    rows = dot(place, side_by_side(back_local[...].reshape(256, 128)))
    pay = paid(iota((1, 128), 1), send_lanes(send_row[...]))
    place = onehot(pay == iota((EDGES, 128), 0))
    send = send_column(send_row[...], 8)
    tags = to_column(tag_row[...])
    rows = side_sum(rows + dot(place, side_by_side(returned[...].reshape(128, 128))))
    back = returned[15]
    tag = tag_late[...] + jnp.concatenate([back_local[15, 0:8], back_local[15, 8:16]], axis=1)
    atom = iota((8, 1), 0)
    for r in range(SEND):
        piece = jnp.concatenate([back[r : r + 1], back[4 + r : 5 + r]], axis=1)
        tag = tag + jnp.where(send[r : r + 1, :] == atom, piece, 0.0)
    grad_atoms[...] = tag
    table = [
        jnp.sum(jnp.where(tags == t, tag, 0.0), axis=0, keepdims=True) for t in range(3)
    ]
    table = jnp.concatenate(table + [jnp.zeros((29, ATOM_W), F32)], axis=0)
    d_trip = rows[:, :64]
    d_quad = rows[:, 64:96] * radial[:, 0:1] + rows[:, 96:128] * radial[:, 1:2]
    total = grad_late[...]
    for k, (d_row, down, weight, out) in enumerate(
        ((d_trip, slice(0, 64), w_trip, first), (d_quad, slice(64, 96), w_quad, second))
    ):
        d_down = d_row * columns[:, 0:1] * act_and_slope(downs[:, down])[1]
        value, slope = act_and_slope(pre[k])
        d_start = times(d_down, weight[...])
        d_pre = d_start * rads[k] * slope
        total = total + times(d_pre, w_in[k], NT)
        out[0:512] = weight_grad(edge[...], d_pre)
        out[512:640] = weight_grad(radial[...], d_start * value)
        down_grad = weight_grad(d_down, value * rads[k])
        if k == 0:
            out[640:704] = down_grad
            out[704:768] = jnp.zeros((64, 512), F32)
        else:
            out[640:672] = down_grad
            out[672:704, 0:256] = table
            out[672:704, 256:512] = jnp.zeros((32, 256), F32)
            out[704:768] = jnp.zeros((64, 512), F32)
    grad_edges[...] = total
    split_cores(core, first, keep_first, send_first)
    split_cores(core, second, keep_second, send_second)


def late_outputs(
    a_mine, a_other, b_mine, b_other, core,
    res, ae, trip_bil, trip_up, quad_bil, quad_up, rad, ea, ad,
):
    upper = core[0] == 1

    def rows(mine, other, at, size):
        half = mine.shape[0]
        where = slice(at % half, at % half + size)
        if at < half:
            return jnp.where(upper, other[where], mine[where])
        return jnp.where(upper, mine[where], other[where])

    a = lambda at, size: rows(a_mine, a_other, at, size)
    b = lambda at, size: rows(b_mine, b_other, at, size)
    for k in range(2):
        res[k] = a(896 * k, 512)
        ae[k] = a(896 * k + 512, 256)
        trip_bil[:, 512 * k : 512 * k + 512] = a(768 + 64 * k, 64)
        quad_bil[:, 512 * k : 512 * k + 512] = a(1728 + 32 * k, 32)
    trip_up[...] = a(1664, 64)
    quad_up[...] = b(1408, 32)
    for k in range(3):
        rad[k] = b(1024 + 128 * k, 128)
    both = b(0, 512)
    ea[0], ea[1] = both[:, :256], both[:, 256:]
    both = b(512, 256)
    ad[0], ad[1] = both[:, :256], both[:, 256:]
    both = b(768, 256)
    ad[2], ad[3] = both[:, :256], both[:, 256:]


def early_outputs(c_mine, c_other, d_mine, d_other, late_rad, core, inputs, rad, trip_down, quad_down, tags):
    upper = core[0] == 1
    for k, (mine, other) in enumerate(((c_mine, c_other), (d_mine, d_other))):
        inputs[k, 0:384] = jnp.where(upper, other[...], mine[...])
        high = jnp.where(upper, mine[...], other[...])
        inputs[k, 384:512] = high[:128]
        rad[k] = high[128:256]
        if k == 0:
            trip_down[...] = high[256:320]
        else:
            quad_down[...] = high[256:288]
            tags[...] = high[288:291, :256]
    rad[2:5] = late_rad[...]


def call(kernel, outs, args, scratch=(), weight=30):
    return pl.pallas_call(
        kernel,
        out_shape=[jax.ShapeDtypeStruct(shape, F32) for shape in outs],
        in_specs=[pl.BlockSpec(memory_space=pltpu.SMEM if x.ndim == 1 else pltpu.VMEM) for x in args],
        out_specs=[pl.BlockSpec(memory_space=pltpu.VMEM)] * len(outs),
        scratch_shapes=list(scratch),
        compiler_params=pltpu.CompilerParams(vmem_limit_bytes=56 * 1024 * 1024),
        cost_estimate=pl.CostEstimate(flops=weight * 10**9, bytes_accessed=0, transcendentals=0),
    )(*args)


def per_device(
    hidden_atoms,
    edge_states,
    edge_vectors,
    atom_tags,
    send_list,
    sources,
    trip_slots,
    triplet_mask,
    quad_slots,
    quad_mask,
    edge_mask,
    w_inputs,
    w_radial,
    w_trip_down,
    triplet_bilinear_weight,
    w_trip_up,
    w_quad_down,
    w_quad_bil,
    w_quad_up,
    w_atom_edge,
    w_residual,
    w_edge_atom,
    w_atom_dense,
    tag_table,
    cot_atoms,
    cot_edges,
    cot_energy,
):
    planes = 2 if lax.axis_size("gz") == 2 else 3
    group = 3 * planes

    offset = jnp.maximum(sources - ATOMS, 0)
    block, border = offset // SEND, offset % SEND
    step_x, step_y, step_z = block // 9, block // 3 % 3, block % 3
    if planes == 2:
        step_z = jnp.clip(step_z - 1 + lax.axis_index("gz"), 0, 1)
    block = (step_y * 3 + step_x) * planes + step_z
    inside = sources < ATOMS
    even = jnp.where(inside, 3 * group * 8 + sources, block * 8 + border)
    src = jnp.stack([even, even + jnp.where(inside, ATOMS, SEND)])
    slots = jnp.concatenate([trip_slots, quad_slots], axis=1)
    masks = jnp.concatenate([triplet_mask, quad_mask], axis=1)
    marks = jnp.where(masks > 0, slots * BLOCK + (jnp.arange(EDGES) % BLOCK)[:, None], -1)
    mark_rows = marks.reshape(BLOCKS, BLOCK, 2 * PICKS).transpose(0, 2, 1)
    mark_rows = mark_rows.reshape(BLOCKS, 1, 2 * PICKS * BLOCK)
    trip_down_t, quad_down_t = w_trip_down.T, w_quad_down.T

    tag_row, send_row = atom_tags[None, :], send_list[None, :]
    payload, local, tagged, pre, downs, rads, radial, columns = call(
        start_kernel,
        [(PAIRS, 8, 128), (PAIRS, 16, 128), (8, 256), (2, EDGES, 512), (EDGES, 128), (5, EDGES, 512)]
        + [(EDGES, 128)] * 2,
        [edge_states, edge_vectors, edge_mask[None, :], hidden_atoms, tag_row, send_row, tag_table,
         w_inputs, w_radial, trip_down_t, quad_down_t],
    )
    core = bit_value("gyl", 0)[None]
    me = jnp.stack([lax.axis_index(axis) for axis in ROWS]).astype(jnp.int32)
    before, here, after = with_halo(payload)
    (
        atoms_out, edges_out, energy_out, grad_edges, grad_tag,
        cosines, grad_sums, grad_src, keep_a, send_a, grad_rads, atom_rows, quad_up_grad,
    ) = call(
        main_kernel,
        [(8, 256), (EDGES, 512), (8, 256), (EDGES, 512), (8, 256)]
        + [(2 * BLOCKS, PICKS, 8, 128), (EDGES, 2048), (EDGES, 256), (896, 512), (896, 512)]
        + [(3, EDGES, 512), (8, 3328), (32, 512)],
        [before, here, after, local, tagged, edge_states, columns, rads, radial,
         src.T, slots, marks,
         triplet_bilinear_weight.T, w_trip_up, w_quad_bil.T, w_quad_up, w_atom_edge, w_residual,
         w_edge_atom, w_atom_dense, cot_atoms, cot_edges, cot_energy, core],
        scratch=[
            pltpu.VMEM((32, EDGES, 256), BF),
            pltpu.VMEM((EDGES, 2048), F32),
            pltpu.VMEM((128, 2048), BF),
            pltpu.VMEM((5, EDGES, 512), F32),
            pltpu.VMEM((EDGES, 128), F32),
            pltpu.VMEM((1792, 512), F32),
        ],
    )
    chain = Chain()
    got_a = swap(send_a, "gyl", 0)
    keep_b, send_b = call(
        late_kernel,
        [(768, 512)] * 2,
        [grad_rads, radial, atom_rows, quad_up_grad, core],
        scratch=[pltpu.VMEM((1536, 512), F32)],
    )
    late = reduction(chain, me, (keep_a, got_a), (keep_b, swap(send_b, "gyl", 0)), lambda step: 30)
    next(late)
    grad_sums = chain.after(grad_sums)
    back_before, back_here, back_after, back_local = chain.step(
        call(
            scatter_kernel,
            [(group, 16, 8, 128)] * 3 + [(16, 16, 128)],
            [cosines, grad_sums, grad_src, src, mark_rows],
            scratch=[pltpu.VMEM((32, EDGES, 256), BF)],
        )
    )
    got = shifted(back_before, GY, -1, True), shifted(back_after, GY, 1, True)
    next(late)
    back_first, back_middle, back_last = return_along(chain, back_here, got, planes)
    got = shifted(back_first, "gx", -1, True), shifted(back_last, "gx", 1, True)
    back = return_up(chain, me, back_middle, got, planes)
    if planes == 2:
        returned = back[0], lax.ppermute(back[1], "gz", [(0, 1), (1, 0)])
    else:
        returned = back[1], shifted(back[0], "gz", -1, False), shifted(back[2], "gz", 1, False)
    next(late)
    returned = sum(returned[1:], returned[0])
    returned = chain.after(returned)
    grad_atoms, grad_edges, keep_c, send_c, keep_d, send_d = call(
        finish_kernel,
        [(8, 256), (EDGES, 512)] + [(384, 512)] * 4,
        [back_local, returned, grad_edges, grad_tag, edge_states, radial, columns, pre, downs, rads,
         tag_row, send_row, w_inputs, trip_down_t, quad_down_t, core],
        scratch=[pltpu.VMEM((768, 512), F32)] * 2,
    )
    got_c, got_d = swap(send_c, "gyl", 0), swap(send_d, "gyl", 0)
    early = reduction(chain, me, (keep_c, got_c), (keep_d, got_d), lambda step: {3: 30, 5: 2, 7: 7}.get(step, 0))
    running = {"L": late, "E": early}
    done = {}

    def resume(name):
        if name in done:
            return
        try:
            next(running[name])
        except StopIteration as end:
            done[name] = end.value

    for name in "LELELELEELEELE":
        resume(name)
    while "L" not in done:
        resume("L")
    (a_mine, a_other), (b_mine, b_other) = done["L"]
    g_res, g_ae, g_trip_bil, g_trip_up, g_quad_bil, g_quad_up, g_rad, g_ea, g_ad = call(
        late_outputs,
        [(2, 512, 512), (2, 256, 512), (64, 1024), (64, 512), (32, 1024), (32, 512), (3, 128, 512)]
        + [(2, 512, 256), (4, 256, 256)],
        [a_mine, a_other, b_mine, b_other, core],
    )
    chain.step(g_rad)
    while "E" not in done:
        resume("E")
    (c_mine, c_other), (d_mine, d_other) = done["E"]
    g_inputs, g_rad, g_trip_down, g_quad_down, g_tags = call(
        early_outputs,
        [(2, 512, 512), (5, 128, 512), (64, 512), (32, 512), (3, 256)],
        [c_mine, c_other, d_mine, d_other, g_rad, core],
    )
    return (
        atoms_out,
        edges_out,
        energy_out,
        grad_atoms,
        grad_edges,
        g_inputs,
        g_rad,
        g_trip_down.T,
        g_trip_bil.T,
        g_trip_up,
        g_quad_down.T,
        g_quad_bil.T,
        g_quad_up,
        g_ae,
        g_res,
        g_ea,
        g_ad,
        g_tags,
    )


def solution(mesh):
    size = dict(mesh.shape)
    inner = Mesh(mesh.devices.reshape(size["gx"], size["gy"] // 2, 2, size["gz"]), ROWS)
    flat, columns, vector, whole = P(ROWS, None), P(None, ROWS), P(ROWS), P()
    placed = [flat, flat, columns] + [vector] * 3 + [flat] * 4 + [vector] + [whole] * 13 + [flat] * 3
    return jax.shard_map(
        per_device,
        mesh=inner,
        in_specs=tuple(placed),
        out_specs=tuple([flat] * 5 + [whole] * 13),
        check_vma=False,
    )
```

```python
import functools
import math

import jax
import jax.numpy as jnp
from jax import lax
from jax.experimental import pallas as pl
from jax.experimental.pallas import tpu as pltpu
from jax.sharding import Mesh
from jax.sharding import PartitionSpec as P

BF = jnp.bfloat16
F32 = jnp.float32
ROWS = ("gx", "gyh", "gyl", "gz")
GY = ("gyh", "gyl")
ATOMS, SEND, SLOTS, EDGES = 8, 4, 30, 240
ATOM_W, EDGE_W, TRIP_W, QUAD_W, RADIAL = 256, 512, 64, 32, 128
ANGLES, PICKS = 16, 8
PAIRS = 17
BLOCK = 16
BLOCKS = EDGES // BLOCK
root_half = 0.7071067811865476
NN = (((1,), (0,)), ((), ()))
NT = (((1,), (1,)), ((), ()))
TN = (((0,), (0,)), ((), ()))


def shifted(value, axis, steps, wrap):
    count = lax.axis_size(axis)
    pairs = [(i, (i + steps) % count) for i in range(count) if wrap or 0 <= i + steps < count]
    return lax.ppermute(value, axis, pairs)


def planes_of(value):
    if lax.axis_size("gz") == 2:
        other = lax.ppermute(value, "gz", [(0, 1), (1, 0)])
        top = lax.axis_index("gz") == 1
        return jnp.stack([jnp.where(top, other, value), jnp.where(top, value, other)])
    return jnp.stack([shifted(value, "gz", 1, False), value, shifted(value, "gz", -1, False)])


def with_halo(value):
    value = planes_of(value)
    value = jnp.concatenate([shifted(value, "gx", 1, True), value, shifted(value, "gx", -1, True)])
    return shifted(value, GY, 1, True), value, shifted(value, GY, -1, True)


def bits_of(axis):
    count = lax.axis_size(axis)
    return [(axis, b) for b in range(count.bit_length() - 1)]


def swap(value, axis, bit):
    count = lax.axis_size(axis)
    return lax.ppermute(value, axis, [(i, i ^ (1 << bit)) for i in range(count)])


def bit_value(axis, bit):
    return (lax.axis_index(axis) >> bit) & 1


def part(arrays, at, size):
    total = lax.dynamic_slice_in_dim(arrays[0], at, size)
    for x in arrays[1:]:
        total = total + lax.dynamic_slice_in_dim(x, at, size)
    return total


class Chain:
    def __init__(self):
        self.last = None

    def after(self, values):
        if self.last is not None:
            self.last, values = lax.optimization_barrier((self.last, values))
        return values

    def step(self, value):
        self.last = value
        return value

    def zero(self):
        first = jax.tree.leaves(self.last)[0]
        corner = first[(slice(0, 1),) * first.ndim].reshape(())
        return jnp.minimum(jnp.abs(corner), 0.0)


def halved(chain, arrays, axis, bit, tight=False):
    arrays = chain.after(arrays)
    half = arrays[0].shape[0] // 2
    one = bit_value(axis, bit)
    send = chain.step(part(arrays, (1 - one) * half, half))
    got = swap(send, axis, bit)
    send, arrays = lax.optimization_barrier((send, arrays))
    keep = part(arrays, one * half, half)
    if tight:
        chain.step((send, keep))
    return [keep, got]


def joined_halves(value, other, axis, bit):
    one = bit_value(axis, bit) == 1
    return jnp.concatenate([jnp.where(one, other, value), jnp.where(one, value, other)])


def reduction(chain, first, second, tight=False, firm=False):
    across, along = bits_of("gz"), bits_of("gyh")
    lanes = [first, second]
    for turn, plan in enumerate(((across, along), (along, across))):
        for i in range(2):
            for axis, bit in plan[i]:
                lanes[i] = halved(chain, lanes[i], axis, bit, tight and turn == 1)
        yield
    sizes = [x[0].shape[0] for x in lanes]
    joint = [jnp.concatenate(pair) for pair in zip(*chain.after(lanes))]
    for axis, bit in bits_of("gx"):
        joint = halved(chain, joint, axis, bit, tight)
        yield
    joint = chain.after(joint)
    value = chain.step(sum(joint[1:], joint[0]))
    for axis, bit in bits_of("gx")[::-1]:
        other = swap(value, axis, bit)
        yield
        value, other = chain.after((value, other))
        value = chain.step(joined_halves(value, other, axis, bit))
    values = [value[: sizes[0]], value[sizes[0] :]]
    for plan in ((along, across), (across, along)):
        for turn in range(max(len(across), len(along))):
            others = [None, None]
            for i in range(2):
                if turn < len(plan[i]):
                    others[i] = swap(values[i], *plan[i][::-1][turn])
            yield
            for i in range(2):
                if turn < len(plan[i]):
                    values[i], others[i] = chain.after((values[i], others[i]))
                    whole = joined_halves(values[i], others[i], *plan[i][::-1][turn])
                    if firm and plan[0] is across:
                        whole = whole + chain.zero()
                    values[i] = chain.step(whole)
    others = [swap(x, "gyl", 0) for x in values]
    yield
    values, others = chain.after((values, others))
    return [(value, chain.step(other)) for value, other in zip(values, others)]


def iota(shape, dim):
    return lax.broadcasted_iota(jnp.int32, shape, dim)


def dot(left, right, dims=NN):
    return lax.dot_general(left, right, dims, preferred_element_type=F32)


def halves(x):
    high = x.astype(BF)
    return high, (x - high.astype(F32)).astype(BF)


def stacked(x):
    high, low = halves(x)
    if x.shape[0] % 16 == 0:
        return jnp.concatenate([high, low], axis=0)
    return jnp.concatenate([high.astype(F32), low.astype(F32)], axis=0).astype(BF)


def folded(x):
    half = x.shape[0] // 2
    return x[:half] + x[half:]


def times(x, weight, dims=NN):
    return folded(dot(stacked(x), weight, dims))


def side_by_side(x):
    return jnp.concatenate(halves(x), axis=1)


def side_sum(x):
    half = x.shape[1] // 2
    return x[:, :half] + x[:, half:]


def weight_grad(x, y):
    x_high, x_low = halves(x)
    y_high, y_low = halves(y)
    left, right = [x_high, x_high, x_low], [y_high, y_low, y_high]
    if x.shape[0] % 16 == 0:
        return dot(jnp.concatenate(left, axis=0), jnp.concatenate(right, axis=0), TN)
    left = jnp.concatenate([p.astype(F32) for p in left], axis=0).astype(BF)
    right = jnp.concatenate([p.astype(F32) for p in right], axis=0).astype(BF)
    return dot(left, right, TN)


def onehot(hit):
    return jnp.where(hit, 1.0, 0.0).astype(BF)


def sigmoid(v):
    return 1.0 / (1.0 + jnp.exp(-v))


def act(v):
    return v * sigmoid(v) * (1.0 / 0.6)


def act_and_slope(v):
    s = sigmoid(v)
    return v * s * (1.0 / 0.6), s * (1.0 + v * (1.0 - s)) * (1.0 / 0.6)


def sin_pi(t):
    n = jnp.floor(t + 0.5)
    r = t - n
    odd = n - 2.0 * jnp.floor(n * 0.5)
    q = r * r
    total = jnp.zeros_like(r)
    for k in range(6, -1, -1):
        total = total * q + (-1.0) ** k * math.pi ** (2 * k + 1) / math.factorial(2 * k + 1)
    return total * r * (1.0 - 2.0 * odd)


def to_column(row):
    n = row.shape[1]
    same = iota((n, n), 0) == iota((n, n), 1)
    return jnp.sum(jnp.where(same, row, jnp.zeros_like(row)), axis=1, keepdims=True)


def send_column(send, rows):
    shape = (rows, SEND)
    hit = (iota(shape, 0) & (SEND - 1)) == iota(shape, 1)
    return jnp.sum(jnp.where(hit, send, 0), axis=1, keepdims=True)


def send_lanes(send):
    shape = (8, 128)
    hit = iota(shape, 0) == (iota(shape, 1) & (SEND - 1))
    return jnp.sum(jnp.where(hit, send_column(send, 8), 0), axis=0, keepdims=True)


def paid(row, send):
    edge = send * SLOTS + 2 * (row >> 3) + ((row >> 2) & 1)
    return jnp.where(row < 120, edge, -1)


def atom_of(edge):
    total = jnp.zeros_like(edge)
    for a in range(1, ATOMS):
        total = total + jnp.where(edge >= a * SLOTS, 1, 0)
    return total


def radial_of(length):
    x = length / 12.0
    x2 = x * x
    x4 = x2 * x2
    envelope = 1.0 - 28.0 * (x4 * x2) + 48.0 * (x4 * x2 * x) - 21.0 * (x4 * x4)
    orders = (iota((1, RADIAL), 1) + 1).astype(F32)
    return envelope * sin_pi(x * orders) / x


def geometry(unit):
    own = atom_of(iota((8, EDGES), 1)) == iota((8, EDGES), 0)
    edge = iota((EDGES, 128), 0)
    slot = edge - atom_of(edge) * SLOTS
    total = jnp.zeros((24, 128), F32)
    for k in range(3):
        x = jnp.where(own, unit[k : k + 1, :], 0.0)
        high = x.astype(BF).astype(F32)
        mid = (x - high).astype(BF).astype(F32)
        parts = jnp.concatenate([high, mid, x - high - mid], axis=0).astype(BF)
        total = total + dot(parts, onehot(iota((EDGES, 128), 1) == slot + 32 * k))
    return total[0:8] + total[8:16] + total[16:24]


def local_rows(index):
    return (index & 7) * SLOTS + 2 * (index >> 4) + ((index >> 3) & 1)


def start_kernel(
    edge, vec, mask, hidden, tag_row, send_row, table, w_in, w_rad, w_trip, w_quad,
    payload, local, tagged, pre, downs, rads, radial_out, columns,
):
    vectors = vec[...]
    length = jnp.sqrt(jnp.sum(vectors * vectors, axis=0, keepdims=True))
    unit = vectors / length
    geo = geometry(unit)
    live = to_column(jnp.where(mask[...] > 0, 1.0, 0.0))
    parts = [live] + [to_column(unit[k : k + 1, :]) for k in range(3)]
    columns[...] = jnp.concatenate(parts + [jnp.zeros((EDGES, 124), F32)], axis=1)
    send = send_column(send_row[...], 8)
    pay = paid(iota((128, 1), 0), send_column(send_row[...], 128))
    tags = to_column(tag_row[...])
    radial = radial_of(to_column(length))
    radial_out[...] = radial
    split = stacked(radial)
    for k in range(5):
        rads[k] = folded(dot(split, w_rad[k]))
    split = stacked(edge[...])
    pre[0] = folded(dot(split, w_in[0]))
    pre[1] = folded(dot(split, w_in[1]))
    trip_pre = times(act(pre[0]) * rads[0], w_trip[...], NT)
    quad_pre = times(act(pre[1]) * rads[1], w_quad[...], NT)
    downs[...] = jnp.concatenate([trip_pre, quad_pre, jnp.zeros((EDGES, 32), F32)], axis=1)
    trip = act(trip_pre) * live
    quad = act(quad_pre) * live
    rows = jnp.concatenate([trip, quad * radial[:, 0:1], quad * radial[:, 1:2]], axis=1)
    rows = side_by_side(rows)
    shape = (EDGES, EDGES)
    place = onehot(local_rows(iota(shape, 0)) == iota(shape, 1))
    local[0:15] = side_sum(dot(place, rows)).reshape(15, 16, 128)
    place = onehot(pay == iota((128, EDGES), 1))
    payload[0:16] = side_sum(dot(place, rows)).reshape(16, 8, 128)
    tag = hidden[...]
    for t in range(3):
        tag = tag + jnp.where(tags == t, table[t : t + 1, :].astype(F32), 0.0)
    tagged[...] = tag
    local[15] = jnp.concatenate([tag[:, :128], tag[:, 128:]], axis=0)
    local[16] = jnp.concatenate([geo, jnp.zeros((8, 128), F32)], axis=0)
    both = jnp.concatenate([tag, geo], axis=1)
    sent = jnp.zeros((8, 384), F32)
    for a in range(ATOMS):
        sent = sent + jnp.where(send == a, both[a : a + 1, :], 0.0)
    payload[15] = jnp.where(iota((8, 128), 0) < 4, sent[:, :128], sent[:, 128:256])
    payload[16] = sent[:, 256:]


def split_cores(core, whole, keep, send):
    half = whole.shape[0] // 2
    upper = core[0] == 1
    low, high = whole[:half], whole[half:]
    keep[...] = jnp.where(upper, high, low)
    send[...] = jnp.where(upper, low, high)


def segments(shape, edge_dim, atom_dim):
    edge, atom = iota(shape, edge_dim), iota(shape, atom_dim) & 7
    return onehot((edge >= atom * SLOTS) & (edge < atom * SLOTS + SLOTS))


def lead(k):
    return math.comb(2 * k, k) / 2.0**k


def ratio(k):
    return k * k / (4.0 * k * k - 1.0)


def monic(cosine):
    before, now = jnp.ones_like(cosine), cosine
    yield before
    yield now
    for k in range(1, ANGLES - 1):
        before, now = now, cosine * now - ratio(k) * before
        yield now


def looped(count, step, body):
    def turn(t, carry):
        for i in range(step):
            body(t * step + i)
        return carry

    lax.fori_loop(0, count // step, turn, 0)


def main_kernel(
    halo_before, halo_here, halo_after, local, tagged, edge, columns, rads, radial,
    src_cols, slots, marks,
    trip_bil, trip_up, quad_bil, quad_up, w_ae, w_res, w_ea, w_ad,
    cot_atoms, cot_edges, cot_energy, core,
    atoms_out, edges_out, energy_out, grad_edges, grad_tag,
    cosines, grad_sums, grad_src, keep, send, grad_rads, atom_rows, quad_up_grad,
    table, sums, weight, kept, cos_table, first,
):
    live = columns[:, 0:1]
    halos = (halo_before, halo_here, halo_after)
    group = halo_here.shape[0] * 8
    depth = 3 * group + 16
    lanes = iota((EDGES, depth), 1)
    place = jnp.concatenate(
        [onehot(src_cols[:, 0:1] == lanes), onehot(src_cols[:, 1:2] == lanes)], axis=0
    )

    def rows_at(p):
        parts = [h[:, p].reshape(group, 128) for h in halos]
        return jnp.concatenate(parts + [local[p]], axis=0)

    def gather_pair(p):
        got = dot(place, side_by_side(rows_at(p))).astype(BF)
        table[2 * p] = got[:EDGES]
        table[2 * p + 1] = got[EDGES:]

    looped(16, 4, gather_pair)

    rows = rows_at(16)
    high, low = halves(rows)
    rest = (rows - high.astype(F32) - low.astype(F32)).astype(BF)
    got = dot(place[:EDGES], jnp.concatenate([high, low, rest], axis=1))
    got = got[:, :128] + got[:, 128:256] + got[:, 256:]
    cos_table[...] = -(
        columns[:, 1:2] * got
        + columns[:, 2:3] * pltpu.roll(got, 96, 1)
        + columns[:, 3:4] * pltpu.roll(got, 64, 1)
    )

    for k in range(ANGLES):
        top = trip_bil[:, k * 64 : k * 64 + 64].astype(F32)
        top = jnp.concatenate([top, jnp.zeros((64, 64), F32)], axis=1)
        low_left = quad_bil[:, k * 32 : k * 32 + 32].astype(F32)
        low_right = quad_bil[:, 512 + k * 32 : 544 + k * 32].astype(F32)
        bottom = jnp.concatenate([jnp.zeros((32, 64), F32), low_left, low_right], axis=1)
        piece = jnp.concatenate([top, bottom, jnp.zeros((32, 128), F32)], axis=0)
        weight[:, k * 128 : (k + 1) * 128] = piece.astype(BF)

    trip_lanes = iota((128, 128), 1) < TRIP_W
    scale = 1.0 / math.sqrt(PICKS)

    def basis_block(b):
        at = pl.multiple_of(b * BLOCK, BLOCK)
        own = pl.ds(at, BLOCK)
        wide = iota((BLOCK, 512), 1)
        mark = marks[own, :]
        hits = [jnp.where(mark[:, t : t + 1] == wide, 1.0, 0.0) for t in range(2 * PICKS)]
        hits = jnp.concatenate(hits, axis=0).astype(BF)
        got = side_sum(dot(hits, table[:, own, :].reshape(512, 256)))
        picked = jnp.where(trip_lanes, got[:128], got[128:])
        picked = picked.reshape(PICKS, BLOCK, 128)
        cos_here = cos_table[own, :]
        slot = slots[own, :]
        low_lanes = iota((BLOCK, 128), 1) < TRIP_W
        for h in range(2):
            rows = slice(8 * h, 8 * h + 8)
            cos = []
            for j in range(PICKS):
                index = jnp.where(
                    low_lanes[rows], slot[rows, j : j + 1], slot[rows, PICKS + j : PICKS + j + 1]
                )
                cos.append(jnp.take_along_axis(cos_here[rows], index, axis=1))
            cos = jnp.stack(cos)
            cosines[2 * b + h] = cos
            values = picked[:, rows]
            for k, poly in enumerate(monic(cos)):
                total = jnp.sum(poly * values, axis=0) * (lead(k) * scale)
                sums[pl.ds(pl.multiple_of(at + 8 * h, 8), 8), k * 128 : (k + 1) * 128] = total

    looped(BLOCKS, 3, basis_block)

    down = times(sums[...], weight[...], NT)
    down_act, down_slope = act_and_slope(down)
    trip_h, quad_h = down_act[:, :64], down_act[:, 64:96]
    trip_pre = times(trip_h, trip_up[...])
    quad_pre = times(quad_h, quad_up[...])
    src = jnp.concatenate(
        [side_sum(table[30].astype(F32)), side_sum(table[31].astype(F32))], axis=1
    )
    target = times(tagged[...], w_ae[1])
    spread = segments((EDGES, 16), 0, 1)
    gathers = segments((8, EDGES), 1, 0)

    def to_edges(x):
        return dot(spread, stacked(x))

    def to_atoms(x):
        return side_sum(dot(gathers, side_by_side(x)))

    atom_pre = times(src, w_ae[0]) + to_edges(target)
    atom_act, atom_slope = act_and_slope(atom_pre)
    trip_act, trip_slope = act_and_slope(trip_pre)
    quad_act, quad_slope = act_and_slope(quad_pre)
    merged = (edge[...] + trip_act + quad_act + atom_act * rads[2]) * 0.5
    kept[0] = merged
    first_act, first_slope = act_and_slope(times(merged, w_res[0]))
    kept[1] = first_act
    second_act, second_slope = act_and_slope(times(first_act, w_res[1]))
    new_edges = (merged + second_act) * root_half
    edges_out[...] = new_edges
    weighted = new_edges * live
    root_slots = 1.0 / math.sqrt(SLOTS)
    gathered = to_atoms(weighted * rads[3]) * root_slots
    summary = to_atoms(weighted * rads[4]) * root_slots
    gate_act, gate_slope = act_and_slope(times(gathered, w_ea[0]))
    updated = (tagged[...] + gate_act) * root_half
    a0_act, a0_slope = act_and_slope(times(updated, w_ad[0]))
    a1_act, a1_slope = act_and_slope(times(a0_act, w_ad[1]))
    new_atoms = (updated + a1_act) * root_half
    atoms_out[...] = new_atoms
    e_act, e_slope = act_and_slope(times(summary, w_ea[1]) + times(new_atoms, w_ad[2]))
    out_act, out_slope = act_and_slope(times(e_act, w_ad[3]))
    energy_out[...] = out_act

    d_out = cot_energy[...] * out_slope
    d_e = times(d_out, w_ad[3], NT) * e_slope
    d_summary = times(d_e, w_ea[1], NT)
    d_atoms = (cot_atoms[...] + times(d_e, w_ad[2], NT)) * root_half
    d_a1 = d_atoms * a1_slope
    d_a0 = times(d_a1, w_ad[1], NT) * a0_slope
    d_updated = (d_atoms + times(d_a0, w_ad[0], NT)) * root_half
    d_gate = d_updated * gate_slope
    d_gathered = times(d_gate, w_ea[0], NT)

    d_gathered = to_edges(d_gathered * root_slots)
    d_summary = to_edges(d_summary * root_slots)
    grad_rads[1] = weighted * d_gathered
    grad_rads[2] = weighted * d_summary
    d_new = cot_edges[...] + live * (d_gathered * rads[3] + d_summary * rads[4])
    d_new = d_new * root_half
    d_second = d_new * second_slope
    kept[3] = d_second
    d_first = times(d_second, w_res[1], NT) * first_slope
    kept[2] = d_first
    d_merged = (d_new + times(d_first, w_res[0], NT)) * 0.5
    grad_edges[...] = d_merged
    grad_rads[0] = d_merged * atom_act
    d_atom = d_merged * rads[2] * atom_slope
    kept[4] = d_atom
    d_trip = d_merged * trip_slope
    d_quad = d_merged * quad_slope
    d_target = to_atoms(d_atom)
    grad_tag[...] = d_updated + times(d_target, w_ae[1], NT)
    d_down = jnp.concatenate(
        [times(d_trip, trip_up[...], NT), times(d_quad, quad_up[...], NT), jnp.zeros((EDGES, 32), F32)],
        axis=1,
    )
    d_down = d_down * down_slope
    grad_src[...] = times(d_atom, w_ae[0], NT)

    first[0:512] = weight_grad(kept[0], kept[2])
    first[512:768] = weight_grad(src, kept[4])
    first[896:1408] = weight_grad(kept[1], kept[3])
    first[1408:1664] = weight_grad(tagged[...], d_target)
    bil = weight_grad(d_down, sums[...])
    for m in range(8):
        tile = [bil[0:64, k * 128 : k * 128 + 64] for k in (2 * m, 2 * m + 1)]
        row = 768 + 64 * (m // 4)
        first[row : row + 64, (m % 4) * 128 : (m % 4 + 1) * 128] = jnp.concatenate(tile, axis=1)
    for half in range(2):
        for m in range(4):
            at = 64 + 32 * half
            tile = [bil[64:96, k * 128 + at : k * 128 + at + 32] for k in range(4 * m, 4 * m + 4)]
            row = 1728 + 32 * half
            first[row : row + 32, m * 128 : (m + 1) * 128] = jnp.concatenate(tile, axis=1)
    first[1664:1728] = weight_grad(down_act, d_trip)[:64]
    quad_up_grad[...] = weight_grad(down_act, d_quad)[64:96]
    atom_rows[...] = jnp.concatenate(
        [gathered, summary, updated, a0_act, new_atoms, e_act, d_a0, d_a1, d_e, d_out, d_gate], axis=1
    )
    split_cores(core, first, keep, send)
    grad_sums[...] = times(d_down, weight[...])


def late_kernel(grad_rads, radial, atom_rows, quad_up_grad, core, keep, send, second):
    atoms = atom_rows[...]
    gathered, summary = atoms[:, :512], atoms[:, 512:1024]
    updated, a0_act, new_atoms, e_act, d_a0, d_a1, d_e, d_out, d_gate = [
        atoms[:, at : at + 256] for at in range(1024, 3328, 256)
    ]
    second[0:512, 0:256] = weight_grad(gathered, d_gate)
    second[0:512, 256:512] = weight_grad(summary, d_e)
    second[512:768, 0:256] = weight_grad(updated, d_a0)
    second[512:768, 256:512] = weight_grad(a0_act, d_a1)
    second[768:1024, 0:256] = weight_grad(new_atoms, d_e)
    second[768:1024, 256:512] = weight_grad(e_act, d_out)
    for k in range(3):
        second[1024 + 128 * k : 1152 + 128 * k] = weight_grad(radial[...], grad_rads[k])
    second[1408:1440] = quad_up_grad[...]
    second[1440:1536] = jnp.zeros((96, 512), F32)
    split_cores(core, second, keep, send)


def scatter_kernel(
    cosines, sums, grad_src, src_rows, mark_rows,
    back_before, back_here, back_after, back_local,
    table,
):
    group = back_here.shape[0] * 8
    depth = 3 * group + 16
    trip_lanes = iota((128, 128), 1) < TRIP_W
    scale = 1.0 / math.sqrt(PICKS)

    def basis_back(b):
        at = pl.multiple_of(b * BLOCK, BLOCK)
        own = pl.ds(at, BLOCK)
        parts = []
        for h in range(2):
            cos = cosines[2 * b + h]
            own_rows = pl.ds(pl.multiple_of(at + 8 * h, 8), 8)
            after = total = None
            for k in range(ANGLES - 1, -1, -1):
                term = sums[own_rows, k * 128 : (k + 1) * 128] * (lead(k) * scale)
                if total is None:
                    after, total = None, jnp.broadcast_to(term, cos.shape)
                elif after is None:
                    after, total = total, term + cos * total
                else:
                    after, total = total, term + cos * total - ratio(k + 1) * after
            parts.append(total)
        grad = jnp.concatenate(parts, axis=1).reshape(128, 128)
        grad = jnp.concatenate(
            [jnp.where(trip_lanes, grad, 0.0), jnp.where(trip_lanes, 0.0, grad)], axis=0
        )
        hits = onehot(mark_rows[b] == iota((512, 256), 0))
        got = side_by_side(side_sum(dot(hits, side_by_side(grad))))
        table[:, own, :] = got.reshape(32, BLOCK, 256)

    looped(BLOCKS, 3, basis_back)
    table[30] = side_by_side(grad_src[:, :128])
    table[31] = side_by_side(grad_src[:, 128:])
    rows = iota((depth, EDGES), 0)
    place_even = onehot(src_rows[0:1, :] == rows)
    place_odd = onehot(src_rows[1:2, :] == rows)

    def scatter_pair(p):
        got = side_sum(dot(place_even, table[2 * p]) + dot(place_odd, table[2 * p + 1]))
        for i, back in enumerate((back_before, back_here, back_after)):
            back[:, p] = got[i * group : (i + 1) * group].reshape(group // 8, 8, 128)
        back_local[p] = got[3 * group :]

    looped(16, 4, scatter_pair)


def finish_kernel(
    back_local, returned, grad_late, tag_late, edge, radial, columns, pre, downs, rads, tag_row, send_row,
    w_in, w_trip, w_quad, core,
    grad_atoms, grad_edges, keep_first, send_first, keep_second, send_second,
    first, second,
):
    shape = (EDGES, 256)
    lane = iota(shape, 1)
    place = onehot((local_rows(lane) == iota(shape, 0)) & (lane < EDGES))
    rows = dot(place, side_by_side(back_local[...].reshape(256, 128)))
    pay = paid(iota((1, 128), 1), send_lanes(send_row[...]))
    place = onehot(pay == iota((EDGES, 128), 0))
    send = send_column(send_row[...], 8)
    tags = to_column(tag_row[...])
    rows = side_sum(rows + dot(place, side_by_side(returned[...].reshape(128, 128))))
    back = returned[15]
    tag = tag_late[...] + jnp.concatenate([back_local[15, 0:8], back_local[15, 8:16]], axis=1)
    atom = iota((8, 1), 0)
    for r in range(SEND):
        piece = jnp.concatenate([back[r : r + 1], back[4 + r : 5 + r]], axis=1)
        tag = tag + jnp.where(send[r : r + 1, :] == atom, piece, 0.0)
    grad_atoms[...] = tag
    table = [
        jnp.sum(jnp.where(tags == t, tag, 0.0), axis=0, keepdims=True) for t in range(3)
    ]
    table = jnp.concatenate(table + [jnp.zeros((29, ATOM_W), F32)], axis=0)
    d_trip = rows[:, :64]
    d_quad = rows[:, 64:96] * radial[:, 0:1] + rows[:, 96:128] * radial[:, 1:2]
    total = grad_late[...]
    for k, (d_row, down, weight, out) in enumerate(
        ((d_trip, slice(0, 64), w_trip, first), (d_quad, slice(64, 96), w_quad, second))
    ):
        d_down = d_row * columns[:, 0:1] * act_and_slope(downs[:, down])[1]
        value, slope = act_and_slope(pre[k])
        d_start = times(d_down, weight[...])
        d_pre = d_start * rads[k] * slope
        total = total + times(d_pre, w_in[k], NT)
        out[0:512] = weight_grad(edge[...], d_pre)
        out[512:640] = weight_grad(radial[...], d_start * value)
        down_grad = weight_grad(d_down, value * rads[k])
        if k == 0:
            out[640:704] = down_grad
            out[704:768] = jnp.zeros((64, 512), F32)
        else:
            out[640:672] = down_grad
            out[672:704, 0:256] = table
            out[672:704, 256:512] = jnp.zeros((32, 256), F32)
            out[704:768] = jnp.zeros((64, 512), F32)
    grad_edges[...] = total
    split_cores(core, first, keep_first, send_first)
    split_cores(core, second, keep_second, send_second)


def late_outputs(
    a_mine, a_other, b_mine, b_other, core,
    res, ae, trip_bil, trip_up, quad_bil, quad_up, rad, ea, ad,
):
    upper = core[0] == 1

    def rows(mine, other, at, size):
        half = mine.shape[0]
        where = slice(at % half, at % half + size)
        if at < half:
            return jnp.where(upper, other[where], mine[where])
        return jnp.where(upper, mine[where], other[where])

    a = lambda at, size: rows(a_mine, a_other, at, size)
    b = lambda at, size: rows(b_mine, b_other, at, size)
    for k in range(2):
        res[k] = a(896 * k, 512)
        ae[k] = a(896 * k + 512, 256)
        trip_bil[:, 512 * k : 512 * k + 512] = a(768 + 64 * k, 64)
        quad_bil[:, 512 * k : 512 * k + 512] = a(1728 + 32 * k, 32)
    trip_up[...] = a(1664, 64)
    quad_up[...] = b(1408, 32)
    for k in range(3):
        rad[k] = b(1024 + 128 * k, 128)
    both = b(0, 512)
    ea[0], ea[1] = both[:, :256], both[:, 256:]
    both = b(512, 256)
    ad[0], ad[1] = both[:, :256], both[:, 256:]
    both = b(768, 256)
    ad[2], ad[3] = both[:, :256], both[:, 256:]


def early_outputs(c_mine, c_other, d_mine, d_other, late_rad, core, inputs, rad, trip_down, quad_down, tags):
    upper = core[0] == 1
    for k, (mine, other) in enumerate(((c_mine, c_other), (d_mine, d_other))):
        inputs[k, 0:384] = jnp.where(upper, other[...], mine[...])
        high = jnp.where(upper, mine[...], other[...])
        inputs[k, 384:512] = high[:128]
        rad[k] = high[128:256]
        if k == 0:
            trip_down[...] = high[256:320]
        else:
            quad_down[...] = high[256:288]
            tags[...] = high[288:291, :256]
    rad[2:5] = late_rad[...]


def call(kernel, outs, args, scratch=(), micros=1):
    flops = int(micros * 1.15e9)
    return pl.pallas_call(
        kernel,
        out_shape=[jax.ShapeDtypeStruct(shape, F32) for shape in outs],
        in_specs=[pl.BlockSpec(memory_space=pltpu.SMEM if x.ndim == 1 else pltpu.VMEM) for x in args],
        out_specs=[pl.BlockSpec(memory_space=pltpu.VMEM)] * len(outs),
        scratch_shapes=list(scratch),
        compiler_params=pltpu.CompilerParams(vmem_limit_bytes=56 * 1024 * 1024),
        cost_estimate=pl.CostEstimate(flops=flops, bytes_accessed=1 << 10, transcendentals=0),
    )(*args)


def per_device(
    hidden_atoms,
    edge_states,
    edge_vectors,
    atom_tags,
    send_list,
    sources,
    trip_slots,
    triplet_mask,
    quad_slots,
    quad_mask,
    edge_mask,
    w_inputs,
    w_radial,
    w_trip_down,
    triplet_bilinear_weight,
    w_trip_up,
    w_quad_down,
    w_quad_bil,
    w_quad_up,
    w_atom_edge,
    w_residual,
    w_edge_atom,
    w_atom_dense,
    tag_table,
    cot_atoms,
    cot_edges,
    cot_energy,
):
    planes = 2 if lax.axis_size("gz") == 2 else 3
    group = 3 * planes

    offset = jnp.maximum(sources - ATOMS, 0)
    block, border = offset // SEND, offset % SEND
    step_x, step_y, step_z = block // 9, block // 3 % 3, block % 3
    if planes == 2:
        step_z = jnp.clip(step_z - 1 + lax.axis_index("gz"), 0, 1)
    block = (step_y * 3 + step_x) * planes + step_z
    inside = sources < ATOMS
    even = jnp.where(inside, 3 * group * 8 + sources, block * 8 + border)
    src = jnp.stack([even, even + jnp.where(inside, ATOMS, SEND)])
    slots = jnp.concatenate([trip_slots, quad_slots], axis=1)
    masks = jnp.concatenate([triplet_mask, quad_mask], axis=1)
    marks = jnp.where(masks > 0, slots * BLOCK + (jnp.arange(EDGES) % BLOCK)[:, None], -1)
    mark_rows = marks.reshape(BLOCKS, BLOCK, 2 * PICKS).transpose(0, 2, 1)
    mark_rows = mark_rows.reshape(BLOCKS, 1, 2 * PICKS * BLOCK)
    trip_down_t, quad_down_t = w_trip_down.T, w_quad_down.T

    tag_row, send_row = atom_tags[None, :], send_list[None, :]
    payload, local, tagged, pre, downs, rads, radial, columns = call(
        start_kernel,
        [(PAIRS, 8, 128), (PAIRS, 16, 128), (8, 256), (2, EDGES, 512), (EDGES, 128), (5, EDGES, 512)]
        + [(EDGES, 128)] * 2,
        [edge_states, edge_vectors, edge_mask[None, :], hidden_atoms, tag_row, send_row, tag_table,
         w_inputs, w_radial, trip_down_t, quad_down_t],
        micros=5,
    )
    core = bit_value("gyl", 0)[None]
    before, here, after = with_halo(payload)
    (
        atoms_out, edges_out, energy_out, grad_edges, grad_tag,
        cosines, grad_sums, grad_src, keep_a, send_a, grad_rads, atom_rows, quad_up_grad,
    ) = call(
        main_kernel,
        [(8, 256), (EDGES, 512), (8, 256), (EDGES, 512), (8, 256)]
        + [(2 * BLOCKS, PICKS, 8, 128), (EDGES, 2048), (EDGES, 256), (896, 512), (896, 512)]
        + [(3, EDGES, 512), (8, 3328), (32, 512)],
        [before, here, after, local, tagged, edge_states, columns, rads, radial,
         src.T, slots, marks,
         triplet_bilinear_weight.T, w_trip_up, w_quad_bil.T, w_quad_up, w_atom_edge, w_residual,
         w_edge_atom, w_atom_dense, cot_atoms, cot_edges, cot_energy, core],
        scratch=[
            pltpu.VMEM((32, EDGES, 256), BF),
            pltpu.VMEM((EDGES, 2048), F32),
            pltpu.VMEM((128, 2048), BF),
            pltpu.VMEM((5, EDGES, 512), F32),
            pltpu.VMEM((EDGES, 128), F32),
            pltpu.VMEM((1792, 512), F32),
        ],
        micros=26,
    )
    chain = Chain()
    got_a = swap(send_a, "gyl", 0)
    keep_b, send_b = call(
        late_kernel,
        [(768, 512)] * 2,
        [grad_rads, radial, atom_rows, quad_up_grad, core],
        scratch=[pltpu.VMEM((1536, 512), F32)],
        micros=4,
    )
    late = reduction(chain, [keep_a, got_a], [keep_b, swap(send_b, "gyl", 0)], True, True)
    next(late)
    grad_sums = chain.after(grad_sums)
    back_before, back_here, back_after, back_local = call(
        scatter_kernel,
        [(group, 16, 8, 128)] * 3 + [(16, 16, 128)],
        [cosines, grad_sums, grad_src, src, mark_rows],
        scratch=[pltpu.VMEM((32, EDGES, 256), BF)],
        micros=13,
    )
    got = shifted(back_before, GY, -1, True), shifted(back_after, GY, 1, True)
    chain.step(back_local)
    next(late)
    got, value = chain.after((got, back_here))
    value = chain.step(value + got[0] + got[1])
    first_plane, middle, last_plane = value[:planes], value[planes : 2 * planes], value[2 * planes :]
    got = shifted(first_plane, "gx", -1, True), shifted(last_plane, "gx", 1, True)
    got, middle = chain.after((got, middle))
    value = chain.step(middle + got[0] + got[1])
    next(late)
    if planes == 2:
        top = lax.axis_index("gz") == 1
        mine = jnp.where(top, value[1], value[0])
        theirs = jnp.where(top, value[0], value[1])
        returned = mine + lax.ppermute(theirs, "gz", [(0, 1), (1, 0)])
    else:
        returned = value[1] + shifted(value[0], "gz", -1, False) + shifted(value[2], "gz", 1, False)
    returned = chain.after(returned)
    grad_atoms, grad_edges, keep_c, send_c, keep_d, send_d = call(
        finish_kernel,
        [(8, 256), (EDGES, 512)] + [(384, 512)] * 4,
        [back_local, returned, grad_edges, grad_tag, edge_states, radial, columns, pre, downs, rads,
         tag_row, send_row, w_inputs, trip_down_t, quad_down_t, core],
        scratch=[pltpu.VMEM((768, 512), F32)] * 2,
        micros=7,
    )
    next(late)
    send_c, send_d = chain.after((send_c, send_d))
    got_c, got_d = swap(send_c, "gyl", 0), swap(send_d, "gyl", 0)
    early = reduction(chain, [keep_c, got_c], [keep_d, got_d])
    running = {"L": late, "E": early}
    done = {}

    def resume(name):
        if name in done:
            return
        try:
            next(running[name])
        except StopIteration as end:
            done[name] = end.value

    for name in "ELELELEELEELE":
        resume(name)
    while "L" not in done:
        resume("L")
    (a_mine, a_other), (b_mine, b_other) = done["L"]
    g_res, g_ae, g_trip_bil, g_trip_up, g_quad_bil, g_quad_up, g_rad, g_ea, g_ad = call(
        late_outputs,
        [(2, 512, 512), (2, 256, 512), (64, 1024), (64, 512), (32, 1024), (32, 512), (3, 128, 512)]
        + [(2, 512, 256), (4, 256, 256)],
        [a_mine, a_other, b_mine, b_other, core],
        micros=5,
    )
    chain.step(g_rad)
    while "E" not in done:
        resume("E")
    (c_mine, c_other), (d_mine, d_other) = done["E"]
    g_inputs, g_rad, g_trip_down, g_quad_down, g_tags = call(
        early_outputs,
        [(2, 512, 512), (5, 128, 512), (64, 512), (32, 512), (3, 256)],
        [c_mine, c_other, d_mine, d_other, g_rad, core],
        micros=3,
    )
    return (
        atoms_out,
        edges_out,
        energy_out,
        grad_atoms,
        grad_edges,
        g_inputs,
        g_rad,
        g_trip_down.T,
        g_trip_bil.T,
        g_trip_up,
        g_quad_down.T,
        g_quad_bil.T,
        g_quad_up,
        g_ae,
        g_res,
        g_ea,
        g_ad,
        g_tags,
    )


def solution(mesh):
    size = dict(mesh.shape)
    inner = Mesh(mesh.devices.reshape(size["gx"], size["gy"] // 2, 2, size["gz"]), ROWS)
    flat, columns, vector, whole = P(ROWS, None), P(None, ROWS), P(ROWS), P()
    placed = [flat, flat, columns] + [vector] * 3 + [flat] * 4 + [vector] + [whole] * 13 + [flat] * 3
    return jax.shard_map(
        per_device,
        mesh=inner,
        in_specs=tuple(placed),
        out_specs=tuple([flat] * 5 + [whole] * 13),
        check_vma=False,
    )
```

```python
import functools
import math

import jax
import jax.numpy as jnp
from jax import lax
from jax.experimental import pallas as pl
from jax.experimental.pallas import tpu as pltpu
from jax.sharding import Mesh
from jax.sharding import PartitionSpec as P

BF = jnp.bfloat16
F32 = jnp.float32
ROWS = ("gx", "gyh", "gyl", "gz")
GY = ("gyh", "gyl")
ATOMS, SEND, SLOTS, EDGES = 8, 4, 30, 240
ATOM_W, EDGE_W, TRIP_W, QUAD_W, RADIAL = 256, 512, 64, 32, 128
ANGLES, PICKS = 16, 8
PAIRS = 17
BLOCK = 16
BLOCKS = EDGES // BLOCK
root_half = 0.7071067811865476
NN = (((1,), (0,)), ((), ()))
NT = (((1,), (1,)), ((), ()))
TN = (((0,), (0,)), ((), ()))


def shifted(value, axis, steps, wrap):
    count = lax.axis_size(axis)
    pairs = [(i, (i + steps) % count) for i in range(count) if wrap or 0 <= i + steps < count]
    return lax.ppermute(value, axis, pairs)


def planes_of(value):
    if lax.axis_size("gz") == 2:
        other = lax.ppermute(value, "gz", [(0, 1), (1, 0)])
        top = lax.axis_index("gz") == 1
        return jnp.stack([jnp.where(top, other, value), jnp.where(top, value, other)])
    return jnp.stack([shifted(value, "gz", 1, False), value, shifted(value, "gz", -1, False)])


def with_halo(value):
    value = planes_of(value)
    value = jnp.concatenate([shifted(value, "gx", 1, True), value, shifted(value, "gx", -1, True)])
    return shifted(value, GY, 1, True), value, shifted(value, GY, -1, True)


def bits_of(axis):
    count = lax.axis_size(axis)
    return [(axis, b) for b in range(count.bit_length() - 1)]


def swap(value, axis, bit):
    count = lax.axis_size(axis)
    return lax.ppermute(value, axis, [(i, i ^ (1 << bit)) for i in range(count)])


def bit_value(axis, bit):
    return (lax.axis_index(axis) >> bit) & 1


def part(arrays, at, size):
    total = lax.dynamic_slice_in_dim(arrays[0], at, size)
    for x in arrays[1:]:
        total = total + lax.dynamic_slice_in_dim(x, at, size)
    return total


class Chain:
    def __init__(self):
        self.last = None

    def after(self, values):
        if self.last is not None:
            self.last, values = lax.optimization_barrier((self.last, values))
        return values

    def step(self, value):
        self.last = value
        return value

    def zero(self):
        first = jax.tree.leaves(self.last)[0]
        corner = first[(slice(0, 1),) * first.ndim].reshape(())
        return jnp.minimum(jnp.abs(corner), 0.0)


def halved(chain, arrays, axis, bit, tight=False):
    arrays = chain.after(arrays)
    half = arrays[0].shape[0] // 2
    one = bit_value(axis, bit)
    send = chain.step(part(arrays, (1 - one) * half, half))
    got = swap(send, axis, bit)
    send, arrays = lax.optimization_barrier((send, arrays))
    keep = part(arrays, one * half, half)
    if tight:
        chain.step((send, keep))
    return [keep, got]


def joined_halves(value, other, axis, bit):
    one = bit_value(axis, bit) == 1
    return jnp.concatenate([jnp.where(one, other, value), jnp.where(one, value, other)])


def reduction(chain, first, second, tight=False, firm=False, firm_total=False):
    across, along = bits_of("gz"), bits_of("gyh")
    lanes = [first, second]
    for turn, plan in enumerate(((across, along), (along, across))):
        for i in range(2):
            for axis, bit in plan[i]:
                lanes[i] = halved(chain, lanes[i], axis, bit, tight and turn == 1)
        yield
    sizes = [x[0].shape[0] for x in lanes]
    joint = [jnp.concatenate(pair) for pair in zip(*chain.after(lanes))]
    for axis, bit in bits_of("gx"):
        joint = halved(chain, joint, axis, bit, tight)
        yield
    joint = chain.after(joint)
    value = sum(joint[1:], joint[0])
    value = chain.step(value + chain.zero() if firm_total else value)
    for axis, bit in bits_of("gx")[::-1]:
        other = swap(value, axis, bit)
        yield
        value, other = chain.after((value, other))
        value = chain.step(joined_halves(value, other, axis, bit))
    values = [value[: sizes[0]], value[sizes[0] :]]
    for plan in ((along, across), (across, along)):
        for turn in range(max(len(across), len(along))):
            others = [None, None]
            for i in range(2):
                if turn < len(plan[i]):
                    others[i] = swap(values[i], *plan[i][::-1][turn])
            yield
            for i in range(2):
                if turn < len(plan[i]):
                    values[i], others[i] = chain.after((values[i], others[i]))
                    whole = joined_halves(values[i], others[i], *plan[i][::-1][turn])
                    if firm and plan[0] is across:
                        whole = whole + chain.zero()
                    values[i] = chain.step(whole)
    others = [swap(x, "gyl", 0) for x in values]
    yield
    values, others = chain.after((values, others))
    return [(value, chain.step(other)) for value, other in zip(values, others)]


def iota(shape, dim):
    return lax.broadcasted_iota(jnp.int32, shape, dim)


def dot(left, right, dims=NN):
    return lax.dot_general(left, right, dims, preferred_element_type=F32)


def halves(x):
    high = x.astype(BF)
    return high, (x - high.astype(F32)).astype(BF)


def stacked(x):
    high, low = halves(x)
    if x.shape[0] % 16 == 0:
        return jnp.concatenate([high, low], axis=0)
    return jnp.concatenate([high.astype(F32), low.astype(F32)], axis=0).astype(BF)


def folded(x):
    half = x.shape[0] // 2
    return x[:half] + x[half:]


def times(x, weight, dims=NN):
    return folded(dot(stacked(x), weight, dims))


def side_by_side(x):
    return jnp.concatenate(halves(x), axis=1)


def side_sum(x):
    half = x.shape[1] // 2
    return x[:, :half] + x[:, half:]


def weight_grad(x, y):
    x_high, x_low = halves(x)
    y_high, y_low = halves(y)
    left, right = [x_high, x_high, x_low], [y_high, y_low, y_high]
    if x.shape[0] % 16 == 0:
        return dot(jnp.concatenate(left, axis=0), jnp.concatenate(right, axis=0), TN)
    left = jnp.concatenate([p.astype(F32) for p in left], axis=0).astype(BF)
    right = jnp.concatenate([p.astype(F32) for p in right], axis=0).astype(BF)
    return dot(left, right, TN)


def onehot(hit):
    return jnp.where(hit, 1.0, 0.0).astype(BF)


def sigmoid(v):
    return 1.0 / (1.0 + jnp.exp(-v))


def act(v):
    return v * sigmoid(v) * (1.0 / 0.6)


def act_and_slope(v):
    s = sigmoid(v)
    return v * s * (1.0 / 0.6), s * (1.0 + v * (1.0 - s)) * (1.0 / 0.6)


def sin_pi(t):
    n = jnp.floor(t + 0.5)
    r = t - n
    odd = n - 2.0 * jnp.floor(n * 0.5)
    q = r * r
    total = jnp.zeros_like(r)
    for k in range(6, -1, -1):
        total = total * q + (-1.0) ** k * math.pi ** (2 * k + 1) / math.factorial(2 * k + 1)
    return total * r * (1.0 - 2.0 * odd)


def to_column(row):
    n = row.shape[1]
    same = iota((n, n), 0) == iota((n, n), 1)
    return jnp.sum(jnp.where(same, row, jnp.zeros_like(row)), axis=1, keepdims=True)


def send_column(send, rows):
    shape = (rows, SEND)
    hit = (iota(shape, 0) & (SEND - 1)) == iota(shape, 1)
    return jnp.sum(jnp.where(hit, send, 0), axis=1, keepdims=True)


def send_lanes(send):
    shape = (8, 128)
    hit = iota(shape, 0) == (iota(shape, 1) & (SEND - 1))
    return jnp.sum(jnp.where(hit, send_column(send, 8), 0), axis=0, keepdims=True)


def paid(row, send):
    edge = send * SLOTS + 2 * (row >> 3) + ((row >> 2) & 1)
    return jnp.where(row < 120, edge, -1)


def atom_of(edge):
    total = jnp.zeros_like(edge)
    for a in range(1, ATOMS):
        total = total + jnp.where(edge >= a * SLOTS, 1, 0)
    return total


def radial_of(length):
    x = length / 12.0
    x2 = x * x
    x4 = x2 * x2
    envelope = 1.0 - 28.0 * (x4 * x2) + 48.0 * (x4 * x2 * x) - 21.0 * (x4 * x4)
    orders = (iota((1, RADIAL), 1) + 1).astype(F32)
    return envelope * sin_pi(x * orders) / x


def geometry(unit):
    own = atom_of(iota((8, EDGES), 1)) == iota((8, EDGES), 0)
    edge = iota((EDGES, 128), 0)
    slot = edge - atom_of(edge) * SLOTS
    total = jnp.zeros((24, 128), F32)
    for k in range(3):
        x = jnp.where(own, unit[k : k + 1, :], 0.0)
        high = x.astype(BF).astype(F32)
        mid = (x - high).astype(BF).astype(F32)
        parts = jnp.concatenate([high, mid, x - high - mid], axis=0).astype(BF)
        total = total + dot(parts, onehot(iota((EDGES, 128), 1) == slot + 32 * k))
    return total[0:8] + total[8:16] + total[16:24]


def local_rows(index):
    return (index & 7) * SLOTS + 2 * (index >> 4) + ((index >> 3) & 1)


def start_kernel(
    edge, vec, mask, hidden, tag_row, send_row, table, w_in, w_rad, w_trip, w_quad,
    payload, local, tagged, pre, downs, rads, radial_out, columns,
):
    vectors = vec[...]
    length = jnp.sqrt(jnp.sum(vectors * vectors, axis=0, keepdims=True))
    unit = vectors / length
    geo = geometry(unit)
    live = to_column(jnp.where(mask[...] > 0, 1.0, 0.0))
    parts = [live] + [to_column(unit[k : k + 1, :]) for k in range(3)]
    columns[...] = jnp.concatenate(parts + [jnp.zeros((EDGES, 124), F32)], axis=1)
    send = send_column(send_row[...], 8)
    pay = paid(iota((128, 1), 0), send_column(send_row[...], 128))
    tags = to_column(tag_row[...])
    radial = radial_of(to_column(length))
    radial_out[...] = radial
    split = stacked(radial)
    for k in range(5):
        rads[k] = folded(dot(split, w_rad[k]))
    split = stacked(edge[...])
    pre[0] = folded(dot(split, w_in[0]))
    pre[1] = folded(dot(split, w_in[1]))
    trip_pre = times(act(pre[0]) * rads[0], w_trip[...], NT)
    quad_pre = times(act(pre[1]) * rads[1], w_quad[...], NT)
    downs[...] = jnp.concatenate([trip_pre, quad_pre, jnp.zeros((EDGES, 32), F32)], axis=1)
    trip = act(trip_pre) * live
    quad = act(quad_pre) * live
    rows = jnp.concatenate([trip, quad * radial[:, 0:1], quad * radial[:, 1:2]], axis=1)
    rows = side_by_side(rows)
    shape = (EDGES, EDGES)
    place = onehot(local_rows(iota(shape, 0)) == iota(shape, 1))
    local[0:15] = side_sum(dot(place, rows)).reshape(15, 16, 128)
    place = onehot(pay == iota((128, EDGES), 1))
    payload[0:16] = side_sum(dot(place, rows)).reshape(16, 8, 128)
    tag = hidden[...]
    for t in range(3):
        tag = tag + jnp.where(tags == t, table[t : t + 1, :].astype(F32), 0.0)
    tagged[...] = tag
    local[15] = jnp.concatenate([tag[:, :128], tag[:, 128:]], axis=0)
    local[16] = jnp.concatenate([geo, jnp.zeros((8, 128), F32)], axis=0)
    both = jnp.concatenate([tag, geo], axis=1)
    sent = jnp.zeros((8, 384), F32)
    for a in range(ATOMS):
        sent = sent + jnp.where(send == a, both[a : a + 1, :], 0.0)
    payload[15] = jnp.where(iota((8, 128), 0) < 4, sent[:, :128], sent[:, 128:256])
    payload[16] = sent[:, 256:]


def split_cores(core, whole, keep, send):
    half = whole.shape[0] // 2
    upper = core[0] == 1
    low, high = whole[:half], whole[half:]
    keep[...] = jnp.where(upper, high, low)
    send[...] = jnp.where(upper, low, high)


def segments(shape, edge_dim, atom_dim):
    edge, atom = iota(shape, edge_dim), iota(shape, atom_dim) & 7
    return onehot((edge >= atom * SLOTS) & (edge < atom * SLOTS + SLOTS))


def lead(k):
    return math.comb(2 * k, k) / 2.0**k


def ratio(k):
    return k * k / (4.0 * k * k - 1.0)


def monic(cosine):
    before, now = jnp.ones_like(cosine), cosine
    yield before
    yield now
    for k in range(1, ANGLES - 1):
        before, now = now, cosine * now - ratio(k) * before
        yield now


def looped(count, step, body):
    def turn(t, carry):
        for i in range(step):
            body(t * step + i)
        return carry

    lax.fori_loop(0, count // step, turn, 0)


def main_kernel(
    halo_before, halo_here, halo_after, local, tagged, edge, columns, rads, radial,
    src_cols, slots, marks,
    trip_bil, trip_up, quad_bil, quad_up, w_ae, w_res, w_ea, w_ad,
    cot_atoms, cot_edges, cot_energy, core,
    atoms_out, edges_out, energy_out, grad_edges, grad_tag,
    cosines, grad_sums, grad_src, keep, send, grad_rads, atom_rows, quad_up_grad,
    table, sums, weight, kept, cos_table, first,
):
    live = columns[:, 0:1]
    halos = (halo_before, halo_here, halo_after)
    group = halo_here.shape[0] * 8
    depth = 3 * group + 16
    lanes = iota((EDGES, depth), 1)
    place = jnp.concatenate(
        [onehot(src_cols[:, 0:1] == lanes), onehot(src_cols[:, 1:2] == lanes)], axis=0
    )

    def rows_at(p):
        parts = [h[:, p].reshape(group, 128) for h in halos]
        return jnp.concatenate(parts + [local[p]], axis=0)

    def gather_pair(p):
        got = dot(place, side_by_side(rows_at(p))).astype(BF)
        table[2 * p] = got[:EDGES]
        table[2 * p + 1] = got[EDGES:]

    looped(16, 4, gather_pair)

    rows = rows_at(16)
    high, low = halves(rows)
    rest = (rows - high.astype(F32) - low.astype(F32)).astype(BF)
    got = dot(place[:EDGES], jnp.concatenate([high, low, rest], axis=1))
    got = got[:, :128] + got[:, 128:256] + got[:, 256:]
    cos_table[...] = -(
        columns[:, 1:2] * got
        + columns[:, 2:3] * pltpu.roll(got, 96, 1)
        + columns[:, 3:4] * pltpu.roll(got, 64, 1)
    )

    for k in range(ANGLES):
        top = trip_bil[:, k * 64 : k * 64 + 64].astype(F32)
        top = jnp.concatenate([top, jnp.zeros((64, 64), F32)], axis=1)
        low_left = quad_bil[:, k * 32 : k * 32 + 32].astype(F32)
        low_right = quad_bil[:, 512 + k * 32 : 544 + k * 32].astype(F32)
        bottom = jnp.concatenate([jnp.zeros((32, 64), F32), low_left, low_right], axis=1)
        piece = jnp.concatenate([top, bottom, jnp.zeros((32, 128), F32)], axis=0)
        weight[:, k * 128 : (k + 1) * 128] = piece.astype(BF)

    trip_lanes = iota((128, 128), 1) < TRIP_W
    scale = 1.0 / math.sqrt(PICKS)

    def basis_block(b):
        at = pl.multiple_of(b * BLOCK, BLOCK)
        own = pl.ds(at, BLOCK)
        wide = iota((BLOCK, 512), 1)
        mark = marks[own, :]
        hits = [jnp.where(mark[:, t : t + 1] == wide, 1.0, 0.0) for t in range(2 * PICKS)]
        hits = jnp.concatenate(hits, axis=0).astype(BF)
        got = side_sum(dot(hits, table[:, own, :].reshape(512, 256)))
        picked = jnp.where(trip_lanes, got[:128], got[128:])
        picked = picked.reshape(PICKS, BLOCK, 128)
        cos_here = cos_table[own, :]
        slot = slots[own, :]
        low_lanes = iota((BLOCK, 128), 1) < TRIP_W
        for h in range(2):
            rows = slice(8 * h, 8 * h + 8)
            cos = []
            for j in range(PICKS):
                index = jnp.where(
                    low_lanes[rows], slot[rows, j : j + 1], slot[rows, PICKS + j : PICKS + j + 1]
                )
                cos.append(jnp.take_along_axis(cos_here[rows], index, axis=1))
            cos = jnp.stack(cos)
            cosines[2 * b + h] = cos
            values = picked[:, rows]
            for k, poly in enumerate(monic(cos)):
                total = jnp.sum(poly * values, axis=0) * (lead(k) * scale)
                sums[pl.ds(pl.multiple_of(at + 8 * h, 8), 8), k * 128 : (k + 1) * 128] = total

    looped(BLOCKS, 3, basis_block)

    down = times(sums[...], weight[...], NT)
    down_act, down_slope = act_and_slope(down)
    trip_h, quad_h = down_act[:, :64], down_act[:, 64:96]
    trip_pre = times(trip_h, trip_up[...])
    quad_pre = times(quad_h, quad_up[...])
    src = jnp.concatenate(
        [side_sum(table[30].astype(F32)), side_sum(table[31].astype(F32))], axis=1
    )
    target = times(tagged[...], w_ae[1])
    spread = segments((EDGES, 16), 0, 1)
    gathers = segments((8, EDGES), 1, 0)

    def to_edges(x):
        return dot(spread, stacked(x))

    def to_atoms(x):
        return side_sum(dot(gathers, side_by_side(x)))

    atom_pre = times(src, w_ae[0]) + to_edges(target)
    atom_act, atom_slope = act_and_slope(atom_pre)
    trip_act, trip_slope = act_and_slope(trip_pre)
    quad_act, quad_slope = act_and_slope(quad_pre)
    merged = (edge[...] + trip_act + quad_act + atom_act * rads[2]) * 0.5
    kept[0] = merged
    first_act, first_slope = act_and_slope(times(merged, w_res[0]))
    kept[1] = first_act
    second_act, second_slope = act_and_slope(times(first_act, w_res[1]))
    new_edges = (merged + second_act) * root_half
    edges_out[...] = new_edges
    weighted = new_edges * live
    root_slots = 1.0 / math.sqrt(SLOTS)
    gathered = to_atoms(weighted * rads[3]) * root_slots
    summary = to_atoms(weighted * rads[4]) * root_slots
    gate_act, gate_slope = act_and_slope(times(gathered, w_ea[0]))
    updated = (tagged[...] + gate_act) * root_half
    a0_act, a0_slope = act_and_slope(times(updated, w_ad[0]))
    a1_act, a1_slope = act_and_slope(times(a0_act, w_ad[1]))
    new_atoms = (updated + a1_act) * root_half
    atoms_out[...] = new_atoms
    e_act, e_slope = act_and_slope(times(summary, w_ea[1]) + times(new_atoms, w_ad[2]))
    out_act, out_slope = act_and_slope(times(e_act, w_ad[3]))
    energy_out[...] = out_act

    d_out = cot_energy[...] * out_slope
    d_e = times(d_out, w_ad[3], NT) * e_slope
    d_summary = times(d_e, w_ea[1], NT)
    d_atoms = (cot_atoms[...] + times(d_e, w_ad[2], NT)) * root_half
    d_a1 = d_atoms * a1_slope
    d_a0 = times(d_a1, w_ad[1], NT) * a0_slope
    d_updated = (d_atoms + times(d_a0, w_ad[0], NT)) * root_half
    d_gate = d_updated * gate_slope
    d_gathered = times(d_gate, w_ea[0], NT)

    d_gathered = to_edges(d_gathered * root_slots)
    d_summary = to_edges(d_summary * root_slots)
    grad_rads[1] = weighted * d_gathered
    grad_rads[2] = weighted * d_summary
    d_new = cot_edges[...] + live * (d_gathered * rads[3] + d_summary * rads[4])
    d_new = d_new * root_half
    d_second = d_new * second_slope
    kept[3] = d_second
    d_first = times(d_second, w_res[1], NT) * first_slope
    kept[2] = d_first
    d_merged = (d_new + times(d_first, w_res[0], NT)) * 0.5
    grad_edges[...] = d_merged
    grad_rads[0] = d_merged * atom_act
    d_atom = d_merged * rads[2] * atom_slope
    kept[4] = d_atom
    d_trip = d_merged * trip_slope
    d_quad = d_merged * quad_slope
    d_target = to_atoms(d_atom)
    grad_tag[...] = d_updated + times(d_target, w_ae[1], NT)
    d_down = jnp.concatenate(
        [times(d_trip, trip_up[...], NT), times(d_quad, quad_up[...], NT), jnp.zeros((EDGES, 32), F32)],
        axis=1,
    )
    d_down = d_down * down_slope
    grad_src[...] = times(d_atom, w_ae[0], NT)

    first[0:512] = weight_grad(kept[0], kept[2])
    first[512:768] = weight_grad(src, kept[4])
    first[896:1408] = weight_grad(kept[1], kept[3])
    first[1408:1664] = weight_grad(tagged[...], d_target)
    bil = weight_grad(d_down, sums[...])
    for m in range(8):
        tile = [bil[0:64, k * 128 : k * 128 + 64] for k in (2 * m, 2 * m + 1)]
        row = 768 + 64 * (m // 4)
        first[row : row + 64, (m % 4) * 128 : (m % 4 + 1) * 128] = jnp.concatenate(tile, axis=1)
    for half in range(2):
        for m in range(4):
            at = 64 + 32 * half
            tile = [bil[64:96, k * 128 + at : k * 128 + at + 32] for k in range(4 * m, 4 * m + 4)]
            row = 1728 + 32 * half
            first[row : row + 32, m * 128 : (m + 1) * 128] = jnp.concatenate(tile, axis=1)
    first[1664:1728] = weight_grad(down_act, d_trip)[:64]
    quad_up_grad[...] = weight_grad(down_act, d_quad)[64:96]
    atom_rows[...] = jnp.concatenate(
        [gathered, summary, updated, a0_act, new_atoms, e_act, d_a0, d_a1, d_e, d_out, d_gate], axis=1
    )
    split_cores(core, first, keep, send)
    grad_sums[...] = times(d_down, weight[...])


def late_kernel(grad_rads, radial, atom_rows, quad_up_grad, core, keep, send, second):
    atoms = atom_rows[...]
    gathered, summary = atoms[:, :512], atoms[:, 512:1024]
    updated, a0_act, new_atoms, e_act, d_a0, d_a1, d_e, d_out, d_gate = [
        atoms[:, at : at + 256] for at in range(1024, 3328, 256)
    ]
    second[0:512, 0:256] = weight_grad(gathered, d_gate)
    second[0:512, 256:512] = weight_grad(summary, d_e)
    second[512:768, 0:256] = weight_grad(updated, d_a0)
    second[512:768, 256:512] = weight_grad(a0_act, d_a1)
    second[768:1024, 0:256] = weight_grad(new_atoms, d_e)
    second[768:1024, 256:512] = weight_grad(e_act, d_out)
    for k in range(3):
        second[1024 + 128 * k : 1152 + 128 * k] = weight_grad(radial[...], grad_rads[k])
    second[1408:1440] = quad_up_grad[...]
    second[1440:1536] = jnp.zeros((96, 512), F32)
    split_cores(core, second, keep, send)


def scatter_kernel(
    cosines, sums, grad_src, src_rows, mark_rows,
    back_before, back_here, back_after, back_local,
    table,
):
    group = back_here.shape[0] * 8
    depth = 3 * group + 16
    trip_lanes = iota((128, 128), 1) < TRIP_W
    scale = 1.0 / math.sqrt(PICKS)

    def basis_back(b):
        at = pl.multiple_of(b * BLOCK, BLOCK)
        own = pl.ds(at, BLOCK)
        parts = []
        for h in range(2):
            cos = cosines[2 * b + h]
            own_rows = pl.ds(pl.multiple_of(at + 8 * h, 8), 8)
            after = total = None
            for k in range(ANGLES - 1, -1, -1):
                term = sums[own_rows, k * 128 : (k + 1) * 128] * (lead(k) * scale)
                if total is None:
                    after, total = None, jnp.broadcast_to(term, cos.shape)
                elif after is None:
                    after, total = total, term + cos * total
                else:
                    after, total = total, term + cos * total - ratio(k + 1) * after
            parts.append(total)
        grad = jnp.concatenate(parts, axis=1).reshape(128, 128)
        grad = jnp.concatenate(
            [jnp.where(trip_lanes, grad, 0.0), jnp.where(trip_lanes, 0.0, grad)], axis=0
        )
        hits = onehot(mark_rows[b] == iota((512, 256), 0))
        got = side_by_side(side_sum(dot(hits, side_by_side(grad))))
        table[:, own, :] = got.reshape(32, BLOCK, 256)

    looped(BLOCKS, 3, basis_back)
    table[30] = side_by_side(grad_src[:, :128])
    table[31] = side_by_side(grad_src[:, 128:])
    rows = iota((depth, EDGES), 0)
    place_even = onehot(src_rows[0:1, :] == rows)
    place_odd = onehot(src_rows[1:2, :] == rows)

    def scatter_pair(p):
        got = side_sum(dot(place_even, table[2 * p]) + dot(place_odd, table[2 * p + 1]))
        for i, back in enumerate((back_before, back_here, back_after)):
            back[:, p] = got[i * group : (i + 1) * group].reshape(group // 8, 8, 128)
        back_local[p] = got[3 * group :]

    looped(16, 4, scatter_pair)


def finish_kernel(
    back_local, returned, grad_late, tag_late, edge, radial, columns, pre, downs, rads, tag_row, send_row,
    w_in, w_trip, w_quad, core,
    grad_atoms, grad_edges, keep_first, send_first, keep_second, send_second,
    first, second,
):
    shape = (EDGES, 256)
    lane = iota(shape, 1)
    place = onehot((local_rows(lane) == iota(shape, 0)) & (lane < EDGES))
    rows = dot(place, side_by_side(back_local[...].reshape(256, 128)))
    pay = paid(iota((1, 128), 1), send_lanes(send_row[...]))
    place = onehot(pay == iota((EDGES, 128), 0))
    send = send_column(send_row[...], 8)
    tags = to_column(tag_row[...])
    rows = side_sum(rows + dot(place, side_by_side(returned[...].reshape(128, 128))))
    back = returned[15]
    tag = tag_late[...] + jnp.concatenate([back_local[15, 0:8], back_local[15, 8:16]], axis=1)
    atom = iota((8, 1), 0)
    for r in range(SEND):
        piece = jnp.concatenate([back[r : r + 1], back[4 + r : 5 + r]], axis=1)
        tag = tag + jnp.where(send[r : r + 1, :] == atom, piece, 0.0)
    grad_atoms[...] = tag
    table = [
        jnp.sum(jnp.where(tags == t, tag, 0.0), axis=0, keepdims=True) for t in range(3)
    ]
    table = jnp.concatenate(table + [jnp.zeros((29, ATOM_W), F32)], axis=0)
    d_trip = rows[:, :64]
    d_quad = rows[:, 64:96] * radial[:, 0:1] + rows[:, 96:128] * radial[:, 1:2]
    total = grad_late[...]
    for k, (d_row, down, weight, out) in enumerate(
        ((d_trip, slice(0, 64), w_trip, first), (d_quad, slice(64, 96), w_quad, second))
    ):
        d_down = d_row * columns[:, 0:1] * act_and_slope(downs[:, down])[1]
        value, slope = act_and_slope(pre[k])
        d_start = times(d_down, weight[...])
        d_pre = d_start * rads[k] * slope
        total = total + times(d_pre, w_in[k], NT)
        out[0:512] = weight_grad(edge[...], d_pre)
        out[512:640] = weight_grad(radial[...], d_start * value)
        down_grad = weight_grad(d_down, value * rads[k])
        if k == 0:
            out[640:704] = down_grad
            out[704:768] = jnp.zeros((64, 512), F32)
        else:
            out[640:672] = down_grad
            out[672:704, 0:256] = table
            out[672:704, 256:512] = jnp.zeros((32, 256), F32)
            out[704:768] = jnp.zeros((64, 512), F32)
    grad_edges[...] = total
    split_cores(core, first, keep_first, send_first)
    split_cores(core, second, keep_second, send_second)


def moved(core, pairs, held, copies, sems):
    arriving = [pltpu.make_async_copy(pair[i % 2], held[i], sems.at[i]) for i, pair in zip(range(len(held)), [p for p in pairs for _ in range(2)])]
    for upper in (0, 1):

        @pl.when(core[0] == upper)
        def _():
            for i in range(len(held)):
                pltpu.make_async_copy(pairs[i // 2][i % 2 ^ upper], held[i], sems.at[i]).start()

    leaving, at = [], len(held)
    for i, copy in enumerate(arriving):
        copy.wait()
        for source, target in copies[i]:
            leaving.append(pltpu.make_async_copy(source, target, sems.at[at]))
            leaving[-1].start()
            at += 1
    for x in leaving:
        x.wait()


def late_outputs(
    a_mine, a_other, b_mine, b_other, core,
    res, ae, trip_bil, trip_up, quad_bil, quad_up, rad, ea, ad,
    a_low, a_high, b_low, b_high, sems,
):
    left, right = slice(0, 256), slice(256, 512)
    copies = [
        [
            (a_low.at[0:512], res.at[0]),
            (a_low.at[512:768], ae.at[0]),
            (a_low.at[768:832], trip_bil.at[:, 0:512]),
            (a_low.at[832:896], trip_bil.at[:, 512:1024]),
        ],
        [
            (a_high.at[0:512], res.at[1]),
            (a_high.at[512:768], ae.at[1]),
            (a_high.at[768:832], trip_up),
            (a_high.at[832:864], quad_bil.at[:, 0:512]),
            (a_high.at[864:896], quad_bil.at[:, 512:1024]),
        ],
        [
            (b_low.at[0:512, left], ea.at[0]),
            (b_low.at[0:512, right], ea.at[1]),
            (b_low.at[512:768, left], ad.at[0]),
            (b_low.at[512:768, right], ad.at[1]),
        ],
        [
            (b_high.at[0:256, left], ad.at[2]),
            (b_high.at[0:256, right], ad.at[3]),
            (b_high.at[640:672], quad_up),
        ]
        + [(b_high.at[256 + 128 * k : 384 + 128 * k], rad.at[k]) for k in range(3)],
    ]
    pairs = [(a_mine, a_other), (b_mine, b_other)]
    moved(core, pairs, (a_low, a_high, b_low, b_high), copies, sems)


def early_outputs(
    c_mine, c_other, d_mine, d_other, late_rad, core,
    inputs, rad, trip_down, quad_down, tags,
    c_low, c_high, d_low, d_high, held_rad, sems,
):
    other_rad = pltpu.make_async_copy(late_rad, held_rad, sems.at[16])
    other_rad.start()
    copies = []
    for k, (low, high) in enumerate(((c_low, c_high), (d_low, d_high))):
        copies.append([(low, inputs.at[k, 0:384])])
        copies.append([(high.at[0:128], inputs.at[k, 384:512]), (high.at[128:256], rad.at[k])])
    copies[1].append((c_high.at[256:320], trip_down))
    copies[3].append((d_high.at[256:288], quad_down))
    pairs = [(c_mine, c_other), (d_mine, d_other)]
    moved(core, pairs, (c_low, c_high, d_low, d_high), copies, sems)
    other_rad.wait()
    last = pltpu.make_async_copy(held_rad, rad.at[2:5], sems.at[17])
    last.start()
    tags[...] = d_high[288:291, 0:256]
    last.wait()


def call(kernel, outs, args, scratch=(), micros=1, inside=None):
    spaces = [pl.ANY if inside is not None and i not in inside else pltpu.VMEM for i in range(len(outs))]
    space = pltpu.VMEM if inside is None else pl.ANY
    flops = int(micros * 1.15e9)
    return pl.pallas_call(
        kernel,
        out_shape=[jax.ShapeDtypeStruct(shape, F32) for shape in outs],
        in_specs=[pl.BlockSpec(memory_space=pltpu.SMEM if x.ndim == 1 else space) for x in args],
        out_specs=[pl.BlockSpec(memory_space=x) for x in spaces],
        scratch_shapes=list(scratch),
        compiler_params=pltpu.CompilerParams(vmem_limit_bytes=56 * 1024 * 1024),
        cost_estimate=pl.CostEstimate(flops=flops, bytes_accessed=1 << 10, transcendentals=0),
    )(*args)


def per_device(
    hidden_atoms,
    edge_states,
    edge_vectors,
    atom_tags,
    send_list,
    sources,
    trip_slots,
    triplet_mask,
    quad_slots,
    quad_mask,
    edge_mask,
    w_inputs,
    w_radial,
    w_trip_down,
    triplet_bilinear_weight,
    w_trip_up,
    w_quad_down,
    w_quad_bil,
    w_quad_up,
    w_atom_edge,
    w_residual,
    w_edge_atom,
    w_atom_dense,
    tag_table,
    cot_atoms,
    cot_edges,
    cot_energy,
):
    planes = 2 if lax.axis_size("gz") == 2 else 3
    group = 3 * planes

    offset = jnp.maximum(sources - ATOMS, 0)
    block, border = offset // SEND, offset % SEND
    step_x, step_y, step_z = block // 9, block // 3 % 3, block % 3
    if planes == 2:
        step_z = jnp.clip(step_z - 1 + lax.axis_index("gz"), 0, 1)
    block = (step_y * 3 + step_x) * planes + step_z
    inside = sources < ATOMS
    even = jnp.where(inside, 3 * group * 8 + sources, block * 8 + border)
    src = jnp.stack([even, even + jnp.where(inside, ATOMS, SEND)])
    slots = jnp.concatenate([trip_slots, quad_slots], axis=1)
    masks = jnp.concatenate([triplet_mask, quad_mask], axis=1)
    marks = jnp.where(masks > 0, slots * BLOCK + (jnp.arange(EDGES) % BLOCK)[:, None], -1)
    mark_rows = marks.reshape(BLOCKS, BLOCK, 2 * PICKS).transpose(0, 2, 1)
    mark_rows = mark_rows.reshape(BLOCKS, 1, 2 * PICKS * BLOCK)
    trip_down_t, quad_down_t = w_trip_down.T, w_quad_down.T

    tag_row, send_row = atom_tags[None, :], send_list[None, :]
    payload, local, tagged, pre, downs, rads, radial, columns = call(
        start_kernel,
        [(PAIRS, 8, 128), (PAIRS, 16, 128), (8, 256), (2, EDGES, 512), (EDGES, 128), (5, EDGES, 512)]
        + [(EDGES, 128)] * 2,
        [edge_states, edge_vectors, edge_mask[None, :], hidden_atoms, tag_row, send_row, tag_table,
         w_inputs, w_radial, trip_down_t, quad_down_t],
        micros=5,
    )
    core = bit_value("gyl", 0)[None]
    before, here, after = with_halo(payload)
    (
        atoms_out, edges_out, energy_out, grad_edges, grad_tag,
        cosines, grad_sums, grad_src, keep_a, send_a, grad_rads, atom_rows, quad_up_grad,
    ) = call(
        main_kernel,
        [(8, 256), (EDGES, 512), (8, 256), (EDGES, 512), (8, 256)]
        + [(2 * BLOCKS, PICKS, 8, 128), (EDGES, 2048), (EDGES, 256), (896, 512), (896, 512)]
        + [(3, EDGES, 512), (8, 3328), (32, 512)],
        [before, here, after, local, tagged, edge_states, columns, rads, radial,
         src.T, slots, marks,
         triplet_bilinear_weight.T, w_trip_up, w_quad_bil.T, w_quad_up, w_atom_edge, w_residual,
         w_edge_atom, w_atom_dense, cot_atoms, cot_edges, cot_energy, core],
        scratch=[
            pltpu.VMEM((32, EDGES, 256), BF),
            pltpu.VMEM((EDGES, 2048), F32),
            pltpu.VMEM((128, 2048), BF),
            pltpu.VMEM((5, EDGES, 512), F32),
            pltpu.VMEM((EDGES, 128), F32),
            pltpu.VMEM((1792, 512), F32),
        ],
        micros=26,
    )
    chain = Chain()
    got_a = swap(send_a, "gyl", 0)
    keep_b, send_b = call(
        late_kernel,
        [(768, 512)] * 2,
        [grad_rads, radial, atom_rows, quad_up_grad, core],
        scratch=[pltpu.VMEM((1536, 512), F32)],
        micros=4,
    )
    late = reduction(chain, [keep_a, got_a], [keep_b, swap(send_b, "gyl", 0)], True, True)
    next(late)
    grad_sums = chain.after(grad_sums)
    back_before, back_here, back_after, back_local = call(
        scatter_kernel,
        [(group, 16, 8, 128)] * 3 + [(16, 16, 128)],
        [cosines, grad_sums, grad_src, src, mark_rows],
        scratch=[pltpu.VMEM((32, EDGES, 256), BF)],
        micros=13,
    )
    got = shifted(back_before, GY, -1, True), shifted(back_after, GY, 1, True)
    chain.step(back_local)
    next(late)
    got, value = chain.after((got, back_here))
    value = chain.step(value + got[0] + got[1])
    first_plane, middle, last_plane = value[:planes], value[planes : 2 * planes], value[2 * planes :]
    got = shifted(first_plane, "gx", -1, True), shifted(last_plane, "gx", 1, True)
    next(late)
    got, middle = chain.after((got, middle))
    value = chain.step(middle + got[0] + got[1])
    if planes == 2:
        top = lax.axis_index("gz") == 1
        mine = jnp.where(top, value[1], value[0])
        theirs = jnp.where(top, value[0], value[1])
        returned = mine + lax.ppermute(theirs, "gz", [(0, 1), (1, 0)])
    else:
        returned = value[1] + shifted(value[0], "gz", -1, False) + shifted(value[2], "gz", 1, False)
    returned = chain.after(returned)
    grad_atoms, grad_edges, keep_c, send_c, keep_d, send_d = call(
        finish_kernel,
        [(8, 256), (EDGES, 512)] + [(384, 512)] * 4,
        [back_local, returned, grad_edges, grad_tag, edge_states, radial, columns, pre, downs, rads,
         tag_row, send_row, w_inputs, trip_down_t, quad_down_t, core],
        scratch=[pltpu.VMEM((768, 512), F32)] * 2,
        micros=7,
    )
    next(late)
    send_c, send_d = chain.after((send_c, send_d))
    got_c, got_d = swap(send_c, "gyl", 0), swap(send_d, "gyl", 0)
    early = reduction(chain, [keep_c, got_c], [keep_d, got_d], firm_total=True)
    running = {"L": late, "E": early}
    done = {}

    def resume(name):
        if name in done:
            return
        try:
            next(running[name])
        except StopIteration as end:
            done[name] = end.value

    for name in "ELEELELEEELEL":
        resume(name)
    while "L" not in done:
        resume("L")
    (a_mine, a_other), (b_mine, b_other) = done["L"]
    g_res, g_ae, g_trip_bil, g_trip_up, g_quad_bil, g_quad_up, g_rad, g_ea, g_ad = call(
        late_outputs,
        [(2, 512, 512), (2, 256, 512), (64, 1024), (64, 512), (32, 1024), (32, 512), (3, 128, 512)]
        + [(2, 512, 256), (4, 256, 256)],
        [a_mine, a_other, b_mine, b_other, core],
        scratch=[pltpu.VMEM((896, 512), F32)] * 2
        + [pltpu.VMEM((768, 512), F32)] * 2
        + [pltpu.SemaphoreType.DMA((23,))],
        micros=0,
        inside=(),
    )
    chain.step(g_quad_up)
    while "E" not in done:
        resume("E")
    (c_mine, c_other), (d_mine, d_other) = done["E"]
    g_inputs, g_rad, g_trip_down, g_quad_down, g_tags = call(
        early_outputs,
        [(2, 512, 512), (5, 128, 512), (64, 512), (32, 512), (3, 256)],
        [c_mine, c_other, d_mine, d_other, g_rad, core],
        scratch=[pltpu.VMEM((384, 512), F32)] * 4
        + [pltpu.VMEM((3, 128, 512), F32), pltpu.SemaphoreType.DMA((18,))],
        micros=3,
        inside=(4,),
    )
    return (
        atoms_out,
        edges_out,
        energy_out,
        grad_atoms,
        grad_edges,
        g_inputs,
        g_rad,
        g_trip_down.T,
        g_trip_bil.T,
        g_trip_up,
        g_quad_down.T,
        g_quad_bil.T,
        g_quad_up,
        g_ae,
        g_res,
        g_ea,
        g_ad,
        g_tags,
    )


def solution(mesh):
    size = dict(mesh.shape)
    inner = Mesh(mesh.devices.reshape(size["gx"], size["gy"] // 2, 2, size["gz"]), ROWS)
    flat, columns, vector, whole = P(ROWS, None), P(None, ROWS), P(ROWS), P()
    placed = [flat, flat, columns] + [vector] * 3 + [flat] * 4 + [vector] + [whole] * 13 + [flat] * 3
    return jax.shard_map(
        per_device,
        mesh=inner,
        in_specs=tuple(placed),
        out_specs=tuple([flat] * 5 + [whole] * 13),
        check_vma=False,
    )
```

```python
import functools
import math

import jax
import jax.numpy as jnp
from jax import lax
from jax.experimental import pallas as pl
from jax.experimental.pallas import tpu as pltpu
from jax.sharding import Mesh
from jax.sharding import PartitionSpec as P

BF = jnp.bfloat16
F32 = jnp.float32
ROWS = ("gx", "gyh", "gyl", "gz")
GY = ("gyh", "gyl")
ATOMS, SEND, SLOTS, EDGES = 8, 4, 30, 240
ATOM_W, EDGE_W, TRIP_W, QUAD_W, RADIAL = 256, 512, 64, 32, 128
ANGLES, PICKS = 16, 8
PAIRS = 17
BLOCK = 16
BLOCKS = EDGES // BLOCK
root_half = 0.7071067811865476
NN = (((1,), (0,)), ((), ()))
NT = (((1,), (1,)), ((), ()))
TN = (((0,), (0,)), ((), ()))


def shifted(value, axis, steps, wrap):
    count = lax.axis_size(axis)
    pairs = [(i, (i + steps) % count) for i in range(count) if wrap or 0 <= i + steps < count]
    return lax.ppermute(value, axis, pairs)


def planes_of(value):
    if lax.axis_size("gz") == 2:
        other = lax.ppermute(value, "gz", [(0, 1), (1, 0)])
        top = lax.axis_index("gz") == 1
        return jnp.stack([jnp.where(top, other, value), jnp.where(top, value, other)])
    return jnp.stack([shifted(value, "gz", 1, False), value, shifted(value, "gz", -1, False)])


def with_halo(value):
    value = planes_of(value)
    value = jnp.concatenate([shifted(value, "gx", 1, True), value, shifted(value, "gx", -1, True)])
    return shifted(value, GY, 1, True), value, shifted(value, GY, -1, True)


def bits_of(axis):
    count = lax.axis_size(axis)
    return [(axis, b) for b in range(count.bit_length() - 1)]


def swap(value, axis, bit):
    count = lax.axis_size(axis)
    return lax.ppermute(value, axis, [(i, i ^ (1 << bit)) for i in range(count)])


def bit_value(axis, bit):
    return (lax.axis_index(axis) >> bit) & 1


def part(arrays, at, size):
    total = lax.dynamic_slice_in_dim(arrays[0], at, size)
    for x in arrays[1:]:
        total = total + lax.dynamic_slice_in_dim(x, at, size)
    return total


class Chain:
    def __init__(self):
        self.last = None

    def after(self, values):
        if self.last is not None:
            self.last, values = lax.optimization_barrier((self.last, values))
        return values

    def step(self, value):
        self.last = value
        return value

    def zero(self):
        first = jax.tree.leaves(self.last)[0]
        corner = first[(slice(0, 1),) * first.ndim].reshape(())
        return jnp.minimum(jnp.abs(corner), 0.0)


def halved(chain, arrays, axis, bit, tight=False):
    arrays = chain.after(arrays)
    half = arrays[0].shape[0] // 2
    one = bit_value(axis, bit)
    send = chain.step(part(arrays, (1 - one) * half, half))
    got = swap(send, axis, bit)
    send, arrays = lax.optimization_barrier((send, arrays))
    keep = part(arrays, one * half, half)
    if tight:
        chain.step((send, keep))
    return [keep, got]


def joined_halves(value, other, axis, bit):
    one = bit_value(axis, bit) == 1
    return jnp.concatenate([jnp.where(one, other, value), jnp.where(one, value, other)])


def reduction(chain, first, second, tight=False, firm=False, firm_total=False):
    across, along = bits_of("gz"), bits_of("gyh")
    lanes = [first, second]
    for turn, plan in enumerate(((across, along), (along, across))):
        for i in range(2):
            for axis, bit in plan[i]:
                lanes[i] = halved(chain, lanes[i], axis, bit, tight and turn == 1)
        yield
    sizes = [x[0].shape[0] for x in lanes]
    joint = [jnp.concatenate(pair) for pair in zip(*chain.after(lanes))]
    for axis, bit in bits_of("gx"):
        joint = halved(chain, joint, axis, bit, tight)
        yield
    joint = chain.after(joint)
    value = sum(joint[1:], joint[0])
    value = chain.step(value + chain.zero() if firm_total else value)
    for axis, bit in bits_of("gx")[::-1]:
        other = swap(value, axis, bit)
        yield
        value, other = chain.after((value, other))
        value = chain.step(joined_halves(value, other, axis, bit))
    values = [value[: sizes[0]], value[sizes[0] :]]
    for plan in ((along, across), (across, along)):
        for turn in range(max(len(across), len(along))):
            others = [None, None]
            for i in range(2):
                if turn < len(plan[i]):
                    others[i] = swap(values[i], *plan[i][::-1][turn])
            yield
            for i in range(2):
                if turn < len(plan[i]):
                    values[i], others[i] = chain.after((values[i], others[i]))
                    whole = joined_halves(values[i], others[i], *plan[i][::-1][turn])
                    if firm and plan[0] is across:
                        whole = whole + chain.zero()
                    values[i] = chain.step(whole)
    others = [swap(x, "gyl", 0) for x in values]
    yield
    values, others = chain.after((values, others))
    return [(value, chain.step(other)) for value, other in zip(values, others)]


def iota(shape, dim):
    return lax.broadcasted_iota(jnp.int32, shape, dim)


def dot(left, right, dims=NN):
    return lax.dot_general(left, right, dims, preferred_element_type=F32)


def halves(x):
    high = x.astype(BF)
    return high, (x - high.astype(F32)).astype(BF)


def stacked(x):
    high, low = halves(x)
    if x.shape[0] % 16 == 0:
        return jnp.concatenate([high, low], axis=0)
    return jnp.concatenate([high.astype(F32), low.astype(F32)], axis=0).astype(BF)


def folded(x):
    half = x.shape[0] // 2
    return x[:half] + x[half:]


def times(x, weight, dims=NN):
    return folded(dot(stacked(x), weight, dims))


def side_by_side(x):
    return jnp.concatenate(halves(x), axis=1)


def side_sum(x):
    half = x.shape[1] // 2
    return x[:, :half] + x[:, half:]


def weight_grad(x, y):
    x_high, x_low = halves(x)
    y_high, y_low = halves(y)
    left, right = [x_high, x_high, x_low], [y_high, y_low, y_high]
    if x.shape[0] % 16 == 0:
        return dot(jnp.concatenate(left, axis=0), jnp.concatenate(right, axis=0), TN)
    left = jnp.concatenate([p.astype(F32) for p in left], axis=0).astype(BF)
    right = jnp.concatenate([p.astype(F32) for p in right], axis=0).astype(BF)
    return dot(left, right, TN)


def onehot(hit):
    return jnp.where(hit, 1.0, 0.0).astype(BF)


def sigmoid(v):
    return 1.0 / (1.0 + jnp.exp(-v))


def act(v):
    return v * sigmoid(v) * (1.0 / 0.6)


def act_and_slope(v):
    s = sigmoid(v)
    return v * s * (1.0 / 0.6), s * (1.0 + v * (1.0 - s)) * (1.0 / 0.6)


def sin_pi(t):
    n = jnp.floor(t + 0.5)
    r = t - n
    odd = n - 2.0 * jnp.floor(n * 0.5)
    q = r * r
    total = jnp.zeros_like(r)
    for k in range(6, -1, -1):
        total = total * q + (-1.0) ** k * math.pi ** (2 * k + 1) / math.factorial(2 * k + 1)
    return total * r * (1.0 - 2.0 * odd)


def to_column(row):
    n = row.shape[1]
    same = iota((n, n), 0) == iota((n, n), 1)
    return jnp.sum(jnp.where(same, row, jnp.zeros_like(row)), axis=1, keepdims=True)


def send_column(send, rows):
    shape = (rows, SEND)
    hit = (iota(shape, 0) & (SEND - 1)) == iota(shape, 1)
    return jnp.sum(jnp.where(hit, send, 0), axis=1, keepdims=True)


def send_lanes(send):
    shape = (8, 128)
    hit = iota(shape, 0) == (iota(shape, 1) & (SEND - 1))
    return jnp.sum(jnp.where(hit, send_column(send, 8), 0), axis=0, keepdims=True)


def paid(row, send):
    edge = send * SLOTS + 2 * (row >> 3) + ((row >> 2) & 1)
    return jnp.where(row < 120, edge, -1)


def atom_of(edge):
    total = jnp.zeros_like(edge)
    for a in range(1, ATOMS):
        total = total + jnp.where(edge >= a * SLOTS, 1, 0)
    return total


def radial_of(length):
    x = length / 12.0
    x2 = x * x
    x4 = x2 * x2
    envelope = 1.0 - 28.0 * (x4 * x2) + 48.0 * (x4 * x2 * x) - 21.0 * (x4 * x4)
    orders = (iota((1, RADIAL), 1) + 1).astype(F32)
    return envelope * sin_pi(x * orders) / x


def geometry(unit):
    own = atom_of(iota((8, EDGES), 1)) == iota((8, EDGES), 0)
    edge = iota((EDGES, 128), 0)
    slot = edge - atom_of(edge) * SLOTS
    total = jnp.zeros((24, 128), F32)
    for k in range(3):
        x = jnp.where(own, unit[k : k + 1, :], 0.0)
        high = x.astype(BF).astype(F32)
        mid = (x - high).astype(BF).astype(F32)
        parts = jnp.concatenate([high, mid, x - high - mid], axis=0).astype(BF)
        total = total + dot(parts, onehot(iota((EDGES, 128), 1) == slot + 32 * k))
    return total[0:8] + total[8:16] + total[16:24]


def local_rows(index):
    return (index & 7) * SLOTS + 2 * (index >> 4) + ((index >> 3) & 1)


def start_kernel(
    edge, vec, mask, hidden, tag_row, send_row, table, w_in, w_rad, w_trip, w_quad,
    payload, local, tagged, pre, downs, rads, radial_out, columns,
):
    vectors = vec[...]
    length = jnp.sqrt(jnp.sum(vectors * vectors, axis=0, keepdims=True))
    unit = vectors / length
    geo = geometry(unit)
    live = to_column(jnp.where(mask[...] > 0, 1.0, 0.0))
    parts = [live] + [to_column(unit[k : k + 1, :]) for k in range(3)]
    columns[...] = jnp.concatenate(parts + [jnp.zeros((EDGES, 124), F32)], axis=1)
    send = send_column(send_row[...], 8)
    pay = paid(iota((128, 1), 0), send_column(send_row[...], 128))
    tags = to_column(tag_row[...])
    radial = radial_of(to_column(length))
    radial_out[...] = radial
    split = stacked(radial)
    for k in range(5):
        rads[k] = folded(dot(split, w_rad[k]))
    split = stacked(edge[...])
    pre[0] = folded(dot(split, w_in[0]))
    pre[1] = folded(dot(split, w_in[1]))
    trip_pre = times(act(pre[0]) * rads[0], w_trip[...], NT)
    quad_pre = times(act(pre[1]) * rads[1], w_quad[...], NT)
    downs[...] = jnp.concatenate([trip_pre, quad_pre, jnp.zeros((EDGES, 32), F32)], axis=1)
    trip = act(trip_pre) * live
    quad = act(quad_pre) * live
    rows = jnp.concatenate([trip, quad * radial[:, 0:1], quad * radial[:, 1:2]], axis=1)
    rows = side_by_side(rows)
    shape = (EDGES, EDGES)
    place = onehot(local_rows(iota(shape, 0)) == iota(shape, 1))
    local[0:15] = side_sum(dot(place, rows)).reshape(15, 16, 128)
    place = onehot(pay == iota((128, EDGES), 1))
    payload[0:16] = side_sum(dot(place, rows)).reshape(16, 8, 128)
    tag = hidden[...]
    for t in range(3):
        tag = tag + jnp.where(tags == t, table[t : t + 1, :].astype(F32), 0.0)
    tagged[...] = tag
    local[15] = jnp.concatenate([tag[:, :128], tag[:, 128:]], axis=0)
    local[16] = jnp.concatenate([geo, jnp.zeros((8, 128), F32)], axis=0)
    both = jnp.concatenate([tag, geo], axis=1)
    sent = jnp.zeros((8, 384), F32)
    for a in range(ATOMS):
        sent = sent + jnp.where(send == a, both[a : a + 1, :], 0.0)
    payload[15] = jnp.where(iota((8, 128), 0) < 4, sent[:, :128], sent[:, 128:256])
    payload[16] = sent[:, 256:]


def split_cores(core, whole, keep, send):
    half = whole.shape[0] // 2
    upper = core[0] == 1
    low, high = whole[:half], whole[half:]
    keep[...] = jnp.where(upper, high, low)
    send[...] = jnp.where(upper, low, high)


def segments(shape, edge_dim, atom_dim):
    edge, atom = iota(shape, edge_dim), iota(shape, atom_dim) & 7
    return onehot((edge >= atom * SLOTS) & (edge < atom * SLOTS + SLOTS))


def lead(k):
    return math.comb(2 * k, k) / 2.0**k


def ratio(k):
    return k * k / (4.0 * k * k - 1.0)


def monic(cosine):
    before, now = jnp.ones_like(cosine), cosine
    yield before
    yield now
    for k in range(1, ANGLES - 1):
        before, now = now, cosine * now - ratio(k) * before
        yield now


def looped(count, step, body):
    def turn(t, carry):
        for i in range(step):
            body(t * step + i)
        return carry

    lax.fori_loop(0, count // step, turn, 0)


def main_kernel(
    halo_before, halo_here, halo_after, local, tagged, edge, columns, rads, radial,
    src_cols, slots, marks,
    trip_bil, trip_up, quad_bil, quad_up, w_ae, w_res, w_ea, w_ad,
    cot_atoms, cot_edges, cot_energy, core,
    atoms_out, edges_out, energy_out, grad_edges, grad_tag,
    cosines, grad_sums, grad_src, keep, send, grad_rads, atom_rows, quad_up_grad,
    table, sums, weight, kept, cos_table, first,
):
    live = columns[:, 0:1]
    halos = (halo_before, halo_here, halo_after)
    group = halo_here.shape[0] * 8
    depth = 3 * group + 16
    lanes = iota((EDGES, depth), 1)
    place = jnp.concatenate(
        [onehot(src_cols[:, 0:1] == lanes), onehot(src_cols[:, 1:2] == lanes)], axis=0
    )

    def rows_at(p):
        parts = [h[:, p].reshape(group, 128) for h in halos]
        return jnp.concatenate(parts + [local[p]], axis=0)

    def gather_pair(p):
        got = dot(place, side_by_side(rows_at(p))).astype(BF)
        table[2 * p] = got[:EDGES]
        table[2 * p + 1] = got[EDGES:]

    looped(16, 4, gather_pair)

    rows = rows_at(16)
    high, low = halves(rows)
    rest = (rows - high.astype(F32) - low.astype(F32)).astype(BF)
    got = dot(place[:EDGES], jnp.concatenate([high, low, rest], axis=1))
    got = got[:, :128] + got[:, 128:256] + got[:, 256:]
    cos_table[...] = -(
        columns[:, 1:2] * got
        + columns[:, 2:3] * pltpu.roll(got, 96, 1)
        + columns[:, 3:4] * pltpu.roll(got, 64, 1)
    )

    for k in range(ANGLES):
        top = trip_bil[:, k * 64 : k * 64 + 64].astype(F32)
        top = jnp.concatenate([top, jnp.zeros((64, 64), F32)], axis=1)
        low_left = quad_bil[:, k * 32 : k * 32 + 32].astype(F32)
        low_right = quad_bil[:, 512 + k * 32 : 544 + k * 32].astype(F32)
        bottom = jnp.concatenate([jnp.zeros((32, 64), F32), low_left, low_right], axis=1)
        piece = jnp.concatenate([top, bottom, jnp.zeros((32, 128), F32)], axis=0)
        weight[:, k * 128 : (k + 1) * 128] = piece.astype(BF)

    trip_lanes = iota((128, 128), 1) < TRIP_W
    scale = 1.0 / math.sqrt(PICKS)

    def basis_block(b):
        at = pl.multiple_of(b * BLOCK, BLOCK)
        own = pl.ds(at, BLOCK)
        wide = iota((BLOCK, 512), 1)
        mark = marks[own, :]
        hits = [jnp.where(mark[:, t : t + 1] == wide, 1.0, 0.0) for t in range(2 * PICKS)]
        hits = jnp.concatenate(hits, axis=0).astype(BF)
        got = side_sum(dot(hits, table[:, own, :].reshape(512, 256)))
        picked = jnp.where(trip_lanes, got[:128], got[128:])
        picked = picked.reshape(PICKS, BLOCK, 128)
        cos_here = cos_table[own, :]
        slot = slots[own, :]
        low_lanes = iota((BLOCK, 128), 1) < TRIP_W
        for h in range(2):
            rows = slice(8 * h, 8 * h + 8)
            cos = []
            for j in range(PICKS):
                index = jnp.where(
                    low_lanes[rows], slot[rows, j : j + 1], slot[rows, PICKS + j : PICKS + j + 1]
                )
                cos.append(jnp.take_along_axis(cos_here[rows], index, axis=1))
            cos = jnp.stack(cos)
            cosines[2 * b + h] = cos
            values = picked[:, rows]
            for k, poly in enumerate(monic(cos)):
                total = jnp.sum(poly * values, axis=0) * (lead(k) * scale)
                sums[pl.ds(pl.multiple_of(at + 8 * h, 8), 8), k * 128 : (k + 1) * 128] = total

    looped(BLOCKS, 3, basis_block)

    down = times(sums[...], weight[...], NT)
    down_act, down_slope = act_and_slope(down)
    trip_h, quad_h = down_act[:, :64], down_act[:, 64:96]
    trip_pre = times(trip_h, trip_up[...])
    quad_pre = times(quad_h, quad_up[...])
    src = jnp.concatenate(
        [side_sum(table[30].astype(F32)), side_sum(table[31].astype(F32))], axis=1
    )
    target = times(tagged[...], w_ae[1])
    spread = segments((EDGES, 16), 0, 1)
    gathers = segments((8, EDGES), 1, 0)

    def to_edges(x):
        return dot(spread, stacked(x))

    def to_atoms(x):
        return side_sum(dot(gathers, side_by_side(x)))

    atom_pre = times(src, w_ae[0]) + to_edges(target)
    atom_act, atom_slope = act_and_slope(atom_pre)
    trip_act, trip_slope = act_and_slope(trip_pre)
    quad_act, quad_slope = act_and_slope(quad_pre)
    merged = (edge[...] + trip_act + quad_act + atom_act * rads[2]) * 0.5
    kept[0] = merged
    first_act, first_slope = act_and_slope(times(merged, w_res[0]))
    kept[1] = first_act
    second_act, second_slope = act_and_slope(times(first_act, w_res[1]))
    new_edges = (merged + second_act) * root_half
    edges_out[...] = new_edges
    weighted = new_edges * live
    root_slots = 1.0 / math.sqrt(SLOTS)
    gathered = to_atoms(weighted * rads[3]) * root_slots
    summary = to_atoms(weighted * rads[4]) * root_slots
    gate_act, gate_slope = act_and_slope(times(gathered, w_ea[0]))
    updated = (tagged[...] + gate_act) * root_half
    a0_act, a0_slope = act_and_slope(times(updated, w_ad[0]))
    a1_act, a1_slope = act_and_slope(times(a0_act, w_ad[1]))
    new_atoms = (updated + a1_act) * root_half
    atoms_out[...] = new_atoms
    e_act, e_slope = act_and_slope(times(summary, w_ea[1]) + times(new_atoms, w_ad[2]))
    out_act, out_slope = act_and_slope(times(e_act, w_ad[3]))
    energy_out[...] = out_act

    d_out = cot_energy[...] * out_slope
    d_e = times(d_out, w_ad[3], NT) * e_slope
    d_summary = times(d_e, w_ea[1], NT)
    d_atoms = (cot_atoms[...] + times(d_e, w_ad[2], NT)) * root_half
    d_a1 = d_atoms * a1_slope
    d_a0 = times(d_a1, w_ad[1], NT) * a0_slope
    d_updated = (d_atoms + times(d_a0, w_ad[0], NT)) * root_half
    d_gate = d_updated * gate_slope
    d_gathered = times(d_gate, w_ea[0], NT)

    d_gathered = to_edges(d_gathered * root_slots)
    d_summary = to_edges(d_summary * root_slots)
    grad_rads[1] = weighted * d_gathered
    grad_rads[2] = weighted * d_summary
    d_new = cot_edges[...] + live * (d_gathered * rads[3] + d_summary * rads[4])
    d_new = d_new * root_half
    d_second = d_new * second_slope
    kept[3] = d_second
    d_first = times(d_second, w_res[1], NT) * first_slope
    kept[2] = d_first
    d_merged = (d_new + times(d_first, w_res[0], NT)) * 0.5
    grad_edges[...] = d_merged
    grad_rads[0] = d_merged * atom_act
    d_atom = d_merged * rads[2] * atom_slope
    kept[4] = d_atom
    d_trip = d_merged * trip_slope
    d_quad = d_merged * quad_slope
    d_target = to_atoms(d_atom)
    grad_tag[...] = d_updated + times(d_target, w_ae[1], NT)
    d_down = jnp.concatenate(
        [times(d_trip, trip_up[...], NT), times(d_quad, quad_up[...], NT), jnp.zeros((EDGES, 32), F32)],
        axis=1,
    )
    d_down = d_down * down_slope
    grad_src[...] = times(d_atom, w_ae[0], NT)

    first[0:512] = weight_grad(kept[0], kept[2])
    first[512:768] = weight_grad(src, kept[4])
    first[896:1408] = weight_grad(kept[1], kept[3])
    first[1408:1664] = weight_grad(tagged[...], d_target)
    bil = weight_grad(d_down, sums[...])
    for m in range(8):
        tile = [bil[0:64, k * 128 : k * 128 + 64] for k in (2 * m, 2 * m + 1)]
        row = 768 + 64 * (m // 4)
        first[row : row + 64, (m % 4) * 128 : (m % 4 + 1) * 128] = jnp.concatenate(tile, axis=1)
    for half in range(2):
        for m in range(4):
            at = 64 + 32 * half
            tile = [bil[64:96, k * 128 + at : k * 128 + at + 32] for k in range(4 * m, 4 * m + 4)]
            row = 1728 + 32 * half
            first[row : row + 32, m * 128 : (m + 1) * 128] = jnp.concatenate(tile, axis=1)
    first[1664:1728] = weight_grad(down_act, d_trip)[:64]
    quad_up_grad[...] = weight_grad(down_act, d_quad)[64:96]
    atom_rows[...] = jnp.concatenate(
        [gathered, summary, updated, a0_act, new_atoms, e_act, d_a0, d_a1, d_e, d_out, d_gate], axis=1
    )
    split_cores(core, first, keep, send)
    grad_sums[...] = times(d_down, weight[...])


def late_kernel(grad_rads, radial, atom_rows, quad_up_grad, core, keep, send, second):
    atoms = atom_rows[...]
    gathered, summary = atoms[:, :512], atoms[:, 512:1024]
    updated, a0_act, new_atoms, e_act, d_a0, d_a1, d_e, d_out, d_gate = [
        atoms[:, at : at + 256] for at in range(1024, 3328, 256)
    ]
    second[0:512, 0:256] = weight_grad(gathered, d_gate)
    second[0:512, 256:512] = weight_grad(summary, d_e)
    second[512:768, 0:256] = weight_grad(updated, d_a0)
    second[512:768, 256:512] = weight_grad(a0_act, d_a1)
    second[768:1024, 0:256] = weight_grad(new_atoms, d_e)
    second[768:1024, 256:512] = weight_grad(e_act, d_out)
    for k in range(3):
        second[1024 + 128 * k : 1152 + 128 * k] = weight_grad(radial[...], grad_rads[k])
    second[1408:1440] = quad_up_grad[...]
    second[1440:1536] = jnp.zeros((96, 512), F32)
    split_cores(core, second, keep, send)


def scatter_kernel(
    cosines, sums, grad_src, src_rows, mark_rows,
    back_before, back_here, back_after, back_local,
    table,
):
    group = back_here.shape[0] * 8
    depth = 3 * group + 16
    trip_lanes = iota((128, 128), 1) < TRIP_W
    scale = 1.0 / math.sqrt(PICKS)

    def basis_back(b):
        at = pl.multiple_of(b * BLOCK, BLOCK)
        own = pl.ds(at, BLOCK)
        parts = []
        for h in range(2):
            cos = cosines[2 * b + h]
            own_rows = pl.ds(pl.multiple_of(at + 8 * h, 8), 8)
            after = total = None
            for k in range(ANGLES - 1, -1, -1):
                term = sums[own_rows, k * 128 : (k + 1) * 128] * (lead(k) * scale)
                if total is None:
                    after, total = None, jnp.broadcast_to(term, cos.shape)
                elif after is None:
                    after, total = total, term + cos * total
                else:
                    after, total = total, term + cos * total - ratio(k + 1) * after
            parts.append(total)
        grad = jnp.concatenate(parts, axis=1).reshape(128, 128)
        grad = jnp.concatenate(
            [jnp.where(trip_lanes, grad, 0.0), jnp.where(trip_lanes, 0.0, grad)], axis=0
        )
        hits = onehot(mark_rows[b] == iota((512, 256), 0))
        got = side_by_side(side_sum(dot(hits, side_by_side(grad))))
        table[:, own, :] = got.reshape(32, BLOCK, 256)

    looped(BLOCKS, 3, basis_back)
    table[30] = side_by_side(grad_src[:, :128])
    table[31] = side_by_side(grad_src[:, 128:])
    rows = iota((depth, EDGES), 0)
    place_even = onehot(src_rows[0:1, :] == rows)
    place_odd = onehot(src_rows[1:2, :] == rows)

    def scatter_pair(p):
        got = side_sum(dot(place_even, table[2 * p]) + dot(place_odd, table[2 * p + 1]))
        for i, back in enumerate((back_before, back_here, back_after)):
            back[:, p] = got[i * group : (i + 1) * group].reshape(group // 8, 8, 128)
        back_local[p] = got[3 * group :]

    looped(16, 4, scatter_pair)


def finish_kernel(
    back_local, returned, grad_late, tag_late, edge, radial, columns, pre, downs, rads, tag_row, send_row,
    w_in, w_trip, w_quad, core,
    grad_atoms, grad_edges, keep_first, send_first, keep_second, send_second,
    first, second,
):
    shape = (EDGES, 256)
    lane = iota(shape, 1)
    place = onehot((local_rows(lane) == iota(shape, 0)) & (lane < EDGES))
    rows = dot(place, side_by_side(back_local[...].reshape(256, 128)))
    pay = paid(iota((1, 128), 1), send_lanes(send_row[...]))
    place = onehot(pay == iota((EDGES, 128), 0))
    send = send_column(send_row[...], 8)
    tags = to_column(tag_row[...])
    rows = side_sum(rows + dot(place, side_by_side(returned[...].reshape(128, 128))))
    back = returned[15]
    tag = tag_late[...] + jnp.concatenate([back_local[15, 0:8], back_local[15, 8:16]], axis=1)
    atom = iota((8, 1), 0)
    for r in range(SEND):
        piece = jnp.concatenate([back[r : r + 1], back[4 + r : 5 + r]], axis=1)
        tag = tag + jnp.where(send[r : r + 1, :] == atom, piece, 0.0)
    grad_atoms[...] = tag
    table = [
        jnp.sum(jnp.where(tags == t, tag, 0.0), axis=0, keepdims=True) for t in range(3)
    ]
    table = jnp.concatenate(table + [jnp.zeros((29, ATOM_W), F32)], axis=0)
    d_trip = rows[:, :64]
    d_quad = rows[:, 64:96] * radial[:, 0:1] + rows[:, 96:128] * radial[:, 1:2]
    total = grad_late[...]
    for k, (d_row, down, weight, out) in enumerate(
        ((d_trip, slice(0, 64), w_trip, first), (d_quad, slice(64, 96), w_quad, second))
    ):
        d_down = d_row * columns[:, 0:1] * act_and_slope(downs[:, down])[1]
        value, slope = act_and_slope(pre[k])
        d_start = times(d_down, weight[...])
        d_pre = d_start * rads[k] * slope
        total = total + times(d_pre, w_in[k], NT)
        out[0:512] = weight_grad(edge[...], d_pre)
        out[512:640] = weight_grad(radial[...], d_start * value)
        down_grad = weight_grad(d_down, value * rads[k])
        if k == 0:
            out[640:704] = down_grad
            out[704:768] = jnp.zeros((64, 512), F32)
        else:
            out[640:672] = down_grad
            out[672:704, 0:256] = table
            out[672:704, 256:512] = jnp.zeros((32, 256), F32)
            out[704:768] = jnp.zeros((64, 512), F32)
    grad_edges[...] = total
    split_cores(core, first, keep_first, send_first)
    split_cores(core, second, keep_second, send_second)


def moved(core, pairs, held, copies, sems):
    arriving = [pltpu.make_async_copy(pair[i % 2], held[i], sems.at[i]) for i, pair in zip(range(len(held)), [p for p in pairs for _ in range(2)])]
    for upper in (0, 1):

        @pl.when(core[0] == upper)
        def _():
            for i in range(len(held)):
                pltpu.make_async_copy(pairs[i // 2][i % 2 ^ upper], held[i], sems.at[i]).start()

    leaving, at = [], len(held)
    for i, copy in enumerate(arriving):
        copy.wait()
        for source, target in copies[i]:
            leaving.append(pltpu.make_async_copy(source, target, sems.at[at]))
            leaving[-1].start()
            at += 1
    for x in leaving:
        x.wait()


def late_outputs(
    a_mine, a_other, b_mine, b_other, core,
    res, ae, trip_bil, trip_up, quad_bil, quad_up, rad, ea, ad,
    a_low, a_high, b_low, b_high, sems,
):
    left, right = slice(0, 256), slice(256, 512)
    copies = [
        [
            (a_low.at[0:512], res.at[0]),
            (a_low.at[512:768], ae.at[0]),
            (a_low.at[768:832], trip_bil.at[:, 0:512]),
            (a_low.at[832:896], trip_bil.at[:, 512:1024]),
        ],
        [
            (a_high.at[0:512], res.at[1]),
            (a_high.at[512:768], ae.at[1]),
            (a_high.at[768:832], trip_up),
            (a_high.at[832:864], quad_bil.at[:, 0:512]),
            (a_high.at[864:896], quad_bil.at[:, 512:1024]),
        ],
        [
            (b_low.at[0:512, left], ea.at[0]),
            (b_low.at[0:512, right], ea.at[1]),
            (b_low.at[512:768, left], ad.at[0]),
            (b_low.at[512:768, right], ad.at[1]),
        ],
        [
            (b_high.at[0:256, left], ad.at[2]),
            (b_high.at[0:256, right], ad.at[3]),
            (b_high.at[640:672], quad_up),
        ]
        + [(b_high.at[256 + 128 * k : 384 + 128 * k], rad.at[k]) for k in range(3)],
    ]
    pairs = [(a_mine, a_other), (b_mine, b_other)]
    moved(core, pairs, (a_low, a_high, b_low, b_high), copies, sems)


def early_outputs(
    c_mine, c_other, d_mine, d_other, late_rad, core,
    inputs, rad, trip_down, quad_down, tags,
    c_low, c_high, d_low, d_high, held_rad, sems,
):
    other_rad = pltpu.make_async_copy(late_rad, held_rad, sems.at[16])
    other_rad.start()
    copies = []
    for k, (low, high) in enumerate(((c_low, c_high), (d_low, d_high))):
        copies.append([(low, inputs.at[k, 0:384])])
        copies.append([(high.at[0:128], inputs.at[k, 384:512]), (high.at[128:256], rad.at[k])])
    copies[1].append((c_high.at[256:320], trip_down))
    copies[3].append((d_high.at[256:288], quad_down))
    pairs = [(c_mine, c_other), (d_mine, d_other)]
    moved(core, pairs, (c_low, c_high, d_low, d_high), copies, sems)
    other_rad.wait()
    last = pltpu.make_async_copy(held_rad, rad.at[2:5], sems.at[17])
    last.start()
    tags[...] = d_high[288:291, 0:256]
    last.wait()


def call(kernel, outs, args, scratch=(), micros=1, inside=None, room=63):
    spaces = [pl.ANY if inside is not None and i not in inside else pltpu.VMEM for i in range(len(outs))]
    space = pltpu.VMEM if inside is None else pl.ANY
    flops = int(micros * 1.15e9)
    return pl.pallas_call(
        kernel,
        out_shape=[jax.ShapeDtypeStruct(shape, F32) for shape in outs],
        in_specs=[pl.BlockSpec(memory_space=pltpu.SMEM if x.ndim == 1 else space) for x in args],
        out_specs=[pl.BlockSpec(memory_space=x) for x in spaces],
        scratch_shapes=list(scratch),
        compiler_params=pltpu.CompilerParams(vmem_limit_bytes=room * 1024 * 1024),
        cost_estimate=pl.CostEstimate(flops=flops, bytes_accessed=1 << 10, transcendentals=0),
    )(*args)


def per_device(
    hidden_atoms,
    edge_states,
    edge_vectors,
    atom_tags,
    send_list,
    sources,
    trip_slots,
    triplet_mask,
    quad_slots,
    quad_mask,
    edge_mask,
    w_inputs,
    w_radial,
    w_trip_down,
    triplet_bilinear_weight,
    w_trip_up,
    w_quad_down,
    w_quad_bil,
    w_quad_up,
    w_atom_edge,
    w_residual,
    w_edge_atom,
    w_atom_dense,
    tag_table,
    cot_atoms,
    cot_edges,
    cot_energy,
):
    planes = 2 if lax.axis_size("gz") == 2 else 3
    group = 3 * planes

    offset = jnp.maximum(sources - ATOMS, 0)
    block, border = offset // SEND, offset % SEND
    step_x, step_y, step_z = block // 9, block // 3 % 3, block % 3
    if planes == 2:
        step_z = jnp.clip(step_z - 1 + lax.axis_index("gz"), 0, 1)
    block = (step_y * 3 + step_x) * planes + step_z
    inside = sources < ATOMS
    even = jnp.where(inside, 3 * group * 8 + sources, block * 8 + border)
    src = jnp.stack([even, even + jnp.where(inside, ATOMS, SEND)])
    slots = jnp.concatenate([trip_slots, quad_slots], axis=1)
    masks = jnp.concatenate([triplet_mask, quad_mask], axis=1)
    marks = jnp.where(masks > 0, slots * BLOCK + (jnp.arange(EDGES) % BLOCK)[:, None], -1)
    mark_rows = marks.reshape(BLOCKS, BLOCK, 2 * PICKS).transpose(0, 2, 1)
    mark_rows = mark_rows.reshape(BLOCKS, 1, 2 * PICKS * BLOCK)
    trip_down_t, quad_down_t = w_trip_down.T, w_quad_down.T

    tag_row, send_row = atom_tags[None, :], send_list[None, :]
    payload, local, tagged, pre, downs, rads, radial, columns = call(
        start_kernel,
        [(PAIRS, 8, 128), (PAIRS, 16, 128), (8, 256), (2, EDGES, 512), (EDGES, 128), (5, EDGES, 512)]
        + [(EDGES, 128)] * 2,
        [edge_states, edge_vectors, edge_mask[None, :], hidden_atoms, tag_row, send_row, tag_table,
         w_inputs, w_radial, trip_down_t, quad_down_t],
        micros=5, room=22,
    )
    core = bit_value("gyl", 0)[None]
    before, here, after = with_halo(payload)
    (
        atoms_out, edges_out, energy_out, grad_edges, grad_tag,
        cosines, grad_sums, grad_src, keep_a, send_a, grad_rads, atom_rows, quad_up_grad,
    ) = call(
        main_kernel,
        [(8, 256), (EDGES, 512), (8, 256), (EDGES, 512), (8, 256)]
        + [(2 * BLOCKS, PICKS, 8, 128), (EDGES, 2048), (EDGES, 256), (896, 512), (896, 512)]
        + [(3, EDGES, 512), (8, 3328), (32, 512)],
        [before, here, after, local, tagged, edge_states, columns, rads, radial,
         src.T, slots, marks,
         triplet_bilinear_weight.T, w_trip_up, w_quad_bil.T, w_quad_up, w_atom_edge, w_residual,
         w_edge_atom, w_atom_dense, cot_atoms, cot_edges, cot_energy, core],
        scratch=[
            pltpu.VMEM((32, EDGES, 256), BF),
            pltpu.VMEM((EDGES, 2048), F32),
            pltpu.VMEM((128, 2048), BF),
            pltpu.VMEM((5, EDGES, 512), F32),
            pltpu.VMEM((EDGES, 128), F32),
            pltpu.VMEM((1792, 512), F32),
        ],
        micros=26, room=44,
    )
    chain = Chain()
    got_a = swap(send_a, "gyl", 0)
    keep_b, send_b = call(
        late_kernel,
        [(768, 512)] * 2,
        [grad_rads, radial, atom_rows, quad_up_grad, core],
        scratch=[pltpu.VMEM((1536, 512), F32)],
        micros=4, room=18,
    )
    late = reduction(chain, [keep_a, got_a], [keep_b, swap(send_b, "gyl", 0)], True, True)
    next(late)
    grad_sums = chain.after(grad_sums)
    back_before, back_here, back_after, back_local = call(
        scatter_kernel,
        [(group, 16, 8, 128)] * 3 + [(16, 16, 128)],
        [cosines, grad_sums, grad_src, src, mark_rows],
        scratch=[pltpu.VMEM((32, EDGES, 256), BF)],
        micros=13, room=18,
    )
    got = shifted(back_before, GY, -1, True), shifted(back_after, GY, 1, True)
    chain.step(back_local)
    next(late)
    got, value = chain.after((got, back_here))
    value = chain.step(value + got[0] + got[1])
    first_plane, middle, last_plane = value[:planes], value[planes : 2 * planes], value[2 * planes :]
    got = shifted(first_plane, "gx", -1, True), shifted(last_plane, "gx", 1, True)
    next(late)
    got, middle = chain.after((got, middle))
    value = chain.step(middle + got[0] + got[1])
    if planes == 2:
        top = lax.axis_index("gz") == 1
        mine = jnp.where(top, value[1], value[0])
        theirs = jnp.where(top, value[0], value[1])
        returned = mine + lax.ppermute(theirs, "gz", [(0, 1), (1, 0)])
    else:
        returned = value[1] + shifted(value[0], "gz", -1, False) + shifted(value[2], "gz", 1, False)
    returned = chain.after(returned)
    grad_atoms, grad_edges, keep_c, send_c, keep_d, send_d = call(
        finish_kernel,
        [(8, 256), (EDGES, 512)] + [(384, 512)] * 4,
        [back_local, returned, grad_edges, grad_tag, edge_states, radial, columns, pre, downs, rads,
         tag_row, send_row, w_inputs, trip_down_t, quad_down_t, core],
        scratch=[pltpu.VMEM((768, 512), F32)] * 2,
        micros=7, room=28,
    )
    next(late)
    send_c, send_d = chain.after((send_c, send_d))
    got_c, got_d = swap(send_c, "gyl", 0), swap(send_d, "gyl", 0)
    early = reduction(chain, [keep_c, got_c], [keep_d, got_d], firm_total=True)
    running = {"L": late, "E": early}
    done = {}

    def resume(name):
        if name in done:
            return
        try:
            next(running[name])
        except StopIteration as end:
            done[name] = end.value

    for name in "ELEELELEEELEL":
        resume(name)
    while "L" not in done:
        resume("L")
    (a_mine, a_other), (b_mine, b_other) = done["L"]
    g_res, g_ae, g_trip_bil, g_trip_up, g_quad_bil, g_quad_up, g_rad, g_ea, g_ad = call(
        late_outputs,
        [(2, 512, 512), (2, 256, 512), (64, 1024), (64, 512), (32, 1024), (32, 512), (3, 128, 512)]
        + [(2, 512, 256), (4, 256, 256)],
        [a_mine, a_other, b_mine, b_other, core],
        scratch=[pltpu.VMEM((896, 512), F32)] * 2
        + [pltpu.VMEM((768, 512), F32)] * 2
        + [pltpu.SemaphoreType.DMA((23,))],
        micros=0,
        room=12,
        inside=(),
    )
    chain.step(g_quad_up)
    while "E" not in done:
        resume("E")
    (c_mine, c_other), (d_mine, d_other) = done["E"]
    g_inputs, g_rad, g_trip_down, g_quad_down, g_tags = call(
        early_outputs,
        [(2, 512, 512), (5, 128, 512), (64, 512), (32, 512), (3, 256)],
        [c_mine, c_other, d_mine, d_other, g_rad, core],
        scratch=[pltpu.VMEM((384, 512), F32)] * 4
        + [pltpu.VMEM((3, 128, 512), F32), pltpu.SemaphoreType.DMA((18,))],
        micros=3,
        room=8,
        inside=(4,),
    )
    return (
        atoms_out,
        edges_out,
        energy_out,
        grad_atoms,
        grad_edges,
        g_inputs,
        g_rad,
        g_trip_down.T,
        g_trip_bil.T,
        g_trip_up,
        g_quad_down.T,
        g_quad_bil.T,
        g_quad_up,
        g_ae,
        g_res,
        g_ea,
        g_ad,
        g_tags,
    )


def solution(mesh):
    size = dict(mesh.shape)
    inner = Mesh(mesh.devices.reshape(size["gx"], size["gy"] // 2, 2, size["gz"]), ROWS)
    flat, columns, vector, whole = P(ROWS, None), P(None, ROWS), P(ROWS), P()
    placed = [flat, flat, columns] + [vector] * 3 + [flat] * 4 + [vector] + [whole] * 13 + [flat] * 3
    return jax.shard_map(
        per_device,
        mesh=inner,
        in_specs=tuple(placed),
        out_specs=tuple([flat] * 5 + [whole] * 13),
        check_vma=False,
    )
```

```python
import functools
import math

import jax
import jax.numpy as jnp
from jax import lax
from jax.experimental import pallas as pl
from jax.experimental.pallas import tpu as pltpu
from jax.sharding import Mesh
from jax.sharding import PartitionSpec as P

BF = jnp.bfloat16
F32 = jnp.float32
ROWS = ("gx", "gyh", "gyl", "gz")
GY = ("gyh", "gyl")
ATOMS, SEND, SLOTS, EDGES = 8, 4, 30, 240
ATOM_W, EDGE_W, TRIP_W, QUAD_W, RADIAL = 256, 512, 64, 32, 128
ANGLES, PICKS = 16, 8
PAIRS = 17
BLOCK = 16
BLOCKS = EDGES // BLOCK
root_half = 0.7071067811865476
NN = (((1,), (0,)), ((), ()))
NT = (((1,), (1,)), ((), ()))
TN = (((0,), (0,)), ((), ()))


def shifted(value, axis, steps, wrap):
    count = lax.axis_size(axis)
    pairs = [(i, (i + steps) % count) for i in range(count) if wrap or 0 <= i + steps < count]
    return lax.ppermute(value, axis, pairs)


def planes_of(value):
    if lax.axis_size("gz") == 2:
        other = lax.ppermute(value, "gz", [(0, 1), (1, 0)])
        top = lax.axis_index("gz") == 1
        return jnp.stack([jnp.where(top, other, value), jnp.where(top, value, other)])
    return jnp.stack([shifted(value, "gz", 1, False), value, shifted(value, "gz", -1, False)])


def with_halo(value):
    value = planes_of(value)
    value = jnp.concatenate([shifted(value, "gx", 1, True), value, shifted(value, "gx", -1, True)])
    return shifted(value, GY, 1, True), value, shifted(value, GY, -1, True)


def bits_of(axis):
    count = lax.axis_size(axis)
    return [(axis, b) for b in range(count.bit_length() - 1)]


def swap(value, axis, bit):
    count = lax.axis_size(axis)
    return lax.ppermute(value, axis, [(i, i ^ (1 << bit)) for i in range(count)])


def bit_value(axis, bit):
    return (lax.axis_index(axis) >> bit) & 1


def part(arrays, at, size):
    total = lax.dynamic_slice_in_dim(arrays[0], at, size)
    for x in arrays[1:]:
        total = total + lax.dynamic_slice_in_dim(x, at, size)
    return total


class Chain:
    def __init__(self):
        self.last = None

    def after(self, values):
        if self.last is not None:
            self.last, values = lax.optimization_barrier((self.last, values))
        return values

    def step(self, value):
        self.last = value
        return value

    def zero(self):
        first = jax.tree.leaves(self.last)[0]
        corner = first[(slice(0, 1),) * first.ndim].reshape(())
        return jnp.minimum(jnp.abs(corner), 0.0)


def halved(chain, arrays, axis, bit, tight=False):
    arrays = chain.after(arrays)
    half = arrays[0].shape[0] // 2
    one = bit_value(axis, bit)
    send = chain.step(part(arrays, (1 - one) * half, half))
    got = swap(send, axis, bit)
    send, arrays = lax.optimization_barrier((send, arrays))
    keep = part(arrays, one * half, half)
    if tight:
        chain.step((send, keep))
    return [keep, got]


def joined_halves(value, other, axis, bit):
    one = bit_value(axis, bit) == 1
    return jnp.concatenate([jnp.where(one, other, value), jnp.where(one, value, other)])


def reduction(chain, first, second, tight=False, firm=False, firm_total=False):
    across, along = bits_of("gz"), bits_of("gyh")
    lanes = [first, second]
    for turn, plan in enumerate(((across, along), (along, across))):
        for i in range(2):
            for axis, bit in plan[i]:
                lanes[i] = halved(chain, lanes[i], axis, bit, tight and turn == 1)
        yield
    sizes = [x[0].shape[0] for x in lanes]
    joint = [jnp.concatenate(pair) for pair in zip(*chain.after(lanes))]
    for axis, bit in bits_of("gx"):
        joint = halved(chain, joint, axis, bit, tight)
        yield
    joint = chain.after(joint)
    value = sum(joint[1:], joint[0])
    value = chain.step(value + chain.zero() if firm_total else value)
    for axis, bit in bits_of("gx")[::-1]:
        other = swap(value, axis, bit)
        yield
        value, other = chain.after((value, other))
        value = chain.step(joined_halves(value, other, axis, bit))
    values = [value[: sizes[0]], value[sizes[0] :]]
    for plan in ((along, across), (across, along)):
        for turn in range(max(len(across), len(along))):
            others = [None, None]
            for i in range(2):
                if turn < len(plan[i]):
                    others[i] = swap(values[i], *plan[i][::-1][turn])
            yield
            for i in range(2):
                if turn < len(plan[i]):
                    values[i], others[i] = chain.after((values[i], others[i]))
                    whole = joined_halves(values[i], others[i], *plan[i][::-1][turn])
                    if firm and plan[0] is across:
                        whole = whole + chain.zero()
                    values[i] = chain.step(whole)
    others = [swap(x, "gyl", 0) for x in values]
    yield
    values, others = chain.after((values, others))
    return [(value, chain.step(other)) for value, other in zip(values, others)]


def iota(shape, dim):
    return lax.broadcasted_iota(jnp.int32, shape, dim)


def dot(left, right, dims=NN):
    return lax.dot_general(left, right, dims, preferred_element_type=F32)


def halves(x):
    high = x.astype(BF)
    return high, (x - high.astype(F32)).astype(BF)


def stacked(x):
    high, low = halves(x)
    if x.shape[0] % 16 == 0:
        return jnp.concatenate([high, low], axis=0)
    return jnp.concatenate([high.astype(F32), low.astype(F32)], axis=0).astype(BF)


def folded(x):
    half = x.shape[0] // 2
    return x[:half] + x[half:]


def times(x, weight, dims=NN):
    return folded(dot(stacked(x), weight, dims))


def side_by_side(x):
    return jnp.concatenate(halves(x), axis=1)


def side_sum(x):
    half = x.shape[1] // 2
    return x[:, :half] + x[:, half:]


def weight_grad(x, y):
    x_high, x_low = halves(x)
    y_high, y_low = halves(y)
    left, right = [x_high, x_high, x_low], [y_high, y_low, y_high]
    if x.shape[0] % 16 == 0:
        return dot(jnp.concatenate(left, axis=0), jnp.concatenate(right, axis=0), TN)
    left = jnp.concatenate([p.astype(F32) for p in left], axis=0).astype(BF)
    right = jnp.concatenate([p.astype(F32) for p in right], axis=0).astype(BF)
    return dot(left, right, TN)


def onehot(hit):
    return jnp.where(hit, 1.0, 0.0).astype(BF)


def sigmoid(v):
    return 1.0 / (1.0 + jnp.exp(-v))


def act(v):
    return v * sigmoid(v) * (1.0 / 0.6)


def act_and_slope(v):
    s = sigmoid(v)
    return v * s * (1.0 / 0.6), s * (1.0 + v * (1.0 - s)) * (1.0 / 0.6)


def sin_pi(t):
    n = jnp.floor(t + 0.5)
    r = t - n
    odd = n - 2.0 * jnp.floor(n * 0.5)
    q = r * r
    total = jnp.zeros_like(r)
    for k in range(6, -1, -1):
        total = total * q + (-1.0) ** k * math.pi ** (2 * k + 1) / math.factorial(2 * k + 1)
    return total * r * (1.0 - 2.0 * odd)


def to_column(row):
    n = row.shape[1]
    same = iota((n, n), 0) == iota((n, n), 1)
    return jnp.sum(jnp.where(same, row, jnp.zeros_like(row)), axis=1, keepdims=True)


def send_column(send, rows):
    shape = (rows, SEND)
    hit = (iota(shape, 0) & (SEND - 1)) == iota(shape, 1)
    return jnp.sum(jnp.where(hit, send, 0), axis=1, keepdims=True)


def send_lanes(send):
    shape = (8, 128)
    hit = iota(shape, 0) == (iota(shape, 1) & (SEND - 1))
    return jnp.sum(jnp.where(hit, send_column(send, 8), 0), axis=0, keepdims=True)


def paid(row, send):
    edge = send * SLOTS + 2 * (row >> 3) + ((row >> 2) & 1)
    return jnp.where(row < 120, edge, -1)


def atom_of(edge):
    total = jnp.zeros_like(edge)
    for a in range(1, ATOMS):
        total = total + jnp.where(edge >= a * SLOTS, 1, 0)
    return total


def radial_of(length):
    x = length / 12.0
    x2 = x * x
    x4 = x2 * x2
    envelope = 1.0 - 28.0 * (x4 * x2) + 48.0 * (x4 * x2 * x) - 21.0 * (x4 * x4)
    orders = (iota((1, RADIAL), 1) + 1).astype(F32)
    return envelope * sin_pi(x * orders) / x


def geometry(unit):
    own = atom_of(iota((8, EDGES), 1)) == iota((8, EDGES), 0)
    edge = iota((EDGES, 128), 0)
    slot = edge - atom_of(edge) * SLOTS
    total = jnp.zeros((24, 128), F32)
    for k in range(3):
        x = jnp.where(own, unit[k : k + 1, :], 0.0)
        high = x.astype(BF).astype(F32)
        mid = (x - high).astype(BF).astype(F32)
        parts = jnp.concatenate([high, mid, x - high - mid], axis=0).astype(BF)
        total = total + dot(parts, onehot(iota((EDGES, 128), 1) == slot + 32 * k))
    return total[0:8] + total[8:16] + total[16:24]


def local_rows(index):
    return (index & 7) * SLOTS + 2 * (index >> 4) + ((index >> 3) & 1)


def start_kernel(
    edge, vec, mask, hidden, tag_row, send_row, table, w_in, w_rad, w_trip, w_quad,
    payload, local, tagged, pre, downs, rads, radial_out, columns,
):
    vectors = vec[...]
    length = jnp.sqrt(jnp.sum(vectors * vectors, axis=0, keepdims=True))
    unit = vectors / length
    geo = geometry(unit)
    live = to_column(jnp.where(mask[...] > 0, 1.0, 0.0))
    parts = [live] + [to_column(unit[k : k + 1, :]) for k in range(3)]
    columns[...] = jnp.concatenate(parts + [jnp.zeros((EDGES, 124), F32)], axis=1)
    send = send_column(send_row[...], 8)
    pay = paid(iota((128, 1), 0), send_column(send_row[...], 128))
    tags = to_column(tag_row[...])
    radial = radial_of(to_column(length))
    radial_out[...] = radial
    split = stacked(radial)
    for k in range(5):
        rads[k] = folded(dot(split, w_rad[k]))
    split = stacked(edge[...])
    pre[0] = folded(dot(split, w_in[0]))
    pre[1] = folded(dot(split, w_in[1]))
    trip_pre = times(act(pre[0]) * rads[0], w_trip[...], NT)
    quad_pre = times(act(pre[1]) * rads[1], w_quad[...], NT)
    downs[...] = jnp.concatenate([trip_pre, quad_pre, jnp.zeros((EDGES, 32), F32)], axis=1)
    trip = act(trip_pre) * live
    quad = act(quad_pre) * live
    rows = jnp.concatenate([trip, quad * radial[:, 0:1], quad * radial[:, 1:2]], axis=1)
    rows = side_by_side(rows)
    shape = (EDGES, EDGES)
    place = onehot(local_rows(iota(shape, 0)) == iota(shape, 1))
    local[0:15] = side_sum(dot(place, rows)).reshape(15, 16, 128)
    place = onehot(pay == iota((128, EDGES), 1))
    payload[0:16] = side_sum(dot(place, rows)).reshape(16, 8, 128)
    tag = hidden[...]
    for t in range(3):
        tag = tag + jnp.where(tags == t, table[t : t + 1, :].astype(F32), 0.0)
    tagged[...] = tag
    local[15] = jnp.concatenate([tag[:, :128], tag[:, 128:]], axis=0)
    local[16] = jnp.concatenate([geo, jnp.zeros((8, 128), F32)], axis=0)
    both = jnp.concatenate([tag, geo], axis=1)
    sent = jnp.zeros((8, 384), F32)
    for a in range(ATOMS):
        sent = sent + jnp.where(send == a, both[a : a + 1, :], 0.0)
    payload[15] = jnp.where(iota((8, 128), 0) < 4, sent[:, :128], sent[:, 128:256])
    payload[16] = sent[:, 256:]


def split_cores(core, whole, keep, send):
    half = whole.shape[0] // 2
    upper = core[0] == 1
    low, high = whole[:half], whole[half:]
    keep[...] = jnp.where(upper, high, low)
    send[...] = jnp.where(upper, low, high)


def segments(shape, edge_dim, atom_dim):
    edge, atom = iota(shape, edge_dim), iota(shape, atom_dim) & 7
    return onehot((edge >= atom * SLOTS) & (edge < atom * SLOTS + SLOTS))


def lead(k):
    return math.comb(2 * k, k) / 2.0**k


def ratio(k):
    return k * k / (4.0 * k * k - 1.0)


def monic(cosine):
    before, now = jnp.ones_like(cosine), cosine
    yield before
    yield now
    for k in range(1, ANGLES - 1):
        before, now = now, cosine * now - ratio(k) * before
        yield now


def looped(count, step, body):
    def turn(t, carry):
        for i in range(step):
            body(t * step + i)
        return carry

    lax.fori_loop(0, count // step, turn, 0)


def main_kernel(
    halo_before, halo_here, halo_after, local, tagged, edge, columns, rads, radial,
    src_cols, slots, marks,
    trip_bil, trip_up, quad_bil, quad_up, w_ae, w_res, w_ea, w_ad,
    cot_atoms, cot_edges, cot_energy, core,
    atoms_out, edges_out, energy_out, grad_edges, grad_tag,
    cosines, grad_sums, grad_src, keep, send, grad_rads, atom_rows, quad_up_grad,
    table, sums, weight, kept, cos_table, first,
):
    live = columns[:, 0:1]
    halos = (halo_before, halo_here, halo_after)
    group = halo_here.shape[0] * 8
    depth = 3 * group + 16
    lanes = iota((EDGES, depth), 1)
    place = jnp.concatenate(
        [onehot(src_cols[:, 0:1] == lanes), onehot(src_cols[:, 1:2] == lanes)], axis=0
    )

    def rows_at(p):
        parts = [h[:, p].reshape(group, 128) for h in halos]
        return jnp.concatenate(parts + [local[p]], axis=0)

    def gather_pair(p):
        got = dot(place, side_by_side(rows_at(p))).astype(BF)
        table[2 * p] = got[:EDGES]
        table[2 * p + 1] = got[EDGES:]

    looped(16, 4, gather_pair)

    rows = rows_at(16)
    high, low = halves(rows)
    rest = (rows - high.astype(F32) - low.astype(F32)).astype(BF)
    got = dot(place[:EDGES], jnp.concatenate([high, low, rest], axis=1))
    got = got[:, :128] + got[:, 128:256] + got[:, 256:]
    cos_table[...] = -(
        columns[:, 1:2] * got
        + columns[:, 2:3] * pltpu.roll(got, 96, 1)
        + columns[:, 3:4] * pltpu.roll(got, 64, 1)
    )

    for k in range(ANGLES):
        top = trip_bil[:, k * 64 : k * 64 + 64].astype(F32)
        top = jnp.concatenate([top, jnp.zeros((64, 64), F32)], axis=1)
        low_left = quad_bil[:, k * 32 : k * 32 + 32].astype(F32)
        low_right = quad_bil[:, 512 + k * 32 : 544 + k * 32].astype(F32)
        bottom = jnp.concatenate([jnp.zeros((32, 64), F32), low_left, low_right], axis=1)
        piece = jnp.concatenate([top, bottom, jnp.zeros((32, 128), F32)], axis=0)
        weight[:, k * 128 : (k + 1) * 128] = piece.astype(BF)

    trip_lanes = iota((128, 128), 1) < TRIP_W
    scale = 1.0 / math.sqrt(PICKS)

    def basis_block(b):
        at = pl.multiple_of(b * BLOCK, BLOCK)
        own = pl.ds(at, BLOCK)
        wide = iota((BLOCK, 512), 1)
        mark = marks[own, :]
        hits = [jnp.where(mark[:, t : t + 1] == wide, 1.0, 0.0) for t in range(2 * PICKS)]
        hits = jnp.concatenate(hits, axis=0).astype(BF)
        got = side_sum(dot(hits, table[:, own, :].reshape(512, 256)))
        picked = jnp.where(trip_lanes, got[:128], got[128:])
        picked = picked.reshape(PICKS, BLOCK, 128)
        cos_here = cos_table[own, :]
        slot = slots[own, :]
        low_lanes = iota((BLOCK, 128), 1) < TRIP_W
        for h in range(2):
            rows = slice(8 * h, 8 * h + 8)
            cos = []
            for j in range(PICKS):
                index = jnp.where(
                    low_lanes[rows], slot[rows, j : j + 1], slot[rows, PICKS + j : PICKS + j + 1]
                )
                cos.append(jnp.take_along_axis(cos_here[rows], index, axis=1))
            cos = jnp.stack(cos)
            cosines[2 * b + h] = cos
            values = picked[:, rows]
            for k, poly in enumerate(monic(cos)):
                total = jnp.sum(poly * values, axis=0) * (lead(k) * scale)
                sums[pl.ds(pl.multiple_of(at + 8 * h, 8), 8), k * 128 : (k + 1) * 128] = total

    looped(BLOCKS, 3, basis_block)

    down = times(sums[...], weight[...], NT)
    down_act, down_slope = act_and_slope(down)
    trip_h, quad_h = down_act[:, :64], down_act[:, 64:96]
    trip_pre = times(trip_h, trip_up[...])
    quad_pre = times(quad_h, quad_up[...])
    src = jnp.concatenate(
        [side_sum(table[30].astype(F32)), side_sum(table[31].astype(F32))], axis=1
    )
    target = times(tagged[...], w_ae[1])
    spread = segments((EDGES, 16), 0, 1)
    gathers = segments((8, EDGES), 1, 0)

    def to_edges(x):
        return dot(spread, stacked(x))

    def to_atoms(x):
        return side_sum(dot(gathers, side_by_side(x)))

    atom_pre = times(src, w_ae[0]) + to_edges(target)
    atom_act, atom_slope = act_and_slope(atom_pre)
    trip_act, trip_slope = act_and_slope(trip_pre)
    quad_act, quad_slope = act_and_slope(quad_pre)
    merged = (edge[...] + trip_act + quad_act + atom_act * rads[2]) * 0.5
    kept[0] = merged
    first_act, first_slope = act_and_slope(times(merged, w_res[0]))
    kept[1] = first_act
    second_act, second_slope = act_and_slope(times(first_act, w_res[1]))
    new_edges = (merged + second_act) * root_half
    edges_out[...] = new_edges
    weighted = new_edges * live
    root_slots = 1.0 / math.sqrt(SLOTS)
    gathered = to_atoms(weighted * rads[3]) * root_slots
    summary = to_atoms(weighted * rads[4]) * root_slots
    gate_act, gate_slope = act_and_slope(times(gathered, w_ea[0]))
    updated = (tagged[...] + gate_act) * root_half
    a0_act, a0_slope = act_and_slope(times(updated, w_ad[0]))
    a1_act, a1_slope = act_and_slope(times(a0_act, w_ad[1]))
    new_atoms = (updated + a1_act) * root_half
    atoms_out[...] = new_atoms
    e_act, e_slope = act_and_slope(times(summary, w_ea[1]) + times(new_atoms, w_ad[2]))
    out_act, out_slope = act_and_slope(times(e_act, w_ad[3]))
    energy_out[...] = out_act

    d_out = cot_energy[...] * out_slope
    d_e = times(d_out, w_ad[3], NT) * e_slope
    d_summary = times(d_e, w_ea[1], NT)
    d_atoms = (cot_atoms[...] + times(d_e, w_ad[2], NT)) * root_half
    d_a1 = d_atoms * a1_slope
    d_a0 = times(d_a1, w_ad[1], NT) * a0_slope
    d_updated = (d_atoms + times(d_a0, w_ad[0], NT)) * root_half
    d_gate = d_updated * gate_slope
    d_gathered = times(d_gate, w_ea[0], NT)

    d_gathered = to_edges(d_gathered * root_slots)
    d_summary = to_edges(d_summary * root_slots)
    grad_rads[1] = weighted * d_gathered
    grad_rads[2] = weighted * d_summary
    d_new = cot_edges[...] + live * (d_gathered * rads[3] + d_summary * rads[4])
    d_new = d_new * root_half
    d_second = d_new * second_slope
    kept[3] = d_second
    d_first = times(d_second, w_res[1], NT) * first_slope
    kept[2] = d_first
    d_merged = (d_new + times(d_first, w_res[0], NT)) * 0.5
    grad_edges[...] = d_merged
    grad_rads[0] = d_merged * atom_act
    d_atom = d_merged * rads[2] * atom_slope
    kept[4] = d_atom
    d_trip = d_merged * trip_slope
    d_quad = d_merged * quad_slope
    d_target = to_atoms(d_atom)
    grad_tag[...] = d_updated + times(d_target, w_ae[1], NT)
    d_down = jnp.concatenate(
        [times(d_trip, trip_up[...], NT), times(d_quad, quad_up[...], NT), jnp.zeros((EDGES, 32), F32)],
        axis=1,
    )
    d_down = d_down * down_slope
    grad_src[...] = times(d_atom, w_ae[0], NT)

    first[0:512] = weight_grad(kept[0], kept[2])
    first[512:768] = weight_grad(src, kept[4])
    first[896:1408] = weight_grad(kept[1], kept[3])
    first[1408:1664] = weight_grad(tagged[...], d_target)
    bil = weight_grad(d_down, sums[...])
    for m in range(8):
        tile = [bil[0:64, k * 128 : k * 128 + 64] for k in (2 * m, 2 * m + 1)]
        row = 768 + 64 * (m // 4)
        first[row : row + 64, (m % 4) * 128 : (m % 4 + 1) * 128] = jnp.concatenate(tile, axis=1)
    for half in range(2):
        for m in range(4):
            at = 64 + 32 * half
            tile = [bil[64:96, k * 128 + at : k * 128 + at + 32] for k in range(4 * m, 4 * m + 4)]
            row = 1728 + 32 * half
            first[row : row + 32, m * 128 : (m + 1) * 128] = jnp.concatenate(tile, axis=1)
    first[1664:1728] = weight_grad(down_act, d_trip)[:64]
    quad_up_grad[...] = weight_grad(down_act, d_quad)[64:96]
    atom_rows[...] = jnp.concatenate(
        [gathered, summary, updated, a0_act, new_atoms, e_act, d_a0, d_a1, d_e, d_out, d_gate], axis=1
    )
    split_cores(core, first, keep, send)
    grad_sums[...] = times(d_down, weight[...])


def late_kernel(grad_rads, radial, atom_rows, quad_up_grad, core, keep, send, second):
    atoms = atom_rows[...]
    gathered, summary = atoms[:, :512], atoms[:, 512:1024]
    updated, a0_act, new_atoms, e_act, d_a0, d_a1, d_e, d_out, d_gate = [
        atoms[:, at : at + 256] for at in range(1024, 3328, 256)
    ]
    second[0:512, 0:256] = weight_grad(gathered, d_gate)
    second[0:512, 256:512] = weight_grad(summary, d_e)
    second[512:768, 0:256] = weight_grad(updated, d_a0)
    second[512:768, 256:512] = weight_grad(a0_act, d_a1)
    second[768:1024, 0:256] = weight_grad(new_atoms, d_e)
    second[768:1024, 256:512] = weight_grad(e_act, d_out)
    for k in range(3):
        second[1024 + 128 * k : 1152 + 128 * k] = weight_grad(radial[...], grad_rads[k])
    second[1408:1440] = quad_up_grad[...]
    second[1440:1536] = jnp.zeros((96, 512), F32)
    split_cores(core, second, keep, send)


def scatter_kernel(
    cosines, sums, grad_src, src_rows, mark_rows,
    back_before, back_here, back_after, back_local,
    table,
):
    group = back_here.shape[0] * 8
    depth = 3 * group + 16
    trip_lanes = iota((128, 128), 1) < TRIP_W
    scale = 1.0 / math.sqrt(PICKS)

    def basis_back(b):
        at = pl.multiple_of(b * BLOCK, BLOCK)
        own = pl.ds(at, BLOCK)
        parts = []
        for h in range(2):
            cos = cosines[2 * b + h]
            own_rows = pl.ds(pl.multiple_of(at + 8 * h, 8), 8)
            after = total = None
            for k in range(ANGLES - 1, -1, -1):
                term = sums[own_rows, k * 128 : (k + 1) * 128] * (lead(k) * scale)
                if total is None:
                    after, total = None, jnp.broadcast_to(term, cos.shape)
                elif after is None:
                    after, total = total, term + cos * total
                else:
                    after, total = total, term + cos * total - ratio(k + 1) * after
            parts.append(total)
        grad = jnp.concatenate(parts, axis=1).reshape(128, 128)
        grad = jnp.concatenate(
            [jnp.where(trip_lanes, grad, 0.0), jnp.where(trip_lanes, 0.0, grad)], axis=0
        )
        hits = onehot(mark_rows[b] == iota((512, 256), 0))
        got = side_by_side(side_sum(dot(hits, side_by_side(grad))))
        table[:, own, :] = got.reshape(32, BLOCK, 256)

    looped(BLOCKS, 3, basis_back)
    table[30] = side_by_side(grad_src[:, :128])
    table[31] = side_by_side(grad_src[:, 128:])
    rows = iota((depth, EDGES), 0)
    place_even = onehot(src_rows[0:1, :] == rows)
    place_odd = onehot(src_rows[1:2, :] == rows)

    def scatter_pair(p):
        got = side_sum(dot(place_even, table[2 * p]) + dot(place_odd, table[2 * p + 1]))
        for i, back in enumerate((back_before, back_here, back_after)):
            back[:, p] = got[i * group : (i + 1) * group].reshape(group // 8, 8, 128)
        back_local[p] = got[3 * group :]

    looped(16, 4, scatter_pair)


def finish_kernel(
    back_local, returned, grad_late, tag_late, edge, radial, columns, pre, downs, rads, tag_row, send_row,
    w_in, w_trip, w_quad, core,
    grad_atoms, grad_edges, keep_first, send_first, keep_second, send_second,
    first, second,
):
    shape = (EDGES, 256)
    lane = iota(shape, 1)
    place = onehot((local_rows(lane) == iota(shape, 0)) & (lane < EDGES))
    rows = dot(place, side_by_side(back_local[...].reshape(256, 128)))
    pay = paid(iota((1, 128), 1), send_lanes(send_row[...]))
    place = onehot(pay == iota((EDGES, 128), 0))
    send = send_column(send_row[...], 8)
    tags = to_column(tag_row[...])
    rows = side_sum(rows + dot(place, side_by_side(returned[...].reshape(128, 128))))
    back = returned[15]
    tag = tag_late[...] + jnp.concatenate([back_local[15, 0:8], back_local[15, 8:16]], axis=1)
    atom = iota((8, 1), 0)
    for r in range(SEND):
        piece = jnp.concatenate([back[r : r + 1], back[4 + r : 5 + r]], axis=1)
        tag = tag + jnp.where(send[r : r + 1, :] == atom, piece, 0.0)
    grad_atoms[...] = tag
    table = [
        jnp.sum(jnp.where(tags == t, tag, 0.0), axis=0, keepdims=True) for t in range(3)
    ]
    table = jnp.concatenate(table + [jnp.zeros((29, ATOM_W), F32)], axis=0)
    d_trip = rows[:, :64]
    d_quad = rows[:, 64:96] * radial[:, 0:1] + rows[:, 96:128] * radial[:, 1:2]
    total = grad_late[...]
    for k, (d_row, down, weight, out) in enumerate(
        ((d_trip, slice(0, 64), w_trip, first), (d_quad, slice(64, 96), w_quad, second))
    ):
        d_down = d_row * columns[:, 0:1] * act_and_slope(downs[:, down])[1]
        value, slope = act_and_slope(pre[k])
        d_start = times(d_down, weight[...])
        d_pre = d_start * rads[k] * slope
        total = total + times(d_pre, w_in[k], NT)
        out[0:512] = weight_grad(edge[...], d_pre)
        out[512:640] = weight_grad(radial[...], d_start * value)
        down_grad = weight_grad(d_down, value * rads[k])
        if k == 0:
            out[640:704] = down_grad
            out[704:768] = jnp.zeros((64, 512), F32)
        else:
            out[640:672] = down_grad
            out[672:704, 0:256] = table
            out[672:704, 256:512] = jnp.zeros((32, 256), F32)
            out[704:768] = jnp.zeros((64, 512), F32)
    grad_edges[...] = total
    split_cores(core, first, keep_first, send_first)
    split_cores(core, second, keep_second, send_second)


def moved(core, pairs, held, copies, sems):
    arriving = [pltpu.make_async_copy(pair[i % 2], held[i], sems.at[i]) for i, pair in zip(range(len(held)), [p for p in pairs for _ in range(2)])]
    for upper in (0, 1):

        @pl.when(core[0] == upper)
        def _():
            for i in range(len(held)):
                pltpu.make_async_copy(pairs[i // 2][i % 2 ^ upper], held[i], sems.at[i]).start()

    leaving, at = [], len(held)
    for i, copy in enumerate(arriving):
        copy.wait()
        for source, target in copies[i]:
            leaving.append(pltpu.make_async_copy(source, target, sems.at[at]))
            leaving[-1].start()
            at += 1
    for x in leaving:
        x.wait()


def late_outputs(
    a_mine, a_other, b_mine, b_other, core,
    res, ae, trip_bil, trip_up, quad_bil, quad_up, rad, ea, ad,
    a_low, a_high, b_low, b_high, sems,
):
    left, right = slice(0, 256), slice(256, 512)
    copies = [
        [
            (a_low.at[0:512], res.at[0]),
            (a_low.at[512:768], ae.at[0]),
            (a_low.at[768:832], trip_bil.at[:, 0:512]),
            (a_low.at[832:896], trip_bil.at[:, 512:1024]),
        ],
        [
            (a_high.at[0:512], res.at[1]),
            (a_high.at[512:768], ae.at[1]),
            (a_high.at[768:832], trip_up),
            (a_high.at[832:864], quad_bil.at[:, 0:512]),
            (a_high.at[864:896], quad_bil.at[:, 512:1024]),
        ],
        [
            (b_low.at[0:512, left], ea.at[0]),
            (b_low.at[0:512, right], ea.at[1]),
            (b_low.at[512:768, left], ad.at[0]),
            (b_low.at[512:768, right], ad.at[1]),
        ],
        [
            (b_high.at[0:256, left], ad.at[2]),
            (b_high.at[0:256, right], ad.at[3]),
            (b_high.at[640:672], quad_up),
        ]
        + [(b_high.at[256 + 128 * k : 384 + 128 * k], rad.at[k]) for k in range(3)],
    ]
    pairs = [(a_mine, a_other), (b_mine, b_other)]
    moved(core, pairs, (a_low, a_high, b_low, b_high), copies, sems)


def early_outputs(
    c_mine, c_other, d_mine, d_other, late_rad, core,
    inputs, rad, trip_down, quad_down, tags,
    c_low, c_high, d_low, d_high, held_rad, sems,
):
    other_rad = pltpu.make_async_copy(late_rad, held_rad, sems.at[16])
    other_rad.start()
    copies = []
    for k, (low, high) in enumerate(((c_low, c_high), (d_low, d_high))):
        copies.append([(low, inputs.at[k, 0:384])])
        copies.append([(high.at[0:128], inputs.at[k, 384:512]), (high.at[128:256], rad.at[k])])
    copies[1].append((c_high.at[256:320], trip_down))
    copies[3].append((d_high.at[256:288], quad_down))
    pairs = [(c_mine, c_other), (d_mine, d_other)]
    moved(core, pairs, (c_low, c_high, d_low, d_high), copies, sems)
    other_rad.wait()
    last = pltpu.make_async_copy(held_rad, rad.at[2:5], sems.at[17])
    last.start()
    tags[...] = d_high[288:291, 0:256]
    last.wait()


def call(kernel, outs, args, scratch=(), micros=1, inside=None, room=63):
    spaces = [pl.ANY if inside is not None and i not in inside else pltpu.VMEM for i in range(len(outs))]
    space = pltpu.VMEM if inside is None else pl.ANY
    flops = int(micros * 1.15e9)
    return pl.pallas_call(
        kernel,
        out_shape=[jax.ShapeDtypeStruct(shape, F32) for shape in outs],
        in_specs=[pl.BlockSpec(memory_space=pltpu.SMEM if x.ndim == 1 else space) for x in args],
        out_specs=[pl.BlockSpec(memory_space=x) for x in spaces],
        scratch_shapes=list(scratch),
        compiler_params=pltpu.CompilerParams(vmem_limit_bytes=room * 1024 * 1024),
        cost_estimate=pl.CostEstimate(flops=flops, bytes_accessed=1 << 10, transcendentals=0),
    )(*args)


def per_device(
    hidden_atoms,
    edge_states,
    edge_vectors,
    atom_tags,
    send_list,
    sources,
    trip_slots,
    triplet_mask,
    quad_slots,
    quad_mask,
    edge_mask,
    w_inputs,
    w_radial,
    w_trip_down,
    triplet_bilinear_weight,
    w_trip_up,
    w_quad_down,
    w_quad_bil,
    w_quad_up,
    w_atom_edge,
    w_residual,
    w_edge_atom,
    w_atom_dense,
    tag_table,
    cot_atoms,
    cot_edges,
    cot_energy,
):
    planes = 2 if lax.axis_size("gz") == 2 else 3
    group = 3 * planes

    offset = jnp.maximum(sources - ATOMS, 0)
    block, border = offset // SEND, offset % SEND
    step_x, step_y, step_z = block // 9, block // 3 % 3, block % 3
    if planes == 2:
        step_z = jnp.clip(step_z - 1 + lax.axis_index("gz"), 0, 1)
    block = (step_y * 3 + step_x) * planes + step_z
    inside = sources < ATOMS
    even = jnp.where(inside, 3 * group * 8 + sources, block * 8 + border)
    src = jnp.stack([even, even + jnp.where(inside, ATOMS, SEND)])
    slots = jnp.concatenate([trip_slots, quad_slots], axis=1)
    masks = jnp.concatenate([triplet_mask, quad_mask], axis=1)
    marks = jnp.where(masks > 0, slots * BLOCK + (jnp.arange(EDGES) % BLOCK)[:, None], -1)
    mark_rows = marks.reshape(BLOCKS, BLOCK, 2 * PICKS).transpose(0, 2, 1)
    mark_rows = mark_rows.reshape(BLOCKS, 1, 2 * PICKS * BLOCK)
    trip_down_t, quad_down_t = w_trip_down.T, w_quad_down.T

    tag_row, send_row = atom_tags[None, :], send_list[None, :]
    payload, local, tagged, pre, downs, rads, radial, columns = call(
        start_kernel,
        [(PAIRS, 8, 128), (PAIRS, 16, 128), (8, 256), (2, EDGES, 512), (EDGES, 128), (5, EDGES, 512)]
        + [(EDGES, 128)] * 2,
        [edge_states, edge_vectors, edge_mask[None, :], hidden_atoms, tag_row, send_row, tag_table,
         w_inputs, w_radial, trip_down_t, quad_down_t],
        micros=5, room=58,
    )
    core = bit_value("gyl", 0)[None]
    before, here, after = with_halo(payload)
    (
        atoms_out, edges_out, energy_out, grad_edges, grad_tag,
        cosines, grad_sums, grad_src, keep_a, send_a, grad_rads, atom_rows, quad_up_grad,
    ) = call(
        main_kernel,
        [(8, 256), (EDGES, 512), (8, 256), (EDGES, 512), (8, 256)]
        + [(2 * BLOCKS, PICKS, 8, 128), (EDGES, 2048), (EDGES, 256), (896, 512), (896, 512)]
        + [(3, EDGES, 512), (8, 3328), (32, 512)],
        [before, here, after, local, tagged, edge_states, columns, rads, radial,
         src.T, slots, marks,
         triplet_bilinear_weight.T, w_trip_up, w_quad_bil.T, w_quad_up, w_atom_edge, w_residual,
         w_edge_atom, w_atom_dense, cot_atoms, cot_edges, cot_energy, core],
        scratch=[
            pltpu.VMEM((32, EDGES, 256), BF),
            pltpu.VMEM((EDGES, 2048), F32),
            pltpu.VMEM((128, 2048), BF),
            pltpu.VMEM((5, EDGES, 512), F32),
            pltpu.VMEM((EDGES, 128), F32),
            pltpu.VMEM((1792, 512), F32),
        ],
        micros=26, room=44,
    )
    chain = Chain()
    got_a = swap(send_a, "gyl", 0)
    keep_b, send_b = call(
        late_kernel,
        [(768, 512)] * 2,
        [grad_rads, radial, atom_rows, quad_up_grad, core],
        scratch=[pltpu.VMEM((1536, 512), F32)],
        micros=4, room=18,
    )
    late = reduction(chain, [keep_a, got_a], [keep_b, swap(send_b, "gyl", 0)], True, True)
    next(late)
    grad_sums = chain.after(grad_sums)
    back_before, back_here, back_after, back_local = call(
        scatter_kernel,
        [(group, 16, 8, 128)] * 3 + [(16, 16, 128)],
        [cosines, grad_sums, grad_src, src, mark_rows],
        scratch=[pltpu.VMEM((32, EDGES, 256), BF)],
        micros=13, room=18,
    )
    got = shifted(back_before, GY, -1, True), shifted(back_after, GY, 1, True)
    chain.step(back_local)
    next(late)
    got, value = chain.after((got, back_here))
    value = chain.step(value + got[0] + got[1])
    first_plane, middle, last_plane = value[:planes], value[planes : 2 * planes], value[2 * planes :]
    got = shifted(first_plane, "gx", -1, True), shifted(last_plane, "gx", 1, True)
    next(late)
    got, middle = chain.after((got, middle))
    value = chain.step(middle + got[0] + got[1])
    if planes == 2:
        top = lax.axis_index("gz") == 1
        mine = jnp.where(top, value[1], value[0])
        theirs = jnp.where(top, value[0], value[1])
        returned = mine + lax.ppermute(theirs, "gz", [(0, 1), (1, 0)])
    else:
        returned = value[1] + shifted(value[0], "gz", -1, False) + shifted(value[2], "gz", 1, False)
    returned = chain.after(returned)
    grad_atoms, grad_edges, keep_c, send_c, keep_d, send_d = call(
        finish_kernel,
        [(8, 256), (EDGES, 512)] + [(384, 512)] * 4,
        [back_local, returned, grad_edges, grad_tag, edge_states, radial, columns, pre, downs, rads,
         tag_row, send_row, w_inputs, trip_down_t, quad_down_t, core],
        scratch=[pltpu.VMEM((768, 512), F32)] * 2,
        micros=7, room=58,
    )
    next(late)
    send_c, send_d = chain.after((send_c, send_d))
    got_c, got_d = swap(send_c, "gyl", 0), swap(send_d, "gyl", 0)
    early = reduction(chain, [keep_c, got_c], [keep_d, got_d], firm_total=True)
    running = {"L": late, "E": early}
    done = {}

    def resume(name):
        if name in done:
            return
        try:
            next(running[name])
        except StopIteration as end:
            done[name] = end.value

    for name in "ELEELELEEELEL":
        resume(name)
    while "L" not in done:
        resume("L")
    (a_mine, a_other), (b_mine, b_other) = done["L"]
    g_res, g_ae, g_trip_bil, g_trip_up, g_quad_bil, g_quad_up, g_rad, g_ea, g_ad = call(
        late_outputs,
        [(2, 512, 512), (2, 256, 512), (64, 1024), (64, 512), (32, 1024), (32, 512), (3, 128, 512)]
        + [(2, 512, 256), (4, 256, 256)],
        [a_mine, a_other, b_mine, b_other, core],
        scratch=[pltpu.VMEM((896, 512), F32)] * 2
        + [pltpu.VMEM((768, 512), F32)] * 2
        + [pltpu.SemaphoreType.DMA((23,))],
        micros=0,
        room=12,
        inside=(),
    )
    chain.step(g_quad_up)
    while "E" not in done:
        resume("E")
    (c_mine, c_other), (d_mine, d_other) = done["E"]
    g_inputs, g_rad, g_trip_down, g_quad_down, g_tags = call(
        early_outputs,
        [(2, 512, 512), (5, 128, 512), (64, 512), (32, 512), (3, 256)],
        [c_mine, c_other, d_mine, d_other, g_rad, core],
        scratch=[pltpu.VMEM((384, 512), F32)] * 4
        + [pltpu.VMEM((3, 128, 512), F32), pltpu.SemaphoreType.DMA((18,))],
        micros=3,
        room=8,
        inside=(4,),
    )
    return (
        atoms_out,
        edges_out,
        energy_out,
        grad_atoms,
        grad_edges,
        g_inputs,
        g_rad,
        g_trip_down.T,
        g_trip_bil.T,
        g_trip_up,
        g_quad_down.T,
        g_quad_bil.T,
        g_quad_up,
        g_ae,
        g_res,
        g_ea,
        g_ad,
        g_tags,
    )


def solution(mesh):
    size = dict(mesh.shape)
    inner = Mesh(mesh.devices.reshape(size["gx"], size["gy"] // 2, 2, size["gz"]), ROWS)
    flat, columns, vector, whole = P(ROWS, None), P(None, ROWS), P(ROWS), P()
    placed = [flat, flat, columns] + [vector] * 3 + [flat] * 4 + [vector] + [whole] * 13 + [flat] * 3
    return jax.shard_map(
        per_device,
        mesh=inner,
        in_specs=tuple(placed),
        out_specs=tuple([flat] * 5 + [whole] * 13),
        check_vma=False,
    )
```

```python
import functools
import math

import jax
import jax.numpy as jnp
from jax import lax
from jax.experimental import pallas as pl
from jax.experimental.pallas import tpu as pltpu
from jax.sharding import Mesh
from jax.sharding import PartitionSpec as P

BF = jnp.bfloat16
F32 = jnp.float32
ROWS = ("gx", "gyh", "gyl", "gz")
GY = ("gyh", "gyl")
ATOMS, SEND, SLOTS, EDGES = 8, 4, 30, 240
ATOM_W, EDGE_W, TRIP_W, QUAD_W, RADIAL = 256, 512, 64, 32, 128
ANGLES, PICKS = 16, 8
PAIRS = 17
BLOCK = 16
BLOCKS = EDGES // BLOCK
root_half = 0.7071067811865476
NN = (((1,), (0,)), ((), ()))
NT = (((1,), (1,)), ((), ()))
TN = (((0,), (0,)), ((), ()))


def shifted(value, axis, steps, wrap):
    count = lax.axis_size(axis)
    pairs = [(i, (i + steps) % count) for i in range(count) if wrap or 0 <= i + steps < count]
    return lax.ppermute(value, axis, pairs)


def planes_of(value):
    if lax.axis_size("gz") == 2:
        other = lax.ppermute(value, "gz", [(0, 1), (1, 0)])
        top = lax.axis_index("gz") == 1
        return jnp.stack([jnp.where(top, other, value), jnp.where(top, value, other)])
    return jnp.stack([shifted(value, "gz", 1, False), value, shifted(value, "gz", -1, False)])


def with_halo(value):
    value = planes_of(value)
    value = jnp.concatenate([shifted(value, "gx", 1, True), value, shifted(value, "gx", -1, True)])
    return shifted(value, GY, 1, True), value, shifted(value, GY, -1, True)


def bits_of(axis):
    count = lax.axis_size(axis)
    return [(axis, b) for b in range(count.bit_length() - 1)]


def swap(value, axis, bit):
    count = lax.axis_size(axis)
    return lax.ppermute(value, axis, [(i, i ^ (1 << bit)) for i in range(count)])


def bit_value(axis, bit):
    return (lax.axis_index(axis) >> bit) & 1


def part(arrays, at, size):
    total = lax.dynamic_slice_in_dim(arrays[0], at, size)
    for x in arrays[1:]:
        total = total + lax.dynamic_slice_in_dim(x, at, size)
    return total


class Chain:
    def __init__(self):
        self.last = None

    def after(self, values):
        if self.last is not None:
            self.last, values = lax.optimization_barrier((self.last, values))
        return values

    def step(self, value):
        self.last = value
        return value

    def zero(self):
        first = jax.tree.leaves(self.last)[0]
        corner = first[(slice(0, 1),) * first.ndim].reshape(())
        return jnp.minimum(jnp.abs(corner), 0.0)


def halved(chain, arrays, axis, bit, tight=False):
    arrays = chain.after(arrays)
    half = arrays[0].shape[0] // 2
    one = bit_value(axis, bit)
    send = chain.step(part(arrays, (1 - one) * half, half))
    got = swap(send, axis, bit)
    send, arrays = lax.optimization_barrier((send, arrays))
    keep = part(arrays, one * half, half)
    if tight:
        chain.step((send, keep))
    return [keep, got]


def joined_halves(value, other, axis, bit):
    one = bit_value(axis, bit) == 1
    return jnp.concatenate([jnp.where(one, other, value), jnp.where(one, value, other)])


def reduction(chain, first, second, tight=False, firm=False, firm_total=False):
    across, along = bits_of("gz"), bits_of("gyh")
    lanes = [first, second]
    for turn, plan in enumerate(((across, along), (along, across))):
        for i in range(2):
            for axis, bit in plan[i]:
                lanes[i] = halved(chain, lanes[i], axis, bit, tight and turn == 1)
        yield
    sizes = [x[0].shape[0] for x in lanes]
    joint = [jnp.concatenate(pair) for pair in zip(*chain.after(lanes))]
    for axis, bit in bits_of("gx"):
        joint = halved(chain, joint, axis, bit, tight)
        yield
    joint = chain.after(joint)
    value = sum(joint[1:], joint[0])
    value = chain.step(value + chain.zero() if firm_total else value)
    for axis, bit in bits_of("gx")[::-1]:
        other = swap(value, axis, bit)
        yield
        value, other = chain.after((value, other))
        value = chain.step(joined_halves(value, other, axis, bit))
    values = [value[: sizes[0]], value[sizes[0] :]]
    for plan in ((along, across), (across, along)):
        for turn in range(max(len(across), len(along))):
            others = [None, None]
            for i in range(2):
                if turn < len(plan[i]):
                    others[i] = swap(values[i], *plan[i][::-1][turn])
            yield
            for i in range(2):
                if turn < len(plan[i]):
                    values[i], others[i] = chain.after((values[i], others[i]))
                    whole = joined_halves(values[i], others[i], *plan[i][::-1][turn])
                    if firm and plan[0] is across:
                        whole = whole + chain.zero()
                    values[i] = chain.step(whole)
    others = [swap(x, "gyl", 0) for x in values]
    yield
    values, others = chain.after((values, others))
    return [(value, chain.step(other)) for value, other in zip(values, others)]


def iota(shape, dim):
    return lax.broadcasted_iota(jnp.int32, shape, dim)


def dot(left, right, dims=NN):
    return lax.dot_general(left, right, dims, preferred_element_type=F32)


def halves(x):
    high = x.astype(BF)
    return high, (x - high.astype(F32)).astype(BF)


def stacked(x):
    high, low = halves(x)
    if x.shape[0] % 16 == 0:
        return jnp.concatenate([high, low], axis=0)
    return jnp.concatenate([high.astype(F32), low.astype(F32)], axis=0).astype(BF)


def folded(x):
    half = x.shape[0] // 2
    return x[:half] + x[half:]


def times(x, weight, dims=NN):
    return folded(dot(stacked(x), weight, dims))


def side_by_side(x):
    return jnp.concatenate(halves(x), axis=1)


def side_sum(x):
    half = x.shape[1] // 2
    return x[:, :half] + x[:, half:]


def weight_grad(x, y):
    x_high, x_low = halves(x)
    y_high, y_low = halves(y)
    left, right = [x_high, x_high, x_low], [y_high, y_low, y_high]
    if x.shape[0] % 16 == 0:
        return dot(jnp.concatenate(left, axis=0), jnp.concatenate(right, axis=0), TN)
    left = jnp.concatenate([p.astype(F32) for p in left], axis=0).astype(BF)
    right = jnp.concatenate([p.astype(F32) for p in right], axis=0).astype(BF)
    return dot(left, right, TN)


def onehot(hit):
    return jnp.where(hit, 1.0, 0.0).astype(BF)


def sigmoid(v):
    return 1.0 / (1.0 + jnp.exp(-v))


def act(v):
    return v * sigmoid(v) * (1.0 / 0.6)


def act_and_slope(v):
    s = sigmoid(v)
    return v * s * (1.0 / 0.6), s * (1.0 + v * (1.0 - s)) * (1.0 / 0.6)


def sin_pi(t):
    n = jnp.floor(t + 0.5)
    r = t - n
    odd = n - 2.0 * jnp.floor(n * 0.5)
    q = r * r
    total = jnp.zeros_like(r)
    for k in range(6, -1, -1):
        total = total * q + (-1.0) ** k * math.pi ** (2 * k + 1) / math.factorial(2 * k + 1)
    return total * r * (1.0 - 2.0 * odd)


def to_column(row):
    n = row.shape[1]
    same = iota((n, n), 0) == iota((n, n), 1)
    return jnp.sum(jnp.where(same, row, jnp.zeros_like(row)), axis=1, keepdims=True)


def send_column(send, rows):
    shape = (rows, SEND)
    hit = (iota(shape, 0) & (SEND - 1)) == iota(shape, 1)
    return jnp.sum(jnp.where(hit, send, 0), axis=1, keepdims=True)


def send_lanes(send):
    shape = (8, 128)
    hit = iota(shape, 0) == (iota(shape, 1) & (SEND - 1))
    return jnp.sum(jnp.where(hit, send_column(send, 8), 0), axis=0, keepdims=True)


def paid(row, send):
    edge = send * SLOTS + 2 * (row >> 3) + ((row >> 2) & 1)
    return jnp.where(row < 120, edge, -1)


def atom_of(edge):
    total = jnp.zeros_like(edge)
    for a in range(1, ATOMS):
        total = total + jnp.where(edge >= a * SLOTS, 1, 0)
    return total


def radial_of(length):
    x = length / 12.0
    x2 = x * x
    x4 = x2 * x2
    envelope = 1.0 - 28.0 * (x4 * x2) + 48.0 * (x4 * x2 * x) - 21.0 * (x4 * x4)
    orders = (iota((1, RADIAL), 1) + 1).astype(F32)
    return envelope * sin_pi(x * orders) / x


def geometry(unit):
    own = atom_of(iota((8, EDGES), 1)) == iota((8, EDGES), 0)
    edge = iota((EDGES, 128), 0)
    slot = edge - atom_of(edge) * SLOTS
    total = jnp.zeros((24, 128), F32)
    for k in range(3):
        x = jnp.where(own, unit[k : k + 1, :], 0.0)
        high = x.astype(BF).astype(F32)
        mid = (x - high).astype(BF).astype(F32)
        parts = jnp.concatenate([high, mid, x - high - mid], axis=0).astype(BF)
        total = total + dot(parts, onehot(iota((EDGES, 128), 1) == slot + 32 * k))
    return total[0:8] + total[8:16] + total[16:24]


def local_rows(index):
    return (index & 7) * SLOTS + 2 * (index >> 4) + ((index >> 3) & 1)


def start_kernel(
    edge, vec, mask, hidden, tag_row, send_row, table, w_in, w_rad, w_trip, w_quad,
    payload, local, tagged, pre, downs, rads, radial_out, columns,
):
    vectors = vec[...]
    length = jnp.sqrt(jnp.sum(vectors * vectors, axis=0, keepdims=True))
    unit = vectors / length
    geo = geometry(unit)
    live = to_column(jnp.where(mask[...] > 0, 1.0, 0.0))
    parts = [live] + [to_column(unit[k : k + 1, :]) for k in range(3)]
    columns[...] = jnp.concatenate(parts + [jnp.zeros((EDGES, 124), F32)], axis=1)
    send = send_column(send_row[...], 8)
    pay = paid(iota((128, 1), 0), send_column(send_row[...], 128))
    tags = to_column(tag_row[...])
    radial = radial_of(to_column(length))
    radial_out[...] = radial
    split = stacked(radial)
    for k in range(5):
        rads[k] = folded(dot(split, w_rad[k]))
    split = stacked(edge[...])
    pre[0] = folded(dot(split, w_in[0]))
    pre[1] = folded(dot(split, w_in[1]))
    trip_pre = times(act(pre[0]) * rads[0], w_trip[...], NT)
    quad_pre = times(act(pre[1]) * rads[1], w_quad[...], NT)
    downs[...] = jnp.concatenate([trip_pre, quad_pre, jnp.zeros((EDGES, 32), F32)], axis=1)
    trip = act(trip_pre) * live
    quad = act(quad_pre) * live
    rows = jnp.concatenate([trip, quad * radial[:, 0:1], quad * radial[:, 1:2]], axis=1)
    rows = side_by_side(rows)
    shape = (EDGES, EDGES)
    place = onehot(local_rows(iota(shape, 0)) == iota(shape, 1))
    local[0:15] = side_sum(dot(place, rows)).reshape(15, 16, 128)
    place = onehot(pay == iota((128, EDGES), 1))
    payload[0:16] = side_sum(dot(place, rows)).reshape(16, 8, 128)
    tag = hidden[...]
    for t in range(3):
        tag = tag + jnp.where(tags == t, table[t : t + 1, :].astype(F32), 0.0)
    tagged[...] = tag
    local[15] = jnp.concatenate([tag[:, :128], tag[:, 128:]], axis=0)
    local[16] = jnp.concatenate([geo, jnp.zeros((8, 128), F32)], axis=0)
    both = jnp.concatenate([tag, geo], axis=1)
    sent = jnp.zeros((8, 384), F32)
    for a in range(ATOMS):
        sent = sent + jnp.where(send == a, both[a : a + 1, :], 0.0)
    payload[15] = jnp.where(iota((8, 128), 0) < 4, sent[:, :128], sent[:, 128:256])
    payload[16] = sent[:, 256:]


def split_cores(core, whole, keep, send):
    half = whole.shape[0] // 2
    upper = core[0] == 1
    low, high = whole[:half], whole[half:]
    keep[...] = jnp.where(upper, high, low)
    send[...] = jnp.where(upper, low, high)


def segments(shape, edge_dim, atom_dim):
    edge, atom = iota(shape, edge_dim), iota(shape, atom_dim) & 7
    return onehot((edge >= atom * SLOTS) & (edge < atom * SLOTS + SLOTS))


def lead(k):
    return math.comb(2 * k, k) / 2.0**k


def ratio(k):
    return k * k / (4.0 * k * k - 1.0)


def monic(cosine):
    before, now = jnp.ones_like(cosine), cosine
    yield before
    yield now
    for k in range(1, ANGLES - 1):
        before, now = now, cosine * now - ratio(k) * before
        yield now


def looped(count, step, body):
    def turn(t, carry):
        for i in range(step):
            body(t * step + i)
        return carry

    lax.fori_loop(0, count // step, turn, 0)


def main_kernel(
    halo_before, halo_here, halo_after, local, tagged, edge, columns, rads, radial,
    src_cols, slots, marks,
    trip_bil, trip_up, quad_bil, quad_up, w_ae, w_res, w_ea, w_ad,
    cot_atoms, cot_edges, cot_energy, core,
    atoms_out, edges_out, energy_out, grad_edges, grad_tag,
    cosines, grad_sums, grad_src, keep, send, grad_rads, atom_rows, quad_up_grad,
    table, sums, weight, kept, cos_table, first,
):
    live = columns[:, 0:1]
    halos = (halo_before, halo_here, halo_after)
    group = halo_here.shape[0] * 8
    depth = 3 * group + 16
    lanes = iota((EDGES, depth), 1)
    place = jnp.concatenate(
        [onehot(src_cols[:, 0:1] == lanes), onehot(src_cols[:, 1:2] == lanes)], axis=0
    )

    def rows_at(p):
        parts = [h[:, p].reshape(group, 128) for h in halos]
        return jnp.concatenate(parts + [local[p]], axis=0)

    def gather_pair(p):
        got = dot(place, side_by_side(rows_at(p))).astype(BF)
        table[2 * p] = got[:EDGES]
        table[2 * p + 1] = got[EDGES:]

    looped(16, 4, gather_pair)

    rows = rows_at(16)
    high, low = halves(rows)
    rest = (rows - high.astype(F32) - low.astype(F32)).astype(BF)
    got = dot(place[:EDGES], jnp.concatenate([high, low, rest], axis=1))
    got = got[:, :128] + got[:, 128:256] + got[:, 256:]
    cos_table[...] = -(
        columns[:, 1:2] * got
        + columns[:, 2:3] * pltpu.roll(got, 96, 1)
        + columns[:, 3:4] * pltpu.roll(got, 64, 1)
    )

    for k in range(ANGLES):
        top = trip_bil[:, k * 64 : k * 64 + 64].astype(F32)
        top = jnp.concatenate([top, jnp.zeros((64, 64), F32)], axis=1)
        low_left = quad_bil[:, k * 32 : k * 32 + 32].astype(F32)
        low_right = quad_bil[:, 512 + k * 32 : 544 + k * 32].astype(F32)
        bottom = jnp.concatenate([jnp.zeros((32, 64), F32), low_left, low_right], axis=1)
        piece = jnp.concatenate([top, bottom, jnp.zeros((32, 128), F32)], axis=0)
        weight[:, k * 128 : (k + 1) * 128] = piece.astype(BF)

    trip_lanes = iota((128, 128), 1) < TRIP_W
    scale = 1.0 / math.sqrt(PICKS)

    def basis_block(b):
        at = pl.multiple_of(b * BLOCK, BLOCK)
        own = pl.ds(at, BLOCK)
        wide = iota((BLOCK, 512), 1)
        mark = marks[own, :]
        hits = [jnp.where(mark[:, t : t + 1] == wide, 1.0, 0.0) for t in range(2 * PICKS)]
        hits = jnp.concatenate(hits, axis=0).astype(BF)
        got = side_sum(dot(hits, table[:, own, :].reshape(512, 256)))
        picked = jnp.where(trip_lanes, got[:128], got[128:])
        picked = picked.reshape(PICKS, BLOCK, 128)
        cos_here = cos_table[own, :]
        slot = slots[own, :]
        low_lanes = iota((BLOCK, 128), 1) < TRIP_W
        for h in range(2):
            rows = slice(8 * h, 8 * h + 8)
            cos = []
            for j in range(PICKS):
                index = jnp.where(
                    low_lanes[rows], slot[rows, j : j + 1], slot[rows, PICKS + j : PICKS + j + 1]
                )
                cos.append(jnp.take_along_axis(cos_here[rows], index, axis=1))
            cos = jnp.stack(cos)
            cosines[2 * b + h] = cos
            values = picked[:, rows]
            for k, poly in enumerate(monic(cos)):
                total = jnp.sum(poly * values, axis=0) * (lead(k) * scale)
                sums[pl.ds(pl.multiple_of(at + 8 * h, 8), 8), k * 128 : (k + 1) * 128] = total

    looped(BLOCKS, 3, basis_block)

    down = times(sums[...], weight[...], NT)
    down_act, down_slope = act_and_slope(down)
    trip_h, quad_h = down_act[:, :64], down_act[:, 64:96]
    trip_pre = times(trip_h, trip_up[...])
    quad_pre = times(quad_h, quad_up[...])
    src = jnp.concatenate(
        [side_sum(table[30].astype(F32)), side_sum(table[31].astype(F32))], axis=1
    )
    target = times(tagged[...], w_ae[1])
    spread = segments((EDGES, 16), 0, 1)
    gathers = segments((8, EDGES), 1, 0)

    def to_edges(x):
        return dot(spread, stacked(x))

    def to_atoms(x):
        return side_sum(dot(gathers, side_by_side(x)))

    atom_pre = times(src, w_ae[0]) + to_edges(target)
    atom_act, atom_slope = act_and_slope(atom_pre)
    trip_act, trip_slope = act_and_slope(trip_pre)
    quad_act, quad_slope = act_and_slope(quad_pre)
    merged = (edge[...] + trip_act + quad_act + atom_act * rads[2]) * 0.5
    kept[0] = merged
    first_act, first_slope = act_and_slope(times(merged, w_res[0]))
    kept[1] = first_act
    second_act, second_slope = act_and_slope(times(first_act, w_res[1]))
    new_edges = (merged + second_act) * root_half
    edges_out[...] = new_edges
    weighted = new_edges * live
    root_slots = 1.0 / math.sqrt(SLOTS)
    gathered = to_atoms(weighted * rads[3]) * root_slots
    summary = to_atoms(weighted * rads[4]) * root_slots
    gate_act, gate_slope = act_and_slope(times(gathered, w_ea[0]))
    updated = (tagged[...] + gate_act) * root_half
    a0_act, a0_slope = act_and_slope(times(updated, w_ad[0]))
    a1_act, a1_slope = act_and_slope(times(a0_act, w_ad[1]))
    new_atoms = (updated + a1_act) * root_half
    atoms_out[...] = new_atoms
    e_act, e_slope = act_and_slope(times(summary, w_ea[1]) + times(new_atoms, w_ad[2]))
    out_act, out_slope = act_and_slope(times(e_act, w_ad[3]))
    energy_out[...] = out_act

    d_out = cot_energy[...] * out_slope
    d_e = times(d_out, w_ad[3], NT) * e_slope
    d_summary = times(d_e, w_ea[1], NT)
    d_atoms = (cot_atoms[...] + times(d_e, w_ad[2], NT)) * root_half
    d_a1 = d_atoms * a1_slope
    d_a0 = times(d_a1, w_ad[1], NT) * a0_slope
    d_updated = (d_atoms + times(d_a0, w_ad[0], NT)) * root_half
    d_gate = d_updated * gate_slope
    d_gathered = times(d_gate, w_ea[0], NT)

    d_gathered = to_edges(d_gathered * root_slots)
    d_summary = to_edges(d_summary * root_slots)
    grad_rads[1] = weighted * d_gathered
    grad_rads[2] = weighted * d_summary
    d_new = cot_edges[...] + live * (d_gathered * rads[3] + d_summary * rads[4])
    d_new = d_new * root_half
    d_second = d_new * second_slope
    kept[3] = d_second
    d_first = times(d_second, w_res[1], NT) * first_slope
    kept[2] = d_first
    d_merged = (d_new + times(d_first, w_res[0], NT)) * 0.5
    grad_edges[...] = d_merged
    grad_rads[0] = d_merged * atom_act
    d_atom = d_merged * rads[2] * atom_slope
    kept[4] = d_atom
    d_trip = d_merged * trip_slope
    d_quad = d_merged * quad_slope
    d_target = to_atoms(d_atom)
    grad_tag[...] = d_updated + times(d_target, w_ae[1], NT)
    d_down = jnp.concatenate(
        [times(d_trip, trip_up[...], NT), times(d_quad, quad_up[...], NT), jnp.zeros((EDGES, 32), F32)],
        axis=1,
    )
    d_down = d_down * down_slope
    grad_src[...] = times(d_atom, w_ae[0], NT)

    first[0:512] = weight_grad(kept[0], kept[2])
    first[512:768] = weight_grad(src, kept[4])
    first[896:1408] = weight_grad(kept[1], kept[3])
    first[1408:1664] = weight_grad(tagged[...], d_target)
    bil = weight_grad(d_down, sums[...])
    for m in range(8):
        tile = [bil[0:64, k * 128 : k * 128 + 64] for k in (2 * m, 2 * m + 1)]
        row = 768 + 64 * (m // 4)
        first[row : row + 64, (m % 4) * 128 : (m % 4 + 1) * 128] = jnp.concatenate(tile, axis=1)
    for half in range(2):
        for m in range(4):
            at = 64 + 32 * half
            tile = [bil[64:96, k * 128 + at : k * 128 + at + 32] for k in range(4 * m, 4 * m + 4)]
            row = 1728 + 32 * half
            first[row : row + 32, m * 128 : (m + 1) * 128] = jnp.concatenate(tile, axis=1)
    first[1664:1728] = weight_grad(down_act, d_trip)[:64]
    quad_up_grad[...] = weight_grad(down_act, d_quad)[64:96]
    atom_rows[...] = jnp.concatenate(
        [gathered, summary, updated, a0_act, new_atoms, e_act, d_a0, d_a1, d_e, d_out, d_gate], axis=1
    )
    split_cores(core, first, keep, send)
    grad_sums[...] = times(d_down, weight[...])


def late_kernel(grad_rads, radial, atom_rows, quad_up_grad, core, keep, send, second):
    atoms = atom_rows[...]
    gathered, summary = atoms[:, :512], atoms[:, 512:1024]
    updated, a0_act, new_atoms, e_act, d_a0, d_a1, d_e, d_out, d_gate = [
        atoms[:, at : at + 256] for at in range(1024, 3328, 256)
    ]
    second[0:512, 0:256] = weight_grad(gathered, d_gate)
    second[0:512, 256:512] = weight_grad(summary, d_e)
    second[512:768, 0:256] = weight_grad(updated, d_a0)
    second[512:768, 256:512] = weight_grad(a0_act, d_a1)
    second[768:1024, 0:256] = weight_grad(new_atoms, d_e)
    second[768:1024, 256:512] = weight_grad(e_act, d_out)
    for k in range(3):
        second[1024 + 128 * k : 1152 + 128 * k] = weight_grad(radial[...], grad_rads[k])
    second[1408:1440] = quad_up_grad[...]
    second[1440:1536] = jnp.zeros((96, 512), F32)
    split_cores(core, second, keep, send)


def scatter_kernel(
    cosines, sums, grad_src, src_rows, mark_rows,
    back_before, back_here, back_after, back_local,
    table,
):
    group = back_here.shape[0] * 8
    depth = 3 * group + 16
    trip_lanes = iota((128, 128), 1) < TRIP_W
    scale = 1.0 / math.sqrt(PICKS)

    def basis_back(b):
        at = pl.multiple_of(b * BLOCK, BLOCK)
        own = pl.ds(at, BLOCK)
        parts = []
        for h in range(2):
            cos = cosines[2 * b + h]
            own_rows = pl.ds(pl.multiple_of(at + 8 * h, 8), 8)
            after = total = None
            for k in range(ANGLES - 1, -1, -1):
                term = sums[own_rows, k * 128 : (k + 1) * 128] * (lead(k) * scale)
                if total is None:
                    after, total = None, jnp.broadcast_to(term, cos.shape)
                elif after is None:
                    after, total = total, term + cos * total
                else:
                    after, total = total, term + cos * total - ratio(k + 1) * after
            parts.append(total)
        grad = jnp.concatenate(parts, axis=1).reshape(128, 128)
        grad = jnp.concatenate(
            [jnp.where(trip_lanes, grad, 0.0), jnp.where(trip_lanes, 0.0, grad)], axis=0
        )
        hits = onehot(mark_rows[b] == iota((512, 256), 0))
        got = side_by_side(side_sum(dot(hits, side_by_side(grad))))
        table[:, own, :] = got.reshape(32, BLOCK, 256)

    looped(BLOCKS, 3, basis_back)
    table[30] = side_by_side(grad_src[:, :128])
    table[31] = side_by_side(grad_src[:, 128:])
    rows = iota((depth, EDGES), 0)
    place_even = onehot(src_rows[0:1, :] == rows)
    place_odd = onehot(src_rows[1:2, :] == rows)

    def scatter_pair(p):
        got = side_sum(dot(place_even, table[2 * p]) + dot(place_odd, table[2 * p + 1]))
        for i, back in enumerate((back_before, back_here, back_after)):
            back[:, p] = got[i * group : (i + 1) * group].reshape(group // 8, 8, 128)
        back_local[p] = got[3 * group :]

    looped(16, 4, scatter_pair)


def finish_kernel(
    back_local, returned, grad_late, tag_late, edge, radial, columns, pre, downs, rads, tag_row, send_row,
    w_in, w_trip, w_quad, core,
    grad_atoms, grad_edges, keep_first, send_first, keep_second, send_second,
    first, second,
):
    shape = (EDGES, 256)
    lane = iota(shape, 1)
    place = onehot((local_rows(lane) == iota(shape, 0)) & (lane < EDGES))
    rows = dot(place, side_by_side(back_local[...].reshape(256, 128)))
    pay = paid(iota((1, 128), 1), send_lanes(send_row[...]))
    place = onehot(pay == iota((EDGES, 128), 0))
    send = send_column(send_row[...], 8)
    tags = to_column(tag_row[...])
    rows = side_sum(rows + dot(place, side_by_side(returned[...].reshape(128, 128))))
    back = returned[15]
    tag = tag_late[...] + jnp.concatenate([back_local[15, 0:8], back_local[15, 8:16]], axis=1)
    atom = iota((8, 1), 0)
    for r in range(SEND):
        piece = jnp.concatenate([back[r : r + 1], back[4 + r : 5 + r]], axis=1)
        tag = tag + jnp.where(send[r : r + 1, :] == atom, piece, 0.0)
    grad_atoms[...] = tag
    table = [
        jnp.sum(jnp.where(tags == t, tag, 0.0), axis=0, keepdims=True) for t in range(3)
    ]
    table = jnp.concatenate(table + [jnp.zeros((29, ATOM_W), F32)], axis=0)
    d_trip = rows[:, :64]
    d_quad = rows[:, 64:96] * radial[:, 0:1] + rows[:, 96:128] * radial[:, 1:2]
    total = grad_late[...]
    for k, (d_row, down, weight, out) in enumerate(
        ((d_trip, slice(0, 64), w_trip, first), (d_quad, slice(64, 96), w_quad, second))
    ):
        d_down = d_row * columns[:, 0:1] * act_and_slope(downs[:, down])[1]
        value, slope = act_and_slope(pre[k])
        d_start = times(d_down, weight[...])
        d_pre = d_start * rads[k] * slope
        total = total + times(d_pre, w_in[k], NT)
        out[0:512] = weight_grad(edge[...], d_pre)
        out[512:640] = weight_grad(radial[...], d_start * value)
        down_grad = weight_grad(d_down, value * rads[k])
        if k == 0:
            out[640:704] = down_grad
            out[704:768] = jnp.zeros((64, 512), F32)
        else:
            out[640:672] = down_grad
            out[672:704, 0:256] = table
            out[672:704, 256:512] = jnp.zeros((32, 256), F32)
            out[704:768] = jnp.zeros((64, 512), F32)
    grad_edges[...] = total
    split_cores(core, first, keep_first, send_first)
    split_cores(core, second, keep_second, send_second)


def moved(core, pairs, held, copies, sems):
    arriving = [pltpu.make_async_copy(pair[i % 2], held[i], sems.at[i]) for i, pair in zip(range(len(held)), [p for p in pairs for _ in range(2)])]
    for upper in (0, 1):

        @pl.when(core[0] == upper)
        def _():
            for i in range(len(held)):
                pltpu.make_async_copy(pairs[i // 2][i % 2 ^ upper], held[i], sems.at[i]).start()

    leaving, at = [], len(held)
    for i, copy in enumerate(arriving):
        copy.wait()
        for source, target in copies[i]:
            leaving.append(pltpu.make_async_copy(source, target, sems.at[at]))
            leaving[-1].start()
            at += 1
    for x in leaving:
        x.wait()


def late_outputs(
    a_mine, a_other, b_mine, b_other, core,
    res, ae, trip_bil, trip_up, quad_bil, quad_up, rad, ea, ad,
    a_low, a_high, b_low, b_high, sems,
):
    left, right = slice(0, 256), slice(256, 512)
    copies = [
        [
            (a_low.at[0:512], res.at[0]),
            (a_low.at[512:768], ae.at[0]),
            (a_low.at[768:832], trip_bil.at[:, 0:512]),
            (a_low.at[832:896], trip_bil.at[:, 512:1024]),
        ],
        [
            (a_high.at[0:512], res.at[1]),
            (a_high.at[512:768], ae.at[1]),
            (a_high.at[768:832], trip_up),
            (a_high.at[832:864], quad_bil.at[:, 0:512]),
            (a_high.at[864:896], quad_bil.at[:, 512:1024]),
        ],
        [
            (b_low.at[0:512, left], ea.at[0]),
            (b_low.at[0:512, right], ea.at[1]),
            (b_low.at[512:768, left], ad.at[0]),
            (b_low.at[512:768, right], ad.at[1]),
        ],
        [
            (b_high.at[0:256, left], ad.at[2]),
            (b_high.at[0:256, right], ad.at[3]),
            (b_high.at[640:672], quad_up),
        ]
        + [(b_high.at[256 + 128 * k : 384 + 128 * k], rad.at[k]) for k in range(3)],
    ]
    pairs = [(a_mine, a_other), (b_mine, b_other)]
    moved(core, pairs, (a_low, a_high, b_low, b_high), copies, sems)


def early_outputs(
    c_mine, c_other, d_mine, d_other, late_rad, core,
    inputs, rad, trip_down, quad_down, tags,
    c_low, c_high, d_low, d_high, held_rad, sems,
):
    other_rad = pltpu.make_async_copy(late_rad, held_rad, sems.at[16])
    other_rad.start()
    copies = []
    for k, (low, high) in enumerate(((c_low, c_high), (d_low, d_high))):
        copies.append([(low, inputs.at[k, 0:384])])
        copies.append([(high.at[0:128], inputs.at[k, 384:512]), (high.at[128:256], rad.at[k])])
    copies[1].append((c_high.at[256:320], trip_down))
    copies[3].append((d_high.at[256:288], quad_down))
    pairs = [(c_mine, c_other), (d_mine, d_other)]
    moved(core, pairs, (c_low, c_high, d_low, d_high), copies, sems)
    other_rad.wait()
    last = pltpu.make_async_copy(held_rad, rad.at[2:5], sems.at[17])
    last.start()
    tags[...] = d_high[288:291, 0:256]
    last.wait()


def call(kernel, outs, args, scratch=(), micros=1, inside=None, room=63):
    spaces = [pl.ANY if inside is not None and i not in inside else pltpu.VMEM for i in range(len(outs))]
    space = pltpu.VMEM if inside is None else pl.ANY
    flops = int(micros * 1.15e9)
    return pl.pallas_call(
        kernel,
        out_shape=[jax.ShapeDtypeStruct(shape, F32) for shape in outs],
        in_specs=[pl.BlockSpec(memory_space=pltpu.SMEM if x.ndim == 1 else space) for x in args],
        out_specs=[pl.BlockSpec(memory_space=x) for x in spaces],
        scratch_shapes=list(scratch),
        compiler_params=pltpu.CompilerParams(vmem_limit_bytes=room * 1024 * 1024),
        cost_estimate=pl.CostEstimate(flops=flops, bytes_accessed=1 << 10, transcendentals=0),
    )(*args)


def per_device(
    hidden_atoms,
    edge_states,
    edge_vectors,
    atom_tags,
    send_list,
    sources,
    trip_slots,
    triplet_mask,
    quad_slots,
    quad_mask,
    edge_mask,
    w_inputs,
    w_radial,
    w_trip_down,
    triplet_bilinear_weight,
    w_trip_up,
    w_quad_down,
    w_quad_bil,
    w_quad_up,
    w_atom_edge,
    w_residual,
    w_edge_atom,
    w_atom_dense,
    tag_table,
    cot_atoms,
    cot_edges,
    cot_energy,
):
    planes = 2 if lax.axis_size("gz") == 2 else 3
    group = 3 * planes

    offset = jnp.maximum(sources - ATOMS, 0)
    block, border = offset // SEND, offset % SEND
    step_x, step_y, step_z = block // 9, block // 3 % 3, block % 3
    if planes == 2:
        step_z = jnp.clip(step_z - 1 + lax.axis_index("gz"), 0, 1)
    block = (step_y * 3 + step_x) * planes + step_z
    inside = sources < ATOMS
    even = jnp.where(inside, 3 * group * 8 + sources, block * 8 + border)
    src = jnp.stack([even, even + jnp.where(inside, ATOMS, SEND)])
    slots = jnp.concatenate([trip_slots, quad_slots], axis=1)
    masks = jnp.concatenate([triplet_mask, quad_mask], axis=1)
    marks = jnp.where(masks > 0, slots * BLOCK + (jnp.arange(EDGES) % BLOCK)[:, None], -1)
    mark_rows = marks.reshape(BLOCKS, BLOCK, 2 * PICKS).transpose(0, 2, 1)
    mark_rows = mark_rows.reshape(BLOCKS, 1, 2 * PICKS * BLOCK)
    trip_down_t, quad_down_t = w_trip_down.T, w_quad_down.T

    tag_row, send_row = atom_tags[None, :], send_list[None, :]
    payload, local, tagged, pre, downs, rads, radial, columns = call(
        start_kernel,
        [(PAIRS, 8, 128), (PAIRS, 16, 128), (8, 256), (2, EDGES, 512), (EDGES, 128), (5, EDGES, 512)]
        + [(EDGES, 128)] * 2,
        [edge_states, edge_vectors, edge_mask[None, :], hidden_atoms, tag_row, send_row, tag_table,
         w_inputs, w_radial, trip_down_t, quad_down_t],
        micros=5, room=58,
    )
    core = bit_value("gyl", 0)[None]
    before, here, after = with_halo(payload)
    (
        atoms_out, edges_out, energy_out, grad_edges, grad_tag,
        cosines, grad_sums, grad_src, keep_a, send_a, grad_rads, atom_rows, quad_up_grad,
    ) = call(
        main_kernel,
        [(8, 256), (EDGES, 512), (8, 256), (EDGES, 512), (8, 256)]
        + [(2 * BLOCKS, PICKS, 8, 128), (EDGES, 2048), (EDGES, 256), (896, 512), (896, 512)]
        + [(3, EDGES, 512), (8, 3328), (32, 512)],
        [before, here, after, local, tagged, edge_states, columns, rads, radial,
         src.T, slots, marks,
         triplet_bilinear_weight.T, w_trip_up, w_quad_bil.T, w_quad_up, w_atom_edge, w_residual,
         w_edge_atom, w_atom_dense, cot_atoms, cot_edges, cot_energy, core],
        scratch=[
            pltpu.VMEM((32, EDGES, 256), BF),
            pltpu.VMEM((EDGES, 2048), F32),
            pltpu.VMEM((128, 2048), BF),
            pltpu.VMEM((5, EDGES, 512), F32),
            pltpu.VMEM((EDGES, 128), F32),
            pltpu.VMEM((1792, 512), F32),
        ],
        micros=26, room=50,
    )
    chain = Chain()
    got_a = swap(send_a, "gyl", 0)
    keep_b, send_b = call(
        late_kernel,
        [(768, 512)] * 2,
        [grad_rads, radial, atom_rows, quad_up_grad, core],
        scratch=[pltpu.VMEM((1536, 512), F32)],
        micros=4, room=18,
    )
    late = reduction(chain, [keep_a, got_a], [keep_b, swap(send_b, "gyl", 0)], True, True)
    next(late)
    grad_sums = chain.after(grad_sums)
    back_before, back_here, back_after, back_local = call(
        scatter_kernel,
        [(group, 16, 8, 128)] * 3 + [(16, 16, 128)],
        [cosines, grad_sums, grad_src, src, mark_rows],
        scratch=[pltpu.VMEM((32, EDGES, 256), BF)],
        micros=13, room=18,
    )
    got = shifted(back_before, GY, -1, True), shifted(back_after, GY, 1, True)
    chain.step(back_local)
    next(late)
    got, value = chain.after((got, back_here))
    value = chain.step(value + got[0] + got[1])
    first_plane, middle, last_plane = value[:planes], value[planes : 2 * planes], value[2 * planes :]
    got = shifted(first_plane, "gx", -1, True), shifted(last_plane, "gx", 1, True)
    next(late)
    got, middle = chain.after((got, middle))
    value = chain.step(middle + got[0] + got[1])
    if planes == 2:
        top = lax.axis_index("gz") == 1
        mine = jnp.where(top, value[1], value[0])
        theirs = jnp.where(top, value[0], value[1])
        returned = mine + lax.ppermute(theirs, "gz", [(0, 1), (1, 0)])
    else:
        returned = value[1] + shifted(value[0], "gz", -1, False) + shifted(value[2], "gz", 1, False)
    returned = chain.after(returned)
    grad_atoms, grad_edges, keep_c, send_c, keep_d, send_d = call(
        finish_kernel,
        [(8, 256), (EDGES, 512)] + [(384, 512)] * 4,
        [back_local, returned, grad_edges, grad_tag, edge_states, radial, columns, pre, downs, rads,
         tag_row, send_row, w_inputs, trip_down_t, quad_down_t, core],
        scratch=[pltpu.VMEM((768, 512), F32)] * 2,
        micros=7, room=50,
    )
    next(late)
    send_c, send_d = chain.after((send_c, send_d))
    got_c, got_d = swap(send_c, "gyl", 0), swap(send_d, "gyl", 0)
    early = reduction(chain, [keep_c, got_c], [keep_d, got_d], firm_total=True)
    running = {"L": late, "E": early}
    done = {}

    def resume(name):
        if name in done:
            return
        try:
            next(running[name])
        except StopIteration as end:
            done[name] = end.value

    for name in "ELEELELEEELEL":
        resume(name)
    while "L" not in done:
        resume("L")
    (a_mine, a_other), (b_mine, b_other) = done["L"]
    g_res, g_ae, g_trip_bil, g_trip_up, g_quad_bil, g_quad_up, g_rad, g_ea, g_ad = call(
        late_outputs,
        [(2, 512, 512), (2, 256, 512), (64, 1024), (64, 512), (32, 1024), (32, 512), (3, 128, 512)]
        + [(2, 512, 256), (4, 256, 256)],
        [a_mine, a_other, b_mine, b_other, core],
        scratch=[pltpu.VMEM((896, 512), F32)] * 2
        + [pltpu.VMEM((768, 512), F32)] * 2
        + [pltpu.SemaphoreType.DMA((23,))],
        micros=0,
        room=12,
        inside=(),
    )
    chain.step(g_quad_up)
    while "E" not in done:
        resume("E")
    (c_mine, c_other), (d_mine, d_other) = done["E"]
    g_inputs, g_rad, g_trip_down, g_quad_down, g_tags = call(
        early_outputs,
        [(2, 512, 512), (5, 128, 512), (64, 512), (32, 512), (3, 256)],
        [c_mine, c_other, d_mine, d_other, g_rad, core],
        scratch=[pltpu.VMEM((384, 512), F32)] * 4
        + [pltpu.VMEM((3, 128, 512), F32), pltpu.SemaphoreType.DMA((18,))],
        micros=3,
        room=8,
        inside=(4,),
    )
    return (
        atoms_out,
        edges_out,
        energy_out,
        grad_atoms,
        grad_edges,
        g_inputs,
        g_rad,
        g_trip_down.T,
        g_trip_bil.T,
        g_trip_up,
        g_quad_down.T,
        g_quad_bil.T,
        g_quad_up,
        g_ae,
        g_res,
        g_ea,
        g_ad,
        g_tags,
    )


def solution(mesh):
    size = dict(mesh.shape)
    inner = Mesh(mesh.devices.reshape(size["gx"], size["gy"] // 2, 2, size["gz"]), ROWS)
    flat, columns, vector, whole = P(ROWS, None), P(None, ROWS), P(ROWS), P()
    placed = [flat, flat, columns] + [vector] * 3 + [flat] * 4 + [vector] + [whole] * 13 + [flat] * 3
    return jax.shard_map(
        per_device,
        mesh=inner,
        in_specs=tuple(placed),
        out_specs=tuple([flat] * 5 + [whole] * 13),
        check_vma=False,
    )
```

```python
import functools
import math

import jax
import jax.numpy as jnp
from jax import lax
from jax.experimental import pallas as pl
from jax.experimental.pallas import tpu as pltpu
from jax.sharding import Mesh
from jax.sharding import PartitionSpec as P

BF = jnp.bfloat16
F32 = jnp.float32
ROWS = ("gx", "gyh", "gyl", "gz")
GY = ("gyh", "gyl")
ATOMS, SEND, SLOTS, EDGES = 8, 4, 30, 240
ATOM_W, EDGE_W, TRIP_W, QUAD_W, RADIAL = 256, 512, 64, 32, 128
ANGLES, PICKS = 16, 8
PAIRS = 17
BLOCK = 16
BLOCKS = EDGES // BLOCK
root_half = 0.7071067811865476
NN = (((1,), (0,)), ((), ()))
NT = (((1,), (1,)), ((), ()))
TN = (((0,), (0,)), ((), ()))


def shifted(value, axis, steps, wrap):
    count = lax.axis_size(axis)
    pairs = [(i, (i + steps) % count) for i in range(count) if wrap or 0 <= i + steps < count]
    return lax.ppermute(value, axis, pairs)


def planes_of(value):
    if lax.axis_size("gz") == 2:
        other = lax.ppermute(value, "gz", [(0, 1), (1, 0)])
        top = lax.axis_index("gz") == 1
        return jnp.stack([jnp.where(top, other, value), jnp.where(top, value, other)])
    return jnp.stack([shifted(value, "gz", 1, False), value, shifted(value, "gz", -1, False)])


def with_halo(value):
    value = planes_of(value)
    value = jnp.concatenate([shifted(value, "gx", 1, True), value, shifted(value, "gx", -1, True)])
    return shifted(value, GY, 1, True), value, shifted(value, GY, -1, True)


def bits_of(axis):
    count = lax.axis_size(axis)
    return [(axis, b) for b in range(count.bit_length() - 1)]


def swap(value, axis, bit):
    count = lax.axis_size(axis)
    return lax.ppermute(value, axis, [(i, i ^ (1 << bit)) for i in range(count)])


def bit_value(axis, bit):
    return (lax.axis_index(axis) >> bit) & 1


def part(arrays, at, size):
    total = lax.dynamic_slice_in_dim(arrays[0], at, size)
    for x in arrays[1:]:
        total = total + lax.dynamic_slice_in_dim(x, at, size)
    return total


class Chain:
    def __init__(self):
        self.last = None

    def after(self, values):
        if self.last is not None:
            self.last, values = lax.optimization_barrier((self.last, values))
        return values

    def step(self, value):
        self.last = value
        return value

    def zero(self):
        first = jax.tree.leaves(self.last)[0]
        corner = first[(slice(0, 1),) * first.ndim].reshape(())
        return jnp.minimum(jnp.abs(corner), 0.0)


def halved(chain, arrays, axis, bit, tight=False):
    arrays = chain.after(arrays)
    half = arrays[0].shape[0] // 2
    one = bit_value(axis, bit)
    send = chain.step(part(arrays, (1 - one) * half, half))
    got = swap(send, axis, bit)
    send, arrays = lax.optimization_barrier((send, arrays))
    keep = part(arrays, one * half, half)
    if tight:
        chain.step((send, keep))
    return [keep, got]


def joined_halves(value, other, axis, bit):
    one = bit_value(axis, bit) == 1
    return jnp.concatenate([jnp.where(one, other, value), jnp.where(one, value, other)])


def reduction(chain, first, second, tight=False, firm=False, firm_total=False):
    across, along = bits_of("gz"), bits_of("gyh")
    lanes = [first, second]
    for turn, plan in enumerate(((across, along), (along, across))):
        for i in range(2):
            for axis, bit in plan[i]:
                lanes[i] = halved(chain, lanes[i], axis, bit, tight and turn == 1)
        yield
    sizes = [x[0].shape[0] for x in lanes]
    joint = [jnp.concatenate(pair) for pair in zip(*chain.after(lanes))]
    for axis, bit in bits_of("gx"):
        joint = halved(chain, joint, axis, bit, tight)
        yield
    joint = chain.after(joint)
    value = sum(joint[1:], joint[0])
    value = chain.step(value + chain.zero() if firm_total else value)
    for axis, bit in bits_of("gx")[::-1]:
        other = swap(value, axis, bit)
        yield
        value, other = chain.after((value, other))
        value = chain.step(joined_halves(value, other, axis, bit))
    values = [value[: sizes[0]], value[sizes[0] :]]
    for plan in ((along, across), (across, along)):
        for turn in range(max(len(across), len(along))):
            others = [None, None]
            for i in range(2):
                if turn < len(plan[i]):
                    others[i] = swap(values[i], *plan[i][::-1][turn])
            yield
            for i in range(2):
                if turn < len(plan[i]):
                    values[i], others[i] = chain.after((values[i], others[i]))
                    whole = joined_halves(values[i], others[i], *plan[i][::-1][turn])
                    if firm and plan[0] is across:
                        whole = whole + chain.zero()
                    values[i] = chain.step(whole)
    others = [swap(x, "gyl", 0) for x in values]
    yield
    values, others = chain.after((values, others))
    return [(value, chain.step(other)) for value, other in zip(values, others)]


def iota(shape, dim):
    return lax.broadcasted_iota(jnp.int32, shape, dim)


def dot(left, right, dims=NN):
    return lax.dot_general(left, right, dims, preferred_element_type=F32)


def halves(x):
    high = x.astype(BF)
    return high, (x - high.astype(F32)).astype(BF)


def stacked(x):
    high, low = halves(x)
    if x.shape[0] % 16 == 0:
        return jnp.concatenate([high, low], axis=0)
    return jnp.concatenate([high.astype(F32), low.astype(F32)], axis=0).astype(BF)


def folded(x):
    half = x.shape[0] // 2
    return x[:half] + x[half:]


def times(x, weight, dims=NN):
    return folded(dot(stacked(x), weight, dims))


def side_by_side(x):
    return jnp.concatenate(halves(x), axis=1)


def side_sum(x):
    half = x.shape[1] // 2
    return x[:, :half] + x[:, half:]


def weight_grad(x, y):
    x_high, x_low = halves(x)
    y_high, y_low = halves(y)
    left, right = [x_high, x_high, x_low], [y_high, y_low, y_high]
    if x.shape[0] % 16 == 0:
        return dot(jnp.concatenate(left, axis=0), jnp.concatenate(right, axis=0), TN)
    left = jnp.concatenate([p.astype(F32) for p in left], axis=0).astype(BF)
    right = jnp.concatenate([p.astype(F32) for p in right], axis=0).astype(BF)
    return dot(left, right, TN)


def onehot(hit):
    return jnp.where(hit, 1.0, 0.0).astype(BF)


def sigmoid(v):
    return 1.0 / (1.0 + jnp.exp(-v))


def act(v):
    return v * sigmoid(v) * (1.0 / 0.6)


def act_and_slope(v):
    s = sigmoid(v)
    return v * s * (1.0 / 0.6), s * (1.0 + v * (1.0 - s)) * (1.0 / 0.6)


def sin_pi(t):
    n = jnp.floor(t + 0.5)
    r = t - n
    odd = n - 2.0 * jnp.floor(n * 0.5)
    q = r * r
    total = jnp.zeros_like(r)
    for k in range(6, -1, -1):
        total = total * q + (-1.0) ** k * math.pi ** (2 * k + 1) / math.factorial(2 * k + 1)
    return total * r * (1.0 - 2.0 * odd)


def to_column(row):
    n = row.shape[1]
    same = iota((n, n), 0) == iota((n, n), 1)
    return jnp.sum(jnp.where(same, row, jnp.zeros_like(row)), axis=1, keepdims=True)


def send_column(send, rows):
    shape = (rows, SEND)
    hit = (iota(shape, 0) & (SEND - 1)) == iota(shape, 1)
    return jnp.sum(jnp.where(hit, send, 0), axis=1, keepdims=True)


def send_lanes(send):
    shape = (8, 128)
    hit = iota(shape, 0) == (iota(shape, 1) & (SEND - 1))
    return jnp.sum(jnp.where(hit, send_column(send, 8), 0), axis=0, keepdims=True)


def paid(row, send):
    edge = send * SLOTS + 2 * (row >> 3) + ((row >> 2) & 1)
    return jnp.where(row < 120, edge, -1)


def atom_of(edge):
    total = jnp.zeros_like(edge)
    for a in range(1, ATOMS):
        total = total + jnp.where(edge >= a * SLOTS, 1, 0)
    return total


def radial_of(length):
    x = length / 12.0
    x2 = x * x
    x4 = x2 * x2
    envelope = 1.0 - 28.0 * (x4 * x2) + 48.0 * (x4 * x2 * x) - 21.0 * (x4 * x4)
    orders = (iota((1, RADIAL), 1) + 1).astype(F32)
    return envelope * sin_pi(x * orders) / x


def geometry(unit):
    own = atom_of(iota((8, EDGES), 1)) == iota((8, EDGES), 0)
    edge = iota((EDGES, 128), 0)
    slot = edge - atom_of(edge) * SLOTS
    total = jnp.zeros((24, 128), F32)
    for k in range(3):
        x = jnp.where(own, unit[k : k + 1, :], 0.0)
        high = x.astype(BF).astype(F32)
        mid = (x - high).astype(BF).astype(F32)
        parts = jnp.concatenate([high, mid, x - high - mid], axis=0).astype(BF)
        total = total + dot(parts, onehot(iota((EDGES, 128), 1) == slot + 32 * k))
    return total[0:8] + total[8:16] + total[16:24]


def local_rows(index):
    return (index & 7) * SLOTS + 2 * (index >> 4) + ((index >> 3) & 1)


def start_kernel(
    edge, vec, mask, hidden, tag_row, send_row, table, w_in, w_rad, w_trip, w_quad,
    payload, local, tagged, pre, downs, rads, radial_out, columns,
):
    vectors = vec[...]
    length = jnp.sqrt(jnp.sum(vectors * vectors, axis=0, keepdims=True))
    unit = vectors / length
    geo = geometry(unit)
    live = to_column(jnp.where(mask[...] > 0, 1.0, 0.0))
    parts = [live] + [to_column(unit[k : k + 1, :]) for k in range(3)]
    columns[...] = jnp.concatenate(parts + [jnp.zeros((EDGES, 124), F32)], axis=1)
    send = send_column(send_row[...], 8)
    pay = paid(iota((128, 1), 0), send_column(send_row[...], 128))
    tags = to_column(tag_row[...])
    radial = radial_of(to_column(length))
    radial_out[...] = radial
    split = stacked(radial)
    for k in range(5):
        rads[k] = folded(dot(split, w_rad[k]))
    split = stacked(edge[...])
    pre[0] = folded(dot(split, w_in[0]))
    pre[1] = folded(dot(split, w_in[1]))
    trip_pre = times(act(pre[0]) * rads[0], w_trip[...], NT)
    quad_pre = times(act(pre[1]) * rads[1], w_quad[...], NT)
    downs[...] = jnp.concatenate([trip_pre, quad_pre, jnp.zeros((EDGES, 32), F32)], axis=1)
    trip = act(trip_pre) * live
    quad = act(quad_pre) * live
    rows = jnp.concatenate([trip, quad * radial[:, 0:1], quad * radial[:, 1:2]], axis=1)
    rows = side_by_side(rows)
    shape = (EDGES, EDGES)
    place = onehot(local_rows(iota(shape, 0)) == iota(shape, 1))
    local[0:15] = side_sum(dot(place, rows)).reshape(15, 16, 128)
    place = onehot(pay == iota((128, EDGES), 1))
    payload[0:16] = side_sum(dot(place, rows)).reshape(16, 8, 128)
    tag = hidden[...]
    for t in range(3):
        tag = tag + jnp.where(tags == t, table[t : t + 1, :].astype(F32), 0.0)
    tagged[...] = tag
    local[15] = jnp.concatenate([tag[:, :128], tag[:, 128:]], axis=0)
    local[16] = jnp.concatenate([geo, jnp.zeros((8, 128), F32)], axis=0)
    both = jnp.concatenate([tag, geo], axis=1)
    sent = jnp.zeros((8, 384), F32)
    for a in range(ATOMS):
        sent = sent + jnp.where(send == a, both[a : a + 1, :], 0.0)
    payload[15] = jnp.where(iota((8, 128), 0) < 4, sent[:, :128], sent[:, 128:256])
    payload[16] = sent[:, 256:]


def split_cores(core, whole, keep, send):
    half = whole.shape[0] // 2
    upper = core[0] == 1
    low, high = whole[:half], whole[half:]
    keep[...] = jnp.where(upper, high, low)
    send[...] = jnp.where(upper, low, high)


def segments(shape, edge_dim, atom_dim):
    edge, atom = iota(shape, edge_dim), iota(shape, atom_dim) & 7
    return onehot((edge >= atom * SLOTS) & (edge < atom * SLOTS + SLOTS))


def lead(k):
    return math.comb(2 * k, k) / 2.0**k


def ratio(k):
    return k * k / (4.0 * k * k - 1.0)


def monic(cosine):
    before, now = jnp.ones_like(cosine), cosine
    yield before
    yield now
    for k in range(1, ANGLES - 1):
        before, now = now, cosine * now - ratio(k) * before
        yield now


def looped(count, step, body):
    def turn(t, carry):
        for i in range(step):
            body(t * step + i)
        return carry

    lax.fori_loop(0, count // step, turn, 0)


def main_kernel(
    halo_before, halo_here, halo_after, local, tagged, edge, columns, rads, radial,
    src_cols, slots, marks,
    trip_bil, trip_up, quad_bil, quad_up, w_ae, w_res, w_ea, w_ad,
    cot_atoms, cot_edges, cot_energy, core,
    atoms_out, edges_out, energy_out, grad_edges, grad_tag,
    cosines, grad_sums, grad_src, keep, send, grad_rads, atom_rows, quad_up_grad,
    table, sums, weight, kept, cos_table, first,
):
    live = columns[:, 0:1]
    halos = (halo_before, halo_here, halo_after)
    group = halo_here.shape[0] * 8
    depth = 3 * group + 16
    lanes = iota((EDGES, depth), 1)
    place = jnp.concatenate(
        [onehot(src_cols[:, 0:1] == lanes), onehot(src_cols[:, 1:2] == lanes)], axis=0
    )

    def rows_at(p):
        parts = [h[:, p].reshape(group, 128) for h in halos]
        return jnp.concatenate(parts + [local[p]], axis=0)

    def gather_pair(p):
        got = dot(place, side_by_side(rows_at(p))).astype(BF)
        table[2 * p] = got[:EDGES]
        table[2 * p + 1] = got[EDGES:]

    looped(16, 4, gather_pair)

    rows = rows_at(16)
    high, low = halves(rows)
    rest = (rows - high.astype(F32) - low.astype(F32)).astype(BF)
    got = dot(place[:EDGES], jnp.concatenate([high, low, rest], axis=1))
    got = got[:, :128] + got[:, 128:256] + got[:, 256:]
    cos_table[...] = -(
        columns[:, 1:2] * got
        + columns[:, 2:3] * pltpu.roll(got, 96, 1)
        + columns[:, 3:4] * pltpu.roll(got, 64, 1)
    )

    for k in range(ANGLES):
        top = trip_bil[:, k * 64 : k * 64 + 64].astype(F32)
        top = jnp.concatenate([top, jnp.zeros((64, 64), F32)], axis=1)
        low_left = quad_bil[:, k * 32 : k * 32 + 32].astype(F32)
        low_right = quad_bil[:, 512 + k * 32 : 544 + k * 32].astype(F32)
        bottom = jnp.concatenate([jnp.zeros((32, 64), F32), low_left, low_right], axis=1)
        piece = jnp.concatenate([top, bottom, jnp.zeros((32, 128), F32)], axis=0)
        weight[:, k * 128 : (k + 1) * 128] = piece.astype(BF)

    trip_lanes = iota((128, 128), 1) < TRIP_W
    scale = 1.0 / math.sqrt(PICKS)

    def basis_block(b):
        at = pl.multiple_of(b * BLOCK, BLOCK)
        own = pl.ds(at, BLOCK)
        wide = iota((BLOCK, 512), 1)
        mark = marks[own, :]
        hits = [jnp.where(mark[:, t : t + 1] == wide, 1.0, 0.0) for t in range(2 * PICKS)]
        hits = jnp.concatenate(hits, axis=0).astype(BF)
        got = side_sum(dot(hits, table[:, own, :].reshape(512, 256)))
        picked = jnp.where(trip_lanes, got[:128], got[128:])
        picked = picked.reshape(PICKS, BLOCK, 128)
        cos_here = cos_table[own, :]
        slot = slots[own, :]
        low_lanes = iota((BLOCK, 128), 1) < TRIP_W
        for h in range(2):
            rows = slice(8 * h, 8 * h + 8)
            cos = []
            for j in range(PICKS):
                index = jnp.where(
                    low_lanes[rows], slot[rows, j : j + 1], slot[rows, PICKS + j : PICKS + j + 1]
                )
                cos.append(jnp.take_along_axis(cos_here[rows], index, axis=1))
            cos = jnp.stack(cos)
            cosines[2 * b + h] = cos
            values = picked[:, rows]
            for k, poly in enumerate(monic(cos)):
                total = jnp.sum(poly * values, axis=0) * (lead(k) * scale)
                sums[pl.ds(pl.multiple_of(at + 8 * h, 8), 8), k * 128 : (k + 1) * 128] = total

    looped(BLOCKS, 3, basis_block)

    down = times(sums[...], weight[...], NT)
    down_act, down_slope = act_and_slope(down)
    trip_h, quad_h = down_act[:, :64], down_act[:, 64:96]
    trip_pre = times(trip_h, trip_up[...])
    quad_pre = times(quad_h, quad_up[...])
    src = jnp.concatenate(
        [side_sum(table[30].astype(F32)), side_sum(table[31].astype(F32))], axis=1
    )
    target = times(tagged[...], w_ae[1])
    spread = segments((EDGES, 16), 0, 1)
    gathers = segments((8, EDGES), 1, 0)

    def to_edges(x):
        return dot(spread, stacked(x))

    def to_atoms(x):
        return side_sum(dot(gathers, side_by_side(x)))

    atom_pre = times(src, w_ae[0]) + to_edges(target)
    atom_act, atom_slope = act_and_slope(atom_pre)
    trip_act, trip_slope = act_and_slope(trip_pre)
    quad_act, quad_slope = act_and_slope(quad_pre)
    merged = (edge[...] + trip_act + quad_act + atom_act * rads[2]) * 0.5
    kept[0] = merged
    first_act, first_slope = act_and_slope(times(merged, w_res[0]))
    kept[1] = first_act
    second_act, second_slope = act_and_slope(times(first_act, w_res[1]))
    new_edges = (merged + second_act) * root_half
    edges_out[...] = new_edges
    weighted = new_edges * live
    root_slots = 1.0 / math.sqrt(SLOTS)
    gathered = to_atoms(weighted * rads[3]) * root_slots
    summary = to_atoms(weighted * rads[4]) * root_slots
    gate_act, gate_slope = act_and_slope(times(gathered, w_ea[0]))
    updated = (tagged[...] + gate_act) * root_half
    a0_act, a0_slope = act_and_slope(times(updated, w_ad[0]))
    a1_act, a1_slope = act_and_slope(times(a0_act, w_ad[1]))
    new_atoms = (updated + a1_act) * root_half
    atoms_out[...] = new_atoms
    e_act, e_slope = act_and_slope(times(summary, w_ea[1]) + times(new_atoms, w_ad[2]))
    out_act, out_slope = act_and_slope(times(e_act, w_ad[3]))
    energy_out[...] = out_act

    d_out = cot_energy[...] * out_slope
    d_e = times(d_out, w_ad[3], NT) * e_slope
    d_summary = times(d_e, w_ea[1], NT)
    d_atoms = (cot_atoms[...] + times(d_e, w_ad[2], NT)) * root_half
    d_a1 = d_atoms * a1_slope
    d_a0 = times(d_a1, w_ad[1], NT) * a0_slope
    d_updated = (d_atoms + times(d_a0, w_ad[0], NT)) * root_half
    d_gate = d_updated * gate_slope
    d_gathered = times(d_gate, w_ea[0], NT)

    d_gathered = to_edges(d_gathered * root_slots)
    d_summary = to_edges(d_summary * root_slots)
    grad_rads[1] = weighted * d_gathered
    grad_rads[2] = weighted * d_summary
    d_new = cot_edges[...] + live * (d_gathered * rads[3] + d_summary * rads[4])
    d_new = d_new * root_half
    d_second = d_new * second_slope
    kept[3] = d_second
    d_first = times(d_second, w_res[1], NT) * first_slope
    kept[2] = d_first
    d_merged = (d_new + times(d_first, w_res[0], NT)) * 0.5
    grad_edges[...] = d_merged
    grad_rads[0] = d_merged * atom_act
    d_atom = d_merged * rads[2] * atom_slope
    kept[4] = d_atom
    d_trip = d_merged * trip_slope
    d_quad = d_merged * quad_slope
    d_target = to_atoms(d_atom)
    grad_tag[...] = d_updated + times(d_target, w_ae[1], NT)
    d_down = jnp.concatenate(
        [times(d_trip, trip_up[...], NT), times(d_quad, quad_up[...], NT), jnp.zeros((EDGES, 32), F32)],
        axis=1,
    )
    d_down = d_down * down_slope
    grad_src[...] = times(d_atom, w_ae[0], NT)

    first[0:512] = weight_grad(kept[0], kept[2])
    first[512:768] = weight_grad(src, kept[4])
    first[896:1408] = weight_grad(kept[1], kept[3])
    first[1408:1664] = weight_grad(tagged[...], d_target)
    bil = weight_grad(d_down, sums[...])
    for m in range(8):
        tile = [bil[0:64, k * 128 : k * 128 + 64] for k in (2 * m, 2 * m + 1)]
        row = 768 + 64 * (m // 4)
        first[row : row + 64, (m % 4) * 128 : (m % 4 + 1) * 128] = jnp.concatenate(tile, axis=1)
    for half in range(2):
        for m in range(4):
            at = 64 + 32 * half
            tile = [bil[64:96, k * 128 + at : k * 128 + at + 32] for k in range(4 * m, 4 * m + 4)]
            row = 1728 + 32 * half
            first[row : row + 32, m * 128 : (m + 1) * 128] = jnp.concatenate(tile, axis=1)
    first[1664:1728] = weight_grad(down_act, d_trip)[:64]
    quad_up_grad[...] = weight_grad(down_act, d_quad)[64:96]
    atom_rows[...] = jnp.concatenate(
        [gathered, summary, updated, a0_act, new_atoms, e_act, d_a0, d_a1, d_e, d_out, d_gate], axis=1
    )
    split_cores(core, first, keep, send)
    grad_sums[...] = times(d_down, weight[...])


def late_kernel(grad_rads, radial, atom_rows, quad_up_grad, core, keep, send, second):
    atoms = atom_rows[...]
    gathered, summary = atoms[:, :512], atoms[:, 512:1024]
    updated, a0_act, new_atoms, e_act, d_a0, d_a1, d_e, d_out, d_gate = [
        atoms[:, at : at + 256] for at in range(1024, 3328, 256)
    ]
    second[0:512, 0:256] = weight_grad(gathered, d_gate)
    second[0:512, 256:512] = weight_grad(summary, d_e)
    second[512:768, 0:256] = weight_grad(updated, d_a0)
    second[512:768, 256:512] = weight_grad(a0_act, d_a1)
    second[768:1024, 0:256] = weight_grad(new_atoms, d_e)
    second[768:1024, 256:512] = weight_grad(e_act, d_out)
    for k in range(3):
        second[1024 + 128 * k : 1152 + 128 * k] = weight_grad(radial[...], grad_rads[k])
    second[1408:1440] = quad_up_grad[...]
    second[1440:1536] = jnp.zeros((96, 512), F32)
    split_cores(core, second, keep, send)


def scatter_kernel(
    cosines, sums, grad_src, src_rows, mark_rows,
    back_before, back_here, back_after, back_local,
    table,
):
    group = back_here.shape[0] * 8
    depth = 3 * group + 16
    trip_lanes = iota((128, 128), 1) < TRIP_W
    scale = 1.0 / math.sqrt(PICKS)

    def basis_back(b):
        at = pl.multiple_of(b * BLOCK, BLOCK)
        own = pl.ds(at, BLOCK)
        parts = []
        for h in range(2):
            cos = cosines[2 * b + h]
            own_rows = pl.ds(pl.multiple_of(at + 8 * h, 8), 8)
            after = total = None
            for k in range(ANGLES - 1, -1, -1):
                term = sums[own_rows, k * 128 : (k + 1) * 128] * (lead(k) * scale)
                if total is None:
                    after, total = None, jnp.broadcast_to(term, cos.shape)
                elif after is None:
                    after, total = total, term + cos * total
                else:
                    after, total = total, term + cos * total - ratio(k + 1) * after
            parts.append(total)
        grad = jnp.concatenate(parts, axis=1).reshape(128, 128)
        grad = jnp.concatenate(
            [jnp.where(trip_lanes, grad, 0.0), jnp.where(trip_lanes, 0.0, grad)], axis=0
        )
        hits = onehot(mark_rows[b] == iota((512, 256), 0))
        got = side_by_side(side_sum(dot(hits, side_by_side(grad))))
        table[:, own, :] = got.reshape(32, BLOCK, 256)

    looped(BLOCKS, 3, basis_back)
    table[30] = side_by_side(grad_src[:, :128])
    table[31] = side_by_side(grad_src[:, 128:])
    rows = iota((depth, EDGES), 0)
    place_even = onehot(src_rows[0:1, :] == rows)
    place_odd = onehot(src_rows[1:2, :] == rows)

    def scatter_pair(p):
        got = side_sum(dot(place_even, table[2 * p]) + dot(place_odd, table[2 * p + 1]))
        for i, back in enumerate((back_before, back_here, back_after)):
            back[:, p] = got[i * group : (i + 1) * group].reshape(group // 8, 8, 128)
        back_local[p] = got[3 * group :]

    looped(16, 4, scatter_pair)


def finish_kernel(
    back_local, returned, grad_late, tag_late, edge, radial, columns, pre, downs, rads, tag_row, send_row,
    w_in, w_trip, w_quad, core,
    grad_atoms, grad_edges, keep_first, send_first, keep_second, send_second,
    first, second,
):
    shape = (EDGES, 256)
    lane = iota(shape, 1)
    place = onehot((local_rows(lane) == iota(shape, 0)) & (lane < EDGES))
    rows = dot(place, side_by_side(back_local[...].reshape(256, 128)))
    pay = paid(iota((1, 128), 1), send_lanes(send_row[...]))
    place = onehot(pay == iota((EDGES, 128), 0))
    send = send_column(send_row[...], 8)
    tags = to_column(tag_row[...])
    rows = side_sum(rows + dot(place, side_by_side(returned[...].reshape(128, 128))))
    back = returned[15]
    tag = tag_late[...] + jnp.concatenate([back_local[15, 0:8], back_local[15, 8:16]], axis=1)
    atom = iota((8, 1), 0)
    for r in range(SEND):
        piece = jnp.concatenate([back[r : r + 1], back[4 + r : 5 + r]], axis=1)
        tag = tag + jnp.where(send[r : r + 1, :] == atom, piece, 0.0)
    grad_atoms[...] = tag
    table = [
        jnp.sum(jnp.where(tags == t, tag, 0.0), axis=0, keepdims=True) for t in range(3)
    ]
    table = jnp.concatenate(table + [jnp.zeros((29, ATOM_W), F32)], axis=0)
    d_trip = rows[:, :64]
    d_quad = rows[:, 64:96] * radial[:, 0:1] + rows[:, 96:128] * radial[:, 1:2]
    total = grad_late[...]
    for k, (d_row, down, weight, out) in enumerate(
        ((d_trip, slice(0, 64), w_trip, first), (d_quad, slice(64, 96), w_quad, second))
    ):
        d_down = d_row * columns[:, 0:1] * act_and_slope(downs[:, down])[1]
        value, slope = act_and_slope(pre[k])
        d_start = times(d_down, weight[...])
        d_pre = d_start * rads[k] * slope
        total = total + times(d_pre, w_in[k], NT)
        out[0:512] = weight_grad(edge[...], d_pre)
        out[512:640] = weight_grad(radial[...], d_start * value)
        down_grad = weight_grad(d_down, value * rads[k])
        if k == 0:
            out[640:704] = down_grad
            out[704:768] = jnp.zeros((64, 512), F32)
        else:
            out[640:672] = down_grad
            out[672:704, 0:256] = table
            out[672:704, 256:512] = jnp.zeros((32, 256), F32)
            out[704:768] = jnp.zeros((64, 512), F32)
    grad_edges[...] = total
    split_cores(core, first, keep_first, send_first)
    split_cores(core, second, keep_second, send_second)


def moved(core, pairs, held, copies, sems):
    arriving = [pltpu.make_async_copy(pair[i % 2], held[i], sems.at[i]) for i, pair in zip(range(len(held)), [p for p in pairs for _ in range(2)])]
    for upper in (0, 1):

        @pl.when(core[0] == upper)
        def _():
            for i in range(len(held)):
                pltpu.make_async_copy(pairs[i // 2][i % 2 ^ upper], held[i], sems.at[i]).start()

    leaving, at = [], len(held)
    for i, copy in enumerate(arriving):
        copy.wait()
        for source, target in copies[i]:
            leaving.append(pltpu.make_async_copy(source, target, sems.at[at]))
            leaving[-1].start()
            at += 1
    for x in leaving:
        x.wait()


def late_outputs(
    a_mine, a_other, b_mine, b_other, core,
    res, ae, trip_bil, trip_up, quad_bil, quad_up, rad, ea, ad,
    a_low, a_high, b_low, b_high, sems,
):
    left, right = slice(0, 256), slice(256, 512)
    copies = [
        [
            (a_low.at[0:512], res.at[0]),
            (a_low.at[512:768], ae.at[0]),
            (a_low.at[768:832], trip_bil.at[:, 0:512]),
            (a_low.at[832:896], trip_bil.at[:, 512:1024]),
        ],
        [
            (a_high.at[0:512], res.at[1]),
            (a_high.at[512:768], ae.at[1]),
            (a_high.at[768:832], trip_up),
            (a_high.at[832:864], quad_bil.at[:, 0:512]),
            (a_high.at[864:896], quad_bil.at[:, 512:1024]),
        ],
        [
            (b_low.at[0:512, left], ea.at[0]),
            (b_low.at[0:512, right], ea.at[1]),
            (b_low.at[512:768, left], ad.at[0]),
            (b_low.at[512:768, right], ad.at[1]),
        ],
        [
            (b_high.at[0:256, left], ad.at[2]),
            (b_high.at[0:256, right], ad.at[3]),
            (b_high.at[640:672], quad_up),
        ]
        + [(b_high.at[256 + 128 * k : 384 + 128 * k], rad.at[k]) for k in range(3)],
    ]
    pairs = [(a_mine, a_other), (b_mine, b_other)]
    moved(core, pairs, (a_low, a_high, b_low, b_high), copies, sems)


def early_outputs(
    c_mine, c_other, d_mine, d_other, late_rad, core,
    inputs, rad, trip_down, quad_down, tags,
    c_low, c_high, d_low, d_high, held_rad, sems,
):
    other_rad = pltpu.make_async_copy(late_rad, held_rad, sems.at[16])
    other_rad.start()
    copies = []
    for k, (low, high) in enumerate(((c_low, c_high), (d_low, d_high))):
        copies.append([(low, inputs.at[k, 0:384])])
        copies.append([(high.at[0:128], inputs.at[k, 384:512]), (high.at[128:256], rad.at[k])])
    copies[1].append((c_high.at[256:320], trip_down))
    copies[3].append((d_high.at[256:288], quad_down))
    pairs = [(c_mine, c_other), (d_mine, d_other)]
    moved(core, pairs, (c_low, c_high, d_low, d_high), copies, sems)
    other_rad.wait()
    last = pltpu.make_async_copy(held_rad, rad.at[2:5], sems.at[17])
    last.start()
    tags[...] = d_high[288:291, 0:256]
    last.wait()


def call(kernel, outs, args, scratch=(), micros=1, inside=None, room=63):
    spaces = [pl.ANY if inside is not None and i not in inside else pltpu.VMEM for i in range(len(outs))]
    space = pltpu.VMEM if inside is None else pl.ANY
    flops = int(micros * 1.15e9)
    return pl.pallas_call(
        kernel,
        out_shape=[jax.ShapeDtypeStruct(shape, F32) for shape in outs],
        in_specs=[pl.BlockSpec(memory_space=pltpu.SMEM if x.ndim == 1 else space) for x in args],
        out_specs=[pl.BlockSpec(memory_space=x) for x in spaces],
        scratch_shapes=list(scratch),
        compiler_params=pltpu.CompilerParams(vmem_limit_bytes=room * 1024 * 1024),
        cost_estimate=pl.CostEstimate(flops=flops, bytes_accessed=1 << 10, transcendentals=0),
    )(*args)


def per_device(
    hidden_atoms,
    edge_states,
    edge_vectors,
    atom_tags,
    send_list,
    sources,
    trip_slots,
    triplet_mask,
    quad_slots,
    quad_mask,
    edge_mask,
    w_inputs,
    w_radial,
    w_trip_down,
    triplet_bilinear_weight,
    w_trip_up,
    w_quad_down,
    w_quad_bil,
    w_quad_up,
    w_atom_edge,
    w_residual,
    w_edge_atom,
    w_atom_dense,
    tag_table,
    cot_atoms,
    cot_edges,
    cot_energy,
):
    planes = 2 if lax.axis_size("gz") == 2 else 3
    group = 3 * planes

    offset = jnp.maximum(sources - ATOMS, 0)
    block, border = offset // SEND, offset % SEND
    step_x, step_y, step_z = block // 9, block // 3 % 3, block % 3
    if planes == 2:
        step_z = jnp.clip(step_z - 1 + lax.axis_index("gz"), 0, 1)
    block = (step_y * 3 + step_x) * planes + step_z
    inside = sources < ATOMS
    even = jnp.where(inside, 3 * group * 8 + sources, block * 8 + border)
    src = jnp.stack([even, even + jnp.where(inside, ATOMS, SEND)])
    slots = jnp.concatenate([trip_slots, quad_slots], axis=1)
    masks = jnp.concatenate([triplet_mask, quad_mask], axis=1)
    marks = jnp.where(masks > 0, slots * BLOCK + (jnp.arange(EDGES) % BLOCK)[:, None], -1)
    mark_rows = marks.reshape(BLOCKS, BLOCK, 2 * PICKS).transpose(0, 2, 1)
    mark_rows = mark_rows.reshape(BLOCKS, 1, 2 * PICKS * BLOCK)
    trip_down_t, quad_down_t = w_trip_down.T, w_quad_down.T

    tag_row, send_row = atom_tags[None, :], send_list[None, :]
    payload, local, tagged, pre, downs, rads, radial, columns = call(
        start_kernel,
        [(PAIRS, 8, 128), (PAIRS, 16, 128), (8, 256), (2, EDGES, 512), (EDGES, 128), (5, EDGES, 512)]
        + [(EDGES, 128)] * 2,
        [edge_states, edge_vectors, edge_mask[None, :], hidden_atoms, tag_row, send_row, tag_table,
         w_inputs, w_radial, trip_down_t, quad_down_t],
        micros=5, room=58,
    )
    core = bit_value("gyl", 0)[None]
    before, here, after = with_halo(payload)
    (
        atoms_out, edges_out, energy_out, grad_edges, grad_tag,
        cosines, grad_sums, grad_src, keep_a, send_a, grad_rads, atom_rows, quad_up_grad,
    ) = call(
        main_kernel,
        [(8, 256), (EDGES, 512), (8, 256), (EDGES, 512), (8, 256)]
        + [(2 * BLOCKS, PICKS, 8, 128), (EDGES, 2048), (EDGES, 256), (896, 512), (896, 512)]
        + [(3, EDGES, 512), (8, 3328), (32, 512)],
        [before, here, after, local, tagged, edge_states, columns, rads, radial,
         src.T, slots, marks,
         triplet_bilinear_weight.T, w_trip_up, w_quad_bil.T, w_quad_up, w_atom_edge, w_residual,
         w_edge_atom, w_atom_dense, cot_atoms, cot_edges, cot_energy, core],
        scratch=[
            pltpu.VMEM((32, EDGES, 256), BF),
            pltpu.VMEM((EDGES, 2048), F32),
            pltpu.VMEM((128, 2048), BF),
            pltpu.VMEM((5, EDGES, 512), F32),
            pltpu.VMEM((EDGES, 128), F32),
            pltpu.VMEM((1792, 512), F32),
        ],
        micros=26, room=50,
    )
    chain = Chain()
    got_a = swap(send_a, "gyl", 0)
    keep_b, send_b = call(
        late_kernel,
        [(768, 512)] * 2,
        [grad_rads, radial, atom_rows, quad_up_grad, core],
        scratch=[pltpu.VMEM((1536, 512), F32)],
        micros=4, room=18,
    )
    late = reduction(chain, [keep_a, got_a], [keep_b, swap(send_b, "gyl", 0)], True, True)
    next(late)
    grad_sums = chain.after(grad_sums)
    back_before, back_here, back_after, back_local = call(
        scatter_kernel,
        [(group, 16, 8, 128)] * 3 + [(16, 16, 128)],
        [cosines, grad_sums, grad_src, src, mark_rows],
        scratch=[pltpu.VMEM((32, EDGES, 256), BF)],
        micros=13, room=18,
    )
    got = shifted(back_before, GY, -1, True), shifted(back_after, GY, 1, True)
    chain.step(back_local)
    next(late)
    got, value = chain.after((got, back_here))
    value = chain.step(value + got[0] + got[1])
    first_plane, middle, last_plane = value[:planes], value[planes : 2 * planes], value[2 * planes :]
    got = shifted(first_plane, "gx", -1, True), shifted(last_plane, "gx", 1, True)
    next(late)
    got, middle = chain.after((got, middle))
    value = chain.step(middle + got[0] + got[1])
    if planes == 2:
        top = lax.axis_index("gz") == 1
        mine = jnp.where(top, value[1], value[0])
        theirs = jnp.where(top, value[0], value[1])
        returned = mine + lax.ppermute(theirs, "gz", [(0, 1), (1, 0)])
    else:
        returned = value[1] + shifted(value[0], "gz", -1, False) + shifted(value[2], "gz", 1, False)
    returned = chain.after(returned)
    grad_atoms, grad_edges, keep_c, send_c, keep_d, send_d = call(
        finish_kernel,
        [(8, 256), (EDGES, 512)] + [(384, 512)] * 4,
        [back_local, returned, grad_edges, grad_tag, edge_states, radial, columns, pre, downs, rads,
         tag_row, send_row, w_inputs, trip_down_t, quad_down_t, core],
        scratch=[pltpu.VMEM((768, 512), F32)] * 2,
        micros=7, room=58,
    )
    next(late)
    send_c, send_d = chain.after((send_c, send_d))
    got_c, got_d = swap(send_c, "gyl", 0), swap(send_d, "gyl", 0)
    early = reduction(chain, [keep_c, got_c], [keep_d, got_d], firm_total=True)
    running = {"L": late, "E": early}
    done = {}

    def resume(name):
        if name in done:
            return
        try:
            next(running[name])
        except StopIteration as end:
            done[name] = end.value

    for name in "ELEELELEEELEL":
        resume(name)
    while "L" not in done:
        resume("L")
    (a_mine, a_other), (b_mine, b_other) = done["L"]
    g_res, g_ae, g_trip_bil, g_trip_up, g_quad_bil, g_quad_up, g_rad, g_ea, g_ad = call(
        late_outputs,
        [(2, 512, 512), (2, 256, 512), (64, 1024), (64, 512), (32, 1024), (32, 512), (3, 128, 512)]
        + [(2, 512, 256), (4, 256, 256)],
        [a_mine, a_other, b_mine, b_other, core],
        scratch=[pltpu.VMEM((896, 512), F32)] * 2
        + [pltpu.VMEM((768, 512), F32)] * 2
        + [pltpu.SemaphoreType.DMA((23,))],
        micros=0,
        room=12,
        inside=(),
    )
    chain.step(g_quad_up)
    while "E" not in done:
        resume("E")
    (c_mine, c_other), (d_mine, d_other) = done["E"]
    g_inputs, g_rad, g_trip_down, g_quad_down, g_tags = call(
        early_outputs,
        [(2, 512, 512), (5, 128, 512), (64, 512), (32, 512), (3, 256)],
        [c_mine, c_other, d_mine, d_other, g_rad, core],
        scratch=[pltpu.VMEM((384, 512), F32)] * 4
        + [pltpu.VMEM((3, 128, 512), F32), pltpu.SemaphoreType.DMA((18,))],
        micros=3,
        room=8,
        inside=(4,),
    )
    return (
        atoms_out,
        edges_out,
        energy_out,
        grad_atoms,
        grad_edges,
        g_inputs,
        g_rad,
        g_trip_down.T,
        g_trip_bil.T,
        g_trip_up,
        g_quad_down.T,
        g_quad_bil.T,
        g_quad_up,
        g_ae,
        g_res,
        g_ea,
        g_ad,
        g_tags,
    )


def solution(mesh):
    size = dict(mesh.shape)
    inner = Mesh(mesh.devices.reshape(size["gx"], size["gy"] // 2, 2, size["gz"]), ROWS)
    flat, columns, vector, whole = P(ROWS, None), P(None, ROWS), P(ROWS), P()
    placed = [flat, flat, columns] + [vector] * 3 + [flat] * 4 + [vector] + [whole] * 13 + [flat] * 3
    return jax.shard_map(
        per_device,
        mesh=inner,
        in_specs=tuple(placed),
        out_specs=tuple([flat] * 5 + [whole] * 13),
        check_vma=False,
    )
```

```python
import functools
import math

import jax
import jax.numpy as jnp
from jax import lax
from jax.experimental import pallas as pl
from jax.experimental.pallas import tpu as pltpu
from jax.sharding import Mesh
from jax.sharding import PartitionSpec as P

BF = jnp.bfloat16
F32 = jnp.float32
ROWS = ("gx", "gyh", "gyl", "gz")
GY = ("gyh", "gyl")
ATOMS, SEND, SLOTS, EDGES = 8, 4, 30, 240
ATOM_W, EDGE_W, TRIP_W, QUAD_W, RADIAL = 256, 512, 64, 32, 128
ANGLES, PICKS = 16, 8
PAIRS = 17
BLOCK = 16
BLOCKS = EDGES // BLOCK
root_half = 0.7071067811865476
NN = (((1,), (0,)), ((), ()))
NT = (((1,), (1,)), ((), ()))
TN = (((0,), (0,)), ((), ()))


def shifted(value, axis, steps, wrap):
    count = lax.axis_size(axis)
    pairs = [(i, (i + steps) % count) for i in range(count) if wrap or 0 <= i + steps < count]
    return lax.ppermute(value, axis, pairs)


def planes_of(value):
    if lax.axis_size("gz") == 2:
        other = lax.ppermute(value, "gz", [(0, 1), (1, 0)])
        top = lax.axis_index("gz") == 1
        return jnp.stack([jnp.where(top, other, value), jnp.where(top, value, other)])
    return jnp.stack([shifted(value, "gz", 1, False), value, shifted(value, "gz", -1, False)])


def with_halo(value):
    value = planes_of(value)
    value = jnp.concatenate([shifted(value, "gx", 1, True), value, shifted(value, "gx", -1, True)])
    return shifted(value, GY, 1, True), value, shifted(value, GY, -1, True)


def bits_of(axis):
    count = lax.axis_size(axis)
    return [(axis, b) for b in range(count.bit_length() - 1)]


def swap(value, axis, bit):
    count = lax.axis_size(axis)
    return lax.ppermute(value, axis, [(i, i ^ (1 << bit)) for i in range(count)])


def bit_value(axis, bit):
    return (lax.axis_index(axis) >> bit) & 1


def part(arrays, at, size):
    total = lax.dynamic_slice_in_dim(arrays[0], at, size)
    for x in arrays[1:]:
        total = total + lax.dynamic_slice_in_dim(x, at, size)
    return total


class Chain:
    def __init__(self):
        self.last = None

    def after(self, values):
        if self.last is not None:
            self.last, values = lax.optimization_barrier((self.last, values))
        return values

    def step(self, value):
        self.last = value
        return value

    def zero(self):
        first = jax.tree.leaves(self.last)[0]
        corner = first[(slice(0, 1),) * first.ndim].reshape(())
        return jnp.minimum(jnp.abs(corner), 0.0)


def halved(chain, arrays, axis, bit, tight=False):
    arrays = chain.after(arrays)
    half = arrays[0].shape[0] // 2
    one = bit_value(axis, bit)
    send = chain.step(part(arrays, (1 - one) * half, half))
    got = swap(send, axis, bit)
    send, arrays = lax.optimization_barrier((send, arrays))
    keep = part(arrays, one * half, half)
    if tight:
        chain.step((send, keep))
    return [keep, got]


def joined_halves(value, other, axis, bit):
    one = bit_value(axis, bit) == 1
    return jnp.concatenate([jnp.where(one, other, value), jnp.where(one, value, other)])


def reduction(chain, first, second, tight=False, firm=False, firm_total=False):
    across, along = bits_of("gz"), bits_of("gyh")
    lanes = [first, second]
    for turn, plan in enumerate(((across, along), (along, across))):
        for i in range(2):
            for axis, bit in plan[i]:
                lanes[i] = halved(chain, lanes[i], axis, bit, tight and turn == 1)
        yield
    sizes = [x[0].shape[0] for x in lanes]
    joint = [jnp.concatenate(pair) for pair in zip(*chain.after(lanes))]
    for axis, bit in bits_of("gx"):
        joint = halved(chain, joint, axis, bit, tight)
        yield
    joint = chain.after(joint)
    value = sum(joint[1:], joint[0])
    value = chain.step(value + chain.zero() if firm_total else value)
    for axis, bit in bits_of("gx")[::-1]:
        other = swap(value, axis, bit)
        yield
        value, other = chain.after((value, other))
        value = chain.step(joined_halves(value, other, axis, bit))
    values = [value[: sizes[0]], value[sizes[0] :]]
    for plan in ((along, across), (across, along)):
        for turn in range(max(len(across), len(along))):
            others = [None, None]
            for i in range(2):
                if turn < len(plan[i]):
                    others[i] = swap(values[i], *plan[i][::-1][turn])
            yield
            for i in range(2):
                if turn < len(plan[i]):
                    values[i], others[i] = chain.after((values[i], others[i]))
                    whole = joined_halves(values[i], others[i], *plan[i][::-1][turn])
                    if firm and plan[0] is across:
                        whole = whole + chain.zero()
                    values[i] = chain.step(whole)
    others = [swap(x, "gyl", 0) for x in values]
    yield
    values, others = chain.after((values, others))
    return [(value, chain.step(other)) for value, other in zip(values, others)]


def iota(shape, dim):
    return lax.broadcasted_iota(jnp.int32, shape, dim)


def dot(left, right, dims=NN):
    return lax.dot_general(left, right, dims, preferred_element_type=F32)


def halves(x):
    high = x.astype(BF)
    return high, (x - high.astype(F32)).astype(BF)


def stacked(x):
    high, low = halves(x)
    if x.shape[0] % 16 == 0:
        return jnp.concatenate([high, low], axis=0)
    return jnp.concatenate([high.astype(F32), low.astype(F32)], axis=0).astype(BF)


def folded(x):
    half = x.shape[0] // 2
    return x[:half] + x[half:]


def times(x, weight, dims=NN):
    return folded(dot(stacked(x), weight, dims))


def side_by_side(x):
    return jnp.concatenate(halves(x), axis=1)


def side_sum(x):
    half = x.shape[1] // 2
    return x[:, :half] + x[:, half:]


def weight_grad(x, y):
    x_high, x_low = halves(x)
    y_high, y_low = halves(y)
    left, right = [x_high, x_high, x_low], [y_high, y_low, y_high]
    if x.shape[0] % 16 == 0:
        return dot(jnp.concatenate(left, axis=0), jnp.concatenate(right, axis=0), TN)
    left = jnp.concatenate([p.astype(F32) for p in left], axis=0).astype(BF)
    right = jnp.concatenate([p.astype(F32) for p in right], axis=0).astype(BF)
    return dot(left, right, TN)


def onehot(hit):
    return jnp.where(hit, 1.0, 0.0).astype(BF)


def sigmoid(v):
    return 1.0 / (1.0 + jnp.exp(-v))


def act(v):
    return v * sigmoid(v) * (1.0 / 0.6)


def act_and_slope(v):
    s = sigmoid(v)
    return v * s * (1.0 / 0.6), s * (1.0 + v * (1.0 - s)) * (1.0 / 0.6)


def sin_pi(t):
    n = jnp.floor(t + 0.5)
    r = t - n
    odd = n - 2.0 * jnp.floor(n * 0.5)
    q = r * r
    total = jnp.zeros_like(r)
    for k in range(6, -1, -1):
        total = total * q + (-1.0) ** k * math.pi ** (2 * k + 1) / math.factorial(2 * k + 1)
    return total * r * (1.0 - 2.0 * odd)


def to_column(row):
    n = row.shape[1]
    same = iota((n, n), 0) == iota((n, n), 1)
    return jnp.sum(jnp.where(same, row, jnp.zeros_like(row)), axis=1, keepdims=True)


def send_column(send, rows):
    shape = (rows, SEND)
    hit = (iota(shape, 0) & (SEND - 1)) == iota(shape, 1)
    return jnp.sum(jnp.where(hit, send, 0), axis=1, keepdims=True)


def send_lanes(send):
    shape = (8, 128)
    hit = iota(shape, 0) == (iota(shape, 1) & (SEND - 1))
    return jnp.sum(jnp.where(hit, send_column(send, 8), 0), axis=0, keepdims=True)


def paid(row, send):
    edge = send * SLOTS + 2 * (row >> 3) + ((row >> 2) & 1)
    return jnp.where(row < 120, edge, -1)


def atom_of(edge):
    total = jnp.zeros_like(edge)
    for a in range(1, ATOMS):
        total = total + jnp.where(edge >= a * SLOTS, 1, 0)
    return total


def radial_of(length):
    x = length / 12.0
    x2 = x * x
    x4 = x2 * x2
    envelope = 1.0 - 28.0 * (x4 * x2) + 48.0 * (x4 * x2 * x) - 21.0 * (x4 * x4)
    orders = (iota((1, RADIAL), 1) + 1).astype(F32)
    return envelope * sin_pi(x * orders) / x


def geometry(unit):
    own = atom_of(iota((8, EDGES), 1)) == iota((8, EDGES), 0)
    edge = iota((EDGES, 128), 0)
    slot = edge - atom_of(edge) * SLOTS
    total = jnp.zeros((24, 128), F32)
    for k in range(3):
        x = jnp.where(own, unit[k : k + 1, :], 0.0)
        high = x.astype(BF).astype(F32)
        mid = (x - high).astype(BF).astype(F32)
        parts = jnp.concatenate([high, mid, x - high - mid], axis=0).astype(BF)
        total = total + dot(parts, onehot(iota((EDGES, 128), 1) == slot + 32 * k))
    return total[0:8] + total[8:16] + total[16:24]


def local_rows(index):
    return (index & 7) * SLOTS + 2 * (index >> 4) + ((index >> 3) & 1)


def start_kernel(
    edge, vec, mask, hidden, tag_row, send_row, table, w_in, w_rad, w_trip, w_quad,
    payload, local, tagged, pre, downs, rads, radial_out, columns,
):
    vectors = vec[...]
    length = jnp.sqrt(jnp.sum(vectors * vectors, axis=0, keepdims=True))
    unit = vectors / length
    geo = geometry(unit)
    live = to_column(jnp.where(mask[...] > 0, 1.0, 0.0))
    parts = [live] + [to_column(unit[k : k + 1, :]) for k in range(3)]
    columns[...] = jnp.concatenate(parts + [jnp.zeros((EDGES, 124), F32)], axis=1)
    send = send_column(send_row[...], 8)
    pay = paid(iota((128, 1), 0), send_column(send_row[...], 128))
    tags = to_column(tag_row[...])
    radial = radial_of(to_column(length))
    radial_out[...] = radial
    split = side_by_side(radial)
    for k in range(5):
        rads[k] = dot(split, jnp.concatenate([w_rad[k], w_rad[k]], axis=0))
    split = stacked(edge[...])
    pre[0] = folded(dot(split, w_in[0]))
    pre[1] = folded(dot(split, w_in[1]))
    trip_pre = times(act(pre[0]) * rads[0], w_trip[...], NT)
    quad_pre = times(act(pre[1]) * rads[1], w_quad[...], NT)
    downs[...] = jnp.concatenate([trip_pre, quad_pre, jnp.zeros((EDGES, 32), F32)], axis=1)
    trip = act(trip_pre) * live
    quad = act(quad_pre) * live
    rows = jnp.concatenate([trip, quad * radial[:, 0:1], quad * radial[:, 1:2]], axis=1)
    rows = side_by_side(rows)
    shape = (EDGES, EDGES)
    place = onehot(local_rows(iota(shape, 0)) == iota(shape, 1))
    local[0:15] = side_sum(dot(place, rows)).reshape(15, 16, 128)
    place = onehot(pay == iota((128, EDGES), 1))
    payload[0:16] = side_sum(dot(place, rows)).reshape(16, 8, 128)
    tag = hidden[...]
    for t in range(3):
        tag = tag + jnp.where(tags == t, table[t : t + 1, :].astype(F32), 0.0)
    tagged[...] = tag
    local[15] = jnp.concatenate([tag[:, :128], tag[:, 128:]], axis=0)
    local[16] = jnp.concatenate([geo, jnp.zeros((8, 128), F32)], axis=0)
    both = jnp.concatenate([tag, geo], axis=1)
    sent = jnp.zeros((8, 384), F32)
    for a in range(ATOMS):
        sent = sent + jnp.where(send == a, both[a : a + 1, :], 0.0)
    payload[15] = jnp.where(iota((8, 128), 0) < 4, sent[:, :128], sent[:, 128:256])
    payload[16] = sent[:, 256:]


def split_cores(core, whole, keep, send):
    half = whole.shape[0] // 2
    upper = core[0] == 1
    low, high = whole[:half], whole[half:]
    keep[...] = jnp.where(upper, high, low)
    send[...] = jnp.where(upper, low, high)


def segments(shape, edge_dim, atom_dim):
    edge, atom = iota(shape, edge_dim), iota(shape, atom_dim) & 7
    return onehot((edge >= atom * SLOTS) & (edge < atom * SLOTS + SLOTS))


def lead(k):
    return math.comb(2 * k, k) / 2.0**k


def ratio(k):
    return k * k / (4.0 * k * k - 1.0)


def monic(cosine):
    before, now = jnp.ones_like(cosine), cosine
    yield before
    yield now
    for k in range(1, ANGLES - 1):
        before, now = now, cosine * now - ratio(k) * before
        yield now


def looped(count, step, body):
    def turn(t, carry):
        for i in range(step):
            body(t * step + i)
        return carry

    lax.fori_loop(0, count // step, turn, 0)


def main_kernel(
    halo_before, halo_here, halo_after, local, tagged, edge, columns, rads, radial,
    src_cols, slots, marks,
    trip_bil, trip_up, quad_bil, quad_up, w_ae, w_res, w_ea, w_ad,
    cot_atoms, cot_edges, cot_energy, core,
    atoms_out, edges_out, energy_out, grad_edges, grad_tag,
    cosines, grad_sums, grad_src, keep, send, grad_rads, atom_rows, quad_up_grad,
    table, sums, weight, kept, cos_table, first,
):
    live = columns[:, 0:1]
    halos = (halo_before, halo_here, halo_after)
    group = halo_here.shape[0] * 8
    depth = 3 * group + 16
    lanes = iota((EDGES, depth), 1)
    place = jnp.concatenate(
        [onehot(src_cols[:, 0:1] == lanes), onehot(src_cols[:, 1:2] == lanes)], axis=0
    )

    def rows_at(p):
        parts = [h[:, p].reshape(group, 128) for h in halos]
        return jnp.concatenate(parts + [local[p]], axis=0)

    def gather_pair(p):
        got = dot(place, side_by_side(rows_at(p))).astype(BF)
        table[2 * p] = got[:EDGES]
        table[2 * p + 1] = got[EDGES:]

    looped(16, 4, gather_pair)

    rows = rows_at(16)
    high, low = halves(rows)
    rest = (rows - high.astype(F32) - low.astype(F32)).astype(BF)
    got = dot(place[:EDGES], jnp.concatenate([high, low, rest], axis=1))
    got = got[:, :128] + got[:, 128:256] + got[:, 256:]
    cos_table[...] = -(
        columns[:, 1:2] * got
        + columns[:, 2:3] * pltpu.roll(got, 96, 1)
        + columns[:, 3:4] * pltpu.roll(got, 64, 1)
    )

    for k in range(ANGLES):
        top = trip_bil[:, k * 64 : k * 64 + 64].astype(F32)
        top = jnp.concatenate([top, jnp.zeros((64, 64), F32)], axis=1)
        low_left = quad_bil[:, k * 32 : k * 32 + 32].astype(F32)
        low_right = quad_bil[:, 512 + k * 32 : 544 + k * 32].astype(F32)
        bottom = jnp.concatenate([jnp.zeros((32, 64), F32), low_left, low_right], axis=1)
        piece = jnp.concatenate([top, bottom, jnp.zeros((32, 128), F32)], axis=0)
        weight[:, k * 128 : (k + 1) * 128] = piece.astype(BF)

    trip_lanes = iota((128, 128), 1) < TRIP_W
    scale = 1.0 / math.sqrt(PICKS)

    def basis_block(b):
        at = pl.multiple_of(b * BLOCK, BLOCK)
        own = pl.ds(at, BLOCK)
        wide = iota((BLOCK, 512), 1)
        mark = marks[own, :]
        hits = [jnp.where(mark[:, t : t + 1] == wide, 1.0, 0.0) for t in range(2 * PICKS)]
        hits = jnp.concatenate(hits, axis=0).astype(BF)
        got = side_sum(dot(hits, table[:, own, :].reshape(512, 256)))
        picked = jnp.where(trip_lanes, got[:128], got[128:])
        picked = picked.reshape(PICKS, BLOCK, 128)
        cos_here = cos_table[own, :]
        slot = slots[own, :]
        low_lanes = iota((BLOCK, 128), 1) < TRIP_W
        for h in range(2):
            rows = slice(8 * h, 8 * h + 8)
            cos = []
            for j in range(PICKS):
                index = jnp.where(
                    low_lanes[rows], slot[rows, j : j + 1], slot[rows, PICKS + j : PICKS + j + 1]
                )
                cos.append(jnp.take_along_axis(cos_here[rows], index, axis=1))
            cos = jnp.stack(cos)
            cosines[2 * b + h] = cos
            values = picked[:, rows]
            for k, poly in enumerate(monic(cos)):
                total = jnp.sum(poly * values, axis=0) * (lead(k) * scale)
                sums[pl.ds(pl.multiple_of(at + 8 * h, 8), 8), k * 128 : (k + 1) * 128] = total

    looped(BLOCKS, 3, basis_block)

    down = times(sums[...], weight[...], NT)
    down_act, down_slope = act_and_slope(down)
    trip_h, quad_h = down_act[:, :64], down_act[:, 64:96]
    trip_pre = times(trip_h, trip_up[...])
    quad_pre = times(quad_h, quad_up[...])
    src = jnp.concatenate(
        [side_sum(table[30].astype(F32)), side_sum(table[31].astype(F32))], axis=1
    )
    target = times(tagged[...], w_ae[1])
    spread = segments((EDGES, 16), 0, 1)
    gathers = segments((8, EDGES), 1, 0)

    def to_edges(x):
        return dot(spread, stacked(x))

    def to_atoms(x):
        return side_sum(dot(gathers, side_by_side(x)))

    atom_pre = times(src, w_ae[0]) + to_edges(target)
    atom_act, atom_slope = act_and_slope(atom_pre)
    trip_act, trip_slope = act_and_slope(trip_pre)
    quad_act, quad_slope = act_and_slope(quad_pre)
    merged = (edge[...] + trip_act + quad_act + atom_act * rads[2]) * 0.5
    kept[0] = merged
    first_act, first_slope = act_and_slope(times(merged, w_res[0]))
    kept[1] = first_act
    second_act, second_slope = act_and_slope(times(first_act, w_res[1]))
    new_edges = (merged + second_act) * root_half
    edges_out[...] = new_edges
    weighted = new_edges * live
    root_slots = 1.0 / math.sqrt(SLOTS)
    gathered = to_atoms(weighted * rads[3]) * root_slots
    summary = to_atoms(weighted * rads[4]) * root_slots
    gate_act, gate_slope = act_and_slope(times(gathered, w_ea[0]))
    updated = (tagged[...] + gate_act) * root_half
    a0_act, a0_slope = act_and_slope(times(updated, w_ad[0]))
    a1_act, a1_slope = act_and_slope(times(a0_act, w_ad[1]))
    new_atoms = (updated + a1_act) * root_half
    atoms_out[...] = new_atoms
    e_act, e_slope = act_and_slope(times(summary, w_ea[1]) + times(new_atoms, w_ad[2]))
    out_act, out_slope = act_and_slope(times(e_act, w_ad[3]))
    energy_out[...] = out_act

    d_out = cot_energy[...] * out_slope
    d_e = times(d_out, w_ad[3], NT) * e_slope
    d_summary = times(d_e, w_ea[1], NT)
    d_atoms = (cot_atoms[...] + times(d_e, w_ad[2], NT)) * root_half
    d_a1 = d_atoms * a1_slope
    d_a0 = times(d_a1, w_ad[1], NT) * a0_slope
    d_updated = (d_atoms + times(d_a0, w_ad[0], NT)) * root_half
    d_gate = d_updated * gate_slope
    d_gathered = times(d_gate, w_ea[0], NT)

    d_gathered = to_edges(d_gathered * root_slots)
    d_summary = to_edges(d_summary * root_slots)
    grad_rads[1] = weighted * d_gathered
    grad_rads[2] = weighted * d_summary
    d_new = cot_edges[...] + live * (d_gathered * rads[3] + d_summary * rads[4])
    d_new = d_new * root_half
    d_second = d_new * second_slope
    kept[3] = d_second
    d_first = times(d_second, w_res[1], NT) * first_slope
    kept[2] = d_first
    d_merged = (d_new + times(d_first, w_res[0], NT)) * 0.5
    grad_edges[...] = d_merged
    grad_rads[0] = d_merged * atom_act
    d_atom = d_merged * rads[2] * atom_slope
    kept[4] = d_atom
    d_trip = d_merged * trip_slope
    d_quad = d_merged * quad_slope
    d_target = to_atoms(d_atom)
    grad_tag[...] = d_updated + times(d_target, w_ae[1], NT)
    d_down = jnp.concatenate(
        [times(d_trip, trip_up[...], NT), times(d_quad, quad_up[...], NT), jnp.zeros((EDGES, 32), F32)],
        axis=1,
    )
    d_down = d_down * down_slope
    grad_src[...] = times(d_atom, w_ae[0], NT)

    first[0:512] = weight_grad(kept[0], kept[2])
    first[512:768] = weight_grad(src, kept[4])
    first[896:1408] = weight_grad(kept[1], kept[3])
    first[1408:1664] = weight_grad(tagged[...], d_target)
    bil = weight_grad(d_down, sums[...])
    for m in range(8):
        tile = [bil[0:64, k * 128 : k * 128 + 64] for k in (2 * m, 2 * m + 1)]
        row = 768 + 64 * (m // 4)
        first[row : row + 64, (m % 4) * 128 : (m % 4 + 1) * 128] = jnp.concatenate(tile, axis=1)
    for half in range(2):
        for m in range(4):
            at = 64 + 32 * half
            tile = [bil[64:96, k * 128 + at : k * 128 + at + 32] for k in range(4 * m, 4 * m + 4)]
            row = 1728 + 32 * half
            first[row : row + 32, m * 128 : (m + 1) * 128] = jnp.concatenate(tile, axis=1)
    first[1664:1728] = weight_grad(down_act, d_trip)[:64]
    quad_up_grad[...] = weight_grad(down_act, d_quad)[64:96]
    atom_rows[...] = jnp.concatenate(
        [gathered, summary, updated, a0_act, new_atoms, e_act, d_a0, d_a1, d_e, d_out, d_gate], axis=1
    )
    split_cores(core, first, keep, send)
    twice = jnp.concatenate([weight[...], weight[...]], axis=0)
    grad_sums[...] = dot(side_by_side(d_down), twice)


def late_kernel(grad_rads, radial, atom_rows, quad_up_grad, core, keep, send, second):
    atoms = atom_rows[...]
    gathered, summary = atoms[:, :512], atoms[:, 512:1024]
    updated, a0_act, new_atoms, e_act, d_a0, d_a1, d_e, d_out, d_gate = [
        atoms[:, at : at + 256] for at in range(1024, 3328, 256)
    ]
    second[0:512, 0:256] = weight_grad(gathered, d_gate)
    second[0:512, 256:512] = weight_grad(summary, d_e)
    second[512:768, 0:256] = weight_grad(updated, d_a0)
    second[512:768, 256:512] = weight_grad(a0_act, d_a1)
    second[768:1024, 0:256] = weight_grad(new_atoms, d_e)
    second[768:1024, 256:512] = weight_grad(e_act, d_out)
    for k in range(3):
        second[1024 + 128 * k : 1152 + 128 * k] = weight_grad(radial[...], grad_rads[k])
    second[1408:1440] = quad_up_grad[...]
    second[1440:1536] = jnp.zeros((96, 512), F32)
    split_cores(core, second, keep, send)


def scatter_kernel(
    cosines, sums, grad_src, src_rows, mark_rows,
    back_before, back_here, back_after, back_local,
    table,
):
    group = back_here.shape[0] * 8
    depth = 3 * group + 16
    trip_lanes = iota((128, 128), 1) < TRIP_W
    scale = 1.0 / math.sqrt(PICKS)

    def basis_back(b):
        at = pl.multiple_of(b * BLOCK, BLOCK)
        own = pl.ds(at, BLOCK)
        parts = []
        for h in range(2):
            cos = cosines[2 * b + h]
            own_rows = pl.ds(pl.multiple_of(at + 8 * h, 8), 8)
            after = total = None
            for k in range(ANGLES - 1, -1, -1):
                term = sums[own_rows, k * 128 : (k + 1) * 128] * (lead(k) * scale)
                if total is None:
                    after, total = None, jnp.broadcast_to(term, cos.shape)
                elif after is None:
                    after, total = total, term + cos * total
                else:
                    after, total = total, term + cos * total - ratio(k + 1) * after
            parts.append(total)
        grad = jnp.concatenate(parts, axis=1).reshape(128, 128)
        grad = jnp.concatenate(
            [jnp.where(trip_lanes, grad, 0.0), jnp.where(trip_lanes, 0.0, grad)], axis=0
        )
        hits = onehot(mark_rows[b] == iota((512, 256), 0))
        got = side_by_side(side_sum(dot(hits, side_by_side(grad))))
        table[:, own, :] = got.reshape(32, BLOCK, 256)

    looped(BLOCKS, 3, basis_back)
    table[30] = side_by_side(grad_src[:, :128])
    table[31] = side_by_side(grad_src[:, 128:])
    rows = iota((depth, EDGES), 0)
    place_even = onehot(src_rows[0:1, :] == rows)
    place_odd = onehot(src_rows[1:2, :] == rows)

    def scatter_pair(p):
        got = side_sum(dot(place_even, table[2 * p]) + dot(place_odd, table[2 * p + 1]))
        for i, back in enumerate((back_before, back_here, back_after)):
            back[:, p] = got[i * group : (i + 1) * group].reshape(group // 8, 8, 128)
        back_local[p] = got[3 * group :]

    looped(16, 4, scatter_pair)


def finish_kernel(
    back_local, returned, grad_late, tag_late, edge, radial, columns, pre, downs, rads, tag_row, send_row,
    w_in, w_trip, w_quad, core,
    grad_atoms, grad_edges, keep_first, send_first, keep_second, send_second,
    first, second,
):
    shape = (EDGES, 256)
    lane = iota(shape, 1)
    place = onehot((local_rows(lane) == iota(shape, 0)) & (lane < EDGES))
    rows = dot(place, side_by_side(back_local[...].reshape(256, 128)))
    pay = paid(iota((1, 128), 1), send_lanes(send_row[...]))
    place = onehot(pay == iota((EDGES, 128), 0))
    send = send_column(send_row[...], 8)
    tags = to_column(tag_row[...])
    rows = side_sum(rows + dot(place, side_by_side(returned[...].reshape(128, 128))))
    back = returned[15]
    tag = tag_late[...] + jnp.concatenate([back_local[15, 0:8], back_local[15, 8:16]], axis=1)
    atom = iota((8, 1), 0)
    for r in range(SEND):
        piece = jnp.concatenate([back[r : r + 1], back[4 + r : 5 + r]], axis=1)
        tag = tag + jnp.where(send[r : r + 1, :] == atom, piece, 0.0)
    grad_atoms[...] = tag
    table = [
        jnp.sum(jnp.where(tags == t, tag, 0.0), axis=0, keepdims=True) for t in range(3)
    ]
    table = jnp.concatenate(table + [jnp.zeros((29, ATOM_W), F32)], axis=0)
    d_trip = rows[:, :64]
    d_quad = rows[:, 64:96] * radial[:, 0:1] + rows[:, 96:128] * radial[:, 1:2]
    total = grad_late[...]
    for k, (d_row, down, weight, out) in enumerate(
        ((d_trip, slice(0, 64), w_trip, first), (d_quad, slice(64, 96), w_quad, second))
    ):
        d_down = d_row * columns[:, 0:1] * act_and_slope(downs[:, down])[1]
        value, slope = act_and_slope(pre[k])
        d_start = times(d_down, weight[...])
        d_pre = d_start * rads[k] * slope
        total = total + times(d_pre, w_in[k], NT)
        out[0:512] = weight_grad(edge[...], d_pre)
        out[512:640] = weight_grad(radial[...], d_start * value)
        down_grad = weight_grad(d_down, value * rads[k])
        if k == 0:
            out[640:704] = down_grad
            out[704:768] = jnp.zeros((64, 512), F32)
        else:
            out[640:672] = down_grad
            out[672:704, 0:256] = table
            out[672:704, 256:512] = jnp.zeros((32, 256), F32)
            out[704:768] = jnp.zeros((64, 512), F32)
    grad_edges[...] = total
    split_cores(core, first, keep_first, send_first)
    split_cores(core, second, keep_second, send_second)


def moved(core, pairs, held, copies, sems):
    arriving = [pltpu.make_async_copy(pair[i % 2], held[i], sems.at[i]) for i, pair in zip(range(len(held)), [p for p in pairs for _ in range(2)])]
    for upper in (0, 1):

        @pl.when(core[0] == upper)
        def _():
            for i in range(len(held)):
                pltpu.make_async_copy(pairs[i // 2][i % 2 ^ upper], held[i], sems.at[i]).start()

    leaving, at = [], len(held)
    for i, copy in enumerate(arriving):
        copy.wait()
        for source, target in copies[i]:
            leaving.append(pltpu.make_async_copy(source, target, sems.at[at]))
            leaving[-1].start()
            at += 1
    for x in leaving:
        x.wait()


def late_outputs(
    a_mine, a_other, b_mine, b_other, core,
    res, ae, trip_bil, trip_up, quad_bil, quad_up, rad, ea, ad,
    a_low, a_high, b_low, b_high, sems,
):
    left, right = slice(0, 256), slice(256, 512)
    copies = [
        [
            (a_low.at[0:512], res.at[0]),
            (a_low.at[512:768], ae.at[0]),
            (a_low.at[768:832], trip_bil.at[:, 0:512]),
            (a_low.at[832:896], trip_bil.at[:, 512:1024]),
        ],
        [
            (a_high.at[0:512], res.at[1]),
            (a_high.at[512:768], ae.at[1]),
            (a_high.at[768:832], trip_up),
            (a_high.at[832:864], quad_bil.at[:, 0:512]),
            (a_high.at[864:896], quad_bil.at[:, 512:1024]),
        ],
        [
            (b_low.at[0:512, left], ea.at[0]),
            (b_low.at[0:512, right], ea.at[1]),
            (b_low.at[512:768, left], ad.at[0]),
            (b_low.at[512:768, right], ad.at[1]),
        ],
        [
            (b_high.at[0:256, left], ad.at[2]),
            (b_high.at[0:256, right], ad.at[3]),
            (b_high.at[640:672], quad_up),
        ]
        + [(b_high.at[256 + 128 * k : 384 + 128 * k], rad.at[k]) for k in range(3)],
    ]
    pairs = [(a_mine, a_other), (b_mine, b_other)]
    moved(core, pairs, (a_low, a_high, b_low, b_high), copies, sems)


def early_outputs(
    c_mine, c_other, d_mine, d_other, late_rad, core,
    inputs, rad, trip_down, quad_down, tags,
    c_low, c_high, d_low, d_high, held_rad, sems,
):
    other_rad = pltpu.make_async_copy(late_rad, held_rad, sems.at[16])
    other_rad.start()
    copies = []
    for k, (low, high) in enumerate(((c_low, c_high), (d_low, d_high))):
        copies.append([(low, inputs.at[k, 0:384])])
        copies.append([(high.at[0:128], inputs.at[k, 384:512]), (high.at[128:256], rad.at[k])])
    copies[1].append((c_high.at[256:320], trip_down))
    copies[3].append((d_high.at[256:288], quad_down))
    pairs = [(c_mine, c_other), (d_mine, d_other)]
    moved(core, pairs, (c_low, c_high, d_low, d_high), copies, sems)
    other_rad.wait()
    last = pltpu.make_async_copy(held_rad, rad.at[2:5], sems.at[17])
    last.start()
    tags[...] = d_high[288:291, 0:256]
    last.wait()


def call(kernel, outs, args, scratch=(), micros=1, inside=None, room=63):
    spaces = [pl.ANY if inside is not None and i not in inside else pltpu.VMEM for i in range(len(outs))]
    space = pltpu.VMEM if inside is None else pl.ANY
    flops = int(micros * 1.15e9)
    return pl.pallas_call(
        kernel,
        out_shape=[jax.ShapeDtypeStruct(shape, F32) for shape in outs],
        in_specs=[pl.BlockSpec(memory_space=pltpu.SMEM if x.ndim == 1 else space) for x in args],
        out_specs=[pl.BlockSpec(memory_space=x) for x in spaces],
        scratch_shapes=list(scratch),
        compiler_params=pltpu.CompilerParams(vmem_limit_bytes=room * 1024 * 1024),
        cost_estimate=pl.CostEstimate(flops=flops, bytes_accessed=1 << 10, transcendentals=0),
    )(*args)


def per_device(
    hidden_atoms,
    edge_states,
    edge_vectors,
    atom_tags,
    send_list,
    sources,
    trip_slots,
    triplet_mask,
    quad_slots,
    quad_mask,
    edge_mask,
    w_inputs,
    w_radial,
    w_trip_down,
    triplet_bilinear_weight,
    w_trip_up,
    w_quad_down,
    w_quad_bil,
    w_quad_up,
    w_atom_edge,
    w_residual,
    w_edge_atom,
    w_atom_dense,
    tag_table,
    cot_atoms,
    cot_edges,
    cot_energy,
):
    planes = 2 if lax.axis_size("gz") == 2 else 3
    group = 3 * planes

    offset = jnp.maximum(sources - ATOMS, 0)
    block, border = offset // SEND, offset % SEND
    step_x, step_y, step_z = block // 9, block // 3 % 3, block % 3
    if planes == 2:
        step_z = jnp.clip(step_z - 1 + lax.axis_index("gz"), 0, 1)
    block = (step_y * 3 + step_x) * planes + step_z
    inside = sources < ATOMS
    even = jnp.where(inside, 3 * group * 8 + sources, block * 8 + border)
    src = jnp.stack([even, even + jnp.where(inside, ATOMS, SEND)])
    slots = jnp.concatenate([trip_slots, quad_slots], axis=1)
    masks = jnp.concatenate([triplet_mask, quad_mask], axis=1)
    marks = jnp.where(masks > 0, slots * BLOCK + (jnp.arange(EDGES) % BLOCK)[:, None], -1)
    mark_rows = marks.reshape(BLOCKS, BLOCK, 2 * PICKS).transpose(0, 2, 1)
    mark_rows = mark_rows.reshape(BLOCKS, 1, 2 * PICKS * BLOCK)
    trip_down_t, quad_down_t = w_trip_down.T, w_quad_down.T

    tag_row, send_row = atom_tags[None, :], send_list[None, :]
    payload, local, tagged, pre, downs, rads, radial, columns = call(
        start_kernel,
        [(PAIRS, 8, 128), (PAIRS, 16, 128), (8, 256), (2, EDGES, 512), (EDGES, 128), (5, EDGES, 512)]
        + [(EDGES, 128)] * 2,
        [edge_states, edge_vectors, edge_mask[None, :], hidden_atoms, tag_row, send_row, tag_table,
         w_inputs, w_radial, trip_down_t, quad_down_t],
        micros=5, room=58,
    )
    core = bit_value("gyl", 0)[None]
    before, here, after = with_halo(payload)
    (
        atoms_out, edges_out, energy_out, grad_edges, grad_tag,
        cosines, grad_sums, grad_src, keep_a, send_a, grad_rads, atom_rows, quad_up_grad,
    ) = call(
        main_kernel,
        [(8, 256), (EDGES, 512), (8, 256), (EDGES, 512), (8, 256)]
        + [(2 * BLOCKS, PICKS, 8, 128), (EDGES, 2048), (EDGES, 256), (896, 512), (896, 512)]
        + [(3, EDGES, 512), (8, 3328), (32, 512)],
        [before, here, after, local, tagged, edge_states, columns, rads, radial,
         src.T, slots, marks,
         triplet_bilinear_weight.T, w_trip_up, w_quad_bil.T, w_quad_up, w_atom_edge, w_residual,
         w_edge_atom, w_atom_dense, cot_atoms, cot_edges, cot_energy, core],
        scratch=[
            pltpu.VMEM((32, EDGES, 256), BF),
            pltpu.VMEM((EDGES, 2048), F32),
            pltpu.VMEM((128, 2048), BF),
            pltpu.VMEM((5, EDGES, 512), F32),
            pltpu.VMEM((EDGES, 128), F32),
            pltpu.VMEM((1792, 512), F32),
        ],
        micros=26, room=50,
    )
    chain = Chain()
    got_a = swap(send_a, "gyl", 0)
    keep_b, send_b = call(
        late_kernel,
        [(768, 512)] * 2,
        [grad_rads, radial, atom_rows, quad_up_grad, core],
        scratch=[pltpu.VMEM((1536, 512), F32)],
        micros=4, room=18,
    )
    late = reduction(chain, [keep_a, got_a], [keep_b, swap(send_b, "gyl", 0)], True, True)
    next(late)
    grad_sums = chain.after(grad_sums)
    back_before, back_here, back_after, back_local = call(
        scatter_kernel,
        [(group, 16, 8, 128)] * 3 + [(16, 16, 128)],
        [cosines, grad_sums, grad_src, src, mark_rows],
        scratch=[pltpu.VMEM((32, EDGES, 256), BF)],
        micros=13, room=18,
    )
    got = shifted(back_before, GY, -1, True), shifted(back_after, GY, 1, True)
    chain.step(back_local)
    next(late)
    got, value = chain.after((got, back_here))
    value = chain.step(value + got[0] + got[1])
    first_plane, middle, last_plane = value[:planes], value[planes : 2 * planes], value[2 * planes :]
    got = shifted(first_plane, "gx", -1, True), shifted(last_plane, "gx", 1, True)
    next(late)
    got, middle = chain.after((got, middle))
    value = chain.step(middle + got[0] + got[1])
    if planes == 2:
        top = lax.axis_index("gz") == 1
        mine = jnp.where(top, value[1], value[0])
        theirs = jnp.where(top, value[0], value[1])
        returned = mine + lax.ppermute(theirs, "gz", [(0, 1), (1, 0)])
    else:
        returned = value[1] + shifted(value[0], "gz", -1, False) + shifted(value[2], "gz", 1, False)
    returned = chain.after(returned)
    grad_atoms, grad_edges, keep_c, send_c, keep_d, send_d = call(
        finish_kernel,
        [(8, 256), (EDGES, 512)] + [(384, 512)] * 4,
        [back_local, returned, grad_edges, grad_tag, edge_states, radial, columns, pre, downs, rads,
         tag_row, send_row, w_inputs, trip_down_t, quad_down_t, core],
        scratch=[pltpu.VMEM((768, 512), F32)] * 2,
        micros=7, room=58,
    )
    next(late)
    send_c, send_d = chain.after((send_c, send_d))
    got_c, got_d = swap(send_c, "gyl", 0), swap(send_d, "gyl", 0)
    early = reduction(chain, [keep_c, got_c], [keep_d, got_d], firm_total=True)
    running = {"L": late, "E": early}
    done = {}

    def resume(name):
        if name in done:
            return
        try:
            next(running[name])
        except StopIteration as end:
            done[name] = end.value

    for name in "ELEELELEEELEL":
        resume(name)
    while "L" not in done:
        resume("L")
    (a_mine, a_other), (b_mine, b_other) = done["L"]
    g_res, g_ae, g_trip_bil, g_trip_up, g_quad_bil, g_quad_up, g_rad, g_ea, g_ad = call(
        late_outputs,
        [(2, 512, 512), (2, 256, 512), (64, 1024), (64, 512), (32, 1024), (32, 512), (3, 128, 512)]
        + [(2, 512, 256), (4, 256, 256)],
        [a_mine, a_other, b_mine, b_other, core],
        scratch=[pltpu.VMEM((896, 512), F32)] * 2
        + [pltpu.VMEM((768, 512), F32)] * 2
        + [pltpu.SemaphoreType.DMA((23,))],
        micros=0,
        room=12,
        inside=(),
    )
    chain.step(g_quad_up)
    while "E" not in done:
        resume("E")
    (c_mine, c_other), (d_mine, d_other) = done["E"]
    g_inputs, g_rad, g_trip_down, g_quad_down, g_tags = call(
        early_outputs,
        [(2, 512, 512), (5, 128, 512), (64, 512), (32, 512), (3, 256)],
        [c_mine, c_other, d_mine, d_other, g_rad, core],
        scratch=[pltpu.VMEM((384, 512), F32)] * 4
        + [pltpu.VMEM((3, 128, 512), F32), pltpu.SemaphoreType.DMA((18,))],
        micros=3,
        room=8,
        inside=(4,),
    )
    return (
        atoms_out,
        edges_out,
        energy_out,
        grad_atoms,
        grad_edges,
        g_inputs,
        g_rad,
        g_trip_down.T,
        g_trip_bil.T,
        g_trip_up,
        g_quad_down.T,
        g_quad_bil.T,
        g_quad_up,
        g_ae,
        g_res,
        g_ea,
        g_ad,
        g_tags,
    )


def solution(mesh):
    size = dict(mesh.shape)
    inner = Mesh(mesh.devices.reshape(size["gx"], size["gy"] // 2, 2, size["gz"]), ROWS)
    flat, columns, vector, whole = P(ROWS, None), P(None, ROWS), P(ROWS), P()
    placed = [flat, flat, columns] + [vector] * 3 + [flat] * 4 + [vector] + [whole] * 13 + [flat] * 3
    return jax.shard_map(
        per_device,
        mesh=inner,
        in_specs=tuple(placed),
        out_specs=tuple([flat] * 5 + [whole] * 13),
        check_vma=False,
    )
```

```python
import functools
import math

import jax
import jax.numpy as jnp
from jax import lax
from jax.experimental import pallas as pl
from jax.experimental.pallas import tpu as pltpu
from jax.sharding import Mesh
from jax.sharding import PartitionSpec as P

BF = jnp.bfloat16
F32 = jnp.float32
ROWS = ("gx", "gyh", "gyl", "gz")
GY = ("gyh", "gyl")
ATOMS, SEND, SLOTS, EDGES = 8, 4, 30, 240
ATOM_W, EDGE_W, TRIP_W, QUAD_W, RADIAL = 256, 512, 64, 32, 128
ANGLES, PICKS = 16, 8
PAIRS = 17
BLOCK = 16
BLOCKS = EDGES // BLOCK
root_half = 0.7071067811865476
NN = (((1,), (0,)), ((), ()))
NT = (((1,), (1,)), ((), ()))
TN = (((0,), (0,)), ((), ()))


def shifted(value, axis, steps, wrap):
    count = lax.axis_size(axis)
    pairs = [(i, (i + steps) % count) for i in range(count) if wrap or 0 <= i + steps < count]
    return lax.ppermute(value, axis, pairs)


def planes_of(value):
    if lax.axis_size("gz") == 2:
        other = lax.ppermute(value, "gz", [(0, 1), (1, 0)])
        top = lax.axis_index("gz") == 1
        return jnp.stack([jnp.where(top, other, value), jnp.where(top, value, other)])
    return jnp.stack([shifted(value, "gz", 1, False), value, shifted(value, "gz", -1, False)])


def with_halo(value):
    value = planes_of(value)
    value = jnp.concatenate([shifted(value, "gx", 1, True), value, shifted(value, "gx", -1, True)])
    return shifted(value, GY, 1, True), value, shifted(value, GY, -1, True)


def bits_of(axis):
    count = lax.axis_size(axis)
    return [(axis, b) for b in range(count.bit_length() - 1)]


def swap(value, axis, bit):
    count = lax.axis_size(axis)
    return lax.ppermute(value, axis, [(i, i ^ (1 << bit)) for i in range(count)])


def bit_value(axis, bit):
    return (lax.axis_index(axis) >> bit) & 1


def part(arrays, at, size):
    total = lax.dynamic_slice_in_dim(arrays[0], at, size)
    for x in arrays[1:]:
        total = total + lax.dynamic_slice_in_dim(x, at, size)
    return total


class Chain:
    def __init__(self):
        self.last = None

    def after(self, values):
        if self.last is not None:
            self.last, values = lax.optimization_barrier((self.last, values))
        return values

    def step(self, value):
        self.last = value
        return value

    def zero(self):
        first = jax.tree.leaves(self.last)[0]
        corner = first[(slice(0, 1),) * first.ndim].reshape(())
        return jnp.minimum(jnp.abs(corner), 0.0)


def halved(chain, arrays, axis, bit, tight=False):
    arrays = chain.after(arrays)
    half = arrays[0].shape[0] // 2
    one = bit_value(axis, bit)
    send = chain.step(part(arrays, (1 - one) * half, half))
    got = swap(send, axis, bit)
    send, arrays = lax.optimization_barrier((send, arrays))
    keep = part(arrays, one * half, half)
    if tight:
        chain.step((send, keep))
    return [keep, got]


def joined_halves(value, other, axis, bit):
    one = bit_value(axis, bit) == 1
    return jnp.concatenate([jnp.where(one, other, value), jnp.where(one, value, other)])


def reduction(chain, first, second, tight=False, firm=False, firm_total=False):
    across, along = bits_of("gz"), bits_of("gyh")
    lanes = [first, second]
    for turn, plan in enumerate(((across, along), (along, across))):
        for i in range(2):
            for axis, bit in plan[i]:
                lanes[i] = halved(chain, lanes[i], axis, bit, tight and turn == 1)
        yield
    sizes = [x[0].shape[0] for x in lanes]
    joint = [jnp.concatenate(pair) for pair in zip(*chain.after(lanes))]
    for axis, bit in bits_of("gx"):
        joint = halved(chain, joint, axis, bit, tight and bit == 0)
        yield
    joint = chain.after(joint)
    value = sum(joint[1:], joint[0])
    value = chain.step(value + chain.zero() if firm_total else value)
    for axis, bit in bits_of("gx")[::-1]:
        other = swap(value, axis, bit)
        yield
        value, other = chain.after((value, other))
        value = chain.step(joined_halves(value, other, axis, bit))
    values = [value[: sizes[0]], value[sizes[0] :]]
    for plan in ((along, across), (across, along)):
        for turn in range(max(len(across), len(along))):
            others = [None, None]
            for i in range(2):
                if turn < len(plan[i]):
                    others[i] = swap(values[i], *plan[i][::-1][turn])
            yield
            for i in range(2):
                if turn < len(plan[i]):
                    values[i], others[i] = chain.after((values[i], others[i]))
                    whole = joined_halves(values[i], others[i], *plan[i][::-1][turn])
                    if firm and plan[0] is across:
                        whole = whole + chain.zero()
                    values[i] = chain.step(whole)
    others = [swap(x, "gyl", 0) for x in values]
    yield
    values, others = chain.after((values, others))
    return [(value, chain.step(other)) for value, other in zip(values, others)]


def iota(shape, dim):
    return lax.broadcasted_iota(jnp.int32, shape, dim)


def dot(left, right, dims=NN):
    return lax.dot_general(left, right, dims, preferred_element_type=F32)


def halves(x):
    high = x.astype(BF)
    return high, (x - high.astype(F32)).astype(BF)


def stacked(x):
    high, low = halves(x)
    if x.shape[0] % 16 == 0:
        return jnp.concatenate([high, low], axis=0)
    return jnp.concatenate([high.astype(F32), low.astype(F32)], axis=0).astype(BF)


def folded(x):
    half = x.shape[0] // 2
    return x[:half] + x[half:]


def times(x, weight, dims=NN):
    return folded(dot(stacked(x), weight, dims))


def side_by_side(x):
    return jnp.concatenate(halves(x), axis=1)


def side_sum(x):
    half = x.shape[1] // 2
    return x[:, :half] + x[:, half:]


def weight_grad(x, y):
    x_high, x_low = halves(x)
    y_high, y_low = halves(y)
    left, right = [x_high, x_high, x_low], [y_high, y_low, y_high]
    if x.shape[0] % 16 == 0:
        return dot(jnp.concatenate(left, axis=0), jnp.concatenate(right, axis=0), TN)
    left = jnp.concatenate([p.astype(F32) for p in left], axis=0).astype(BF)
    right = jnp.concatenate([p.astype(F32) for p in right], axis=0).astype(BF)
    return dot(left, right, TN)


def onehot(hit):
    return jnp.where(hit, 1.0, 0.0).astype(BF)


def sigmoid(v):
    return 1.0 / (1.0 + jnp.exp(-v))


def act(v):
    return v * sigmoid(v) * (1.0 / 0.6)


def act_and_slope(v):
    s = sigmoid(v)
    return v * s * (1.0 / 0.6), s * (1.0 + v * (1.0 - s)) * (1.0 / 0.6)


def sin_pi(t):
    n = jnp.floor(t + 0.5)
    r = t - n
    odd = n - 2.0 * jnp.floor(n * 0.5)
    q = r * r
    total = jnp.zeros_like(r)
    for k in range(6, -1, -1):
        total = total * q + (-1.0) ** k * math.pi ** (2 * k + 1) / math.factorial(2 * k + 1)
    return total * r * (1.0 - 2.0 * odd)


def to_column(row):
    n = row.shape[1]
    same = iota((n, n), 0) == iota((n, n), 1)
    return jnp.sum(jnp.where(same, row, jnp.zeros_like(row)), axis=1, keepdims=True)


def send_column(send, rows):
    shape = (rows, SEND)
    hit = (iota(shape, 0) & (SEND - 1)) == iota(shape, 1)
    return jnp.sum(jnp.where(hit, send, 0), axis=1, keepdims=True)


def send_lanes(send):
    shape = (8, 128)
    hit = iota(shape, 0) == (iota(shape, 1) & (SEND - 1))
    return jnp.sum(jnp.where(hit, send_column(send, 8), 0), axis=0, keepdims=True)


def paid(row, send):
    edge = send * SLOTS + 2 * (row >> 3) + ((row >> 2) & 1)
    return jnp.where(row < 120, edge, -1)


def atom_of(edge):
    total = jnp.zeros_like(edge)
    for a in range(1, ATOMS):
        total = total + jnp.where(edge >= a * SLOTS, 1, 0)
    return total


def radial_of(length):
    x = length / 12.0
    x2 = x * x
    x4 = x2 * x2
    envelope = 1.0 - 28.0 * (x4 * x2) + 48.0 * (x4 * x2 * x) - 21.0 * (x4 * x4)
    orders = (iota((1, RADIAL), 1) + 1).astype(F32)
    return envelope * sin_pi(x * orders) / x


def geometry(unit):
    own = atom_of(iota((8, EDGES), 1)) == iota((8, EDGES), 0)
    edge = iota((EDGES, 128), 0)
    slot = edge - atom_of(edge) * SLOTS
    total = jnp.zeros((24, 128), F32)
    for k in range(3):
        x = jnp.where(own, unit[k : k + 1, :], 0.0)
        high = x.astype(BF).astype(F32)
        mid = (x - high).astype(BF).astype(F32)
        parts = jnp.concatenate([high, mid, x - high - mid], axis=0).astype(BF)
        total = total + dot(parts, onehot(iota((EDGES, 128), 1) == slot + 32 * k))
    return total[0:8] + total[8:16] + total[16:24]


def local_rows(index):
    return (index & 7) * SLOTS + 2 * (index >> 4) + ((index >> 3) & 1)


def start_kernel(
    edge, vec, mask, hidden, tag_row, send_row, table, w_in, w_rad, w_trip, w_quad,
    payload, local, tagged, pre, downs, rads, radial_out, columns,
):
    vectors = vec[...]
    length = jnp.sqrt(jnp.sum(vectors * vectors, axis=0, keepdims=True))
    unit = vectors / length
    geo = geometry(unit)
    live = to_column(jnp.where(mask[...] > 0, 1.0, 0.0))
    parts = [live] + [to_column(unit[k : k + 1, :]) for k in range(3)]
    columns[...] = jnp.concatenate(parts + [jnp.zeros((EDGES, 124), F32)], axis=1)
    send = send_column(send_row[...], 8)
    pay = paid(iota((128, 1), 0), send_column(send_row[...], 128))
    tags = to_column(tag_row[...])
    radial = radial_of(to_column(length))
    radial_out[...] = radial
    split = side_by_side(radial)
    for k in range(5):
        rads[k] = dot(split, jnp.concatenate([w_rad[k], w_rad[k]], axis=0))
    split = stacked(edge[...])
    pre[0] = folded(dot(split, w_in[0]))
    pre[1] = folded(dot(split, w_in[1]))
    trip_pre = times(act(pre[0]) * rads[0], w_trip[...], NT)
    quad_pre = times(act(pre[1]) * rads[1], w_quad[...], NT)
    downs[...] = jnp.concatenate([trip_pre, quad_pre, jnp.zeros((EDGES, 32), F32)], axis=1)
    trip = act(trip_pre) * live
    quad = act(quad_pre) * live
    rows = jnp.concatenate([trip, quad * radial[:, 0:1], quad * radial[:, 1:2]], axis=1)
    rows = side_by_side(rows)
    shape = (EDGES, EDGES)
    place = onehot(local_rows(iota(shape, 0)) == iota(shape, 1))
    local[0:15] = side_sum(dot(place, rows)).reshape(15, 16, 128)
    place = onehot(pay == iota((128, EDGES), 1))
    payload[0:16] = side_sum(dot(place, rows)).reshape(16, 8, 128)
    tag = hidden[...]
    for t in range(3):
        tag = tag + jnp.where(tags == t, table[t : t + 1, :].astype(F32), 0.0)
    tagged[...] = tag
    local[15] = jnp.concatenate([tag[:, :128], tag[:, 128:]], axis=0)
    local[16] = jnp.concatenate([geo, jnp.zeros((8, 128), F32)], axis=0)
    both = jnp.concatenate([tag, geo], axis=1)
    sent = jnp.zeros((8, 384), F32)
    for a in range(ATOMS):
        sent = sent + jnp.where(send == a, both[a : a + 1, :], 0.0)
    payload[15] = jnp.where(iota((8, 128), 0) < 4, sent[:, :128], sent[:, 128:256])
    payload[16] = sent[:, 256:]


def split_cores(core, whole, keep, send):
    half = whole.shape[0] // 2
    upper = core[0] == 1
    low, high = whole[:half], whole[half:]
    keep[...] = jnp.where(upper, high, low)
    send[...] = jnp.where(upper, low, high)


def segments(shape, edge_dim, atom_dim):
    edge, atom = iota(shape, edge_dim), iota(shape, atom_dim) & 7
    return onehot((edge >= atom * SLOTS) & (edge < atom * SLOTS + SLOTS))


def lead(k):
    return math.comb(2 * k, k) / 2.0**k


def ratio(k):
    return k * k / (4.0 * k * k - 1.0)


def monic(cosine):
    before, now = jnp.ones_like(cosine), cosine
    yield before
    yield now
    for k in range(1, ANGLES - 1):
        before, now = now, cosine * now - ratio(k) * before
        yield now


def looped(count, step, body):
    def turn(t, carry):
        for i in range(step):
            body(t * step + i)
        return carry

    lax.fori_loop(0, count // step, turn, 0)


def main_kernel(
    halo_before, halo_here, halo_after, local, tagged, edge, columns, rads, radial,
    src_cols, slots, marks,
    trip_bil, trip_up, quad_bil, quad_up, w_ae, w_res, w_ea, w_ad,
    cot_atoms, cot_edges, cot_energy, core,
    atoms_out, edges_out, energy_out, grad_edges, grad_tag,
    cosines, grad_sums, grad_src, keep, send, grad_rads, atom_rows, quad_up_grad,
    table, sums, weight, kept, cos_table, first,
):
    live = columns[:, 0:1]
    halos = (halo_before, halo_here, halo_after)
    group = halo_here.shape[0] * 8
    depth = 3 * group + 16
    lanes = iota((EDGES, depth), 1)
    place = jnp.concatenate(
        [onehot(src_cols[:, 0:1] == lanes), onehot(src_cols[:, 1:2] == lanes)], axis=0
    )

    def rows_at(p):
        parts = [h[:, p].reshape(group, 128) for h in halos]
        return jnp.concatenate(parts + [local[p]], axis=0)

    def gather_pair(p):
        got = dot(place, side_by_side(rows_at(p))).astype(BF)
        table[2 * p] = got[:EDGES]
        table[2 * p + 1] = got[EDGES:]

    looped(16, 4, gather_pair)

    rows = rows_at(16)
    high, low = halves(rows)
    rest = (rows - high.astype(F32) - low.astype(F32)).astype(BF)
    got = dot(place[:EDGES], jnp.concatenate([high, low, rest], axis=1))
    got = got[:, :128] + got[:, 128:256] + got[:, 256:]
    cos_table[...] = -(
        columns[:, 1:2] * got
        + columns[:, 2:3] * pltpu.roll(got, 96, 1)
        + columns[:, 3:4] * pltpu.roll(got, 64, 1)
    )

    for k in range(ANGLES):
        top = trip_bil[:, k * 64 : k * 64 + 64].astype(F32)
        top = jnp.concatenate([top, jnp.zeros((64, 64), F32)], axis=1)
        low_left = quad_bil[:, k * 32 : k * 32 + 32].astype(F32)
        low_right = quad_bil[:, 512 + k * 32 : 544 + k * 32].astype(F32)
        bottom = jnp.concatenate([jnp.zeros((32, 64), F32), low_left, low_right], axis=1)
        piece = jnp.concatenate([top, bottom, jnp.zeros((32, 128), F32)], axis=0)
        weight[:, k * 128 : (k + 1) * 128] = piece.astype(BF)

    trip_lanes = iota((128, 128), 1) < TRIP_W
    scale = 1.0 / math.sqrt(PICKS)

    def basis_block(b):
        at = pl.multiple_of(b * BLOCK, BLOCK)
        own = pl.ds(at, BLOCK)
        wide = iota((BLOCK, 512), 1)
        mark = marks[own, :]
        hits = [jnp.where(mark[:, t : t + 1] == wide, 1.0, 0.0) for t in range(2 * PICKS)]
        hits = jnp.concatenate(hits, axis=0).astype(BF)
        got = side_sum(dot(hits, table[:, own, :].reshape(512, 256)))
        picked = jnp.where(trip_lanes, got[:128], got[128:])
        picked = picked.reshape(PICKS, BLOCK, 128)
        cos_here = cos_table[own, :]
        slot = slots[own, :]
        low_lanes = iota((BLOCK, 128), 1) < TRIP_W
        for h in range(2):
            rows = slice(8 * h, 8 * h + 8)
            cos = []
            for j in range(PICKS):
                index = jnp.where(
                    low_lanes[rows], slot[rows, j : j + 1], slot[rows, PICKS + j : PICKS + j + 1]
                )
                cos.append(jnp.take_along_axis(cos_here[rows], index, axis=1))
            cos = jnp.stack(cos)
            cosines[2 * b + h] = cos
            values = picked[:, rows]
            for k, poly in enumerate(monic(cos)):
                total = jnp.sum(poly * values, axis=0) * (lead(k) * scale)
                sums[pl.ds(pl.multiple_of(at + 8 * h, 8), 8), k * 128 : (k + 1) * 128] = total

    looped(BLOCKS, 3, basis_block)

    down = times(sums[...], weight[...], NT)
    down_act, down_slope = act_and_slope(down)
    trip_h, quad_h = down_act[:, :64], down_act[:, 64:96]
    trip_pre = times(trip_h, trip_up[...])
    quad_pre = times(quad_h, quad_up[...])
    src = jnp.concatenate(
        [side_sum(table[30].astype(F32)), side_sum(table[31].astype(F32))], axis=1
    )
    target = times(tagged[...], w_ae[1])
    spread = segments((EDGES, 16), 0, 1)
    gathers = segments((8, EDGES), 1, 0)

    def to_edges(x):
        return dot(spread, stacked(x))

    def to_atoms(x):
        return side_sum(dot(gathers, side_by_side(x)))

    atom_pre = times(src, w_ae[0]) + to_edges(target)
    atom_act, atom_slope = act_and_slope(atom_pre)
    trip_act, trip_slope = act_and_slope(trip_pre)
    quad_act, quad_slope = act_and_slope(quad_pre)
    merged = (edge[...] + trip_act + quad_act + atom_act * rads[2]) * 0.5
    kept[0] = merged
    first_act, first_slope = act_and_slope(times(merged, w_res[0]))
    kept[1] = first_act
    second_act, second_slope = act_and_slope(times(first_act, w_res[1]))
    new_edges = (merged + second_act) * root_half
    edges_out[...] = new_edges
    weighted = new_edges * live
    root_slots = 1.0 / math.sqrt(SLOTS)
    gathered = to_atoms(weighted * rads[3]) * root_slots
    summary = to_atoms(weighted * rads[4]) * root_slots
    gate_act, gate_slope = act_and_slope(times(gathered, w_ea[0]))
    updated = (tagged[...] + gate_act) * root_half
    a0_act, a0_slope = act_and_slope(times(updated, w_ad[0]))
    a1_act, a1_slope = act_and_slope(times(a0_act, w_ad[1]))
    new_atoms = (updated + a1_act) * root_half
    atoms_out[...] = new_atoms
    e_act, e_slope = act_and_slope(times(summary, w_ea[1]) + times(new_atoms, w_ad[2]))
    out_act, out_slope = act_and_slope(times(e_act, w_ad[3]))
    energy_out[...] = out_act

    d_out = cot_energy[...] * out_slope
    d_e = times(d_out, w_ad[3], NT) * e_slope
    d_summary = times(d_e, w_ea[1], NT)
    d_atoms = (cot_atoms[...] + times(d_e, w_ad[2], NT)) * root_half
    d_a1 = d_atoms * a1_slope
    d_a0 = times(d_a1, w_ad[1], NT) * a0_slope
    d_updated = (d_atoms + times(d_a0, w_ad[0], NT)) * root_half
    d_gate = d_updated * gate_slope
    d_gathered = times(d_gate, w_ea[0], NT)

    d_gathered = to_edges(d_gathered * root_slots)
    d_summary = to_edges(d_summary * root_slots)
    grad_rads[1] = weighted * d_gathered
    grad_rads[2] = weighted * d_summary
    d_new = cot_edges[...] + live * (d_gathered * rads[3] + d_summary * rads[4])
    d_new = d_new * root_half
    d_second = d_new * second_slope
    kept[3] = d_second
    d_first = times(d_second, w_res[1], NT) * first_slope
    kept[2] = d_first
    d_merged = (d_new + times(d_first, w_res[0], NT)) * 0.5
    grad_edges[...] = d_merged
    grad_rads[0] = d_merged * atom_act
    d_atom = d_merged * rads[2] * atom_slope
    kept[4] = d_atom
    d_trip = d_merged * trip_slope
    d_quad = d_merged * quad_slope
    d_target = to_atoms(d_atom)
    grad_tag[...] = d_updated + times(d_target, w_ae[1], NT)
    d_down = jnp.concatenate(
        [times(d_trip, trip_up[...], NT), times(d_quad, quad_up[...], NT), jnp.zeros((EDGES, 32), F32)],
        axis=1,
    )
    d_down = d_down * down_slope
    grad_src[...] = times(d_atom, w_ae[0], NT)

    first[0:512] = weight_grad(kept[0], kept[2])
    first[512:768] = weight_grad(src, kept[4])
    first[896:1408] = weight_grad(kept[1], kept[3])
    first[1408:1664] = weight_grad(tagged[...], d_target)
    bil = weight_grad(d_down, sums[...])
    for m in range(8):
        tile = [bil[0:64, k * 128 : k * 128 + 64] for k in (2 * m, 2 * m + 1)]
        row = 768 + 64 * (m // 4)
        first[row : row + 64, (m % 4) * 128 : (m % 4 + 1) * 128] = jnp.concatenate(tile, axis=1)
    for half in range(2):
        for m in range(4):
            at = 64 + 32 * half
            tile = [bil[64:96, k * 128 + at : k * 128 + at + 32] for k in range(4 * m, 4 * m + 4)]
            row = 1728 + 32 * half
            first[row : row + 32, m * 128 : (m + 1) * 128] = jnp.concatenate(tile, axis=1)
    first[1664:1728] = weight_grad(down_act, d_trip)[:64]
    quad_up_grad[...] = weight_grad(down_act, d_quad)[64:96]
    atom_rows[...] = jnp.concatenate(
        [gathered, summary, updated, a0_act, new_atoms, e_act, d_a0, d_a1, d_e, d_out, d_gate], axis=1
    )
    split_cores(core, first, keep, send)
    twice = jnp.concatenate([weight[...], weight[...]], axis=0)
    grad_sums[...] = dot(side_by_side(d_down), twice)


def late_kernel(grad_rads, radial, atom_rows, quad_up_grad, core, keep, send, second):
    atoms = atom_rows[...]
    gathered, summary = atoms[:, :512], atoms[:, 512:1024]
    updated, a0_act, new_atoms, e_act, d_a0, d_a1, d_e, d_out, d_gate = [
        atoms[:, at : at + 256] for at in range(1024, 3328, 256)
    ]
    second[0:512, 0:256] = weight_grad(gathered, d_gate)
    second[0:512, 256:512] = weight_grad(summary, d_e)
    second[512:768, 0:256] = weight_grad(updated, d_a0)
    second[512:768, 256:512] = weight_grad(a0_act, d_a1)
    second[768:1024, 0:256] = weight_grad(new_atoms, d_e)
    second[768:1024, 256:512] = weight_grad(e_act, d_out)
    for k in range(3):
        second[1024 + 128 * k : 1152 + 128 * k] = weight_grad(radial[...], grad_rads[k])
    second[1408:1440] = quad_up_grad[...]
    second[1440:1536] = jnp.zeros((96, 512), F32)
    split_cores(core, second, keep, send)


def scatter_kernel(
    cosines, sums, grad_src, src_rows, mark_rows,
    back_before, back_here, back_after, back_local,
    table,
):
    group = back_here.shape[0] * 8
    depth = 3 * group + 16
    trip_lanes = iota((128, 128), 1) < TRIP_W
    scale = 1.0 / math.sqrt(PICKS)

    def basis_back(b):
        at = pl.multiple_of(b * BLOCK, BLOCK)
        own = pl.ds(at, BLOCK)
        parts = []
        for h in range(2):
            cos = cosines[2 * b + h]
            own_rows = pl.ds(pl.multiple_of(at + 8 * h, 8), 8)
            after = total = None
            for k in range(ANGLES - 1, -1, -1):
                term = sums[own_rows, k * 128 : (k + 1) * 128] * (lead(k) * scale)
                if total is None:
                    after, total = None, jnp.broadcast_to(term, cos.shape)
                elif after is None:
                    after, total = total, term + cos * total
                else:
                    after, total = total, term + cos * total - ratio(k + 1) * after
            parts.append(total)
        grad = jnp.concatenate(parts, axis=1).reshape(128, 128)
        grad = jnp.concatenate(
            [jnp.where(trip_lanes, grad, 0.0), jnp.where(trip_lanes, 0.0, grad)], axis=0
        )
        hits = onehot(mark_rows[b] == iota((512, 256), 0))
        got = side_by_side(side_sum(dot(hits, side_by_side(grad))))
        table[:, own, :] = got.reshape(32, BLOCK, 256)

    looped(BLOCKS, 3, basis_back)
    table[30] = side_by_side(grad_src[:, :128])
    table[31] = side_by_side(grad_src[:, 128:])
    rows = iota((depth, EDGES), 0)
    place_even = onehot(src_rows[0:1, :] == rows)
    place_odd = onehot(src_rows[1:2, :] == rows)

    def scatter_pair(p):
        got = side_sum(dot(place_even, table[2 * p]) + dot(place_odd, table[2 * p + 1]))
        for i, back in enumerate((back_before, back_here, back_after)):
            back[:, p] = got[i * group : (i + 1) * group].reshape(group // 8, 8, 128)
        back_local[p] = got[3 * group :]

    looped(16, 4, scatter_pair)


def finish_kernel(
    back_local, returned, grad_late, tag_late, edge, radial, columns, pre, downs, rads, tag_row, send_row,
    w_in, w_trip, w_quad, core,
    grad_atoms, grad_edges, keep_first, send_first, keep_second, send_second,
    first, second,
):
    shape = (EDGES, 256)
    lane = iota(shape, 1)
    place = onehot((local_rows(lane) == iota(shape, 0)) & (lane < EDGES))
    rows = dot(place, side_by_side(back_local[...].reshape(256, 128)))
    pay = paid(iota((1, 128), 1), send_lanes(send_row[...]))
    place = onehot(pay == iota((EDGES, 128), 0))
    send = send_column(send_row[...], 8)
    tags = to_column(tag_row[...])
    rows = side_sum(rows + dot(place, side_by_side(returned[...].reshape(128, 128))))
    back = returned[15]
    tag = tag_late[...] + jnp.concatenate([back_local[15, 0:8], back_local[15, 8:16]], axis=1)
    atom = iota((8, 1), 0)
    for r in range(SEND):
        piece = jnp.concatenate([back[r : r + 1], back[4 + r : 5 + r]], axis=1)
        tag = tag + jnp.where(send[r : r + 1, :] == atom, piece, 0.0)
    grad_atoms[...] = tag
    table = [
        jnp.sum(jnp.where(tags == t, tag, 0.0), axis=0, keepdims=True) for t in range(3)
    ]
    table = jnp.concatenate(table + [jnp.zeros((29, ATOM_W), F32)], axis=0)
    d_trip = rows[:, :64]
    d_quad = rows[:, 64:96] * radial[:, 0:1] + rows[:, 96:128] * radial[:, 1:2]
    total = grad_late[...]
    for k, (d_row, down, weight, out) in enumerate(
        ((d_trip, slice(0, 64), w_trip, first), (d_quad, slice(64, 96), w_quad, second))
    ):
        d_down = d_row * columns[:, 0:1] * act_and_slope(downs[:, down])[1]
        value, slope = act_and_slope(pre[k])
        d_start = times(d_down, weight[...])
        d_pre = d_start * rads[k] * slope
        total = total + times(d_pre, w_in[k], NT)
        out[0:512] = weight_grad(edge[...], d_pre)
        out[512:640] = weight_grad(radial[...], d_start * value)
        down_grad = weight_grad(d_down, value * rads[k])
        if k == 0:
            out[640:704] = down_grad
            out[704:768] = jnp.zeros((64, 512), F32)
        else:
            out[640:672] = down_grad
            out[672:704, 0:256] = table
            out[672:704, 256:512] = jnp.zeros((32, 256), F32)
            out[704:768] = jnp.zeros((64, 512), F32)
    grad_edges[...] = total
    split_cores(core, first, keep_first, send_first)
    split_cores(core, second, keep_second, send_second)


def moved(core, pairs, held, copies, sems):
    arriving = [pltpu.make_async_copy(pair[i % 2], held[i], sems.at[i]) for i, pair in zip(range(len(held)), [p for p in pairs for _ in range(2)])]
    for upper in (0, 1):

        @pl.when(core[0] == upper)
        def _():
            for i in range(len(held)):
                pltpu.make_async_copy(pairs[i // 2][i % 2 ^ upper], held[i], sems.at[i]).start()

    leaving, at = [], len(held)
    for i, copy in enumerate(arriving):
        copy.wait()
        for source, target in copies[i]:
            leaving.append(pltpu.make_async_copy(source, target, sems.at[at]))
            leaving[-1].start()
            at += 1
    for x in leaving:
        x.wait()


def late_outputs(
    a_mine, a_other, b_mine, b_other, core,
    res, ae, trip_bil, trip_up, quad_bil, quad_up, rad, ea, ad,
    a_low, a_high, b_low, b_high, sems,
):
    left, right = slice(0, 256), slice(256, 512)
    copies = [
        [
            (a_low.at[0:512], res.at[0]),
            (a_low.at[512:768], ae.at[0]),
            (a_low.at[768:832], trip_bil.at[:, 0:512]),
            (a_low.at[832:896], trip_bil.at[:, 512:1024]),
        ],
        [
            (a_high.at[0:512], res.at[1]),
            (a_high.at[512:768], ae.at[1]),
            (a_high.at[768:832], trip_up),
            (a_high.at[832:864], quad_bil.at[:, 0:512]),
            (a_high.at[864:896], quad_bil.at[:, 512:1024]),
        ],
        [
            (b_low.at[0:512, left], ea.at[0]),
            (b_low.at[0:512, right], ea.at[1]),
            (b_low.at[512:768, left], ad.at[0]),
            (b_low.at[512:768, right], ad.at[1]),
        ],
        [
            (b_high.at[0:256, left], ad.at[2]),
            (b_high.at[0:256, right], ad.at[3]),
            (b_high.at[640:672], quad_up),
        ]
        + [(b_high.at[256 + 128 * k : 384 + 128 * k], rad.at[k]) for k in range(3)],
    ]
    pairs = [(a_mine, a_other), (b_mine, b_other)]
    moved(core, pairs, (a_low, a_high, b_low, b_high), copies, sems)


def early_outputs(
    c_mine, c_other, d_mine, d_other, late_rad, core,
    inputs, rad, trip_down, quad_down, tags,
    c_low, c_high, d_low, d_high, held_rad, sems,
):
    other_rad = pltpu.make_async_copy(late_rad, held_rad, sems.at[16])
    other_rad.start()
    copies = []
    for k, (low, high) in enumerate(((c_low, c_high), (d_low, d_high))):
        copies.append([(low, inputs.at[k, 0:384])])
        copies.append([(high.at[0:128], inputs.at[k, 384:512]), (high.at[128:256], rad.at[k])])
    copies[1].append((c_high.at[256:320], trip_down))
    copies[3].append((d_high.at[256:288], quad_down))
    pairs = [(c_mine, c_other), (d_mine, d_other)]
    moved(core, pairs, (c_low, c_high, d_low, d_high), copies, sems)
    other_rad.wait()
    last = pltpu.make_async_copy(held_rad, rad.at[2:5], sems.at[17])
    last.start()
    tags[...] = d_high[288:291, 0:256]
    last.wait()


def call(kernel, outs, args, scratch=(), micros=1, inside=None, room=63):
    spaces = [pl.ANY if inside is not None and i not in inside else pltpu.VMEM for i in range(len(outs))]
    space = pltpu.VMEM if inside is None else pl.ANY
    flops = int(micros * 1.15e9)
    return pl.pallas_call(
        kernel,
        out_shape=[jax.ShapeDtypeStruct(shape, F32) for shape in outs],
        in_specs=[pl.BlockSpec(memory_space=pltpu.SMEM if x.ndim == 1 else space) for x in args],
        out_specs=[pl.BlockSpec(memory_space=x) for x in spaces],
        scratch_shapes=list(scratch),
        compiler_params=pltpu.CompilerParams(vmem_limit_bytes=room * 1024 * 1024),
        cost_estimate=pl.CostEstimate(flops=flops, bytes_accessed=1 << 10, transcendentals=0),
    )(*args)


def per_device(
    hidden_atoms,
    edge_states,
    edge_vectors,
    atom_tags,
    send_list,
    sources,
    trip_slots,
    triplet_mask,
    quad_slots,
    quad_mask,
    edge_mask,
    w_inputs,
    w_radial,
    w_trip_down,
    triplet_bilinear_weight,
    w_trip_up,
    w_quad_down,
    w_quad_bil,
    w_quad_up,
    w_atom_edge,
    w_residual,
    w_edge_atom,
    w_atom_dense,
    tag_table,
    cot_atoms,
    cot_edges,
    cot_energy,
):
    planes = 2 if lax.axis_size("gz") == 2 else 3
    group = 3 * planes

    offset = jnp.maximum(sources - ATOMS, 0)
    block, border = offset // SEND, offset % SEND
    step_x, step_y, step_z = block // 9, block // 3 % 3, block % 3
    if planes == 2:
        step_z = jnp.clip(step_z - 1 + lax.axis_index("gz"), 0, 1)
    block = (step_y * 3 + step_x) * planes + step_z
    inside = sources < ATOMS
    even = jnp.where(inside, 3 * group * 8 + sources, block * 8 + border)
    src = jnp.stack([even, even + jnp.where(inside, ATOMS, SEND)])
    slots = jnp.concatenate([trip_slots, quad_slots], axis=1)
    masks = jnp.concatenate([triplet_mask, quad_mask], axis=1)
    marks = jnp.where(masks > 0, slots * BLOCK + (jnp.arange(EDGES) % BLOCK)[:, None], -1)
    mark_rows = marks.reshape(BLOCKS, BLOCK, 2 * PICKS).transpose(0, 2, 1)
    mark_rows = mark_rows.reshape(BLOCKS, 1, 2 * PICKS * BLOCK)
    trip_down_t, quad_down_t = w_trip_down.T, w_quad_down.T

    tag_row, send_row = atom_tags[None, :], send_list[None, :]
    payload, local, tagged, pre, downs, rads, radial, columns = call(
        start_kernel,
        [(PAIRS, 8, 128), (PAIRS, 16, 128), (8, 256), (2, EDGES, 512), (EDGES, 128), (5, EDGES, 512)]
        + [(EDGES, 128)] * 2,
        [edge_states, edge_vectors, edge_mask[None, :], hidden_atoms, tag_row, send_row, tag_table,
         w_inputs, w_radial, trip_down_t, quad_down_t],
        micros=5, room=58,
    )
    core = bit_value("gyl", 0)[None]
    before, here, after = with_halo(payload)
    (
        atoms_out, edges_out, energy_out, grad_edges, grad_tag,
        cosines, grad_sums, grad_src, keep_a, send_a, grad_rads, atom_rows, quad_up_grad,
    ) = call(
        main_kernel,
        [(8, 256), (EDGES, 512), (8, 256), (EDGES, 512), (8, 256)]
        + [(2 * BLOCKS, PICKS, 8, 128), (EDGES, 2048), (EDGES, 256), (896, 512), (896, 512)]
        + [(3, EDGES, 512), (8, 3328), (32, 512)],
        [before, here, after, local, tagged, edge_states, columns, rads, radial,
         src.T, slots, marks,
         triplet_bilinear_weight.T, w_trip_up, w_quad_bil.T, w_quad_up, w_atom_edge, w_residual,
         w_edge_atom, w_atom_dense, cot_atoms, cot_edges, cot_energy, core],
        scratch=[
            pltpu.VMEM((32, EDGES, 256), BF),
            pltpu.VMEM((EDGES, 2048), F32),
            pltpu.VMEM((128, 2048), BF),
            pltpu.VMEM((5, EDGES, 512), F32),
            pltpu.VMEM((EDGES, 128), F32),
            pltpu.VMEM((1792, 512), F32),
        ],
        micros=26, room=50,
    )
    chain = Chain()
    got_a = swap(send_a, "gyl", 0)
    keep_b, send_b = call(
        late_kernel,
        [(768, 512)] * 2,
        [grad_rads, radial, atom_rows, quad_up_grad, core],
        scratch=[pltpu.VMEM((1536, 512), F32)],
        micros=4, room=18,
    )
    late = reduction(chain, [keep_a, got_a], [keep_b, swap(send_b, "gyl", 0)], True, True)
    next(late)
    grad_sums = chain.after(grad_sums)
    back_before, back_here, back_after, back_local = call(
        scatter_kernel,
        [(group, 16, 8, 128)] * 3 + [(16, 16, 128)],
        [cosines, grad_sums, grad_src, src, mark_rows],
        scratch=[pltpu.VMEM((32, EDGES, 256), BF)],
        micros=13, room=18,
    )
    got = shifted(back_before, GY, -1, True), shifted(back_after, GY, 1, True)
    chain.step(back_local)
    next(late)
    got, value = chain.after((got, back_here))
    value = chain.step(value + got[0] + got[1])
    first_plane, middle, last_plane = value[:planes], value[planes : 2 * planes], value[2 * planes :]
    got = shifted(first_plane, "gx", -1, True), shifted(last_plane, "gx", 1, True)
    next(late)
    got, middle = chain.after((got, middle))
    value = chain.step(middle + got[0] + got[1])
    if planes == 2:
        top = lax.axis_index("gz") == 1
        mine = jnp.where(top, value[1], value[0])
        theirs = jnp.where(top, value[0], value[1])
        returned = mine + lax.ppermute(theirs, "gz", [(0, 1), (1, 0)])
    else:
        returned = value[1] + shifted(value[0], "gz", -1, False) + shifted(value[2], "gz", 1, False)
    returned = chain.after(returned)
    grad_atoms, grad_edges, keep_c, send_c, keep_d, send_d = call(
        finish_kernel,
        [(8, 256), (EDGES, 512)] + [(384, 512)] * 4,
        [back_local, returned, grad_edges, grad_tag, edge_states, radial, columns, pre, downs, rads,
         tag_row, send_row, w_inputs, trip_down_t, quad_down_t, core],
        scratch=[pltpu.VMEM((768, 512), F32)] * 2,
        micros=7, room=58,
    )
    next(late)
    send_c, send_d = chain.after((send_c, send_d))
    got_c, got_d = swap(send_c, "gyl", 0), swap(send_d, "gyl", 0)
    early = reduction(chain, [keep_c, got_c], [keep_d, got_d], firm_total=True)
    running = {"L": late, "E": early}
    done = {}

    def resume(name):
        if name in done:
            return
        try:
            next(running[name])
        except StopIteration as end:
            done[name] = end.value

    for name in "ELEELELEEELEL":
        resume(name)
    while "L" not in done:
        resume("L")
    (a_mine, a_other), (b_mine, b_other) = done["L"]
    g_res, g_ae, g_trip_bil, g_trip_up, g_quad_bil, g_quad_up, g_rad, g_ea, g_ad = call(
        late_outputs,
        [(2, 512, 512), (2, 256, 512), (64, 1024), (64, 512), (32, 1024), (32, 512), (3, 128, 512)]
        + [(2, 512, 256), (4, 256, 256)],
        [a_mine, a_other, b_mine, b_other, core],
        scratch=[pltpu.VMEM((896, 512), F32)] * 2
        + [pltpu.VMEM((768, 512), F32)] * 2
        + [pltpu.SemaphoreType.DMA((23,))],
        micros=0,
        room=12,
        inside=(),
    )
    chain.step(g_quad_up)
    while "E" not in done:
        resume("E")
    (c_mine, c_other), (d_mine, d_other) = done["E"]
    g_inputs, g_rad, g_trip_down, g_quad_down, g_tags = call(
        early_outputs,
        [(2, 512, 512), (5, 128, 512), (64, 512), (32, 512), (3, 256)],
        [c_mine, c_other, d_mine, d_other, g_rad, core],
        scratch=[pltpu.VMEM((384, 512), F32)] * 4
        + [pltpu.VMEM((3, 128, 512), F32), pltpu.SemaphoreType.DMA((18,))],
        micros=3,
        room=8,
        inside=(4,),
    )
    return (
        atoms_out,
        edges_out,
        energy_out,
        grad_atoms,
        grad_edges,
        g_inputs,
        g_rad,
        g_trip_down.T,
        g_trip_bil.T,
        g_trip_up,
        g_quad_down.T,
        g_quad_bil.T,
        g_quad_up,
        g_ae,
        g_res,
        g_ea,
        g_ad,
        g_tags,
    )


def solution(mesh):
    size = dict(mesh.shape)
    inner = Mesh(mesh.devices.reshape(size["gx"], size["gy"] // 2, 2, size["gz"]), ROWS)
    flat, columns, vector, whole = P(ROWS, None), P(None, ROWS), P(ROWS), P()
    placed = [flat, flat, columns] + [vector] * 3 + [flat] * 4 + [vector] + [whole] * 13 + [flat] * 3
    return jax.shard_map(
        per_device,
        mesh=inner,
        in_specs=tuple(placed),
        out_specs=tuple([flat] * 5 + [whole] * 13),
        check_vma=False,
    )
```
